32 devices in a mesh: batch: 4 (over x, core), ctx: 4 (over z), fsdp: 2 (over y).
Axes of the slice: x: 2, y: 2, z: 4, core: 2. Of those that a mesh axis runs over, the one named last changes fastest.
Arguments:
- layer_input: bfloat16 [8, 512, 1024], P(('batch', 'fsdp'), 'ctx'), may hold values from -6 to 6
- out_grad: bfloat16 [8, 512, 1024], P(('batch', 'fsdp'), 'ctx'), may hold values from -6 to 6
- span_order: int32 [4], replicated, may hold values from 0 to 3, each once
- inward: bfloat16 [1024, 3072], P('fsdp')
- inward_bias: bfloat16 [3072], P('fsdp'), may hold values from -3 to 3
- outward: bfloat16 [1024, 1024], P('fsdp'), may hold values from -1 to 1
- outward_bias: bfloat16 [1024], P('fsdp'), may hold values from -3 to 3
- expand: bfloat16 [1024, 4096], P('fsdp'), may hold values from -0.1875 to 0.1875
- expand_bias: bfloat16 [4096], P('fsdp'), may hold values from -3 to 3
- contract: bfloat16 [4096, 1024], P('fsdp'), may hold values from -0.09375 to 0.09375
- contract_bias: bfloat16 [1024], P('fsdp'), may hold values from -3 to 3
- first_gain: bfloat16 [1024], P('fsdp'), may hold values from 0.099609375 to 1.8984375
- first_bias: bfloat16 [1024], P('fsdp'), may hold values from -3 to 3
- second_gain: bfloat16 [1024], P('fsdp'), may hold values from 0.099609375 to 1.8984375
- second_bias: bfloat16 [1024], P('fsdp'), may hold values from -3 to 3
Outputs:
- output: bfloat16 [8, 512, 1024], P(('batch', 'fsdp'), 'ctx')
- input_grad: float32 [8, 512, 1024], P(('batch', 'fsdp'), 'ctx')
- inward_grad: float32 [1024, 3072], P('fsdp')
- inward_shift: float32 [3072], P('fsdp')
- outward_grad: float32 [1024, 1024], P('fsdp')
- outward_shift: float32 [1024], P('fsdp')
- expand_grad: float32 [1024, 4096], P('fsdp')
- expand_shift: float32 [4096], P('fsdp')
- contract_grad: float32 [4096, 1024], P('fsdp')
- contract_shift: float32 [1024], P('fsdp')
- first_scale: float32 [1024], P('fsdp')
- first_shift: float32 [1024], P('fsdp')
- second_scale: float32 [1024], P('fsdp')
- second_shift: float32 [1024], P('fsdp')
The draws below stay inside these ranges and needn't reach their ends.
Inputs may be any that keep to these rules, and one draw needn't show every extreme that they name: `span_order`: each value appears once.
All inputs are finite; a program needn't handle non-finite values.
Results may differ from the reference program's by a relative error of at most 0.012.
The reference program's roundings to bfloat16 on the way (of `soft_weights`, `context`, `activated`, `before_rows`, `context_grad`, `score_grad` and `projected_rows`) count: a program that leaves them out, or rounds other values in their place, can miss the bound.
Values may be sent and summed in bfloat16 or wider, within the bound.
A program may use at most 320 MiB of HBM per device.

```python
import math
import jax
import jax.numpy as jnp
from jax import lax

D = 1024
HEADS = 16
HEAD_DIM = 64
ROT = 16
FF = 4096
LENGTH = 512
SPAN = 64
SPANS = 8
SEQS = 8
N_CTX = 4


def draw_inward(key, part):
    drawn_draw = jax.random.normal(key, (D, 3 * D), jnp.float32) * (1.0 / D ** 0.5)
    return drawn_draw.astype(jnp.bfloat16)


def shard_levels(key, dims, cuts, smallest, top_value):
    gain, own = 1.0, jax.random.fold_in(key, 6)
    for position, shards_of in cuts:
        draws = jnp.exp(jax.random.uniform(jax.random.fold_in(own, position), (shards_of,), jnp.float32, smallest / len(cuts), top_value / len(cuts)))
        gain = gain * jnp.repeat(draws, dims[position] // shards_of).reshape([-1 if axis == position else 1 for axis in range(len(dims))])
    return gain


def bell_draw(own_key, dims, width, reach, cuts=(), held_as=jnp.bfloat16):
    drawn = width * jax.random.normal(own_key, dims, jnp.float32)
    if cuts:
        drawn = drawn * shard_levels(own_key, dims, cuts, -0.22, 0.18)
    return jnp.clip(drawn, -reach, reach).astype(held_as)


def setup_inputs(seed: int = 0) -> dict:
    seeds = jax.random.split(jax.random.key(seed), 16)
    return {
        "layer_input": bell_draw(seeds[0], (SEQS, LENGTH, D), 1.0, 6.0, ((0, 8), (1, 4))),
        "out_grad": bell_draw(seeds[1], (SEQS, LENGTH, D), 1.0, 6.0, ((0, 8), (1, 4))),
        "span_order": jax.random.permutation(seeds[2], N_CTX).astype(jnp.int32),
        "inward": draw_inward(jax.random.fold_in(seeds[15], 71), 0),
        "inward_bias": bell_draw(seeds[4], (3 * D,), 0.5, 3.0, ((0, 2),)),
        "outward": bell_draw(seeds[5], (D, D), (max(1, D * 16 // LENGTH)) ** -0.5, 1.0, ((0, 2),)),
        "outward_bias": bell_draw(seeds[6], (D,), 0.5, 3.0, ((0, 2),)),
        "expand": bell_draw(seeds[7], (D, FF), D ** -0.5, 0.1875, ((0, 2),)),
        "expand_bias": bell_draw(seeds[8], (FF,), 0.5, 3.0, ((0, 2),)),
        "contract": bell_draw(seeds[9], (FF, D), FF ** -0.5, 0.09375, ((0, 2),)),
        "contract_bias": bell_draw(seeds[10], (D,), 0.5, 3.0, ((0, 2),)),
        "first_gain": jnp.clip(1.0 + 0.18 * jax.random.normal(seeds[11], (D,), jnp.float32), 0.099609375, 1.8984375).astype(jnp.bfloat16),
        "first_bias": bell_draw(seeds[12], (D,), 0.5, 3.0, ((0, 2),)),
        "second_gain": jnp.clip(1.0 + 0.18 * jax.random.normal(seeds[13], (D,), jnp.float32), 0.099609375, 1.8984375).astype(jnp.bfloat16),
        "second_bias": bell_draw(seeds[14], (D,), 0.5, 3.0, ((0, 2),)),
    }


EPSILON = 1e-05
ROTARY_BASE = 10000.0
MASKED = -1e+30
HALF_ROOT = 0.7071067811865476
NORMAL_PEAK = 0.3989422804014327

def norm_forward(values, factor, offset):
    center = values - lax.optimization_barrier(jnp.mean(values, axis=-1, keepdims=True))
    inverse = lax.rsqrt(lax.optimization_barrier(jnp.mean(center * center, axis=-1, keepdims=True)) + EPSILON)
    normed = center * inverse
    return (normed * factor + offset, normed, inverse)

def norm_backward(upstream, normed, inverse, factor):
    scaled = upstream * factor
    middle = lax.optimization_barrier(jnp.mean(scaled, axis=-1, keepdims=True))
    coupled = lax.optimization_barrier(jnp.mean(scaled * normed, axis=-1, keepdims=True))
    result = inverse * (scaled - middle - normed * coupled)
    return (result, lax.optimization_barrier(jnp.sum(upstream * normed, axis=0)), lax.optimization_barrier(jnp.sum(upstream, axis=0)))

def gelu_value(before):
    return 0.5 * before * (1.0 + lax.erf(before * HALF_ROOT))

def gelu_slope(before):
    return 0.5 * (1.0 + lax.erf(before * HALF_ROOT)) + before * jnp.exp(-0.5 * before * before) * NORMAL_PEAK

def rotary_tables(positions):
    half_rot = ROT // 2
    angular = jnp.exp(jnp.arange(half_rot, dtype=jnp.float32) * (-2.0 * math.log(ROTARY_BASE) / ROT))
    angles = positions.astype(jnp.float32)[:, None] * angular[None, :]
    angles = jnp.concatenate([angles, angles], axis=1)
    return (jnp.cos(angles), jnp.sin(angles))

def rotate(tensor, cosine, sine_table):
    half_rot = ROT // 2
    leading_part = tensor[..., :ROT]
    turned = jnp.concatenate([-leading_part[..., half_rot:], leading_part[..., :half_rot]], axis=-1)
    rotated = leading_part * cosine[:, None, :] + turned * sine_table[:, None, :]
    return jnp.concatenate([rotated, tensor[..., ROT:]], axis=-1)

def unrotate(tensor, cosine, sine_table):
    half_rot = ROT // 2
    leading_part = tensor[..., :ROT]
    weighted = leading_part * sine_table[:, None, :]
    turned = jnp.concatenate([weighted[..., half_rot:], -weighted[..., :half_rot]], axis=-1)
    return jnp.concatenate([leading_part * cosine[:, None, :] + turned, tensor[..., ROT:]], axis=-1)

def reference(layer_input, out_grad, span_order, inward, inward_bias, outward, outward_bias, expand, expand_bias, contract, contract_bias, first_gain, first_bias, second_gain, second_bias):
    slot_index = jnp.arange(LENGTH, dtype=jnp.int32)
    owners = slot_index // (2 * SPAN)
    leading = span_order[owners].astype(jnp.int32)
    picked = jnp.where(slot_index // SPAN % 2 == 0, leading, SPANS - 1 - leading)
    places = (picked * SPAN + slot_index % SPAN).astype(jnp.int32)
    cosine, sine_table = rotary_tables(places)
    allowed = places[None, :] <= places[:, None]
    score_scale = 1.0 / math.sqrt(HEAD_DIM)
    gain_first = first_gain.astype(jnp.float32)
    offset_first = first_bias.astype(jnp.float32)
    gain_second = second_gain.astype(jnp.float32)
    offset_second = second_bias.astype(jnp.float32)
    inward_offset = inward_bias.astype(jnp.float32)
    outward_offset = outward_bias.astype(jnp.float32)
    expand_offset = expand_bias.astype(jnp.float32)
    contract_offset = contract_bias.astype(jnp.float32)

    def head_scores(query_head, key_head):
        scores = jnp.dot(query_head, key_head.T, preferred_element_type=jnp.float32) * score_scale
        return jnp.where(allowed, scores, MASKED)

    def head_forward(pieces):
        query_head, key_head, value_head = pieces
        scores = head_scores(query_head, key_head)
        row_peak = lax.optimization_barrier(jnp.max(scores, axis=1, keepdims=True))
        log_total = row_peak + jnp.log(lax.optimization_barrier(jnp.sum(jnp.exp(scores - row_peak), axis=1, keepdims=True)))
        soft_weights = jnp.exp(scores - log_total).astype(jnp.bfloat16)
        context = jnp.dot(soft_weights, value_head, preferred_element_type=jnp.float32).astype(jnp.bfloat16)
        return (context, log_total[:, 0])

    def head_backward(pieces):
        query_head, key_head, value_head, log_row, delta_row, grad_head = pieces
        scores = head_scores(query_head, key_head)
        exact_probs = jnp.exp(scores - log_row[:, None])
        soft_weights = exact_probs.astype(jnp.bfloat16)
        value_grad = jnp.dot(soft_weights.T, grad_head, preferred_element_type=jnp.float32)
        probs_grad = jnp.dot(grad_head, value_head.T, preferred_element_type=jnp.float32)
        score_grad = (exact_probs * (probs_grad - delta_row[:, None]) * score_scale).astype(jnp.bfloat16)
        query_grad = jnp.dot(score_grad, key_head, preferred_element_type=jnp.float32)
        key_grad = jnp.dot(score_grad.T, query_head, preferred_element_type=jnp.float32)
        return (query_grad, key_grad, value_grad)

    def one_sequence(running_sums, pieces):
        input_rows, grad_rows = pieces
        hidden = input_rows.astype(jnp.float32)
        first_float, first_normed, first_inverse = norm_forward(hidden, gain_first, offset_first)
        first_rows = first_float.astype(jnp.bfloat16)
        second_float, second_normed, second_inverse = norm_forward(hidden, gain_second, offset_second)
        second_rows = second_float.astype(jnp.bfloat16)
        projected = jnp.dot(first_rows, inward, preferred_element_type=jnp.float32) + inward_offset
        queries = rotate(projected[:, :D].reshape(LENGTH, HEADS, HEAD_DIM), cosine, sine_table).astype(jnp.bfloat16)
        keys_all = rotate(projected[:, D:2 * D].reshape(LENGTH, HEADS, HEAD_DIM), cosine, sine_table).astype(jnp.bfloat16)
        values_all = projected[:, 2 * D:].astype(jnp.bfloat16).reshape(LENGTH, HEADS, HEAD_DIM)
        query_heads = jnp.swapaxes(queries, 0, 1)
        key_heads = jnp.swapaxes(keys_all, 0, 1)
        value_heads = jnp.swapaxes(values_all, 0, 1)
        context, log_total = lax.map(head_forward, (query_heads, key_heads, value_heads))
        context_rows = jnp.swapaxes(context, 0, 1).reshape(LENGTH, D)
        attended = jnp.dot(context_rows, outward, preferred_element_type=jnp.float32) + outward_offset
        before = jnp.dot(second_rows, expand, preferred_element_type=jnp.float32) + expand_offset
        activated = gelu_value(before).astype(jnp.bfloat16)
        mixed = jnp.dot(activated, contract, preferred_element_type=jnp.float32) + contract_offset
        result = (hidden + attended + mixed).astype(jnp.bfloat16)
        grad_float = grad_rows.astype(jnp.float32)
        bias_total = lax.optimization_barrier(jnp.sum(grad_float, axis=0))
        outward_delta = jnp.dot(context_rows.T, grad_rows, preferred_element_type=jnp.float32)
        contract_delta = jnp.dot(activated.T, grad_rows, preferred_element_type=jnp.float32)
        before_grad = jnp.dot(grad_rows, contract.T, preferred_element_type=jnp.float32) * gelu_slope(before)
        expand_sum = lax.optimization_barrier(jnp.sum(before_grad, axis=0))
        before_rows = before_grad.astype(jnp.bfloat16)
        expand_delta = jnp.dot(second_rows.T, before_rows, preferred_element_type=jnp.float32)
        second_back = jnp.dot(before_rows, expand.T, preferred_element_type=jnp.float32)
        second_input, second_scale, second_shift = norm_backward(second_back, second_normed, second_inverse, gain_second)
        context_grad = jnp.dot(grad_rows, outward.T, preferred_element_type=jnp.float32).astype(jnp.bfloat16)
        grad_heads = jnp.swapaxes(context_grad.reshape(LENGTH, HEADS, HEAD_DIM), 0, 1)
        delta_rows = lax.optimization_barrier(jnp.sum(grad_heads.astype(jnp.float32) * context.astype(jnp.float32), axis=-1))
        query_grad, key_grad, value_grad = lax.map(head_backward, (query_heads, key_heads, value_heads, log_total, delta_rows, grad_heads))
        query_mine = unrotate(jnp.swapaxes(query_grad, 0, 1), cosine, sine_table).reshape(LENGTH, D)
        key_mine = unrotate(jnp.swapaxes(key_grad, 0, 1), cosine, sine_table).reshape(LENGTH, D)
        value_mine = jnp.swapaxes(value_grad, 0, 1).reshape(LENGTH, D)
        projected_grad = jnp.concatenate([query_mine, key_mine, value_mine], axis=1)
        inward_sum = lax.optimization_barrier(jnp.sum(projected_grad, axis=0))
        projected_rows = projected_grad.astype(jnp.bfloat16)
        inward_delta = jnp.dot(first_rows.T, projected_rows, preferred_element_type=jnp.float32)
        first_back = jnp.dot(projected_rows, inward.T, preferred_element_type=jnp.float32)
        first_input, first_scale, first_shift = norm_backward(first_back, first_normed, first_inverse, gain_first)
        input_delta = grad_float + first_input + second_input
        deltas = (inward_delta, inward_sum, outward_delta, bias_total, expand_delta, expand_sum, contract_delta, bias_total, first_scale, first_shift, second_scale, second_shift)
        running_sums = tuple((total + member for total, member in zip(running_sums, deltas)))
        return (running_sums, (result, input_delta))
    shapes = (inward.shape, inward_bias.shape, outward.shape, outward_bias.shape, expand.shape, expand_bias.shape, contract.shape, contract_bias.shape, first_gain.shape, first_bias.shape, second_gain.shape, second_bias.shape)
    initial = tuple((jnp.zeros(shape_entry, jnp.float32) for shape_entry in shapes))
    final_sums, (outputs, input_grads) = lax.scan(one_sequence, initial, (layer_input, out_grad))
    return (outputs, input_grads, final_sums[0], final_sums[1], final_sums[2], final_sums[3], final_sums[4], final_sums[5], final_sums[6], final_sums[7], final_sums[8], final_sums[9], final_sums[10], final_sums[11])
```

```python
import math

import jax
import jax.numpy as jnp
from jax import lax
from jax.sharding import PartitionSpec as P

HEAD_DIM = 64
ROT = 16

EPSILON = 1e-05
ROTARY_BASE = 10000.0
MASKED = -1e30
HALF_ROOT = 0.7071067811865476
NORMAL_PEAK = 0.3989422804014327
PLANE = ("batch", "fsdp")


def dot(left, right, contract=((1,), (0,))):
    return lax.dot_general(left, right, (contract, ((), ())), preferred_element_type=jnp.float32)


def normalize(values):
    center = values - jnp.mean(values, axis=-1, keepdims=True)
    inverse = lax.rsqrt(jnp.mean(center * center, axis=-1, keepdims=True) + EPSILON)
    return (center * inverse, inverse)


def norm_backward(upstream, normed, inverse, factor):
    scaled = upstream * factor
    middle = jnp.mean(scaled, axis=-1, keepdims=True)
    coupled = jnp.mean(scaled * normed, axis=-1, keepdims=True)
    result = inverse * (scaled - middle - normed * coupled)
    return (result, jnp.sum(upstream * normed, axis=0), jnp.sum(upstream, axis=0))


def slot_positions(span_order, first_slot, slot_count, span_size):
    slot_index = first_slot + jnp.arange(slot_count, dtype=jnp.int32)
    owners = slot_index // (2 * span_size)
    places = jnp.arange(span_order.shape[0], dtype=jnp.int32)
    leading = jnp.sum(jnp.where(owners[:, None] == places[None, :], span_order[None, :], 0), axis=1)
    spans = 2 * span_order.shape[0]
    picked = jnp.where(slot_index // span_size % 2 == 0, leading, spans - 1 - leading)
    return picked * span_size + slot_index % span_size


def rotary_tables(positions):
    half_rot = ROT // 2
    angular = jnp.exp(
        jnp.arange(half_rot, dtype=jnp.float32) * (-2.0 * math.log(ROTARY_BASE) / ROT)
    )
    angles = positions.astype(jnp.float32)[:, None] * angular[None, :]
    angles = jnp.concatenate([angles, angles], axis=1)
    return (jnp.cos(angles), jnp.sin(angles))


def rotate(tensor, cosine, sine_table):
    half_rot = ROT // 2
    leading_part = tensor[..., :ROT]
    turned = jnp.concatenate([-leading_part[..., half_rot:], leading_part[..., :half_rot]], axis=-1)
    rotated = leading_part * cosine[:, None, :] + turned * sine_table[:, None, :]
    return jnp.concatenate([rotated, tensor[..., ROT:]], axis=-1)


def unrotate(tensor, cosine, sine_table):
    half_rot = ROT // 2
    leading_part = tensor[..., :ROT]
    weighted = leading_part * sine_table[:, None, :]
    turned = jnp.concatenate([weighted[..., half_rot:], -weighted[..., :half_rot]], axis=-1)
    return jnp.concatenate([leading_part * cosine[:, None, :] + turned, tensor[..., ROT:]], axis=-1)


def attention(mixed, place, cosine, sine_table, heads):
    sequences, length, _ = mixed.shape
    parts = mixed.reshape(sequences, length, 4, heads, HEAD_DIM)
    queries, keys, values, grads = (parts[:, :, i] for i in range(4))
    scale = 1.0 / math.sqrt(HEAD_DIM)
    scores = jnp.einsum("sqhd,skhd->shqk", queries, keys, preferred_element_type=jnp.float32)
    allowed = place[None, :] <= place[:, None]
    scores = jnp.where(allowed, scores * scale, MASKED)
    peak = jnp.max(scores, axis=-1, keepdims=True)
    log_total = peak + jnp.log(jnp.sum(jnp.exp(scores - peak), axis=-1, keepdims=True))
    probs = jnp.exp(scores - log_total)
    soft = probs.astype(jnp.bfloat16)
    context = jnp.einsum("shqk,skhd->sqhd", soft, values, preferred_element_type=jnp.float32)
    context = context.astype(jnp.bfloat16)
    delta = jnp.einsum(
        "sqhd,sqhd->shq", grads.astype(jnp.float32), context.astype(jnp.float32)
    )
    value_grad = jnp.einsum("shqk,sqhd->skhd", soft, grads, preferred_element_type=jnp.float32)
    probs_grad = jnp.einsum("sqhd,skhd->shqk", grads, values, preferred_element_type=jnp.float32)
    score_grad = (probs * (probs_grad - delta[..., None]) * scale).astype(jnp.bfloat16)
    query_grad = jnp.einsum("shqk,skhd->sqhd", score_grad, keys, preferred_element_type=jnp.float32)
    key_grad = jnp.einsum("shqk,sqhd->skhd", score_grad, queries, preferred_element_type=jnp.float32)
    query_grad = unrotate(query_grad, cosine, sine_table)
    key_grad = unrotate(key_grad, cosine, sine_table)
    back = jnp.stack([query_grad, key_grad, value_grad], axis=2)
    shift = jnp.sum(back, axis=(0, 1)).reshape(-1)
    full = jnp.concatenate([context[:, :, None], back.astype(jnp.bfloat16)], axis=2)
    return (full.reshape(sequences, length, 4 * heads * HEAD_DIM), shift)


def body(
    layer_input,
    out_grad,
    span_order,
    inward,
    inward_bias,
    outward,
    outward_bias,
    expand,
    expand_bias,
    contract,
    contract_bias,
    first_gain,
    first_bias,
    second_gain,
    second_bias,
):
    batch_count, fsdp_count = (lax.axis_size("batch"), lax.axis_size("fsdp"))
    context_count = lax.axis_size("ctx")
    context_index = lax.axis_index("ctx")
    batch_index, fsdp_index = (lax.axis_index("batch"), lax.axis_index("fsdp"))
    plane = batch_count * fsdp_count
    tokens, width = layer_input.shape[1:]
    hidden_units = expand.shape[1]
    head_cols = width // plane
    unit_cols = hidden_units // plane
    heads = head_cols // HEAD_DIM
    length = tokens * context_count
    span_size = tokens // 2
    own_sequences = plane // context_count

    def full_vectors(*vectors):
        sizes = [v.shape[0] for v in vectors]
        gathered = lax.all_gather(jnp.concatenate(vectors), "fsdp")
        out, start = ([], 0)
        for size in sizes:
            out.append(gathered[:, start : start + size].reshape(-1).astype(jnp.float32))
            start += size
        return out

    (
        inward_offset,
        outward_offset,
        expand_offset,
        contract_offset,
        gain_first,
        offset_first,
        gain_second,
        offset_second,
    ) = full_vectors(
        inward_bias,
        outward_bias,
        expand_bias,
        contract_bias,
        first_gain,
        first_bias,
        second_gain,
        second_bias,
    )

    def chunk(array, cols):
        rows = array.shape[0]
        parts = array.reshape(rows, -1, fsdp_count, batch_count, cols)
        mine = lax.dynamic_index_in_dim(parts, batch_index, 3, keepdims=False)
        return mine.transpose(2, 0, 1, 3).reshape(fsdp_count, rows, -1)

    to_send = jnp.concatenate([chunk(inward, head_cols), chunk(expand, unit_cols)], axis=2)
    weights = lax.all_to_all(to_send, "fsdp", 0, 0).reshape(width, -1)
    inward_cols = weights[:, : 3 * head_cols]
    expand_cols = weights[:, 3 * head_cols :]
    outward_rows = lax.dynamic_slice_in_dim(outward, batch_index * head_cols, head_cols, 0)
    contract_rows = lax.dynamic_slice_in_dim(contract, batch_index * unit_cols, unit_cols, 0)
    plane_index = fsdp_index * batch_count + batch_index
    inward_shift_in = lax.dynamic_index_in_dim(
        inward_offset.reshape(3, plane, head_cols), plane_index, 1, keepdims=False
    ).reshape(-1)
    expand_shift_in = lax.dynamic_slice_in_dim(expand_offset, plane_index * unit_cols, unit_cols, 0)

    pair = jnp.stack([layer_input[0], out_grad[0]])
    pair_all = lax.all_gather(pair, PLANE, axis=1, tiled=True)
    grads_all = pair_all[1]
    normed, _ = normalize(pair_all[0].astype(jnp.float32))
    first_rows = (normed * gain_first + offset_first).astype(jnp.bfloat16)
    second_rows = (normed * gain_second + offset_second).astype(jnp.bfloat16)

    local_place = slot_positions(span_order, context_index * tokens, tokens, span_size)
    cosine, sine_table = rotary_tables(local_place)
    cosine_plane = jnp.tile(cosine, (plane, 1))
    sine_plane = jnp.tile(sine_table, (plane, 1))
    projected = dot(first_rows, inward_cols) + inward_shift_in
    projected = projected.reshape(plane * tokens, 3 * heads, HEAD_DIM)
    turned = rotate(projected[:, : 2 * heads], cosine_plane, sine_plane)
    context_grad = dot(grads_all, outward_rows, ((1,), (1,)))
    mixed = jnp.concatenate(
        [
            turned.reshape(plane * tokens, -1),
            projected[:, 2 * heads :].reshape(plane * tokens, -1),
            context_grad,
        ],
        axis=1,
    ).astype(jnp.bfloat16)
    mixed = mixed.reshape(context_count, own_sequences, tokens, 4 * head_cols)
    mixed = lax.all_to_all(mixed, "ctx", 0, 0)
    mixed = mixed.transpose(1, 0, 2, 3).reshape(own_sequences, length, 4 * head_cols)
    place = slot_positions(span_order, 0, length, span_size)
    cosine_all, sine_all = rotary_tables(place)
    back, inward_sum = attention(mixed, place, cosine_all, sine_all, heads)
    back = back.reshape(own_sequences, context_count, tokens, 4 * head_cols).transpose(1, 0, 2, 3)
    back = lax.all_to_all(back, "ctx", 0, 0).reshape(plane * tokens, 4 * head_cols)
    context_rows = back[:, :head_cols]
    projected_rows = back[:, head_cols:]

    before = dot(second_rows, expand_cols) + expand_shift_in
    tail = 1.0 + lax.erf(before * HALF_ROOT)
    activated = (0.5 * before * tail).astype(jnp.bfloat16)
    slope = 0.5 * tail + before * jnp.exp(-0.5 * before * before) * NORMAL_PEAK
    before_grad = dot(grads_all, contract_rows, ((1,), (1,))) * slope
    expand_sum = jnp.sum(before_grad, axis=0)
    before_rows = before_grad.astype(jnp.bfloat16)

    expand_delta = dot(second_rows, before_rows, ((0,), (0,)))
    contract_delta = dot(activated, grads_all, ((0,), (0,)))
    inward_delta = dot(first_rows, projected_rows, ((0,), (0,)))
    outward_delta = dot(context_rows, grads_all, ((0,), (0,)))

    out_part = dot(activated, contract_rows) + dot(context_rows, outward_rows)
    second_part = dot(before_rows, expand_cols, ((1,), (1,)))
    first_part = dot(projected_rows, inward_cols, ((1,), (1,)))
    stacked = jnp.stack([out_part, second_part, first_part], axis=1).astype(jnp.bfloat16)
    mine = lax.psum_scatter(stacked, PLANE, scatter_dimension=0, tiled=True).astype(jnp.float32)

    hidden = layer_input[0].astype(jnp.float32)
    grad_float = out_grad[0].astype(jnp.float32)
    normed_mine, inverse_mine = normalize(hidden)
    result = (hidden + (mine[:, 0] + outward_offset) + contract_offset).astype(jnp.bfloat16)
    second_input, second_scale, second_shift = norm_backward(
        mine[:, 1], normed_mine, inverse_mine, gain_second
    )
    first_input, first_scale, first_shift = norm_backward(
        mine[:, 2], normed_mine, inverse_mine, gain_first
    )
    input_delta = grad_float + first_input + second_input

    columns = jnp.concatenate([inward_delta, expand_delta], axis=1).astype(jnp.bfloat16)
    rows = jnp.concatenate([outward_delta, contract_delta], axis=0).astype(jnp.bfloat16)
    columns, rows = lax.psum((columns, rows), "ctx")
    half = width // fsdp_count
    columns = lax.all_to_all(columns.reshape(fsdp_count, half, -1), "fsdp", 0, 0)
    columns = lax.all_gather(columns, "batch")
    rows = lax.all_gather(rows, "batch")
    columns = columns.transpose(2, 1, 0, 3).astype(jnp.float32)
    inward_total = columns[..., : 3 * head_cols].reshape(
        half, fsdp_count, batch_count, 3, head_cols
    )
    inward_total = inward_total.transpose(0, 3, 1, 2, 4).reshape(half, 3 * width)
    expand_total = columns[..., 3 * head_cols :].reshape(half, hidden_units)
    rows = rows.astype(jnp.float32)
    outward_total = rows[:, :head_cols].reshape(half, width)
    contract_total = rows[:, head_cols:].reshape(-1, width)

    inward_wide = jnp.zeros((3, plane, head_cols), jnp.float32)
    inward_wide = lax.dynamic_update_index_in_dim(
        inward_wide, inward_sum.reshape(3, head_cols), plane_index, 1
    ).reshape(-1)
    expand_wide = jnp.zeros((plane, unit_cols), jnp.float32)
    expand_wide = lax.dynamic_update_index_in_dim(expand_wide, expand_sum, plane_index, 0).reshape(-1)
    bias_total = jnp.sum(grad_float, axis=0)
    vectors = [
        inward_wide,
        bias_total,
        expand_wide,
        first_scale,
        first_shift,
        second_scale,
        second_shift,
    ]
    whole = lax.psum(jnp.concatenate(vectors), ("batch", "ctx", "fsdp"))
    halves, start = ([], 0)
    for vector in vectors:
        part = vector.shape[0] // fsdp_count
        halves.append(lax.dynamic_slice_in_dim(whole, start + fsdp_index * part, part, 0))
        start += vector.shape[0]
    return (
        result[None],
        input_delta[None],
        inward_total,
        halves[0],
        outward_total,
        halves[1],
        expand_total,
        halves[2],
        contract_total,
        halves[1],
        halves[3],
        halves[4],
        halves[5],
        halves[6],
    )


def solution(mesh):
    rows = P(PLANE, "ctx", None)
    matrix, vector = (P("fsdp", None), P("fsdp"))
    in_specs = (rows, rows, P()) + (matrix, vector) * 4 + (vector,) * 4
    out_specs = (rows, rows) + (matrix, vector) * 4 + (vector,) * 4
    return jax.shard_map(body, mesh=mesh, in_specs=in_specs, out_specs=out_specs, check_vma=False)
```

```python
import functools
import math

import jax
import jax.numpy as jnp
from jax import lax
from jax.experimental import pallas as pl
from jax.experimental.pallas import tpu as pltpu
from jax.sharding import PartitionSpec as P

HEAD_DIM = 64
ROT = 16

EPSILON = 1e-05
ROTARY_BASE = 10000.0
MASKED = -1e30
HALF_ROOT = 0.7071067811865476
NORMAL_PEAK = 0.3989422804014327
PLANE = ("batch", "fsdp")


MESH = pl.DeviceIdType.MESH
CORES = 2
VMEM_LIMIT = 56 * 2**20


def here():
    return (lax.axis_index("batch"), lax.axis_index("ctx"), lax.axis_index("fsdp"))


def swapped(index, step):
    return index + step * (1 - 2 * (index // step % 2))


def greet(partners):
    barrier = pltpu.get_barrier_semaphore()
    for partner in partners:
        pl.semaphore_signal(barrier, inc=1, device_id=partner, device_id_type=MESH)
    pl.semaphore_wait(barrier, len(partners))


def remote(src, dst, send, recv, target):
    return pltpu.make_async_remote_copy(
        src_ref=src,
        dst_ref=dst,
        send_sem=send,
        recv_sem=recv,
        device_id=target,
        device_id_type=MESH,
    )


def total_kernel(
    sizes,
    other_rows,
    piece,
    part_ref,
    vector_ref,
    out_ref,
    vector_out,
    final,
    reduced,
    vector_in,
    vector_sum,
    out_sem,
    reduce_sems,
    back_sems,
    row_sems,
    chip_sems,
    core_sems,
    vector_sems,
):
    batch_count, context_count, fsdp_count = sizes
    b, z, y = here()
    chips = batch_count // CORES
    core = b % CORES
    chip = b // CORES
    rows = part_ref.shape[0]
    steps = rows // 2 // piece
    other_steps = other_rows // 2 // piece
    last = context_count - 1
    sibling = (chip * CORES + (1 - core), z, y)
    across = (b, z, 1 - y)
    peers = [((chip + d) % chips * CORES + core, z, y) for d in range(1, chips)]
    sources = [(chip + chips - d) % chips * CORES + core for d in range(1, chips)]
    stages = []
    step = 1
    while step < batch_count:
        stages.append((swapped(b, step), z, y))
        step *= 2
    stages.append(across)
    step = 1
    while step < context_count:
        stages.append((b, swapped(z, step), y))
        step *= 2
    ring = [(b, (z + 1) % context_count, y), (b, (z + last) % context_count, y)]
    greet(stages + ring + peers + [(s, z, y) for s in sources])

    def vector_copy(i):
        source = vector_ref if i == 0 else vector_sum.at[i - 1]
        return remote(
            source, vector_in.at[i], vector_sems.at[0, i], vector_sems.at[1, i], stages[i]
        )

    def place(half, k):
        first = (half * other_steps + k) * piece
        second = other_rows + (half * (steps - other_steps) + k - other_steps) * piece
        is_second = jnp.minimum(k // other_steps, 1)
        return pl.multiple_of(first * (1 - is_second) + second * is_second, piece)

    def slot_of(k):
        is_second = jnp.minimum(k // other_steps, 1)
        return batch_count * (1 - is_second) + b * is_second

    def rows_at(ref, row):
        return ref.at[pl.ds(row, piece), :]

    def final_at(slot, row):
        return final.at[slot, pl.ds(row, piece), :]

    def sem(sems, *index):
        return (sems.at[(0, *index)], sems.at[(1, *index)])

    def back_copy(half, k, target):
        at = final_at(slot_of(k), place(half, k))
        return remote(at, at, *sem(back_sems, half, k), target)

    def row_copy(half, k):
        row = place(half, k)
        source = final_at(batch_count, row)
        return remote(source, final_at(b, row), *sem(row_sems, half, k), across)

    def chip_copy(d, half, k, slot):
        at = final_at(slot, place(half, k))
        return remote(at, at, *sem(chip_sems, d, half, k), peers[d])

    def core_copy(d, half, k, slot):
        at = final_at(slot, place(half, k))
        return remote(at, at, *sem(core_sems, d, half, k), sibling)

    def spread(half, k):
        for d in range(chips - 1):
            chip_copy(d, half, k, b).start()
        core_copy(0, half, k, b).start()

    def finish(half, k, position, behind):
        @pl.when(position > 0)
        def _():
            back_copy(half, k, behind).start()

        @pl.when(k < other_steps)
        def _():
            row_copy(half, k).start()

        @pl.when(k >= other_steps)
        def _():
            spread(half, k)

    vector_copy(0).start()

    def slot_step(t, carry):
        for half in range(2):
            position = z if half == 0 else last - z
            ahead = (b, (z + 1 if half == 0 else z + last) % context_count, y)
            behind = (b, (z + last if half == 0 else z + 1) % context_count, y)
            k = t - position

            @pl.when((k >= 0) & (k < steps))
            def _():
                row = place(half, k)
                to_next = remote(
                    rows_at(reduced, row), rows_at(reduced, row), *sem(reduce_sems, half, k), ahead
                )

                @pl.when(position == 0)
                def _():
                    remote(
                        rows_at(part_ref, row),
                        rows_at(reduced, row),
                        *sem(reduce_sems, half, k),
                        ahead,
                    ).start()

                @pl.when(position > 0)
                def _():
                    to_next.wait_recv()
                    mine = part_ref[pl.ds(row, piece), :].astype(jnp.float32)
                    came = reduced[pl.ds(row, piece), :].astype(jnp.float32)
                    summed = (mine + came).astype(part_ref.dtype)

                    @pl.when(position < last)
                    def _():
                        reduced[pl.ds(row, piece), :] = summed
                        to_next.start()

                    @pl.when(position == last)
                    def _():
                        final[slot_of(k), pl.ds(row, piece), :] = summed
                        finish(half, k, position, behind)

            k_back = t - 2 * last + position

            @pl.when((position < last) & (k_back >= 0) & (k_back < steps))
            def _():
                back_copy(half, k_back, behind).wait_recv()
                finish(half, k_back, position, behind)

            k_row = t - 2 * last + position - 1

            @pl.when((k_row >= 0) & (k_row < other_steps))
            def _():
                row_copy(half, k_row).wait_recv()
                spread(half, k_row)

            @pl.when((k_row >= other_steps) & (k_row < steps))
            def _():
                for d in range(chips - 1):
                    chip_copy(d, half, k_row, sources[d]).wait_recv()
                    core_copy(1 + d, half, k_row, sources[d]).start()

            k_chip = k_row - 2

            @pl.when((k_chip >= 0) & (k_chip < other_steps))
            def _():
                for d in range(chips - 1):
                    chip_copy(d, half, k_chip, sources[d]).wait_recv()
                    core_copy(1 + d, half, k_chip, sources[d]).start()

        for i in range(len(stages)):

            @pl.when(t == 2 * i + 1)
            def _():
                vector_copy(i).wait_recv()
                before = vector_ref[...] if i == 0 else vector_sum[i - 1]
                vector_sum[i] = before + vector_in[i]
                if i + 1 < len(stages):
                    vector_copy(i + 1).start()

        return carry

    slots = max(steps + 2 * last + 1, other_steps + 2 * last + 3, 2 * len(stages)) + 1
    lax.fori_loop(0, slots, slot_step, 0)
    vector_out[...] = vector_sum[len(stages) - 1]

    def drain(k, carry):
        for half in range(2):
            position = z if half == 0 else last - z
            for d in range(chips):
                core_copy(d, half, k, b).wait_recv()
                core_copy(d, half, k, b).wait_send()
                if d:
                    chip_copy(d - 1, half, k, b).wait_send()

            @pl.when(position < last)
            def _():
                row = place(half, k)
                remote(
                    rows_at(reduced, row), rows_at(reduced, row), *sem(reduce_sems, half, k), across
                ).wait_send()

            @pl.when(position > 0)
            def _():
                back_copy(half, k, across).wait_send()

            @pl.when(k < other_steps)
            def _():
                row_copy(half, k).wait_send()

        return carry

    lax.fori_loop(0, steps, drain, 0)
    for i in range(len(stages)):
        vector_copy(i).wait_send()
    copy = pltpu.make_async_copy(final.at[pl.ds(0, batch_count)], out_ref, out_sem)
    copy.start()
    copy.wait()


def total_sums(part, vector, other_rows):
    sizes = tuple(lax.axis_size(name) for name in ("batch", "ctx", "fsdp"))
    batch_count, context_count, fsdp_count = sizes
    rows, width = part.shape
    piece = math.gcd(math.gcd(other_rows // 2, (rows - other_rows) // 2), 32)
    steps = rows // 2 // piece
    other_steps = other_rows // 2 // piece
    chips = batch_count // CORES
    stage_count = (batch_count * context_count * fsdp_count).bit_length() - 1
    dma = pltpu.SemaphoreType.DMA
    return pl.pallas_call(
        functools.partial(total_kernel, sizes, other_rows, piece),
        out_shape=(
            jax.ShapeDtypeStruct((batch_count, rows, width), part.dtype),
            jax.ShapeDtypeStruct(vector.shape, vector.dtype),
        ),
        in_specs=[pl.BlockSpec(memory_space=pltpu.VMEM)] * 2,
        out_specs=(pl.BlockSpec(memory_space=pl.ANY), pl.BlockSpec(memory_space=pltpu.VMEM)),
        scratch_shapes=[
            pltpu.VMEM((batch_count + 1, rows, width), part.dtype),
            pltpu.VMEM((rows, width), part.dtype),
            pltpu.VMEM((stage_count,) + vector.shape, vector.dtype),
            pltpu.VMEM((stage_count,) + vector.shape, vector.dtype),
            dma,
            dma((2, 2, steps)),
            dma((2, 2, steps)),
            dma((2, 2, other_steps)),
            dma((2, chips - 1, 2, steps)),
            dma((2, chips, 2, steps)),
            dma((2, stage_count)),
        ],
        name="total_sums",
        compiler_params=pltpu.CompilerParams(
            collective_id=0, has_side_effects=True, vmem_limit_bytes=VMEM_LIMIT
        ),
    )(part, vector)


def widen_kernel(cols, unit, turn_ref, all_ref, inward_ref, outward_ref, expand_ref, contract_ref,
                 held, inward, outward, expand, contract, in_sems, out_sems):
    batch_count, rows, width = all_ref.shape
    half = inward_ref.shape[0]
    unit_rows, unit_blocks = (unit * half // width, width // unit)
    head_rows, head_blocks = (cols * half // width, width // cols)
    slot_rows = unit_rows + 3 * head_rows
    y = turn_ref[0]

    def load(b):
        return pltpu.make_async_copy(all_ref.at[b], held.at[b % 2], in_sems.at[b % 2])

    def stores(b):
        at = b % 2
        sems = iter(range(2 + 2 * 4))
        out = [
            pltpu.make_async_copy(
                outward.at[at],
                outward_ref.at[pl.ds(b * cols, cols), :],
                out_sems.at[at, next(sems)],
            ),
            pltpu.make_async_copy(
                contract.at[at],
                contract_ref.at[pl.ds(b * unit, unit), :],
                out_sems.at[at, next(sems)],
            ),
        ]
        for s in range(2):
            owner = y if s else 1 - y
            column = pl.multiple_of((owner * batch_count + b) * unit, unit)
            out.append(
                pltpu.make_async_copy(
                    expand.at[at, s],
                    expand_ref.at[:, pl.ds(column, unit)],
                    out_sems.at[at, next(sems)],
                )
            )
            for i in range(3):
                column = pl.multiple_of(i * width + (owner * batch_count + b) * cols, cols)
                out.append(
                    pltpu.make_async_copy(
                        inward.at[at, s, i],
                        inward_ref.at[:, pl.ds(column, cols)],
                        out_sems.at[at, next(sems)],
                    )
                )
        return out

    load(0).start()

    def step(b, carry):
        at = b % 2
        load(b).wait()

        @pl.when(b + 1 < batch_count)
        def _():
            load(b + 1).start()

        @pl.when(b >= 2)
        def _():
            for copy in stores(b - 2):
                copy.wait()

        for s in range(2):
            first = s * slot_rows
            for i in range(unit_blocks):
                expand[at, s, i * unit_rows : (i + 1) * unit_rows, :] = held[
                    at, first : first + unit_rows, i * unit : (i + 1) * unit
                ].astype(jnp.float32)
            for part in range(3):
                top = first + unit_rows + part * head_rows
                for i in range(head_blocks):
                    inward[at, s, part, i * head_rows : (i + 1) * head_rows, :] = held[
                        at, top : top + head_rows, i * cols : (i + 1) * cols
                    ].astype(jnp.float32)
        contract[at] = held[at, 2 * slot_rows : 2 * slot_rows + unit, :].astype(jnp.float32)
        outward[at] = held[at, 2 * slot_rows + unit :, :].astype(jnp.float32)
        for copy in stores(b):
            copy.start()
        return carry

    lax.fori_loop(0, batch_count, step, 0)
    for b in range(max(0, batch_count - 2), batch_count):
        for copy in stores(b):
            copy.wait()


def widen(gathered, cols, unit, half, hidden):
    batch_count, rows, width = gathered.shape
    turn = lax.axis_index("fsdp").astype(jnp.int32)[None]
    f32 = jnp.float32
    dma = pltpu.SemaphoreType.DMA
    hbm = pl.BlockSpec(memory_space=pl.ANY)
    return pl.pallas_call(
        functools.partial(widen_kernel, cols, unit),
        out_shape=(
            jax.ShapeDtypeStruct((half, 3 * width), f32),
            jax.ShapeDtypeStruct((half, width), f32),
            jax.ShapeDtypeStruct((half, hidden), f32),
            jax.ShapeDtypeStruct((hidden // 2, width), f32),
        ),
        in_specs=[pl.BlockSpec(memory_space=pltpu.SMEM), hbm],
        out_specs=(hbm,) * 4,
        scratch_shapes=[
            pltpu.VMEM((2, rows, width), gathered.dtype),
            pltpu.VMEM((2, 2, 3, half, cols), f32),
            pltpu.VMEM((2, cols, width), f32),
            pltpu.VMEM((2, 2, half, unit), f32),
            pltpu.VMEM((2, unit, width), f32),
            dma((2,)),
            dma((2, 10)),
        ],
        name="widen",
        compiler_params=pltpu.CompilerParams(vmem_limit_bytes=VMEM_LIMIT),
    )(turn, gathered)


def widen_plain(gathered, cols, unit, half, hidden):
    batch_count, rows, width = gathered.shape
    unit_rows = unit * half // width
    head_rows = cols * half // width
    slot_rows = unit_rows + 3 * head_rows
    slots = gathered[:, : 2 * slot_rows].reshape(batch_count, 2, slot_rows, width)
    slots = jnp.where(lax.axis_index("fsdp") == 0, slots[:, ::-1], slots)
    slots = slots.astype(jnp.float32)
    expand = slots[:, :, :unit_rows].reshape(batch_count, 2, unit_rows, width // unit, unit)
    expand = expand.transpose(3, 2, 1, 0, 4).reshape(half, hidden)
    inward = slots[:, :, unit_rows:].reshape(batch_count, 2, 3, head_rows, width // cols, cols)
    inward = inward.transpose(4, 3, 2, 1, 0, 5).reshape(half, 3 * width)
    last = gathered[:, 2 * slot_rows :].astype(jnp.float32)
    return (
        inward,
        last[:, unit:].reshape(half, width),
        expand,
        last[:, :unit].reshape(hidden // 2, width),
    )


def fold(columns, unit, half):
    width = columns.shape[0]
    blocks = width // unit
    parts = columns.reshape(2, blocks, half // blocks, -1, unit).transpose(0, 3, 2, 1, 4)
    return parts.reshape(2, -1, width)


def dot(left, right, contract=((1,), (0,))):
    return lax.dot_general(left, right, (contract, ((), ())), preferred_element_type=jnp.float32)


def normalize(values):
    center = values - jnp.mean(values, axis=-1, keepdims=True)
    inverse = lax.rsqrt(jnp.mean(center * center, axis=-1, keepdims=True) + EPSILON)
    return (center * inverse, inverse)


def norm_backward(upstream, normed, inverse, factor):
    scaled = upstream * factor
    middle = jnp.mean(scaled, axis=-1, keepdims=True)
    coupled = jnp.mean(scaled * normed, axis=-1, keepdims=True)
    result = inverse * (scaled - middle - normed * coupled)
    return (result, jnp.sum(upstream * normed, axis=0), jnp.sum(upstream, axis=0))


def slot_positions(span_order, first_slot, slot_count, span_size):
    slot_index = first_slot + jnp.arange(slot_count, dtype=jnp.int32)
    owners = slot_index // (2 * span_size)
    places = jnp.arange(span_order.shape[0], dtype=jnp.int32)
    leading = jnp.sum(jnp.where(owners[:, None] == places[None, :], span_order[None, :], 0), axis=1)
    spans = 2 * span_order.shape[0]
    picked = jnp.where(slot_index // span_size % 2 == 0, leading, spans - 1 - leading)
    return picked * span_size + slot_index % span_size


def rotary_tables(positions):
    half_rot = ROT // 2
    angular = jnp.exp(
        jnp.arange(half_rot, dtype=jnp.float32) * (-2.0 * math.log(ROTARY_BASE) / ROT)
    )
    angles = positions.astype(jnp.float32)[:, None] * angular[None, :]
    angles = jnp.concatenate([angles, angles], axis=1)
    return (jnp.cos(angles), jnp.sin(angles))


def rotate(tensor, cosine, sine_table):
    half_rot = ROT // 2
    leading_part = tensor[..., :ROT]
    turned = jnp.concatenate([-leading_part[..., half_rot:], leading_part[..., :half_rot]], axis=-1)
    rotated = leading_part * cosine[:, None, :] + turned * sine_table[:, None, :]
    return jnp.concatenate([rotated, tensor[..., ROT:]], axis=-1)


def unrotate(tensor, cosine, sine_table):
    half_rot = ROT // 2
    leading_part = tensor[..., :ROT]
    weighted = leading_part * sine_table[:, None, :]
    turned = jnp.concatenate([weighted[..., half_rot:], -weighted[..., :half_rot]], axis=-1)
    return jnp.concatenate([leading_part * cosine[:, None, :] + turned, tensor[..., ROT:]], axis=-1)


def attention(mixed, place, cosine, sine_table, heads):
    sequences, length, _ = mixed.shape
    parts = mixed.reshape(sequences, length, 4, heads, HEAD_DIM)
    queries, keys, values, grads = (parts[:, :, i] for i in range(4))
    scale = 1.0 / math.sqrt(HEAD_DIM)
    scores = jnp.einsum("sqhd,skhd->shqk", queries, keys, preferred_element_type=jnp.float32)
    allowed = place[None, :] <= place[:, None]
    scores = jnp.where(allowed, scores * scale, MASKED)
    peak = jnp.max(scores, axis=-1, keepdims=True)
    log_total = peak + jnp.log(jnp.sum(jnp.exp(scores - peak), axis=-1, keepdims=True))
    probs = jnp.exp(scores - log_total)
    soft = probs.astype(jnp.bfloat16)
    context = jnp.einsum("shqk,skhd->sqhd", soft, values, preferred_element_type=jnp.float32)
    context = context.astype(jnp.bfloat16)
    delta = jnp.einsum(
        "sqhd,sqhd->shq", grads.astype(jnp.float32), context.astype(jnp.float32)
    )
    value_grad = jnp.einsum("shqk,sqhd->skhd", soft, grads, preferred_element_type=jnp.float32)
    probs_grad = jnp.einsum("sqhd,skhd->shqk", grads, values, preferred_element_type=jnp.float32)
    score_grad = (probs * (probs_grad - delta[..., None]) * scale).astype(jnp.bfloat16)
    query_grad = jnp.einsum("shqk,skhd->sqhd", score_grad, keys, preferred_element_type=jnp.float32)
    key_grad = jnp.einsum("shqk,sqhd->skhd", score_grad, queries, preferred_element_type=jnp.float32)
    query_grad = unrotate(query_grad, cosine, sine_table)
    key_grad = unrotate(key_grad, cosine, sine_table)
    back = jnp.stack([query_grad, key_grad, value_grad], axis=2)
    shift = jnp.sum(back, axis=(0, 1)).reshape(-1)
    full = jnp.concatenate([context[:, :, None], back.astype(jnp.bfloat16)], axis=2)
    return (full.reshape(sequences, length, 4 * heads * HEAD_DIM), shift)


def body(
    layer_input,
    out_grad,
    span_order,
    inward,
    inward_bias,
    outward,
    outward_bias,
    expand,
    expand_bias,
    contract,
    contract_bias,
    first_gain,
    first_bias,
    second_gain,
    second_bias,
):
    batch_count, fsdp_count = (lax.axis_size("batch"), lax.axis_size("fsdp"))
    context_count = lax.axis_size("ctx")
    context_index = lax.axis_index("ctx")
    batch_index, fsdp_index = (lax.axis_index("batch"), lax.axis_index("fsdp"))
    plane = batch_count * fsdp_count
    tokens, width = layer_input.shape[1:]
    hidden_units = expand.shape[1]
    head_cols = width // plane
    unit_cols = hidden_units // plane
    heads = head_cols // HEAD_DIM
    length = tokens * context_count
    span_size = tokens // 2
    own_sequences = plane // context_count

    def full_vectors(*vectors):
        sizes = [v.shape[0] for v in vectors]
        gathered = lax.all_gather(jnp.concatenate(vectors), "fsdp")
        out, start = ([], 0)
        for size in sizes:
            out.append(gathered[:, start : start + size].reshape(-1).astype(jnp.float32))
            start += size
        return out

    (
        inward_offset,
        outward_offset,
        expand_offset,
        contract_offset,
        gain_first,
        offset_first,
        gain_second,
        offset_second,
    ) = full_vectors(
        inward_bias,
        outward_bias,
        expand_bias,
        contract_bias,
        first_gain,
        first_bias,
        second_gain,
        second_bias,
    )

    def chunk(array, cols):
        rows = array.shape[0]
        parts = array.reshape(rows, -1, fsdp_count, batch_count, cols)
        mine = lax.dynamic_index_in_dim(parts, batch_index, 3, keepdims=False)
        return mine.transpose(2, 0, 1, 3).reshape(fsdp_count, rows, -1)

    to_send = jnp.concatenate([chunk(inward, head_cols), chunk(expand, unit_cols)], axis=2)
    weights = lax.all_to_all(to_send, "fsdp", 0, 0).reshape(width, -1)
    inward_cols = weights[:, : 3 * head_cols]
    expand_cols = weights[:, 3 * head_cols :]
    outward_rows = lax.dynamic_slice_in_dim(outward, batch_index * head_cols, head_cols, 0)
    contract_rows = lax.dynamic_slice_in_dim(contract, batch_index * unit_cols, unit_cols, 0)
    plane_index = fsdp_index * batch_count + batch_index
    inward_shift_in = lax.dynamic_index_in_dim(
        inward_offset.reshape(3, plane, head_cols), plane_index, 1, keepdims=False
    ).reshape(-1)
    expand_shift_in = lax.dynamic_slice_in_dim(expand_offset, plane_index * unit_cols, unit_cols, 0)

    pair = jnp.stack([layer_input[0], out_grad[0]])
    pair_all = lax.all_gather(pair, PLANE, axis=1, tiled=True)
    grads_all = pair_all[1]
    normed, _ = normalize(pair_all[0].astype(jnp.float32))
    first_rows = (normed * gain_first + offset_first).astype(jnp.bfloat16)
    second_rows = (normed * gain_second + offset_second).astype(jnp.bfloat16)

    local_place = slot_positions(span_order, context_index * tokens, tokens, span_size)
    cosine, sine_table = rotary_tables(local_place)
    cosine_plane = jnp.tile(cosine, (plane, 1))
    sine_plane = jnp.tile(sine_table, (plane, 1))
    projected = dot(first_rows, inward_cols) + inward_shift_in
    projected = projected.reshape(plane * tokens, 3 * heads, HEAD_DIM)
    turned = rotate(projected[:, : 2 * heads], cosine_plane, sine_plane)
    context_grad = dot(grads_all, outward_rows, ((1,), (1,)))
    mixed = jnp.concatenate(
        [
            turned.reshape(plane * tokens, -1),
            projected[:, 2 * heads :].reshape(plane * tokens, -1),
            context_grad,
        ],
        axis=1,
    ).astype(jnp.bfloat16)
    mixed = mixed.reshape(context_count, own_sequences, tokens, 4 * head_cols)
    mixed = lax.all_to_all(mixed, "ctx", 0, 0)
    mixed = mixed.transpose(1, 0, 2, 3).reshape(own_sequences, length, 4 * head_cols)
    place = slot_positions(span_order, 0, length, span_size)
    cosine_all, sine_all = rotary_tables(place)
    back, inward_sum = attention(mixed, place, cosine_all, sine_all, heads)
    back = back.reshape(own_sequences, context_count, tokens, 4 * head_cols).transpose(1, 0, 2, 3)
    back = lax.all_to_all(back, "ctx", 0, 0).reshape(plane * tokens, 4 * head_cols)
    context_rows = back[:, :head_cols]
    projected_rows = back[:, head_cols:]

    before = dot(second_rows, expand_cols) + expand_shift_in
    tail = 1.0 + lax.erf(before * HALF_ROOT)
    activated = (0.5 * before * tail).astype(jnp.bfloat16)
    slope = 0.5 * tail + before * jnp.exp(-0.5 * before * before) * NORMAL_PEAK
    before_grad = dot(grads_all, contract_rows, ((1,), (1,))) * slope
    expand_sum = jnp.sum(before_grad, axis=0)
    before_rows = before_grad.astype(jnp.bfloat16)

    expand_delta = dot(second_rows, before_rows, ((0,), (0,)))
    contract_delta = dot(activated, grads_all, ((0,), (0,)))
    inward_delta = dot(first_rows, projected_rows, ((0,), (0,)))
    outward_delta = dot(context_rows, grads_all, ((0,), (0,)))

    out_part = dot(activated, contract_rows) + dot(context_rows, outward_rows)
    second_part = dot(before_rows, expand_cols, ((1,), (1,)))
    first_part = dot(projected_rows, inward_cols, ((1,), (1,)))
    stacked = jnp.stack([out_part, second_part, first_part], axis=1).astype(jnp.bfloat16)
    mine = lax.psum_scatter(stacked, PLANE, scatter_dimension=0, tiled=True).astype(jnp.float32)

    hidden = layer_input[0].astype(jnp.float32)
    grad_float = out_grad[0].astype(jnp.float32)
    normed_mine, inverse_mine = normalize(hidden)
    result = (hidden + (mine[:, 0] + outward_offset) + contract_offset).astype(jnp.bfloat16)
    second_input, second_scale, second_shift = norm_backward(
        mine[:, 1], normed_mine, inverse_mine, gain_second
    )
    first_input, first_scale, first_shift = norm_backward(
        mine[:, 2], normed_mine, inverse_mine, gain_first
    )
    input_delta = grad_float + first_input + second_input

    half = width // fsdp_count
    slots = jnp.concatenate(
        [fold(expand_delta, unit_cols, half), fold(inward_delta, head_cols, half)], axis=1
    ).astype(jnp.bfloat16)
    slots = jnp.where(fsdp_index == 0, slots[::-1], slots).reshape(-1, width)
    part = jnp.concatenate(
        [slots, contract_delta.astype(jnp.bfloat16), outward_delta.astype(jnp.bfloat16)], axis=0
    )

    inward_wide = jnp.zeros((3, plane, head_cols), jnp.float32)
    inward_wide = lax.dynamic_update_index_in_dim(
        inward_wide, inward_sum.reshape(3, head_cols), plane_index, 1
    ).reshape(-1)
    expand_wide = jnp.zeros((plane, unit_cols), jnp.float32)
    expand_wide = lax.dynamic_update_index_in_dim(expand_wide, expand_sum, plane_index, 0).reshape(-1)
    bias_total = jnp.sum(grad_float, axis=0)
    vectors = [
        inward_wide,
        bias_total,
        expand_wide,
        first_scale,
        first_shift,
        second_scale,
        second_shift,
    ]
    gathered, whole = total_sums(
        part, jnp.concatenate(vectors).reshape(-1, 128), slots.shape[0] // 2
    )
    whole = whole.reshape(-1)
    finish = widen if head_cols % 128 == 0 else widen_plain
    inward_total, outward_total, expand_total, contract_total = finish(
        gathered, head_cols, unit_cols, half, hidden_units
    )
    halves, start = ([], 0)
    for vector in vectors:
        part = vector.shape[0] // fsdp_count
        halves.append(lax.dynamic_slice_in_dim(whole, start + fsdp_index * part, part, 0))
        start += vector.shape[0]
    return (
        result[None],
        input_delta[None],
        inward_total,
        halves[0],
        outward_total,
        halves[1],
        expand_total,
        halves[2],
        contract_total,
        halves[1],
        halves[3],
        halves[4],
        halves[5],
        halves[6],
    )


def solution(mesh):
    rows = P(PLANE, "ctx", None)
    matrix, vector = (P("fsdp", None), P("fsdp"))
    in_specs = (rows, rows, P()) + (matrix, vector) * 4 + (vector,) * 4
    out_specs = (rows, rows) + (matrix, vector) * 4 + (vector,) * 4
    return jax.shard_map(body, mesh=mesh, in_specs=in_specs, out_specs=out_specs, check_vma=False)
```

```python
import functools
import math

import jax
import jax.numpy as jnp
from jax import lax
from jax.experimental import pallas as pl
from jax.experimental.pallas import tpu as pltpu
from jax.sharding import PartitionSpec as P

HEAD_DIM = 64
ROT = 16

EPSILON = 1e-05
ROTARY_BASE = 10000.0
MASKED = -1e30
HALF_ROOT = 0.7071067811865476
NORMAL_PEAK = 0.3989422804014327
PLANE = ("batch", "fsdp")


MESH = pl.DeviceIdType.MESH
CORES = 2
VMEM_LIMIT = 56 * 2**20


def here():
    return (lax.axis_index("batch"), lax.axis_index("ctx"), lax.axis_index("fsdp"))


def swapped(index, step):
    return index + step * (1 - 2 * (index // step % 2))


def greet(partners):
    barrier = pltpu.get_barrier_semaphore()
    for partner in partners:
        pl.semaphore_signal(barrier, inc=1, device_id=partner, device_id_type=MESH)
    pl.semaphore_wait(barrier, len(partners))


def remote(src, dst, send, recv, target):
    return pltpu.make_async_remote_copy(
        src_ref=src,
        dst_ref=dst,
        send_sem=send,
        recv_sem=recv,
        device_id=target,
        device_id_type=MESH,
    )


def back_kernel(
    sizes,
    tokens,
    heads,
    counts,
    piece,
    part_in,
    mixed_in,
    out_in,
    second_in,
    first_rows_in,
    grads_in,
    inputs_in,
    mean_ref,
    inverse_ref,
    inward_in,
    outward_in,
    place_col,
    place_row,
    cosine_ref,
    fore_ref,
    aft_ref,
    vector_ref,
    sums_ref,
    token_ref,
    vector_out,
    part,
    mixed,
    out_rows,
    second_rows,
    first_back,
    first_rows,
    grads,
    inputs,
    inward,
    outward,
    attended,
    heads_sum,
    back_out,
    back_in,
    inward_sum,
    final,
    reduced,
    near,
    across_in,
    far,
    token_sum,
    vector_in,
    vector_sum,
    load_sems,
    store_sems,
    own_sems,
    turn_sems,
    reduce_sems,
    back_sems,
    row_sems,
    chip_sems,
    core_sems,
    near_sems,
    across_sems,
    far_sems,
    vector_sems,
):
    batch_count, context_count, fsdp_count = sizes
    early_other, early, late_other, late = counts
    b, z, y = here()
    chips = batch_count // CORES
    core = b % CORES
    chip = b // CORES
    width = part.shape[1]
    cols = heads * HEAD_DIM
    plane = batch_count * fsdp_count
    own_sequences = plane // context_count
    length = tokens * context_count
    steps = early + late
    early_rows = 2 * early * piece
    last = context_count - 1
    f32, half_type = (jnp.float32, part.dtype)

    sibling = (chip * CORES + (1 - core), z, y)
    across = (b, z, 1 - y)
    peers = [((chip + d) % chips * CORES + core, z, y) for d in range(1, chips)]
    sources = [(chip + chips - d) % chips * CORES + core for d in range(1, chips)]
    others = [(b, (z + d) % context_count, y) for d in range(1, context_count)]
    stages = []
    step = 1
    while step < batch_count:
        stages.append((swapped(b, step), z, y))
        step *= 2
    stages.append(across)
    step = 1
    while step < context_count:
        stages.append((b, swapped(z, step), y))
        step *= 2

    loads = [
        pltpu.make_async_copy(source, target, load_sems.at[i])
        for i, (source, target) in enumerate(
            [
                (part_in, part.at[pl.ds(0, early_rows), :]),
                (mixed_in, mixed),
                (second_in, second_rows),
                (out_in, out_rows),
                (first_rows_in, first_rows),
                (grads_in, grads),
                (inputs_in, inputs),
                (inward_in, inward),
                (outward_in, outward),
            ]
        )
    ]
    for load in loads:
        load.start()
    greet([sibling, across] + peers + others)

    def sem(sems, *index):
        return (sems.at[(0, *index)], sems.at[(1, *index)])


    def place(half, k):
        is_late = jnp.minimum(k // early, 1)
        other = early_other * (1 - is_late) + late_other * is_late
        count = early * (1 - is_late) + late * is_late
        j = k - early * is_late
        is_own = jnp.minimum(j // other, 1)
        row = (half * other + j) * (1 - is_own) + (
            2 * other + half * (count - other) + j - other
        ) * is_own
        return pl.multiple_of((2 * early * is_late + row) * piece, piece)

    def own(k):
        is_late = jnp.minimum(k // early, 1)
        other = early_other * (1 - is_late) + late_other * is_late
        return jnp.minimum((k - early * is_late) // other, 1)

    def rows_at(ref, row):
        return ref.at[pl.ds(row, piece), :]

    def final_at(slot, row):
        return final.at[slot, pl.ds(row, piece), :]

    def slot_of(k):
        return batch_count * (1 - own(k)) + b * own(k)

    def back_copy(half, k, target):
        at = final_at(slot_of(k), place(half, k))
        return remote(at, at, *sem(back_sems, half, k), target)

    def row_copy(half, k):
        row = place(half, k)
        source = final_at(batch_count, row)
        return remote(source, final_at(b, row), *sem(row_sems, half, k), across)

    def chip_copy(d, half, k, slot):
        at = final_at(slot, place(half, k))
        return remote(at, at, *sem(chip_sems, d, half, k), peers[d])

    def core_copy(d, half, k, slot):
        at = final_at(slot, place(half, k))
        return remote(at, at, *sem(core_sems, d, half, k), sibling)

    def spread(half, k):
        for d in range(chips - 1):
            chip_copy(d, half, k, b).start()
        core_copy(0, half, k, b).start()

    def finish(half, k, position, behind):
        @pl.when(position > 0)
        def _():
            back_copy(half, k, behind).start()

        @pl.when(own(k) == 0)
        def _():
            row_copy(half, k).start()

        @pl.when(own(k) == 1)
        def _():
            spread(half, k)

    def arrived(half, k):
        for d in range(chips - 1):
            chip_copy(d, half, k, sources[d]).wait_recv()
            core_copy(1 + d, half, k, sources[d]).start()

    def pieces(t, half):
        position = z if half == 0 else last - z
        ahead = (b, (z + 1 if half == 0 else z + last) % context_count, y)
        behind = (b, (z + last if half == 0 else z + 1) % context_count, y)
        k = t - position

        @pl.when((k >= 0) & (k < steps))
        def _():
            row = place(half, k)
            to_next = remote(
                rows_at(reduced, row), rows_at(reduced, row), *sem(reduce_sems, half, k), ahead
            )

            @pl.when(position == 0)
            def _():
                remote(
                    rows_at(part, row), rows_at(reduced, row), *sem(reduce_sems, half, k), ahead
                ).start()

            @pl.when(position > 0)
            def _():
                to_next.wait_recv()
                mine = part[pl.ds(row, piece), :].astype(f32)
                came = reduced[pl.ds(row, piece), :].astype(f32)
                summed = (mine + came).astype(half_type)

                @pl.when(position < last)
                def _():
                    reduced[pl.ds(row, piece), :] = summed
                    to_next.start()

                @pl.when(position == last)
                def _():
                    final[slot_of(k), pl.ds(row, piece), :] = summed
                    finish(half, k, position, behind)

        k_back = t - 2 * last + position

        @pl.when((position < last) & (k_back >= 0) & (k_back < steps))
        def _():
            back_copy(half, k_back, behind).wait_recv()
            finish(half, k_back, position, behind)

        k_row = k_back - 1

        @pl.when((k_row >= 0) & (k_row < steps))
        def _():
            @pl.when(own(k_row) == 0)
            def _():
                row_copy(half, k_row).wait_recv()
                spread(half, k_row)

            @pl.when(own(k_row) == 1)
            def _():
                arrived(half, k_row)

        k_chip = k_row - 2

        @pl.when((k_chip >= 0) & (k_chip < steps))
        def _():
            @pl.when(own(k_chip) == 0)
            def _():
                arrived(half, k_chip)


    def attend(n):
        s, h = (n // heads, n % heads)
        columns = [mixed[s, :, i * cols : (i + 1) * cols] for i in range(4)]
        lane = lax.broadcasted_iota(jnp.int32, (length, cols), 1) // HEAD_DIM
        picked = lane == h
        nothing = jnp.zeros((length, cols), half_type)
        queries, keys, values, upstream = columns
        queries_h, keys_h, values_h, upstream_h = [
            jnp.where(picked, column, nothing) for column in columns
        ]
        scale = 1.0 / math.sqrt(HEAD_DIM)
        scores = dot(queries_h, keys, ((1,), (1,))) * scale
        scores = jnp.where(place_row[...] <= place_col[...], scores, MASKED)
        peak = jnp.max(scores, axis=1, keepdims=True)
        log_total = peak + jnp.log(jnp.sum(jnp.exp(scores - peak), axis=1, keepdims=True))
        probs = jnp.exp(scores - log_total)
        soft = probs.astype(half_type)
        context = dot(soft, values_h)
        delta = jnp.sum(
            upstream_h.astype(f32) * context.astype(half_type).astype(f32), axis=1, keepdims=True
        )
        probs_grad = dot(upstream_h, values, ((1,), (1,)))
        score_grad = (probs * (probs_grad - delta) * scale).astype(half_type)
        results = (
            context,
            dot(score_grad, keys_h),
            dot(score_grad, queries_h, ((0,), (0,))),
            dot(soft, upstream_h, ((0,), (0,))),
        )
        for i, value in enumerate(results):

            @pl.when(h == 0)
            def _():
                heads_sum[i] = value

            @pl.when(h > 0)
            def _():
                heads_sum[i] += value

        @pl.when(h == heads - 1)
        def _():
            back_out[s, :, :cols] = heads_sum[0].astype(half_type)
            for i in range(1, 4):
                value = heads_sum[i]
                if i < 3:
                    value = (
                        value * cosine_ref[...]
                        + pltpu.roll(value * fore_ref[...], cols - ROT // 2, 1)
                        + pltpu.roll(value * aft_ref[...], ROT // 2, 1)
                    )
                back_out[s, :, i * cols : (i + 1) * cols] = value.astype(half_type)
                total = jnp.sum(value, axis=0, keepdims=True)

                @pl.when(s == 0)
                def _():
                    inward_sum[i - 1 : i, :] = total

                @pl.when(s > 0)
                def _():
                    inward_sum[i - 1 : i, :] += total

            for d in range(context_count):
                turn_copy(s, d).start()

    def turn_copy(s, d):
        target = (z + d) % context_count
        source = back_out.at[s, pl.ds(pl.multiple_of(target * tokens, tokens), tokens), :]
        row = pl.multiple_of((z * own_sequences + s) * tokens, tokens)
        destination = back_in.at[pl.ds(row, tokens), :]
        if d == 0:
            return pltpu.make_async_copy(source, destination, own_sems.at[s])
        return remote(source, destination, *sem(turn_sems, s, d - 1), others[d - 1])

    def turned():
        for s in range(own_sequences):
            turn_copy(s, 0).wait()
            for d in range(1, context_count):
                turn_copy(s, d).wait_recv()


    def head_gradients():
        rows = first_rows.shape[0]
        context_rows = back_in[:, :cols]
        delta = dot(context_rows, grads[...], ((0,), (0,))).astype(half_type)
        part[early_rows + 2 * late_other * piece * 2 :, :] = delta
        half = width // 2
        group = cols * half // width
        blocks = width // cols

        def half_rows(s, carry):
            owner = (1 - y) * (1 - s) + y * s
            column = pl.multiple_of(owner * half, half)
            delta = dot(
                first_rows[:, pl.ds(column, half)], back_in[:, cols:], ((0,), (0,))
            ).astype(half_type)
            top = pl.multiple_of(early_rows + s * 3 * group, group)
            for i in range(3):
                for j in range(blocks):
                    part[pl.ds(top + i * group, group), j * cols : (j + 1) * cols] = delta[
                        j * group : (j + 1) * group, i * cols : (i + 1) * cols
                    ]
            return carry

        lax.fori_loop(0, 2, half_rows, 0)

    tile = min(256, plane * tokens)
    tiles = plane * tokens // tile

    def output_rows():
        def step(i, carry):
            rows = pl.ds(pl.multiple_of(i * tile, tile), tile)
            value = dot(back_in[rows, :cols], outward[...])
            out_rows[rows, :] = (out_rows[rows, :].astype(f32) + value).astype(half_type)
            return carry

        lax.fori_loop(0, tiles, step, 0)

    def first_back_rows():
        def step(i, carry):
            scale_total, shift_total = carry
            rows = pl.ds(pl.multiple_of(i * tile, tile), tile)
            value = dot(back_in[rows, cols:], inward[...], ((1,), (1,)))
            first_back[rows, :] = value.astype(half_type)
            normed = (inputs[rows, :].astype(f32) - mean_ref[rows, :]) * inverse_ref[rows, :]
            return (
                scale_total + jnp.sum(value * normed, axis=0, keepdims=True),
                shift_total + jnp.sum(value, axis=0, keepdims=True),
            )

        nothing = jnp.zeros((1, width), f32)
        totals = lax.fori_loop(0, tiles, step, (nothing, nothing))
        lines = width // 128
        vector_sum[len(stages)] = vector_ref[...]
        index = y * batch_count + b
        for i in range(3):
            for j in range(cols // 128):
                line = i * lines + index * (cols // 128) + j
                vector_sum[len(stages), pl.ds(line, 1), :] = inward_sum[
                    i : i + 1, j * 128 : (j + 1) * 128
                ]
        first = vector_ref.shape[0] - 2 * lines
        for i, total in enumerate(totals):
            for j in range(lines):
                line = first + i * lines + j
                vector_sum[len(stages), line : line + 1, :] = total[:, j * 128 : (j + 1) * 128]

    def vector_copy(i):
        source = vector_sum.at[len(stages) if i == 0 else i - 1]
        return remote(source, vector_in.at[i], *sem(vector_sems, i), stages[i])


    arrays = (second_rows, out_rows, first_back)
    block = fsdp_count * tokens

    def near_copy(a, c):
        row = pl.multiple_of((c * CORES + 1 - core) * block, block)
        return remote(
            arrays[a].at[pl.ds(row, block), :],
            near.at[a, pl.ds(c * block, block), :],
            *sem(near_sems, a, c),
            sibling,
        )

    def across_copy(a, c):
        row = pl.multiple_of(c * block + (1 - y) * tokens, tokens)
        return remote(
            near.at[a, pl.ds(row, tokens), :],
            across_in.at[a, pl.ds(c * tokens, tokens), :],
            *sem(across_sems, a, c),
            across,
        )

    def far_copy(a, d):
        row = pl.multiple_of((chip + d + 1) % chips * tokens, tokens)
        return remote(
            across_in.at[a, pl.ds(row, tokens), :], far.at[a, d], *sem(far_sems, a, d), peers[d]
        )

    def scatter_first(a):
        for c in range(chips):
            near_copy(a, c).start()

    def scatter_second(a):
        for c in range(chips):
            near_copy(a, c).wait_recv()

            def step(i, carry):
                row = pl.multiple_of((c * CORES + core) * block + i * tokens, tokens)
                mine = arrays[a][pl.ds(row, tokens), :].astype(f32)
                at = pl.ds(pl.multiple_of(c * block + i * tokens, tokens), tokens)
                near[a, at, :] = (mine + near[a, at, :].astype(f32)).astype(half_type)
                return carry

            lax.fori_loop(0, fsdp_count, step, 0)
            across_copy(a, c).start()

    def scatter_third(a):
        for c in range(chips):
            across_copy(a, c).wait_recv()

        def both(c):
            row = pl.multiple_of(c * block + y * tokens, tokens)
            at = pl.ds(pl.multiple_of(c * tokens, tokens), tokens)
            return (
                near[a, pl.ds(row, tokens), :].astype(f32) + across_in[a, at, :].astype(f32),
                at,
            )

        for d in range(chips - 1):
            value, at = both((chip + d + 1) % chips)
            across_in[a, at, :] = value.astype(half_type)
            far_copy(a, d).start()
        token_sum[a] = both(chip)[0]

    def scatter_last(a):
        value = token_sum[a]
        for d in range(chips - 1):
            far_copy(a, d).wait_recv()
            value = value + far[a, d].astype(f32)
        token_ref[a] = value


    problems = own_sequences * heads
    ready = max(early - 4, problems)
    plan = {}

    def at(slot, work):
        plan.setdefault(slot, []).append(work)

    def scatter(a, slot):
        at(slot, lambda: scatter_first(a))
        at(slot + 3, lambda: scatter_second(a))
        at(slot + 6, lambda: scatter_third(a))
        at(slot + 9, lambda: scatter_last(a))

    at(0, lambda: loads[2].wait())
    scatter(0, 0)
    at(ready, lambda: [load.wait() for load in loads[3:]])
    at(ready, turned)
    at(ready, head_gradients)
    at(ready + 1, output_rows)
    scatter(1, ready + 1)
    at(ready + 2, first_back_rows)
    scatter(2, ready + 2)
    at(ready + 2, lambda: vector_copy(0).start())
    for i in range(len(stages)):

        def vector_step(i=i):
            vector_copy(i).wait_recv()
            before = vector_sum[len(stages) if i == 0 else i - 1]
            vector_sum[i] = before + vector_in[i]
            if i + 1 < len(stages):
                vector_copy(i + 1).start()

        at(ready + 4 + 2 * i, vector_step)

    loads[0].wait()
    loads[1].wait()

    def slot_step(t, carry):
        for half in range(2):
            pieces(t, half)

        @pl.when(t < problems)
        def _():
            attend(t)

        for slot, works in sorted(plan.items()):

            @pl.when(t == slot)
            def _():
                for work in works:
                    work()

        return carry

    slots = max(steps + 2 * last + 4, max(plan) + 1)
    lax.fori_loop(0, slots, slot_step, 0)
    vector_out[...] = vector_sum[len(stages) - 1]

    def drain(k, carry):
        for half in range(2):
            position = z if half == 0 else last - z
            for d in range(chips):
                core_copy(d, half, k, b).wait_recv()
                core_copy(d, half, k, b).wait_send()
                if d:
                    chip_copy(d - 1, half, k, b).wait_send()

            @pl.when(position < last)
            def _():
                row = place(half, k)
                remote(
                    rows_at(reduced, row), rows_at(reduced, row), *sem(reduce_sems, half, k), across
                ).wait_send()

            @pl.when(position > 0)
            def _():
                back_copy(half, k, across).wait_send()

            @pl.when(own(k) == 0)
            def _():
                row_copy(half, k).wait_send()

        return carry

    lax.fori_loop(0, steps, drain, 0)
    store = pltpu.make_async_copy(final.at[pl.ds(0, batch_count)], sums_ref, store_sems)
    store.start()
    for i in range(len(stages)):
        vector_copy(i).wait_send()
    for s in range(own_sequences):
        for d in range(1, context_count):
            turn_copy(s, d).wait_send()
    for a in range(3):
        for c in range(chips):
            near_copy(a, c).wait_send()
            across_copy(a, c).wait_send()
        for d in range(chips - 1):
            far_copy(a, d).wait_send()
    store.wait()


def back_part(
    part,
    mixed,
    out_part,
    second_part,
    first_rows,
    grads,
    inputs,
    mean,
    inverse,
    inward,
    outward,
    places,
    tables,
    vector,
    tokens,
    heads,
    hidden,
):
    sizes = tuple(lax.axis_size(name) for name in ("batch", "ctx", "fsdp"))
    batch_count, context_count, fsdp_count = sizes
    plane = batch_count * fsdp_count
    chips = batch_count // CORES
    width = part.shape[1]
    cols = heads * HEAD_DIM
    length = tokens * context_count
    own_sequences = plane // context_count
    half = width // 2
    unit = hidden // plane
    early_other, early = (unit * half // width, 2 * unit * half // width + unit)
    late_other, late = (3 * cols * half // width, 6 * cols * half // width + cols)
    piece = 32
    for rows in (early_other, early - early_other, late_other, late - late_other):
        piece = math.gcd(piece, rows // 2)
    counts = tuple(n // 2 // piece for n in (early_other, early, late_other, late))
    steps = counts[1] + counts[3]
    rows = early + late
    stage_count = (plane * context_count).bit_length() - 1
    all_tokens = plane * tokens
    dma = pltpu.SemaphoreType.DMA
    f32, half_type = (jnp.float32, part.dtype)
    vmem = pl.BlockSpec(memory_space=pltpu.VMEM)
    hbm = pl.BlockSpec(memory_space=pl.ANY)

    def held(*shape, dtype=half_type):
        return pltpu.VMEM(shape, dtype)

    return pl.pallas_call(
        functools.partial(back_kernel, sizes, tokens, heads, counts, piece),
        out_shape=(
            jax.ShapeDtypeStruct((batch_count, rows, width), half_type),
            jax.ShapeDtypeStruct((3, tokens, width), f32),
            jax.ShapeDtypeStruct(vector.shape, f32),
        ),
        in_specs=[hbm] * 7 + [vmem] * 2 + [hbm] * 2 + [vmem] * 6,
        out_specs=(hbm, vmem, vmem),
        scratch_shapes=[
            held(rows, width),
            held(own_sequences, length, 4 * cols),
            held(all_tokens, width),
            held(all_tokens, width),
            held(all_tokens, width),
            held(all_tokens, width),
            held(all_tokens, width),
            held(all_tokens, width),
            held(width, 3 * cols),
            held(cols, width),
            held(8, 128),
            held(4, length, cols, dtype=f32),
            held(own_sequences, length, 4 * cols),
            held(all_tokens, 4 * cols),
            held(8, cols, dtype=f32),
            held(batch_count + 1, rows, width),
            held(rows, width),
            held(3, chips * fsdp_count * tokens, width),
            held(3, chips * tokens, width),
            held(3, chips - 1, tokens, width),
            held(3, tokens, width, dtype=f32),
            held(stage_count, *vector.shape, dtype=f32),
            held(stage_count + 1, *vector.shape, dtype=f32),
            dma((9,)),
            dma,
            dma((own_sequences,)),
            dma((2, own_sequences, context_count - 1)),
            dma((2, 2, steps)),
            dma((2, 2, steps)),
            dma((2, 2, steps)),
            dma((2, chips - 1, 2, steps)),
            dma((2, chips, 2, steps)),
            dma((2, 3, chips)),
            dma((2, 3, chips)),
            dma((2, 3, chips - 1)),
            dma((2, stage_count)),
        ],
        name="back_part",
        compiler_params=pltpu.CompilerParams(
            collective_id=0, has_side_effects=True, vmem_limit_bytes=VMEM_LIMIT
        ),
    )(
        part,
        mixed,
        out_part,
        second_part,
        first_rows,
        grads,
        inputs,
        mean,
        inverse,
        inward,
        outward,
        *places,
        *tables,
        vector,
    )


def widen_kernel(cols, unit, turn_ref, all_ref, inward_ref, outward_ref, expand_ref, contract_ref,
                 held, inward, outward, expand, contract, in_sems, out_sems):
    batch_count, rows, width = all_ref.shape
    half = inward_ref.shape[0]
    unit_rows, unit_blocks = (unit * half // width, width // unit)
    head_rows, head_blocks = (cols * half // width, width // cols)
    late = 2 * unit_rows + unit
    y = turn_ref[0]

    def load(b):
        return pltpu.make_async_copy(all_ref.at[b], held.at[b % 2], in_sems.at[b % 2])

    def stores(b):
        at = b % 2
        sems = iter(range(2 + 2 * 4))
        out = [
            pltpu.make_async_copy(
                outward.at[at],
                outward_ref.at[pl.ds(b * cols, cols), :],
                out_sems.at[at, next(sems)],
            ),
            pltpu.make_async_copy(
                contract.at[at],
                contract_ref.at[pl.ds(b * unit, unit), :],
                out_sems.at[at, next(sems)],
            ),
        ]
        for s in range(2):
            owner = y if s else 1 - y
            column = pl.multiple_of((owner * batch_count + b) * unit, unit)
            out.append(
                pltpu.make_async_copy(
                    expand.at[at, s],
                    expand_ref.at[:, pl.ds(column, unit)],
                    out_sems.at[at, next(sems)],
                )
            )
            for i in range(3):
                column = pl.multiple_of(i * width + (owner * batch_count + b) * cols, cols)
                out.append(
                    pltpu.make_async_copy(
                        inward.at[at, s, i],
                        inward_ref.at[:, pl.ds(column, cols)],
                        out_sems.at[at, next(sems)],
                    )
                )
        return out

    load(0).start()

    def step(b, carry):
        at = b % 2
        load(b).wait()

        @pl.when(b + 1 < batch_count)
        def _():
            load(b + 1).start()

        @pl.when(b >= 2)
        def _():
            for copy in stores(b - 2):
                copy.wait()

        for s in range(2):
            first = s * unit_rows
            for i in range(unit_blocks):
                expand[at, s, i * unit_rows : (i + 1) * unit_rows, :] = held[
                    at, first : first + unit_rows, i * unit : (i + 1) * unit
                ].astype(jnp.float32)
            for part in range(3):
                top = late + (s * 3 + part) * head_rows
                for i in range(head_blocks):
                    inward[at, s, part, i * head_rows : (i + 1) * head_rows, :] = held[
                        at, top : top + head_rows, i * cols : (i + 1) * cols
                    ].astype(jnp.float32)
        contract[at] = held[at, 2 * unit_rows : late, :].astype(jnp.float32)
        outward[at] = held[at, late + 6 * head_rows :, :].astype(jnp.float32)
        for copy in stores(b):
            copy.start()
        return carry

    lax.fori_loop(0, batch_count, step, 0)
    for b in range(max(0, batch_count - 2), batch_count):
        for copy in stores(b):
            copy.wait()


def widen(gathered, cols, unit, half, hidden):
    batch_count, rows, width = gathered.shape
    turn = lax.axis_index("fsdp").astype(jnp.int32)[None]
    f32 = jnp.float32
    dma = pltpu.SemaphoreType.DMA
    hbm = pl.BlockSpec(memory_space=pl.ANY)
    return pl.pallas_call(
        functools.partial(widen_kernel, cols, unit),
        out_shape=(
            jax.ShapeDtypeStruct((half, 3 * width), f32),
            jax.ShapeDtypeStruct((half, width), f32),
            jax.ShapeDtypeStruct((half, hidden), f32),
            jax.ShapeDtypeStruct((hidden // 2, width), f32),
        ),
        in_specs=[pl.BlockSpec(memory_space=pltpu.SMEM), hbm],
        out_specs=(hbm,) * 4,
        scratch_shapes=[
            pltpu.VMEM((2, rows, width), gathered.dtype),
            pltpu.VMEM((2, 2, 3, half, cols), f32),
            pltpu.VMEM((2, cols, width), f32),
            pltpu.VMEM((2, 2, half, unit), f32),
            pltpu.VMEM((2, unit, width), f32),
            dma((2,)),
            dma((2, 10)),
        ],
        name="widen",
        compiler_params=pltpu.CompilerParams(vmem_limit_bytes=VMEM_LIMIT),
    )(turn, gathered)


def fold(columns, unit, half):
    width = columns.shape[0]
    blocks = width // unit
    parts = columns.reshape(2, blocks, half // blocks, unit).transpose(0, 2, 1, 3)
    return parts.reshape(2, -1, width)


def dot(left, right, contract=((1,), (0,))):
    return lax.dot_general(left, right, (contract, ((), ())), preferred_element_type=jnp.float32)


def normalize(values):
    center = values - jnp.mean(values, axis=-1, keepdims=True)
    inverse = lax.rsqrt(jnp.mean(center * center, axis=-1, keepdims=True) + EPSILON)
    return (center * inverse, inverse)


def norm_backward(upstream, normed, inverse, factor):
    scaled = upstream * factor
    middle = jnp.mean(scaled, axis=-1, keepdims=True)
    coupled = jnp.mean(scaled * normed, axis=-1, keepdims=True)
    result = inverse * (scaled - middle - normed * coupled)
    return (result, jnp.sum(upstream * normed, axis=0), jnp.sum(upstream, axis=0))


def slot_positions(span_order, first_slot, slot_count, span_size):
    slot_index = first_slot + jnp.arange(slot_count, dtype=jnp.int32)
    owners = slot_index // (2 * span_size)
    places = jnp.arange(span_order.shape[0], dtype=jnp.int32)
    leading = jnp.sum(jnp.where(owners[:, None] == places[None, :], span_order[None, :], 0), axis=1)
    spans = 2 * span_order.shape[0]
    picked = jnp.where(slot_index // span_size % 2 == 0, leading, spans - 1 - leading)
    return picked * span_size + slot_index % span_size


def rotary_tables(positions):
    half_rot = ROT // 2
    angular = jnp.exp(
        jnp.arange(half_rot, dtype=jnp.float32) * (-2.0 * math.log(ROTARY_BASE) / ROT)
    )
    angles = positions.astype(jnp.float32)[:, None] * angular[None, :]
    angles = jnp.concatenate([angles, angles], axis=1)
    return (jnp.cos(angles), jnp.sin(angles))


def rotate(tensor, cosine, sine_table):
    half_rot = ROT // 2
    leading_part = tensor[..., :ROT]
    turned = jnp.concatenate([-leading_part[..., half_rot:], leading_part[..., :half_rot]], axis=-1)
    rotated = leading_part * cosine[:, None, :] + turned * sine_table[:, None, :]
    return jnp.concatenate([rotated, tensor[..., ROT:]], axis=-1)


def unrotate(tensor, cosine, sine_table):
    half_rot = ROT // 2
    leading_part = tensor[..., :ROT]
    weighted = leading_part * sine_table[:, None, :]
    turned = jnp.concatenate([weighted[..., half_rot:], -weighted[..., :half_rot]], axis=-1)
    return jnp.concatenate([leading_part * cosine[:, None, :] + turned, tensor[..., ROT:]], axis=-1)


def attention(mixed, place, cosine, sine_table, heads):
    sequences, length, _ = mixed.shape
    parts = mixed.reshape(sequences, length, 4, heads, HEAD_DIM)
    queries, keys, values, grads = (parts[:, :, i] for i in range(4))
    scale = 1.0 / math.sqrt(HEAD_DIM)
    scores = jnp.einsum("sqhd,skhd->shqk", queries, keys, preferred_element_type=jnp.float32)
    allowed = place[None, :] <= place[:, None]
    scores = jnp.where(allowed, scores * scale, MASKED)
    peak = jnp.max(scores, axis=-1, keepdims=True)
    log_total = peak + jnp.log(jnp.sum(jnp.exp(scores - peak), axis=-1, keepdims=True))
    probs = jnp.exp(scores - log_total)
    soft = probs.astype(jnp.bfloat16)
    context = jnp.einsum("shqk,skhd->sqhd", soft, values, preferred_element_type=jnp.float32)
    context = context.astype(jnp.bfloat16)
    delta = jnp.einsum(
        "sqhd,sqhd->shq", grads.astype(jnp.float32), context.astype(jnp.float32)
    )
    value_grad = jnp.einsum("shqk,sqhd->skhd", soft, grads, preferred_element_type=jnp.float32)
    probs_grad = jnp.einsum("sqhd,skhd->shqk", grads, values, preferred_element_type=jnp.float32)
    score_grad = (probs * (probs_grad - delta[..., None]) * scale).astype(jnp.bfloat16)
    query_grad = jnp.einsum("shqk,skhd->sqhd", score_grad, keys, preferred_element_type=jnp.float32)
    key_grad = jnp.einsum("shqk,sqhd->skhd", score_grad, queries, preferred_element_type=jnp.float32)
    query_grad = unrotate(query_grad, cosine, sine_table)
    key_grad = unrotate(key_grad, cosine, sine_table)
    back = jnp.stack([query_grad, key_grad, value_grad], axis=2)
    shift = jnp.sum(back, axis=(0, 1)).reshape(-1)
    full = jnp.concatenate([context[:, :, None], back.astype(jnp.bfloat16)], axis=2)
    return (full.reshape(sequences, length, 4 * heads * HEAD_DIM), shift)


def body(
    layer_input,
    out_grad,
    span_order,
    inward,
    inward_bias,
    outward,
    outward_bias,
    expand,
    expand_bias,
    contract,
    contract_bias,
    first_gain,
    first_bias,
    second_gain,
    second_bias,
):
    batch_count, fsdp_count = (lax.axis_size("batch"), lax.axis_size("fsdp"))
    context_count = lax.axis_size("ctx")
    context_index = lax.axis_index("ctx")
    batch_index, fsdp_index = (lax.axis_index("batch"), lax.axis_index("fsdp"))
    plane = batch_count * fsdp_count
    tokens, width = layer_input.shape[1:]
    hidden_units = expand.shape[1]
    head_cols = width // plane
    unit_cols = hidden_units // plane
    heads = head_cols // HEAD_DIM
    length = tokens * context_count
    span_size = tokens // 2
    own_sequences = plane // context_count

    def full_vectors(*vectors):
        sizes = [v.shape[0] for v in vectors]
        gathered = lax.all_gather(jnp.concatenate(vectors), "fsdp")
        out, start = ([], 0)
        for size in sizes:
            out.append(gathered[:, start : start + size].reshape(-1).astype(jnp.float32))
            start += size
        return out

    (
        inward_offset,
        outward_offset,
        expand_offset,
        contract_offset,
        gain_first,
        offset_first,
        gain_second,
        offset_second,
    ) = full_vectors(
        inward_bias,
        outward_bias,
        expand_bias,
        contract_bias,
        first_gain,
        first_bias,
        second_gain,
        second_bias,
    )

    def chunk(array, cols):
        rows = array.shape[0]
        parts = array.reshape(rows, -1, fsdp_count, batch_count, cols)
        mine = lax.dynamic_index_in_dim(parts, batch_index, 3, keepdims=False)
        return mine.transpose(2, 0, 1, 3).reshape(fsdp_count, rows, -1)

    to_send = jnp.concatenate([chunk(inward, head_cols), chunk(expand, unit_cols)], axis=2)
    weights = lax.all_to_all(to_send, "fsdp", 0, 0).reshape(width, -1)
    inward_cols = weights[:, : 3 * head_cols]
    expand_cols = weights[:, 3 * head_cols :]
    outward_rows = lax.dynamic_slice_in_dim(outward, batch_index * head_cols, head_cols, 0)
    contract_rows = lax.dynamic_slice_in_dim(contract, batch_index * unit_cols, unit_cols, 0)
    plane_index = fsdp_index * batch_count + batch_index
    inward_shift_in = lax.dynamic_index_in_dim(
        inward_offset.reshape(3, plane, head_cols), plane_index, 1, keepdims=False
    ).reshape(-1)
    expand_shift_in = lax.dynamic_slice_in_dim(expand_offset, plane_index * unit_cols, unit_cols, 0)

    pair = jnp.stack([layer_input[0], out_grad[0]])
    pair_all = lax.all_gather(pair, PLANE, axis=1, tiled=True)
    grads_all = pair_all[1]
    rows_all = pair_all[0].astype(jnp.float32)
    normed, inverse = normalize(rows_all)
    first_rows = (normed * gain_first + offset_first).astype(jnp.bfloat16)
    second_rows = (normed * gain_second + offset_second).astype(jnp.bfloat16)

    local_place = slot_positions(span_order, context_index * tokens, tokens, span_size)
    cosine, sine_table = rotary_tables(local_place)
    cosine_plane = jnp.tile(cosine, (plane, 1))
    sine_plane = jnp.tile(sine_table, (plane, 1))
    projected = dot(first_rows, inward_cols) + inward_shift_in
    projected = projected.reshape(plane * tokens, 3 * heads, HEAD_DIM)
    turned = rotate(projected[:, : 2 * heads], cosine_plane, sine_plane)
    context_grad = dot(grads_all, outward_rows, ((1,), (1,)))
    mixed = jnp.concatenate(
        [
            turned.reshape(plane * tokens, -1),
            projected[:, 2 * heads :].reshape(plane * tokens, -1),
            context_grad,
        ],
        axis=1,
    ).astype(jnp.bfloat16)
    mixed = mixed.reshape(context_count, own_sequences, tokens, 4 * head_cols)
    mixed = lax.all_to_all(mixed, "ctx", 0, 0)
    mixed = mixed.transpose(1, 0, 2, 3).reshape(own_sequences, length, 4 * head_cols)
    place = slot_positions(span_order, 0, length, span_size)
    cosine_all, sine_all = rotary_tables(place)

    before = dot(second_rows, expand_cols) + expand_shift_in
    tail = 1.0 + lax.erf(before * HALF_ROOT)
    activated = (0.5 * before * tail).astype(jnp.bfloat16)
    slope = 0.5 * tail + before * jnp.exp(-0.5 * before * before) * NORMAL_PEAK
    before_grad = dot(grads_all, contract_rows, ((1,), (1,))) * slope
    expand_sum = jnp.sum(before_grad, axis=0)
    before_rows = before_grad.astype(jnp.bfloat16)
    expand_delta = dot(second_rows, before_rows, ((0,), (0,)))
    contract_delta = dot(activated, grads_all, ((0,), (0,)))
    out_part = dot(activated, contract_rows)
    second_part = dot(before_rows, expand_cols, ((1,), (1,)))

    hidden = layer_input[0].astype(jnp.float32)
    grad_float = out_grad[0].astype(jnp.float32)
    normed_mine, inverse_mine = normalize(hidden)
    half = width // fsdp_count

    def spread(values, sizes):
        wide = jnp.zeros((sizes[0], plane, sizes[1]), jnp.float32)
        values = values.reshape(sizes[0], sizes[1])
        return lax.dynamic_update_index_in_dim(wide, values, plane_index, 1).reshape(-1)

    bias_total = jnp.sum(grad_float, axis=0)
    expand_wide = spread(expand_sum, (1, unit_cols))

    if head_cols % 128 == 0:
        slots = fold(expand_delta, unit_cols, half).astype(jnp.bfloat16)
        slots = jnp.where(fsdp_index == 0, slots[::-1], slots).reshape(-1, width)
        part = jnp.concatenate([slots, contract_delta.astype(jnp.bfloat16)], axis=0)
        second_sums = [jnp.sum(second_part * normed, axis=0), jnp.sum(second_part, axis=0)]
        nothing = jnp.zeros((width,), jnp.float32)
        inward_wide = jnp.zeros((3 * width,), jnp.float32)
        vectors = [inward_wide, bias_total, expand_wide, *second_sums, nothing, nothing]
        half_rot = ROT // 2
        blank = jnp.zeros((length, HEAD_DIM - ROT), jnp.float32)
        zero = jnp.zeros((length, half_rot), jnp.float32)
        tables = [
            jnp.concatenate([cosine_all, blank + 1.0], axis=1),
            jnp.concatenate([zero, sine_all[:, half_rot:], blank], axis=1),
            jnp.concatenate([-sine_all[:, :half_rot], zero, blank], axis=1),
        ]
        tables = [jnp.tile(table, (1, heads)) for table in tables]
        gathered, mine, whole = back_part(
            part,
            mixed,
            out_part.astype(jnp.bfloat16),
            second_part.astype(jnp.bfloat16),
            first_rows,
            grads_all,
            pair_all[0],
            jnp.mean(rows_all, axis=-1, keepdims=True),
            inverse,
            inward_cols,
            outward_rows,
            (place[:, None], place[None, :]),
            tables,
            jnp.concatenate(vectors).reshape(-1, 128),
            tokens,
            heads,
            hidden_units,
        )
        totals = widen(gathered, head_cols, unit_cols, half, hidden_units)
        whole = whole.reshape(-1)
        order = (0, 1, 2, 5, 6, 3, 4)
    else:
        back, inward_sum = attention(mixed, place, cosine_all, sine_all, heads)
        back = back.reshape(own_sequences, context_count, tokens, 4 * head_cols)
        back = lax.all_to_all(back.transpose(1, 0, 2, 3), "ctx", 0, 0)
        back = back.reshape(plane * tokens, 4 * head_cols)
        context_rows = back[:, :head_cols]
        projected_rows = back[:, head_cols:]
        inward_delta = dot(first_rows, projected_rows, ((0,), (0,)))
        outward_delta = dot(context_rows, grads_all, ((0,), (0,)))
        out_part = out_part + dot(context_rows, outward_rows)
        first_part = dot(projected_rows, inward_cols, ((1,), (1,)))
        stacked = jnp.stack([second_part, out_part, first_part], axis=1).astype(jnp.bfloat16)
        mine = lax.psum_scatter(stacked, PLANE, scatter_dimension=0, tiled=True)
        mine = mine.transpose(1, 0, 2).astype(jnp.float32)
        columns = jnp.concatenate([inward_delta, expand_delta], axis=1).astype(jnp.bfloat16)
        rows = jnp.concatenate([outward_delta, contract_delta], axis=0).astype(jnp.bfloat16)
        columns, rows = lax.psum((columns, rows), "ctx")
        columns = lax.all_to_all(columns.reshape(fsdp_count, half, -1), "fsdp", 0, 0)
        columns = lax.all_gather(columns, "batch")
        rows = lax.all_gather(rows, "batch").astype(jnp.float32)
        columns = columns.transpose(2, 1, 0, 3).astype(jnp.float32)
        inward_total = columns[..., : 3 * head_cols].reshape(
            half, fsdp_count, batch_count, 3, head_cols
        )
        totals = (
            inward_total.transpose(0, 3, 1, 2, 4).reshape(half, 3 * width),
            rows[:, :head_cols].reshape(half, width),
            columns[..., 3 * head_cols :].reshape(half, hidden_units),
            rows[:, head_cols:].reshape(-1, width),
        )
        _, second_scale, second_shift = norm_backward(
            mine[0], normed_mine, inverse_mine, gain_second
        )
        _, first_scale, first_shift = norm_backward(mine[2], normed_mine, inverse_mine, gain_first)
        vectors = [
            spread(inward_sum, (3, head_cols)),
            bias_total,
            expand_wide,
            first_scale,
            first_shift,
            second_scale,
            second_shift,
        ]
        whole = lax.psum(jnp.concatenate(vectors), ("batch", "ctx", "fsdp"))
        order = tuple(range(7))

    result = (hidden + (mine[1] + outward_offset) + contract_offset).astype(jnp.bfloat16)
    second_input, _, _ = norm_backward(mine[0], normed_mine, inverse_mine, gain_second)
    first_input, _, _ = norm_backward(mine[2], normed_mine, inverse_mine, gain_first)
    input_delta = grad_float + first_input + second_input
    halves, start = ([], 0)
    for vector in vectors:
        size = vector.shape[0] // fsdp_count
        halves.append(lax.dynamic_slice_in_dim(whole, start + fsdp_index * size, size, 0))
        start += vector.shape[0]
    halves = [halves[i] for i in order]
    return (
        result[None],
        input_delta[None],
        totals[0],
        halves[0],
        totals[1],
        halves[1],
        totals[2],
        halves[2],
        totals[3],
        halves[1],
        halves[3],
        halves[4],
        halves[5],
        halves[6],
    )


def solution(mesh):
    rows = P(PLANE, "ctx", None)
    matrix, vector = (P("fsdp", None), P("fsdp"))
    in_specs = (rows, rows, P()) + (matrix, vector) * 4 + (vector,) * 4
    out_specs = (rows, rows) + (matrix, vector) * 4 + (vector,) * 4
    return jax.shard_map(body, mesh=mesh, in_specs=in_specs, out_specs=out_specs, check_vma=False)
```

```python
import functools
import math

import jax
import jax.numpy as jnp
from jax import lax
from jax.experimental import pallas as pl
from jax.experimental.pallas import tpu as pltpu
from jax.sharding import PartitionSpec as P

HEAD_DIM = 64
ROT = 16

EPSILON = 1e-05
ROTARY_BASE = 10000.0
MASKED = -1e30
HALF_ROOT = 0.7071067811865476
NORMAL_PEAK = 0.3989422804014327
PLANE = ("batch", "fsdp")


MESH = pl.DeviceIdType.MESH
CORES = 2
VMEM_LIMIT = 56 * 2**20


def here():
    return (lax.axis_index("batch"), lax.axis_index("ctx"), lax.axis_index("fsdp"))


def swapped(index, step):
    return index + step * (1 - 2 * (index // step % 2))


def greet(partners):
    barrier = pltpu.get_barrier_semaphore()
    for partner in partners:
        pl.semaphore_signal(barrier, inc=1, device_id=partner, device_id_type=MESH)
    pl.semaphore_wait(barrier, len(partners))


def remote(src, dst, send, recv, target):
    return pltpu.make_async_remote_copy(
        src_ref=src,
        dst_ref=dst,
        send_sem=send,
        recv_sem=recv,
        device_id=target,
        device_id_type=MESH,
    )


LAG = 2


def layer_kernel(
    sizes,
    tokens,
    heads,
    counts,
    piece,
    input_ref,
    grad_ref,
    order_ref,
    small_ref,
    inward_ref,
    outward_ref,
    expand_ref,
    contract_ref,
    sums_ref,
    result_ref,
    input_grad_ref,
    shifts_ref,
    inputs,
    grads,
    small,
    inward,
    outward,
    expand,
    contract,
    cosine,
    sine,
    stats,
    first_rows,
    second_rows,
    work,
    out_rows,
    second_back,
    mixed_out,
    mixed,
    heads_sum,
    back_out,
    back_in,
    inward_sum,
    part,
    mine,
    reduced,
    reduced_right,
    near,
    across_in,
    far,
    token_sum,
    vector_in,
    vector_sum,
    load_sems,
    small_sems,
    weight_sems,
    gather_sems,
    share_sems,
    there_sends,
    there_recvs,
    there_own,
    back_own,
    turn_sems,
    reduce_sems,
    back_sends,
    back_recvs,
    row_sems,
    chip_sems,
    core_sems,
    keep_sems,
    near_sems,
    across_sems,
    far_sems,
    vector_sems,
):
    batch_count, context_count, fsdp_count = sizes
    early_other, early, late_other, late = counts
    b, z, y = here()
    chips = batch_count // CORES
    core = b % CORES
    chip = b // CORES
    width = part.shape[1]
    half_width = width // 2
    cols = heads * HEAD_DIM
    unit = contract.shape[0]
    plane = batch_count * fsdp_count
    index = y * batch_count + b
    own_sequences = plane // context_count
    length = tokens * context_count
    steps = early + late
    early_rows = 2 * early * piece
    last = context_count - 1
    lines = width // 128
    f32, half_type = (jnp.float32, part.dtype)
    group_rows = fsdp_count * tokens

    sibling = (chip * CORES + (1 - core), z, y)
    across = (b, z, 1 - y)
    peers = [((chip + d) % chips * CORES + core, z, y) for d in range(1, chips)]
    sources = [(chip + chips - d) % chips * CORES + core for d in range(1, chips)]
    others = [(b, (z + d) % context_count, y) for d in range(1, context_count)]
    stages = []
    step = 1
    while step < batch_count:
        stages.append((swapped(b, step), z, y))
        step *= 2
    stages.append(across)
    step = 1
    while step < context_count:
        stages.append((b, swapped(z, step), y))
        step *= 2

    def sem(sems, *index):
        return (sems.at[(0, *index)], sems.at[(1, *index)])


    plane_arrays = (inputs, grads)
    plane_sources = (input_ref.at[0], grad_ref.at[0])

    def block(array, batch, fsdp):
        row = pl.multiple_of((batch * fsdp_count + fsdp) * tokens, tokens)
        return plane_arrays[array].at[pl.ds(row, tokens), :]

    def own_load(array):
        return pltpu.make_async_copy(
            plane_sources[array], block(array, b, y), load_sems.at[array]
        )

    def to_across(array):
        return remote(
            plane_sources[array], block(array, b, y), *sem(gather_sems, array, 0), across
        )

    def to_peer(array, d):
        return remote(
            plane_sources[array], block(array, b, y), *sem(gather_sems, array, 1 + d), peers[d]
        )

    def on_to_peer(array, d):
        at = block(array, b, 1 - y)
        return remote(at, at, *sem(gather_sems, array, chips + d), peers[d])

    def share(array, i):
        if i == 0:
            return remote(
                plane_sources[array], block(array, b, y), *sem(share_sems, array, 0), sibling
            )
        if i == 1:
            at = block(array, b, 1 - y)
        else:
            d = (i - 2) % (chips - 1)
            at = block(array, sources[d], y if i - 2 < chips - 1 else 1 - y)
        return remote(at, at, *sem(share_sems, array, i), sibling)

    def weight_copies(owner, local):
        rows = pl.ds(pl.multiple_of(y * half_width, half_width), half_width)
        place = owner * batch_count + b
        out = []
        for i in range(4):
            if i < 3:
                column = pl.multiple_of(i * width + place * cols, cols)
                source = inward_ref.at[:, pl.ds(column, cols)]
                target = inward.at[rows, i * cols : (i + 1) * cols]
            else:
                column = pl.multiple_of(place * unit, unit)
                source = expand_ref.at[:, pl.ds(column, unit)]
                target = expand.at[rows, :]
            if local:
                out.append(pltpu.make_async_copy(source, target, load_sems.at[2 + i]))
            else:
                out.append(remote(source, target, *sem(weight_sems, i), across))
        return out

    row_loads = [
        pltpu.make_async_copy(
            outward_ref.at[pl.ds(pl.multiple_of(b * cols, cols), cols), :],
            outward,
            load_sems.at[6],
        ),
        pltpu.make_async_copy(
            contract_ref.at[pl.ds(pl.multiple_of(b * unit, unit), unit), :],
            contract,
            load_sems.at[7],
        ),
    ]
    weight_loads = weight_copies(y, True)
    weight_sends = weight_copies(1 - y, False)
    small_copy = remote(small_ref, small.at[1], *sem(small_sems, 0), across)

    own_load(0).start()
    own_load(1).start()
    for load in weight_loads + row_loads:
        load.start()
    greet([sibling, across] + peers + others)
    small_copy.start()
    for array in range(2):
        to_across(array).start()
        for d in range(chips - 1):
            to_peer(array, d).start()
        share(array, 0).start()
        if array == 0:
            for send in weight_sends[:3]:
                send.start()
    weight_sends[3].start()
    small[0] = small_ref[...]


    def positions(shape, dimension):
        slot = lax.broadcasted_iota(jnp.int32, shape, dimension)
        owner = slot // tokens
        leading = jnp.zeros(shape, jnp.int32)
        for c in range(context_count):
            leading = jnp.where(owner == c, order_ref[c], leading)
        span = tokens // 2
        second = slot // span % 2
        picked = jnp.where(second == 0, leading, 2 * context_count - 1 - leading)
        return picked * span + slot % span

    half_rot = ROT // 2
    lane = lax.broadcasted_iota(jnp.int32, (1, cols), 1) % HEAD_DIM
    angular = jnp.exp((lane % half_rot).astype(f32) * (-2.0 * math.log(ROTARY_BASE) / ROT))
    angles = positions((length, cols), 0).astype(f32) * angular
    cosine[...] = jnp.where(lane < ROT, jnp.cos(angles), 1.0)
    sine[...] = jnp.where(lane < ROT, jnp.sin(angles), 0.0)
    low = (lane < half_rot).astype(f32)
    high = 1.0 - low

    def turn(value, rows, sign):
        weight = sine[rows, :] * sign
        return (
            value * cosine[rows, :]
            - pltpu.roll(value, cols - half_rot, 1) * (weight * low)
            + pltpu.roll(value, half_rot, 1) * (weight * high)
        )


    small_copy.wait_recv()
    vector_rows = [3 * lines, lines, unit * plane // 128] + [lines] * 5
    starts = [sum(vector_rows[:i]) // fsdp_count for i in range(8)]

    def vector_line(which, line):
        share_lines = vector_rows[which] // fsdp_count
        owner = line // share_lines
        at = (owner - y) * (owner - y)
        return small[at, pl.ds(starts[which] + line % share_lines, 1), :]

    def whole(which):
        return jnp.concatenate([vector_line(which, line) for line in range(lines)], axis=1)

    def chunk(which, first, count):
        return jnp.concatenate([vector_line(which, first + i) for i in range(count)], axis=1)


    def group(u):
        return (chip + u // CORES) % chips * CORES + (core + u % CORES) % CORES

    def rows_of(u):
        return pl.ds(pl.multiple_of(group(u) * group_rows, group_rows), group_rows)

    def bring(array, u):
        distance, other = (u // CORES, u % CORES)
        if other == 0 and distance == 0:
            own_load(array).wait()
            to_across(array).wait_recv()
            for d in range(chips - 1):
                on_to_peer(array, d).start()
            share(array, 1).start()
        elif other == 0:
            d = chips - distance - 1
            to_peer(array, d).wait_recv()
            share(array, 2 + d).start()
            on_to_peer(array, d).wait_recv()
            share(array, 1 + chips + d).start()
        elif distance == 0:
            share(array, 0).wait_recv()
            share(array, 1).wait_recv()
        else:
            d = chips - distance - 1
            share(array, 2 + d).wait_recv()
            share(array, 1 + chips + d).wait_recv()

    gains = [whole(4), whole(5), whole(6), whole(7)]
    inward_bias = jnp.concatenate(
        [
            chunk(0, i * lines + index * (cols // 128), cols // 128)
            for i in range(3)
        ],
        axis=1,
    )

    def project(u):
        rows = rows_of(u)
        x = inputs[rows, :].astype(f32)
        mean = jnp.mean(x, axis=-1, keepdims=True)
        center = x - mean
        inverse = lax.rsqrt(jnp.mean(center * center, axis=-1, keepdims=True) + EPSILON)
        stats[rows, 0:1] = mean
        stats[rows, 1:2] = inverse
        normed = center * inverse
        first = (normed * gains[0] + gains[1]).astype(half_type)
        first_rows[rows, :] = first
        second_rows[rows, :] = (normed * gains[2] + gains[3]).astype(half_type)
        projected = dot(first, inward[...]) + inward_bias
        local = pl.ds(pl.multiple_of(z * tokens, tokens), tokens)
        for f in range(fsdp_count):
            at = pl.ds(pl.multiple_of((group(u) * fsdp_count + f) * tokens, tokens), tokens)
            piece_rows = projected[f * tokens : (f + 1) * tokens, :]
            for i in range(3):
                value = piece_rows[:, i * cols : (i + 1) * cols]
                if i < 2:
                    value = turn(value, local, 1.0)
                mixed_out[at, i * cols : (i + 1) * cols] = value.astype(half_type)

    def there_copy(p):
        owner, s = (p // own_sequences, p % own_sequences)
        source = mixed_out.at[pl.ds(pl.multiple_of(p * tokens, tokens), tokens), :]
        target = mixed.at[s, pl.ds(pl.multiple_of(z * tokens, tokens), tokens), :]
        return (owner, s, source, target)

    def upstream(u):
        rows = rows_of(u)
        value = dot(grads[rows, :], outward[...], ((1,), (1,)))
        mixed_out[rows, 3 * cols :] = value.astype(half_type)
        for f in range(fsdp_count):
            p = group(u) * fsdp_count + f
            owner, s, source, target = there_copy(p)

            @pl.when(owner == z)
            def _():
                pltpu.make_async_copy(source, target, there_own.at[s]).start()

            @pl.when(owner != z)
            def _():
                remote(
                    source, target, there_sends.at[p], there_recvs.at[s, z], (b, owner, y)
                ).start()

    def there(s):
        block_at = mixed.at[s, pl.ds(0, tokens), :]
        pltpu.make_async_copy(block_at, block_at, there_own.at[s]).wait()
        for d in range(1, context_count):
            source = (z + d) % context_count
            at = mixed.at[s, pl.ds(pl.multiple_of(source * tokens, tokens), tokens), :]
            remote(at, at, there_sends.at[0], there_recvs.at[s, source], others[0]).wait_recv()

    order = [u for u in range(0, batch_count, CORES)] + [u for u in range(1, batch_count, CORES)]
    for array in range(2):
        for u in order:
            bring(array, u)
            if array == 0:
                if u == 0:
                    for i in range(3):
                        weight_loads[i].wait()
                        weight_sends[i].wait_recv()
                project(u)
            else:
                if u == 0:
                    row_loads[0].wait()
                upstream(u)


    row_loads[1].wait()
    weight_loads[3].wait()
    weight_sends[3].wait_recv()
    expand_bias = chunk(2, index * (unit // 128), unit // 128)
    nothing = jnp.zeros((1, width), f32)

    def normed_rows(rows):
        return (inputs[rows, :].astype(f32) - stats[rows, 0:1]) * stats[rows, 1:2]

    def forward_tile(i, carry):
        expand_total, scale_total, shift_total = carry
        rows = pl.ds(pl.multiple_of(i * group_rows, group_rows), group_rows)
        before = dot(second_rows[rows, :], expand[...]) + expand_bias
        tail = 1.0 + lax.erf(before * HALF_ROOT)
        activated = (0.5 * before * tail).astype(half_type)
        slope = 0.5 * tail + before * jnp.exp(-0.5 * before * before) * NORMAL_PEAK
        before_grad = dot(grads[rows, :], contract[...], ((1,), (1,))) * slope
        before_rows = before_grad.astype(half_type)
        work[rows, :unit] = activated
        work[rows, unit:] = before_rows
        out_rows[rows, :] = dot(activated, contract[...]).astype(half_type)
        value = dot(before_rows, expand[...], ((1,), (1,)))
        second_back[rows, :] = value.astype(half_type)
        return (
            expand_total + jnp.sum(before_grad, axis=0, keepdims=True),
            scale_total + jnp.sum(value * normed_rows(rows), axis=0, keepdims=True),
            shift_total + jnp.sum(value, axis=0, keepdims=True),
        )

    forward_sums = lax.fori_loop(
        0, batch_count, forward_tile, (jnp.zeros((1, unit), f32), nothing, nothing)
    )

    def expand_half(s, carry):
        owner = (1 - y) * (1 - s) + y * s
        column = pl.multiple_of(owner * half_width, half_width)
        delta = dot(second_rows[:, pl.ds(column, half_width)], work[:, unit:], ((0,), (0,)))
        group = unit * half_width // width
        at = pl.ds(pl.multiple_of(s * group, group), group)
        for j in range(width // unit):
            part[at, j * unit : (j + 1) * unit] = delta[j * group : (j + 1) * group, :].astype(
                half_type
            )
        return carry

    lax.fori_loop(0, 2, expand_half, 0)
    part[early_rows - unit : early_rows, :] = dot(
        work[:, :unit], grads[...], ((0,), (0,))
    ).astype(half_type)


    def place(half, k):
        is_late = jnp.minimum(k // early, 1)
        other = early_other * (1 - is_late) + late_other * is_late
        count = early * (1 - is_late) + late * is_late
        j = k - early * is_late
        is_own = jnp.minimum(j // other, 1)
        row = (half * other + j) * (1 - is_own) + (
            2 * other + half * (count - other) + j - other
        ) * is_own
        return pl.multiple_of((2 * early * is_late + row) * piece, piece)

    def own(k):
        is_late = jnp.minimum(k // early, 1)
        other = early_other * (1 - is_late) + late_other * is_late
        return jnp.minimum((k - early * is_late) // other, 1)

    def rows_at(ref, row):
        return ref.at[pl.ds(row, piece), :]

    def sums_at(batch, row):
        return sums_ref.at[batch, pl.ds(row, piece), :]

    def back_copy(half, k, side, target):
        at = rows_at(mine, place(half, k))
        return remote(at, at, back_sends.at[side, half, k], back_recvs.at[half, k], target)

    def row_copy(half, k):
        row = place(half, k)
        return remote(rows_at(mine, row), sums_at(b, row), *sem(row_sems, half, k), across)

    def keep_copy(half, k):
        row = place(half, k)
        return pltpu.make_async_copy(rows_at(mine, row), sums_at(b, row), keep_sems.at[half, k])

    def chip_copy(d, half, k, from_mine):
        row = place(half, k)
        source = rows_at(mine, row) if from_mine else sums_at(b, row)
        return remote(source, sums_at(b, row), *sem(chip_sems, d, half, k), peers[d])

    def core_copy(d, half, k, from_mine, batch):
        row = place(half, k)
        source = rows_at(mine, row) if from_mine else sums_at(batch, row)
        return remote(source, sums_at(batch, row), *sem(core_sems, d, half, k), sibling)

    def spread(half, k, from_mine):
        for d in range(chips - 1):
            chip_copy(d, half, k, from_mine).start()
        core_copy(0, half, k, from_mine, b).start()

    def arrived(half, k):
        for d in range(chips - 1):
            chip_copy(d, half, k, False).wait_recv()
            core_copy(1 + d, half, k, False, sources[d]).start()

    def finish(half, k):
        @pl.when(own(k) == 0)
        def _():
            row_copy(half, k).start()

        @pl.when(own(k) == 1)
        def _():
            keep_copy(half, k).start()
            spread(half, k, True)

    left = (b, (z + last) % context_count, y)
    right = (b, (z + 1) % context_count, y)

    def reduce_copy(half, k, source, stream, target):
        row = place(half, k)
        if stream:
            landing = reduced_right.at[pl.ds(pl.multiple_of(k * piece, piece), piece), :]
        else:
            landing = rows_at(reduced, row)
        return remote(
            rows_at(source, row), landing, *sem(reduce_sems, stream, half, k), target
        )

    def pieces(t, half):
        root = last // 2 if half == 0 else context_count // 2
        depth = max(root, last - root)
        at_root = z == root
        is_left = z < root
        distance = jnp.where(is_left, root - z, z - root)
        leaf = (z == 0) | (z == last)
        k = t - LAG * (depth - distance)

        def send(source):
            @pl.when(z == root + 1)
            def _():
                reduce_copy(half, k, source, 1, left).start()

            @pl.when(z > root + 1)
            def _():
                reduce_copy(half, k, source, 0, left).start()

            @pl.when(is_left)
            def _():
                reduce_copy(half, k, source, 0, right).start()

        @pl.when((k >= 0) & (k < steps))
        def _():
            row = place(half, k)
            here_at = pl.ds(row, piece)

            @pl.when(at_root)
            def _():
                value = part[here_at, :].astype(f32)
                if root > 0:
                    reduce_copy(half, k, part, 0, right).wait_recv()
                    value = value + reduced[here_at, :].astype(f32)
                if root < last:
                    reduce_copy(half, k, part, 1, left).wait_recv()
                    came = reduced_right[pl.ds(pl.multiple_of(k * piece, piece), piece), :]
                    value = value + came.astype(f32)
                mine[here_at, :] = value.astype(half_type)
                if root > 0:
                    back_copy(half, k, 0, left).start()
                if root < last:
                    back_copy(half, k, 1, right).start()
                finish(half, k)

            @pl.when(leaf & jnp.logical_not(at_root))
            def _():
                send(part)

            @pl.when(jnp.logical_not(leaf | at_root))
            def _():
                reduce_copy(half, k, part, 0, right).wait_recv()
                value = part[here_at, :].astype(f32) + reduced[here_at, :].astype(f32)
                reduced[here_at, :] = value.astype(half_type)
                send(reduced)

        k_back = t - LAG * (depth + distance)

        @pl.when(jnp.logical_not(at_root) & (k_back >= 0) & (k_back < steps))
        def _():
            back_copy(half, k_back, 0, left).wait_recv()

            @pl.when(is_left & (z > 0))
            def _():
                back_copy(half, k_back, 0, left).start()

            @pl.when((z > root) & (z < last))
            def _():
                back_copy(half, k_back, 1, right).start()

            finish(half, k_back)

        k_row = k_back - LAG

        @pl.when((k_row >= 0) & (k_row < steps))
        def _():
            @pl.when(own(k_row) == 0)
            def _():
                row_copy(half, k_row).wait_recv()
                spread(half, k_row, False)

            @pl.when(own(k_row) == 1)
            def _():
                arrived(half, k_row)

        k_chip = k_row - 2 * LAG + 1

        @pl.when((k_chip >= 0) & (k_chip < steps))
        def _():
            @pl.when(own(k_chip) == 0)
            def _():
                arrived(half, k_chip)

    def drain(k, carry):
        for half in range(2):
            root = last // 2 if half == 0 else context_count // 2
            for d in range(chips):
                core_copy(d, half, k, False, b).wait_recv()
                core_copy(d, half, k, False, b).wait_send()
                if d:
                    chip_copy(d - 1, half, k, False).wait_send()

            @pl.when(z == root + 1)
            def _():
                reduce_copy(half, k, part, 1, left).wait_send()

            @pl.when((z < root) | (z > root + 1))
            def _():
                reduce_copy(half, k, part, 0, left).wait_send()

            @pl.when((z <= root) & (z > 0))
            def _():
                back_copy(half, k, 0, left).wait_send()

            @pl.when((z >= root) & (z < last))
            def _():
                back_copy(half, k, 1, right).wait_send()

            @pl.when(own(k) == 0)
            def _():
                row_copy(half, k).wait_send()

            @pl.when(own(k) == 1)
            def _():
                keep_copy(half, k).wait()

        return carry


    def attend(n):
        s, h = (n // heads, n % heads)
        columns = [mixed[s, :, i * cols : (i + 1) * cols] for i in range(4)]
        head = lax.broadcasted_iota(jnp.int32, (length, cols), 1) // HEAD_DIM
        picked = head == h
        blank = jnp.zeros((length, cols), half_type)
        _, keys, values, _ = columns
        queries_h, keys_h, values_h, upstream_h = [
            jnp.where(picked, column, blank) for column in columns
        ]
        scale = 1.0 / math.sqrt(HEAD_DIM)
        allowed = positions((1, length), 1) <= positions((length, 1), 0)
        scores = dot(queries_h, keys, ((1,), (1,))) * scale
        scores = jnp.where(allowed, scores, MASKED)
        peak = jnp.max(scores, axis=1, keepdims=True)
        log_total = peak + jnp.log(jnp.sum(jnp.exp(scores - peak), axis=1, keepdims=True))
        probs = jnp.exp(scores - log_total)
        soft = probs.astype(half_type)
        context = dot(soft, values_h)
        delta = jnp.sum(
            upstream_h.astype(f32) * context.astype(half_type).astype(f32), axis=1, keepdims=True
        )
        probs_grad = dot(upstream_h, values, ((1,), (1,)))
        score_grad = (probs * (probs_grad - delta) * scale).astype(half_type)
        results = (
            context,
            dot(score_grad, keys_h),
            dot(score_grad, queries_h, ((0,), (0,))),
            dot(soft, upstream_h, ((0,), (0,))),
        )
        for i, value in enumerate(results):

            @pl.when(h == 0)
            def _():
                heads_sum[i] = value

            @pl.when(h > 0)
            def _():
                heads_sum[i] += value

        @pl.when(h == heads - 1)
        def _():
            back_out[s, :, :cols] = heads_sum[0].astype(half_type)
            for i in range(1, 4):
                value = heads_sum[i]
                if i < 3:
                    value = turn(value, slice(None), -1.0)
                back_out[s, :, i * cols : (i + 1) * cols] = value.astype(half_type)
                total = jnp.sum(value, axis=0, keepdims=True)

                @pl.when(s == 0)
                def _():
                    inward_sum[i - 1 : i, :] = total

                @pl.when(s > 0)
                def _():
                    inward_sum[i - 1 : i, :] += total

            for d in range(context_count):
                turn_copy(s, d).start()

    def turn_copy(s, d):
        target = (z + d) % context_count
        source = back_out.at[s, pl.ds(pl.multiple_of(target * tokens, tokens), tokens), :]
        row = pl.multiple_of((z * own_sequences + s) * tokens, tokens)
        destination = back_in.at[pl.ds(row, tokens), :]
        if d == 0:
            return pltpu.make_async_copy(source, destination, back_own.at[s])
        return remote(source, destination, *sem(turn_sems, s, d - 1), others[d - 1])

    def turned():
        for s in range(own_sequences):
            turn_copy(s, 0).wait()
            for d in range(1, context_count):
                turn_copy(s, d).wait_recv()


    def head_gradients():
        delta = dot(back_in[:, :cols], grads[...], ((0,), (0,))).astype(half_type)
        part[early_rows + 4 * late_other * piece :, :] = delta
        group = cols * half_width // width

        def half_rows(s, carry):
            owner = (1 - y) * (1 - s) + y * s
            column = pl.multiple_of(owner * half_width, half_width)
            delta = dot(
                first_rows[:, pl.ds(column, half_width)], back_in[:, cols:], ((0,), (0,))
            ).astype(half_type)
            top = pl.multiple_of(early_rows + s * 3 * group, group)
            for i in range(3):
                for j in range(width // cols):
                    part[pl.ds(top + i * group, group), j * cols : (j + 1) * cols] = delta[
                        j * group : (j + 1) * group, i * cols : (i + 1) * cols
                    ]
            return carry

        lax.fori_loop(0, 2, half_rows, 0)

    def output_rows():
        def step(i, carry):
            rows = pl.ds(pl.multiple_of(i * group_rows, group_rows), group_rows)
            value = dot(back_in[rows, :cols], outward[...])
            out_rows[rows, :] = (out_rows[rows, :].astype(f32) + value).astype(half_type)
            return carry

        lax.fori_loop(0, batch_count, step, 0)

    first_back = second_rows
    vector_start = len(stages)

    def first_back_rows():
        def step(i, carry):
            scale_total, shift_total = carry
            rows = pl.ds(pl.multiple_of(i * group_rows, group_rows), group_rows)
            value = dot(back_in[rows, cols:], inward[...], ((1,), (1,)))
            first_back[rows, :] = value.astype(half_type)
            return (
                scale_total + jnp.sum(value * normed_rows(rows), axis=0, keepdims=True),
                shift_total + jnp.sum(value, axis=0, keepdims=True),
            )

        first_sums = lax.fori_loop(0, batch_count, step, (nothing, nothing))
        out = vector_sum.at[vector_start]
        out[...] = jnp.zeros(out.shape, f32)

        def put(line, value):
            for j in range(value.shape[1] // 128):
                out[pl.ds(line + j, 1), :] = value[:, j * 128 : (j + 1) * 128]

        for i in range(3):
            put(i * lines + index * (cols // 128), inward_sum[i : i + 1, :])
        first = 3 * lines
        own_rows = pl.ds(pl.multiple_of((b * fsdp_count + y) * tokens, tokens), tokens)
        put(first, jnp.sum(grads[own_rows, :].astype(f32), axis=0, keepdims=True))
        first += lines
        put(first + index * (unit // 128), forward_sums[0])
        first += unit * plane // 128
        for value in forward_sums[1:] + first_sums:
            put(first, value)
            first += lines

    def vector_copy(i):
        source = vector_sum.at[vector_start if i == 0 else i - 1]
        return remote(source, vector_in.at[i], *sem(vector_sems, i), stages[i])


    arrays = (second_back, out_rows, first_back)

    def near_copy(a, c):
        row = pl.multiple_of((c * CORES + 1 - core) * group_rows, group_rows)
        return remote(
            arrays[a].at[pl.ds(row, group_rows), :],
            near.at[a, pl.ds(c * group_rows, group_rows), :],
            *sem(near_sems, a, c),
            sibling,
        )

    def across_copy(a, c):
        row = pl.multiple_of(c * group_rows + (1 - y) * tokens, tokens)
        return remote(
            near.at[a, pl.ds(row, tokens), :],
            across_in.at[a, pl.ds(c * tokens, tokens), :],
            *sem(across_sems, a, c),
            across,
        )

    def far_copy(a, d):
        row = pl.multiple_of((chip + d + 1) % chips * tokens, tokens)
        return remote(
            across_in.at[a, pl.ds(row, tokens), :], far.at[a, d], *sem(far_sems, a, d), peers[d]
        )

    def scatter_first(a):
        for c in range(chips):
            near_copy(a, c).start()

    def scatter_second(a):
        for c in range(chips):
            near_copy(a, c).wait_recv()

            def step(i, carry):
                row = pl.multiple_of((c * CORES + core) * group_rows + i * tokens, tokens)
                value = arrays[a][pl.ds(row, tokens), :].astype(f32)
                at = pl.ds(pl.multiple_of(c * group_rows + i * tokens, tokens), tokens)
                near[a, at, :] = (value + near[a, at, :].astype(f32)).astype(half_type)
                return carry

            lax.fori_loop(0, fsdp_count, step, 0)
            across_copy(a, c).start()

    def scatter_third(a):
        for c in range(chips):
            across_copy(a, c).wait_recv()

        def both(c):
            row = pl.multiple_of(c * group_rows + y * tokens, tokens)
            at = pl.ds(pl.multiple_of(c * tokens, tokens), tokens)
            return (
                near[a, pl.ds(row, tokens), :].astype(f32) + across_in[a, at, :].astype(f32),
                at,
            )

        for d in range(chips - 1):
            value, at = both((chip + d + 1) % chips)
            across_in[a, at, :] = value.astype(half_type)
            far_copy(a, d).start()
        token_sum[a] = both(chip)[0]

    def scatter_last(a):
        value = token_sum[a]
        for d in range(chips - 1):
            far_copy(a, d).wait_recv()
            value = value + far[a, d].astype(f32)
        own_rows = pl.ds(pl.multiple_of((b * fsdp_count + y) * tokens, tokens), tokens)
        x = inputs[own_rows, :].astype(f32)
        if a == 1:
            result_ref[...] = (x + (value + whole(1)) + whole(3)).astype(half_type)
            return
        normed = normed_rows(own_rows)
        scaled = value * (gains[2] if a == 0 else gains[0])
        middle = jnp.mean(scaled, axis=-1, keepdims=True)
        coupled = jnp.mean(scaled * normed, axis=-1, keepdims=True)
        value = stats[own_rows, 1:2] * (scaled - middle - normed * coupled)
        if a == 0:
            input_grad_ref[...] = grads[own_rows, :].astype(f32) + value
        else:
            input_grad_ref[...] += value


    problems = own_sequences * heads
    ready = max(early - 4, problems)
    plan = {}

    def at(slot, work):
        plan.setdefault(slot, []).append(work)

    def scatter(a, slot):
        at(slot, lambda: scatter_first(a))
        at(slot + 3, lambda: scatter_second(a))
        at(slot + 6, lambda: scatter_third(a))
        at(slot + 9, lambda: scatter_last(a))

    scatter(0, 0)
    for s in range(own_sequences):
        at(s * heads, lambda s=s: there(s))
    at(ready, turned)
    at(ready, head_gradients)
    at(ready + 1, output_rows)
    scatter(1, ready + 1)
    at(ready + 2, first_back_rows)
    scatter(2, ready + 2)
    at(ready + 2, lambda: vector_copy(0).start())
    for i in range(len(stages)):

        def vector_step(i=i):
            vector_copy(i).wait_recv()
            before = vector_sum[vector_start if i == 0 else i - 1]
            vector_sum[i] = before + vector_in[i]
            if i + 1 < len(stages):
                vector_copy(i + 1).start()

        at(ready + 4 + 2 * i, vector_step)

    def slot_step(t, carry):
        for half in range(2):
            pieces(t, half)

        for slot, works in sorted(plan.items()):

            @pl.when(t == slot)
            def _():
                for work in works:
                    work()

        @pl.when(t < problems)
        def _():
            attend(t)

        return carry

    depth = context_count // 2
    tail = LAG * (2 * depth + 1)
    slots = max(steps + tail, early + late_other + tail + 2 * LAG - 1, max(plan) + 1)
    lax.fori_loop(0, slots, slot_step, 0)
    first = 0
    out_first = 0
    for count in (3 * lines, lines, unit * plane // 128, lines, lines, lines, lines):
        share_lines = count // fsdp_count
        for j in range(share_lines):
            line = first + y * share_lines + j
            shifts_ref[out_first + j : out_first + j + 1, :] = vector_sum[
                len(stages) - 1, pl.ds(line, 1), :
            ]
        first += count
        out_first += share_lines

    lax.fori_loop(0, steps, drain, 0)
    small_copy.wait_send()
    for send in weight_sends:
        send.wait_send()
    for array in range(2):
        to_across(array).wait_send()
        for d in range(chips - 1):
            to_peer(array, d).wait_send()
            on_to_peer(array, d).wait_send()
        for i in range(2 * chips):
            share(array, i).wait_send()
    for p in range(plane):
        _, _, source, target = there_copy(p)

        @pl.when(p // own_sequences != z)
        def _():
            remote(
                source, target, there_sends.at[p], there_recvs.at[0, 0], others[0]
            ).wait_send()

    for i in range(len(stages)):
        vector_copy(i).wait_send()
    for s in range(own_sequences):
        for d in range(1, context_count):
            turn_copy(s, d).wait_send()
    for a in range(3):
        for c in range(chips):
            near_copy(a, c).wait_send()
            across_copy(a, c).wait_send()
        for d in range(chips - 1):
            far_copy(a, d).wait_send()


def layer(layer_input, out_grad, span_order, small, inward, outward, expand, contract):
    sizes = tuple(lax.axis_size(name) for name in ("batch", "ctx", "fsdp"))
    batch_count, context_count, fsdp_count = sizes
    plane = batch_count * fsdp_count
    chips = batch_count // CORES
    tokens, width = layer_input.shape[1:]
    hidden = expand.shape[1]
    cols = width // plane
    heads = cols // HEAD_DIM
    length = tokens * context_count
    own_sequences = plane // context_count
    half = width // 2
    unit = hidden // plane
    early_other, early = (unit * half // width, 2 * unit * half // width + unit)
    late_other, late = (3 * cols * half // width, 6 * cols * half // width + cols)
    piece = 32
    for rows in (early_other, early - early_other, late_other, late - late_other):
        piece = math.gcd(piece, rows // 2)
    counts = tuple(n // 2 // piece for n in (early_other, early, late_other, late))
    steps = counts[1] + counts[3]
    rows = early + late
    stage_count = (plane * context_count).bit_length() - 1
    all_tokens = plane * tokens
    vector_lines = (8 * width + hidden) // 128
    dma = pltpu.SemaphoreType.DMA
    f32, half_type = (jnp.float32, layer_input.dtype)
    vmem = pl.BlockSpec(memory_space=pltpu.VMEM)
    hbm = pl.BlockSpec(memory_space=pl.ANY)

    def held(*shape, dtype=half_type):
        return pltpu.VMEM(shape, dtype)

    return pl.pallas_call(
        functools.partial(layer_kernel, sizes, tokens, heads, counts, piece),
        out_shape=(
            jax.ShapeDtypeStruct((batch_count, rows, width), half_type),
            jax.ShapeDtypeStruct((tokens, width), half_type),
            jax.ShapeDtypeStruct((tokens, width), f32),
            jax.ShapeDtypeStruct((vector_lines // fsdp_count, 128), f32),
        ),
        in_specs=[hbm, hbm, pl.BlockSpec(memory_space=pltpu.SMEM), vmem] + [hbm] * 4,
        out_specs=(hbm, vmem, vmem, vmem),
        scratch_shapes=[
            held(all_tokens, width),
            held(all_tokens, width),
            held(2, *small.shape, dtype=f32),
            held(width, 3 * cols),
            held(cols, width),
            held(width, unit),
            held(unit, width),
            held(length, cols, dtype=f32),
            held(length, cols, dtype=f32),
            held(all_tokens, 2, dtype=f32),
            held(all_tokens, width),
            held(all_tokens, width),
            held(all_tokens, 2 * unit),
            held(all_tokens, width),
            held(all_tokens, width),
            held(all_tokens, 4 * cols),
            held(own_sequences, length, 4 * cols),
            held(4, length, cols, dtype=f32),
            held(own_sequences, length, 4 * cols),
            held(all_tokens, 4 * cols),
            held(8, cols, dtype=f32),
            held(rows, width),
            held(rows, width),
            held(rows, width),
            held(rows // 2, width),
            held(3, chips * fsdp_count * tokens, width),
            held(3, chips * tokens, width),
            held(3, chips - 1, tokens, width),
            held(3, tokens, width, dtype=f32),
            held(stage_count, vector_lines, 128, dtype=f32),
            held(stage_count + 1, vector_lines, 128, dtype=f32),
            dma((8,)),
            dma((2, 1)),
            dma((2, 4)),
            dma((2, 2, 2 * chips - 1)),
            dma((2, 2, 2 * chips)),
            dma((plane,)),
            dma((own_sequences, context_count)),
            dma((own_sequences,)),
            dma((own_sequences,)),
            dma((2, own_sequences, context_count - 1)),
            dma((2, 2, 2, steps)),
            dma((2, 2, steps)),
            dma((2, steps)),
            dma((2, 2, steps)),
            dma((2, chips - 1, 2, steps)),
            dma((2, chips, 2, steps)),
            dma((2, steps)),
            dma((2, 3, chips)),
            dma((2, 3, chips)),
            dma((2, 3, chips - 1)),
            dma((2, stage_count)),
        ],
        name="layer",
        compiler_params=pltpu.CompilerParams(
            collective_id=0, has_side_effects=True, vmem_limit_bytes=VMEM_LIMIT
        ),
    )(layer_input, out_grad, span_order, small, inward, outward, expand, contract)


def widen_kernel(
    cols,
    unit,
    turn_ref,
    all_ref,
    result_in,
    input_in,
    shifts_in,
    result_ref,
    input_ref,
    inward_ref,
    inward_shift,
    outward_ref,
    outward_shift,
    expand_ref,
    expand_shift,
    contract_ref,
    contract_shift,
    first_scale,
    first_shift,
    second_scale,
    second_shift,
    held,
    inward,
    outward,
    expand,
    contract,
    in_sems,
    out_sems,
    pass_sems,
):
    batch_count, rows, width = all_ref.shape
    half = inward_ref.shape[0]
    unit_rows, unit_blocks = (unit * half // width, width // unit)
    head_rows, head_blocks = (cols * half // width, width // cols)
    late = 2 * unit_rows + unit
    y = turn_ref[0]

    handed = [
        pltpu.make_async_copy(source, target, pass_sems.at[i])
        for i, (source, target) in enumerate(
            [(result_in, result_ref.at[0]), (input_in, input_ref.at[0])]
        )
    ]

    def load(b):
        return pltpu.make_async_copy(all_ref.at[b], held.at[b % 2], in_sems.at[b % 2])

    def stores(b):
        at = b % 2
        sems = iter(range(2 + 2 * 4))
        out = [
            pltpu.make_async_copy(
                outward.at[at],
                outward_ref.at[pl.ds(b * cols, cols), :],
                out_sems.at[at, next(sems)],
            ),
            pltpu.make_async_copy(
                contract.at[at],
                contract_ref.at[pl.ds(b * unit, unit), :],
                out_sems.at[at, next(sems)],
            ),
        ]
        for s in range(2):
            owner = y if s else 1 - y
            column = pl.multiple_of((owner * batch_count + b) * unit, unit)
            out.append(
                pltpu.make_async_copy(
                    expand.at[at, s],
                    expand_ref.at[:, pl.ds(column, unit)],
                    out_sems.at[at, next(sems)],
                )
            )
            for i in range(3):
                column = pl.multiple_of(i * width + (owner * batch_count + b) * cols, cols)
                out.append(
                    pltpu.make_async_copy(
                        inward.at[at, s, i],
                        inward_ref.at[:, pl.ds(column, cols)],
                        out_sems.at[at, next(sems)],
                    )
                )
        return out

    load(0).start()
    for copy in handed:
        copy.start()
    line = 0
    for target in (
        inward_shift,
        outward_shift,
        expand_shift,
        second_scale,
        second_shift,
        first_scale,
        first_shift,
    ):
        count = target.shape[0]
        target[...] = shifts_in[line : line + count, :]
        line += count
    contract_shift[...] = outward_shift[...]

    def step(b, carry):
        at = b % 2
        load(b).wait()

        @pl.when(b + 1 < batch_count)
        def _():
            load(b + 1).start()

        @pl.when(b >= 2)
        def _():
            for copy in stores(b - 2):
                copy.wait()

        for s in range(2):
            first = s * unit_rows
            for i in range(unit_blocks):
                expand[at, s, i * unit_rows : (i + 1) * unit_rows, :] = held[
                    at, first : first + unit_rows, i * unit : (i + 1) * unit
                ].astype(jnp.float32)
            for part in range(3):
                top = late + (s * 3 + part) * head_rows
                for i in range(head_blocks):
                    inward[at, s, part, i * head_rows : (i + 1) * head_rows, :] = held[
                        at, top : top + head_rows, i * cols : (i + 1) * cols
                    ].astype(jnp.float32)
        contract[at] = held[at, 2 * unit_rows : late, :].astype(jnp.float32)
        outward[at] = held[at, late + 6 * head_rows :, :].astype(jnp.float32)
        for copy in stores(b):
            copy.start()
        return carry

    lax.fori_loop(0, batch_count, step, 0)
    for b in range(max(0, batch_count - 2), batch_count):
        for copy in stores(b):
            copy.wait()
    for copy in handed:
        copy.wait()


def widen(gathered, result, input_delta, shifts, cols, unit):
    batch_count, rows, width = gathered.shape
    fsdp_count = lax.axis_size("fsdp")
    hidden = unit * batch_count * fsdp_count
    half = width // 2
    turn = lax.axis_index("fsdp").astype(jnp.int32)[None]
    f32 = jnp.float32
    dma = pltpu.SemaphoreType.DMA
    hbm = pl.BlockSpec(memory_space=pl.ANY)
    vmem = pl.BlockSpec(memory_space=pltpu.VMEM)

    def matrix(rows, columns):
        return jax.ShapeDtypeStruct((rows, columns), f32)

    def vector(size):
        return jax.ShapeDtypeStruct((size // fsdp_count // 128, 128), f32)

    out = pl.pallas_call(
        functools.partial(widen_kernel, cols, unit),
        out_shape=(
            jax.ShapeDtypeStruct((1,) + result.shape, result.dtype),
            jax.ShapeDtypeStruct((1,) + input_delta.shape, f32),
            matrix(half, 3 * width),
            vector(3 * width),
            matrix(half, width),
            vector(width),
            matrix(half, hidden),
            vector(hidden),
            matrix(hidden // 2, width),
            vector(width),
        )
        + (vector(width),) * 4,
        in_specs=[pl.BlockSpec(memory_space=pltpu.SMEM), hbm, hbm, hbm, vmem],
        out_specs=(hbm, hbm) + (hbm, vmem) * 4 + (vmem,) * 4,
        scratch_shapes=[
            pltpu.VMEM((2, rows, width), gathered.dtype),
            pltpu.VMEM((2, 2, 3, half, cols), f32),
            pltpu.VMEM((2, cols, width), f32),
            pltpu.VMEM((2, 2, half, unit), f32),
            pltpu.VMEM((2, unit, width), f32),
            dma((2,)),
            dma((2, 10)),
            dma((2,)),
        ],
        name="widen",
        compiler_params=pltpu.CompilerParams(vmem_limit_bytes=VMEM_LIMIT),
    )(turn, gathered, result, input_delta, shifts)
    return tuple(a.reshape(-1) if a.ndim == 2 and a.shape[1] == 128 else a for a in out)


def dot(left, right, contract=((1,), (0,))):
    return lax.dot_general(left, right, (contract, ((), ())), preferred_element_type=jnp.float32)


def normalize(values):
    center = values - jnp.mean(values, axis=-1, keepdims=True)
    inverse = lax.rsqrt(jnp.mean(center * center, axis=-1, keepdims=True) + EPSILON)
    return (center * inverse, inverse)


def norm_backward(upstream, normed, inverse, factor):
    scaled = upstream * factor
    middle = jnp.mean(scaled, axis=-1, keepdims=True)
    coupled = jnp.mean(scaled * normed, axis=-1, keepdims=True)
    result = inverse * (scaled - middle - normed * coupled)
    return (result, jnp.sum(upstream * normed, axis=0), jnp.sum(upstream, axis=0))


def slot_positions(span_order, first_slot, slot_count, span_size):
    slot_index = first_slot + jnp.arange(slot_count, dtype=jnp.int32)
    owners = slot_index // (2 * span_size)
    places = jnp.arange(span_order.shape[0], dtype=jnp.int32)
    leading = jnp.sum(jnp.where(owners[:, None] == places[None, :], span_order[None, :], 0), axis=1)
    spans = 2 * span_order.shape[0]
    picked = jnp.where(slot_index // span_size % 2 == 0, leading, spans - 1 - leading)
    return picked * span_size + slot_index % span_size


def rotary_tables(positions):
    half_rot = ROT // 2
    angular = jnp.exp(
        jnp.arange(half_rot, dtype=jnp.float32) * (-2.0 * math.log(ROTARY_BASE) / ROT)
    )
    angles = positions.astype(jnp.float32)[:, None] * angular[None, :]
    angles = jnp.concatenate([angles, angles], axis=1)
    return (jnp.cos(angles), jnp.sin(angles))


def rotate(tensor, cosine, sine_table):
    half_rot = ROT // 2
    leading_part = tensor[..., :ROT]
    turned = jnp.concatenate([-leading_part[..., half_rot:], leading_part[..., :half_rot]], axis=-1)
    rotated = leading_part * cosine[:, None, :] + turned * sine_table[:, None, :]
    return jnp.concatenate([rotated, tensor[..., ROT:]], axis=-1)


def unrotate(tensor, cosine, sine_table):
    half_rot = ROT // 2
    leading_part = tensor[..., :ROT]
    weighted = leading_part * sine_table[:, None, :]
    turned = jnp.concatenate([weighted[..., half_rot:], -weighted[..., :half_rot]], axis=-1)
    return jnp.concatenate([leading_part * cosine[:, None, :] + turned, tensor[..., ROT:]], axis=-1)


def attention(mixed, place, cosine, sine_table, heads):
    sequences, length, _ = mixed.shape
    parts = mixed.reshape(sequences, length, 4, heads, HEAD_DIM)
    queries, keys, values, grads = (parts[:, :, i] for i in range(4))
    scale = 1.0 / math.sqrt(HEAD_DIM)
    scores = jnp.einsum("sqhd,skhd->shqk", queries, keys, preferred_element_type=jnp.float32)
    allowed = place[None, :] <= place[:, None]
    scores = jnp.where(allowed, scores * scale, MASKED)
    peak = jnp.max(scores, axis=-1, keepdims=True)
    log_total = peak + jnp.log(jnp.sum(jnp.exp(scores - peak), axis=-1, keepdims=True))
    probs = jnp.exp(scores - log_total)
    soft = probs.astype(jnp.bfloat16)
    context = jnp.einsum("shqk,skhd->sqhd", soft, values, preferred_element_type=jnp.float32)
    context = context.astype(jnp.bfloat16)
    delta = jnp.einsum(
        "sqhd,sqhd->shq", grads.astype(jnp.float32), context.astype(jnp.float32)
    )
    value_grad = jnp.einsum("shqk,sqhd->skhd", soft, grads, preferred_element_type=jnp.float32)
    probs_grad = jnp.einsum("sqhd,skhd->shqk", grads, values, preferred_element_type=jnp.float32)
    score_grad = (probs * (probs_grad - delta[..., None]) * scale).astype(jnp.bfloat16)
    query_grad = jnp.einsum("shqk,skhd->sqhd", score_grad, keys, preferred_element_type=jnp.float32)
    key_grad = jnp.einsum("shqk,sqhd->skhd", score_grad, queries, preferred_element_type=jnp.float32)
    query_grad = unrotate(query_grad, cosine, sine_table)
    key_grad = unrotate(key_grad, cosine, sine_table)
    back = jnp.stack([query_grad, key_grad, value_grad], axis=2)
    shift = jnp.sum(back, axis=(0, 1)).reshape(-1)
    full = jnp.concatenate([context[:, :, None], back.astype(jnp.bfloat16)], axis=2)
    return (full.reshape(sequences, length, 4 * heads * HEAD_DIM), shift)


def plain_body(
    layer_input,
    out_grad,
    span_order,
    inward,
    inward_bias,
    outward,
    outward_bias,
    expand,
    expand_bias,
    contract,
    contract_bias,
    first_gain,
    first_bias,
    second_gain,
    second_bias,
):
    batch_count, fsdp_count = (lax.axis_size("batch"), lax.axis_size("fsdp"))
    context_count = lax.axis_size("ctx")
    context_index = lax.axis_index("ctx")
    batch_index, fsdp_index = (lax.axis_index("batch"), lax.axis_index("fsdp"))
    plane = batch_count * fsdp_count
    tokens, width = layer_input.shape[1:]
    hidden_units = expand.shape[1]
    head_cols = width // plane
    unit_cols = hidden_units // plane
    heads = head_cols // HEAD_DIM
    length = tokens * context_count
    span_size = tokens // 2
    own_sequences = plane // context_count

    def full_vectors(*vectors):
        sizes = [v.shape[0] for v in vectors]
        gathered = lax.all_gather(jnp.concatenate(vectors), "fsdp")
        out, start = ([], 0)
        for size in sizes:
            out.append(gathered[:, start : start + size].reshape(-1).astype(jnp.float32))
            start += size
        return out

    (
        inward_offset,
        outward_offset,
        expand_offset,
        contract_offset,
        gain_first,
        offset_first,
        gain_second,
        offset_second,
    ) = full_vectors(
        inward_bias,
        outward_bias,
        expand_bias,
        contract_bias,
        first_gain,
        first_bias,
        second_gain,
        second_bias,
    )

    def chunk(array, cols):
        rows = array.shape[0]
        parts = array.reshape(rows, -1, fsdp_count, batch_count, cols)
        mine = lax.dynamic_index_in_dim(parts, batch_index, 3, keepdims=False)
        return mine.transpose(2, 0, 1, 3).reshape(fsdp_count, rows, -1)

    to_send = jnp.concatenate([chunk(inward, head_cols), chunk(expand, unit_cols)], axis=2)
    weights = lax.all_to_all(to_send, "fsdp", 0, 0).reshape(width, -1)
    inward_cols = weights[:, : 3 * head_cols]
    expand_cols = weights[:, 3 * head_cols :]
    outward_rows = lax.dynamic_slice_in_dim(outward, batch_index * head_cols, head_cols, 0)
    contract_rows = lax.dynamic_slice_in_dim(contract, batch_index * unit_cols, unit_cols, 0)
    plane_index = fsdp_index * batch_count + batch_index
    inward_shift_in = lax.dynamic_index_in_dim(
        inward_offset.reshape(3, plane, head_cols), plane_index, 1, keepdims=False
    ).reshape(-1)
    expand_shift_in = lax.dynamic_slice_in_dim(expand_offset, plane_index * unit_cols, unit_cols, 0)

    pair = jnp.stack([layer_input[0], out_grad[0]])
    pair_all = lax.all_gather(pair, PLANE, axis=1, tiled=True)
    grads_all = pair_all[1]
    rows_all = pair_all[0].astype(jnp.float32)
    normed, inverse = normalize(rows_all)
    first_rows = (normed * gain_first + offset_first).astype(jnp.bfloat16)
    second_rows = (normed * gain_second + offset_second).astype(jnp.bfloat16)

    local_place = slot_positions(span_order, context_index * tokens, tokens, span_size)
    cosine, sine_table = rotary_tables(local_place)
    cosine_plane = jnp.tile(cosine, (plane, 1))
    sine_plane = jnp.tile(sine_table, (plane, 1))
    projected = dot(first_rows, inward_cols) + inward_shift_in
    projected = projected.reshape(plane * tokens, 3 * heads, HEAD_DIM)
    turned = rotate(projected[:, : 2 * heads], cosine_plane, sine_plane)
    context_grad = dot(grads_all, outward_rows, ((1,), (1,)))
    mixed = jnp.concatenate(
        [
            turned.reshape(plane * tokens, -1),
            projected[:, 2 * heads :].reshape(plane * tokens, -1),
            context_grad,
        ],
        axis=1,
    ).astype(jnp.bfloat16)
    mixed = mixed.reshape(context_count, own_sequences, tokens, 4 * head_cols)
    mixed = lax.all_to_all(mixed, "ctx", 0, 0)
    mixed = mixed.transpose(1, 0, 2, 3).reshape(own_sequences, length, 4 * head_cols)
    place = slot_positions(span_order, 0, length, span_size)
    cosine_all, sine_all = rotary_tables(place)

    before = dot(second_rows, expand_cols) + expand_shift_in
    tail = 1.0 + lax.erf(before * HALF_ROOT)
    activated = (0.5 * before * tail).astype(jnp.bfloat16)
    slope = 0.5 * tail + before * jnp.exp(-0.5 * before * before) * NORMAL_PEAK
    before_grad = dot(grads_all, contract_rows, ((1,), (1,))) * slope
    expand_sum = jnp.sum(before_grad, axis=0)
    before_rows = before_grad.astype(jnp.bfloat16)
    expand_delta = dot(second_rows, before_rows, ((0,), (0,)))
    contract_delta = dot(activated, grads_all, ((0,), (0,)))
    out_part = dot(activated, contract_rows)
    second_part = dot(before_rows, expand_cols, ((1,), (1,)))

    hidden = layer_input[0].astype(jnp.float32)
    grad_float = out_grad[0].astype(jnp.float32)
    normed_mine, inverse_mine = normalize(hidden)
    half = width // fsdp_count

    def spread(values, sizes):
        wide = jnp.zeros((sizes[0], plane, sizes[1]), jnp.float32)
        values = values.reshape(sizes[0], sizes[1])
        return lax.dynamic_update_index_in_dim(wide, values, plane_index, 1).reshape(-1)

    bias_total = jnp.sum(grad_float, axis=0)
    expand_wide = spread(expand_sum, (1, unit_cols))

    back, inward_sum = attention(mixed, place, cosine_all, sine_all, heads)
    back = back.reshape(own_sequences, context_count, tokens, 4 * head_cols)
    back = lax.all_to_all(back.transpose(1, 0, 2, 3), "ctx", 0, 0)
    back = back.reshape(plane * tokens, 4 * head_cols)
    context_rows = back[:, :head_cols]
    projected_rows = back[:, head_cols:]
    inward_delta = dot(first_rows, projected_rows, ((0,), (0,)))
    outward_delta = dot(context_rows, grads_all, ((0,), (0,)))
    out_part = out_part + dot(context_rows, outward_rows)
    first_part = dot(projected_rows, inward_cols, ((1,), (1,)))
    stacked = jnp.stack([second_part, out_part, first_part], axis=1).astype(jnp.bfloat16)
    mine = lax.psum_scatter(stacked, PLANE, scatter_dimension=0, tiled=True)
    mine = mine.transpose(1, 0, 2).astype(jnp.float32)
    columns = jnp.concatenate([inward_delta, expand_delta], axis=1).astype(jnp.bfloat16)
    rows = jnp.concatenate([outward_delta, contract_delta], axis=0).astype(jnp.bfloat16)
    columns, rows = lax.psum((columns, rows), "ctx")
    columns = lax.all_to_all(columns.reshape(fsdp_count, half, -1), "fsdp", 0, 0)
    columns = lax.all_gather(columns, "batch")
    rows = lax.all_gather(rows, "batch").astype(jnp.float32)
    columns = columns.transpose(2, 1, 0, 3).astype(jnp.float32)
    inward_total = columns[..., : 3 * head_cols].reshape(
        half, fsdp_count, batch_count, 3, head_cols
    )
    totals = (
        inward_total.transpose(0, 3, 1, 2, 4).reshape(half, 3 * width),
        rows[:, :head_cols].reshape(half, width),
        columns[..., 3 * head_cols :].reshape(half, hidden_units),
        rows[:, head_cols:].reshape(-1, width),
    )
    _, second_scale, second_shift = norm_backward(
        mine[0], normed_mine, inverse_mine, gain_second
    )
    _, first_scale, first_shift = norm_backward(mine[2], normed_mine, inverse_mine, gain_first)
    vectors = [
        spread(inward_sum, (3, head_cols)),
        bias_total,
        expand_wide,
        first_scale,
        first_shift,
        second_scale,
        second_shift,
    ]
    whole = lax.psum(jnp.concatenate(vectors), ("batch", "ctx", "fsdp"))

    result = (hidden + (mine[1] + outward_offset) + contract_offset).astype(jnp.bfloat16)
    second_input, _, _ = norm_backward(mine[0], normed_mine, inverse_mine, gain_second)
    first_input, _, _ = norm_backward(mine[2], normed_mine, inverse_mine, gain_first)
    input_delta = grad_float + first_input + second_input
    halves, start = ([], 0)
    for vector in vectors:
        size = vector.shape[0] // fsdp_count
        halves.append(lax.dynamic_slice_in_dim(whole, start + fsdp_index * size, size, 0))
        start += vector.shape[0]
    return (
        result[None],
        input_delta[None],
        totals[0],
        halves[0],
        totals[1],
        halves[1],
        totals[2],
        halves[2],
        totals[3],
        halves[1],
        halves[3],
        halves[4],
        halves[5],
        halves[6],
    )


def body(
    layer_input,
    out_grad,
    span_order,
    inward,
    inward_bias,
    outward,
    outward_bias,
    expand,
    expand_bias,
    contract,
    contract_bias,
    first_gain,
    first_bias,
    second_gain,
    second_bias,
):
    plane = lax.axis_size("batch") * lax.axis_size("fsdp")
    width = layer_input.shape[2]
    if width // plane % 128:
        return plain_body(
            layer_input,
            out_grad,
            span_order,
            inward,
            inward_bias,
            outward,
            outward_bias,
            expand,
            expand_bias,
            contract,
            contract_bias,
            first_gain,
            first_bias,
            second_gain,
            second_bias,
        )
    vectors = (
        inward_bias,
        outward_bias,
        expand_bias,
        contract_bias,
        first_gain,
        first_bias,
        second_gain,
        second_bias,
    )
    small = jnp.concatenate(vectors).astype(jnp.float32).reshape(-1, 128)
    small = jnp.pad(small, ((0, -small.shape[0] % 8), (0, 0)))
    sums, result, input_delta, shifts = layer(
        layer_input, out_grad, span_order, small, inward, outward, expand, contract
    )
    return widen(sums, result, input_delta, shifts, width // plane, expand.shape[1] // plane)


def solution(mesh):
    rows = P(PLANE, "ctx", None)
    matrix, vector = (P("fsdp", None), P("fsdp"))
    in_specs = (rows, rows, P()) + (matrix, vector) * 4 + (vector,) * 4
    out_specs = (rows, rows) + (matrix, vector) * 4 + (vector,) * 4
    return jax.shard_map(body, mesh=mesh, in_specs=in_specs, out_specs=out_specs, check_vma=False)
```

```python
import functools
import math

import jax
import jax.numpy as jnp
from jax import lax
from jax.experimental import pallas as pl
from jax.experimental.pallas import tpu as pltpu
from jax.sharding import PartitionSpec as P

HEAD_DIM = 64
ROT = 16

EPSILON = 1e-05
ROTARY_BASE = 10000.0
MASKED = -1e30
HALF_ROOT = 0.7071067811865476
NORMAL_PEAK = 0.3989422804014327
PLANE = ("batch", "fsdp")


MESH = pl.DeviceIdType.MESH
CORES = 2
VMEM_LIMIT = 56 * 2**20


def here():
    return (lax.axis_index("batch"), lax.axis_index("ctx"), lax.axis_index("fsdp"))


def swapped(index, step):
    return index + step * (1 - 2 * (index // step % 2))


def greet(partners):
    barrier = pltpu.get_barrier_semaphore()
    for partner in partners:
        pl.semaphore_signal(barrier, inc=1, device_id=partner, device_id_type=MESH)
    pl.semaphore_wait(barrier, len(partners))


def remote(src, dst, send, recv, target):
    return pltpu.make_async_remote_copy(
        src_ref=src,
        dst_ref=dst,
        send_sem=send,
        recv_sem=recv,
        device_id=target,
        device_id_type=MESH,
    )


LAG = 2


def layer_kernel(
    sizes,
    tokens,
    heads,
    counts,
    piece,
    input_ref,
    grad_ref,
    order_ref,
    small_ref,
    inward_ref,
    outward_ref,
    expand_ref,
    contract_ref,
    sums_ref,
    result_ref,
    input_grad_ref,
    shifts_ref,
    inputs,
    grads,
    small,
    inward,
    outward,
    expand,
    contract,
    cosine,
    sine,
    stats,
    first_rows,
    second_rows,
    work,
    out_rows,
    scaled,
    mixed_out,
    mixed,
    heads_sum,
    back_out,
    back_in,
    inward_sum,
    part,
    mine,
    reduced,
    reduced_right,
    near,
    across_in,
    far,
    token_sum,
    vector_in,
    vector_sum,
    load_sems,
    small_sems,
    weight_sems,
    gather_sems,
    share_sems,
    there_sends,
    there_recvs,
    there_own,
    back_own,
    turn_sems,
    reduce_sems,
    back_sends,
    back_recvs,
    row_sems,
    chip_sems,
    core_sems,
    keep_sems,
    near_sems,
    across_sems,
    far_sems,
    vector_sems,
):
    batch_count, context_count, fsdp_count = sizes
    early_other, early, late_other, late = counts
    b, z, y = here()
    chips = batch_count // CORES
    core = b % CORES
    chip = b // CORES
    width = part.shape[1]
    half_width = width // 2
    cols = heads * HEAD_DIM
    unit = contract.shape[0]
    plane = batch_count * fsdp_count
    index = y * batch_count + b
    own_sequences = plane // context_count
    length = tokens * context_count
    steps = early + late
    early_rows = 2 * early * piece
    last = context_count - 1
    lines = width // 128
    f32, half_type = (jnp.float32, part.dtype)
    group_rows = fsdp_count * tokens

    sibling = (chip * CORES + (1 - core), z, y)
    across = (b, z, 1 - y)
    peers = [((chip + d) % chips * CORES + core, z, y) for d in range(1, chips)]
    sources = [(chip + chips - d) % chips * CORES + core for d in range(1, chips)]
    others = [(b, (z + d) % context_count, y) for d in range(1, context_count)]
    stages = []
    step = 1
    while step < batch_count:
        stages.append((swapped(b, step), z, y))
        step *= 2
    stages.append(across)
    step = 1
    while step < context_count:
        stages.append((b, swapped(z, step), y))
        step *= 2

    def sem(sems, *index):
        return (sems.at[(0, *index)], sems.at[(1, *index)])


    plane_arrays = (inputs, grads)
    plane_sources = (input_ref.at[0], grad_ref.at[0])

    def block(array, batch, fsdp):
        row = pl.multiple_of((batch * fsdp_count + fsdp) * tokens, tokens)
        return plane_arrays[array].at[pl.ds(row, tokens), :]

    def own_load(array):
        return pltpu.make_async_copy(
            plane_sources[array], block(array, b, y), load_sems.at[array]
        )

    def to_across(array):
        return remote(
            plane_sources[array], block(array, b, y), *sem(gather_sems, array, 0), across
        )

    def to_peer(array, d):
        return remote(
            plane_sources[array], block(array, b, y), *sem(gather_sems, array, 1 + d), peers[d]
        )

    def on_to_peer(array, d):
        at = block(array, b, 1 - y)
        return remote(at, at, *sem(gather_sems, array, chips + d), peers[d])

    def share(array, i):
        if i == 0:
            return remote(
                plane_sources[array], block(array, b, y), *sem(share_sems, array, 0), sibling
            )
        if i == 1:
            at = block(array, b, 1 - y)
        else:
            d = (i - 2) % (chips - 1)
            at = block(array, sources[d], y if i - 2 < chips - 1 else 1 - y)
        return remote(at, at, *sem(share_sems, array, i), sibling)

    def weight_copies(owner, local):
        rows = pl.ds(pl.multiple_of(y * half_width, half_width), half_width)
        place = owner * batch_count + b
        out = []
        for i in range(4):
            if i < 3:
                column = pl.multiple_of(i * width + place * cols, cols)
                source = inward_ref.at[:, pl.ds(column, cols)]
                target = inward.at[rows, i * cols : (i + 1) * cols]
            else:
                column = pl.multiple_of(place * unit, unit)
                source = expand_ref.at[:, pl.ds(column, unit)]
                target = expand.at[rows, :]
            if local:
                out.append(pltpu.make_async_copy(source, target, load_sems.at[2 + i]))
            else:
                out.append(remote(source, target, *sem(weight_sems, i), across))
        return out

    row_loads = [
        pltpu.make_async_copy(
            outward_ref.at[pl.ds(pl.multiple_of(b * cols, cols), cols), :],
            outward,
            load_sems.at[6],
        ),
        pltpu.make_async_copy(
            contract_ref.at[pl.ds(pl.multiple_of(b * unit, unit), unit), :],
            contract,
            load_sems.at[7],
        ),
    ]
    weight_loads = weight_copies(y, True)
    weight_sends = weight_copies(1 - y, False)
    small_copy = remote(small_ref, small.at[1], *sem(small_sems, 0), across)

    own_load(0).start()
    own_load(1).start()
    for load in weight_loads + row_loads:
        load.start()
    greet([sibling, across] + peers + others)
    small_copy.start()

    def offer(array):
        to_across(array).start()
        for d in range(chips - 1):
            to_peer(array, d).start()
        share(array, 0).start()

    offer(0)
    for send in weight_sends[:3]:
        send.start()
    small[0] = small_ref[...]


    def positions(shape, dimension):
        slot = lax.broadcasted_iota(jnp.int32, shape, dimension)
        owner = slot // tokens
        leading = jnp.zeros(shape, jnp.int32)
        for c in range(context_count):
            leading = jnp.where(owner == c, order_ref[c], leading)
        span = tokens // 2
        second = slot // span % 2
        picked = jnp.where(second == 0, leading, 2 * context_count - 1 - leading)
        return picked * span + slot % span

    half_rot = ROT // 2
    lane = lax.broadcasted_iota(jnp.int32, (1, cols), 1) % HEAD_DIM
    angular = jnp.exp((lane % half_rot).astype(f32) * (-2.0 * math.log(ROTARY_BASE) / ROT))
    angles = positions((length, cols), 0).astype(f32) * angular
    cosine[...] = jnp.where(lane < ROT, jnp.cos(angles), 1.0)
    sine[...] = jnp.where(lane < ROT, jnp.sin(angles), 0.0)
    low = (lane < half_rot).astype(f32)
    high = 1.0 - low

    def turn(value, rows, sign):
        weight = sine[rows, :] * sign
        return (
            value * cosine[rows, :]
            - pltpu.roll(value, cols - half_rot, 1) * (weight * low)
            + pltpu.roll(value, half_rot, 1) * (weight * high)
        )


    small_copy.wait_recv()
    vector_rows = [3 * lines, lines, unit * plane // 128] + [lines] * 5
    starts = [sum(vector_rows[:i]) // fsdp_count for i in range(8)]

    def vector_line(which, line):
        share_lines = vector_rows[which] // fsdp_count
        owner = line // share_lines
        at = (owner - y) * (owner - y)
        return small[at, pl.ds(starts[which] + line % share_lines, 1), :]

    def whole(which):
        return jnp.concatenate([vector_line(which, line) for line in range(lines)], axis=1)

    def chunk(which, first, count):
        return jnp.concatenate([vector_line(which, first + i) for i in range(count)], axis=1)


    def group(u):
        return (chip + u // CORES) % chips * CORES + (core + u % CORES) % CORES

    def rows_of(u):
        return pl.ds(pl.multiple_of(group(u) * group_rows, group_rows), group_rows)

    def bring(array, u):
        distance, other = (u // CORES, u % CORES)
        if other == 0 and distance == 0:
            own_load(array).wait()
            to_across(array).wait_recv()
            for d in range(chips - 1):
                on_to_peer(array, d).start()
            share(array, 1).start()
            if array == 0:
                offer(1)
            else:
                weight_sends[3].start()
        elif other == 0:
            d = chips - distance - 1
            to_peer(array, d).wait_recv()
            share(array, 2 + d).start()
            on_to_peer(array, d).wait_recv()
            share(array, 1 + chips + d).start()
        elif distance == 0:
            share(array, 0).wait_recv()
            share(array, 1).wait_recv()
        else:
            d = chips - distance - 1
            share(array, 2 + d).wait_recv()
            share(array, 1 + chips + d).wait_recv()

    gains = [whole(4), whole(5), whole(6), whole(7)]
    inward_bias = jnp.concatenate(
        [
            chunk(0, i * lines + index * (cols // 128), cols // 128)
            for i in range(3)
        ],
        axis=1,
    )

    def project(u):
        rows = rows_of(u)
        x = inputs[rows, :].astype(f32)
        mean = jnp.mean(x, axis=-1, keepdims=True)
        center = x - mean
        inverse = lax.rsqrt(jnp.mean(center * center, axis=-1, keepdims=True) + EPSILON)
        stats[rows, 0:1] = mean
        stats[rows, 1:2] = inverse
        normed = center * inverse
        first = (normed * gains[0] + gains[1]).astype(half_type)
        first_rows[rows, :] = first
        second_rows[rows, :] = (normed * gains[2] + gains[3]).astype(half_type)
        projected = dot(first, inward[...]) + inward_bias
        local = pl.ds(pl.multiple_of(z * tokens, tokens), tokens)
        for f in range(fsdp_count):
            at = pl.ds(pl.multiple_of((group(u) * fsdp_count + f) * tokens, tokens), tokens)
            piece_rows = projected[f * tokens : (f + 1) * tokens, :]
            for i in range(3):
                value = piece_rows[:, i * cols : (i + 1) * cols]
                if i < 2:
                    value = turn(value, local, 1.0)
                mixed_out[at, i * cols : (i + 1) * cols] = value.astype(half_type)

    def there_copy(p):
        owner, s = (p // own_sequences, p % own_sequences)
        source = mixed_out.at[pl.ds(pl.multiple_of(p * tokens, tokens), tokens), :]
        target = mixed.at[s, pl.ds(pl.multiple_of(z * tokens, tokens), tokens), :]
        return (owner, s, source, target)

    def upstream(u):
        rows = rows_of(u)
        value = dot(grads[rows, :], outward[...], ((1,), (1,)))
        mixed_out[rows, 3 * cols :] = value.astype(half_type)
        for f in range(fsdp_count):
            p = group(u) * fsdp_count + f
            owner, s, source, target = there_copy(p)

            @pl.when(owner == z)
            def _():
                pltpu.make_async_copy(source, target, there_own.at[s]).start()

            @pl.when(owner != z)
            def _():
                remote(
                    source, target, there_sends.at[p], there_recvs.at[s, z], (b, owner, y)
                ).start()

    def there(s):
        block_at = mixed.at[s, pl.ds(0, tokens), :]
        pltpu.make_async_copy(block_at, block_at, there_own.at[s]).wait()
        for d in range(1, context_count):
            source = (z + d) % context_count
            at = mixed.at[s, pl.ds(pl.multiple_of(source * tokens, tokens), tokens), :]
            remote(at, at, there_sends.at[0], there_recvs.at[s, source], others[0]).wait_recv()

    order = [u for u in range(0, batch_count, CORES)] + [u for u in range(1, batch_count, CORES)]
    for array in range(2):
        for u in order:
            bring(array, u)
            if array == 0:
                if u == 0:
                    for i in range(3):
                        weight_loads[i].wait()
                        weight_sends[i].wait_recv()
                project(u)
            else:
                if u == 0:
                    row_loads[0].wait()
                upstream(u)


    row_loads[1].wait()
    weight_loads[3].wait()
    weight_sends[3].wait_recv()
    expand_bias = chunk(2, index * (unit // 128), unit // 128)
    nothing = jnp.zeros((1, width), f32)

    def normed_rows(rows):
        return (inputs[rows, :].astype(f32) - stats[rows, 0:1]) * stats[rows, 1:2]

    def forward_tile(i, carry):
        expand_total, scale_total, shift_total = carry
        rows = pl.ds(pl.multiple_of(i * group_rows, group_rows), group_rows)
        before = dot(second_rows[rows, :], expand[...]) + expand_bias
        tail = 1.0 + lax.erf(before * HALF_ROOT)
        activated = (0.5 * before * tail).astype(half_type)
        slope = 0.5 * tail + before * jnp.exp(-0.5 * before * before) * NORMAL_PEAK
        before_grad = dot(grads[rows, :], contract[...], ((1,), (1,))) * slope
        before_rows = before_grad.astype(half_type)
        work[rows, :unit] = activated
        work[rows, unit:] = before_rows
        out_rows[rows, :] = dot(activated, contract[...]).astype(half_type)
        value = dot(before_rows, expand[...], ((1,), (1,)))
        scaled[rows, :] = (value * gains[2]).astype(half_type)
        return (
            expand_total + jnp.sum(before_grad, axis=0, keepdims=True),
            scale_total + jnp.sum(value * normed_rows(rows), axis=0, keepdims=True),
            shift_total + jnp.sum(value, axis=0, keepdims=True),
        )

    forward_sums = lax.fori_loop(
        0, batch_count, forward_tile, (jnp.zeros((1, unit), f32), nothing, nothing)
    )

    def expand_half(s, carry):
        owner = (1 - y) * (1 - s) + y * s
        column = pl.multiple_of(owner * half_width, half_width)
        delta = dot(second_rows[:, pl.ds(column, half_width)], work[:, unit:], ((0,), (0,)))
        group = unit * half_width // width
        at = pl.ds(pl.multiple_of(s * group, group), group)
        for j in range(width // unit):
            part[at, j * unit : (j + 1) * unit] = delta[j * group : (j + 1) * group, :].astype(
                half_type
            )
        return carry

    lax.fori_loop(0, 2, expand_half, 0)
    part[early_rows - unit : early_rows, :] = dot(
        work[:, :unit], grads[...], ((0,), (0,))
    ).astype(half_type)


    def place(half, k):
        is_late = jnp.minimum(k // early, 1)
        other = early_other * (1 - is_late) + late_other * is_late
        count = early * (1 - is_late) + late * is_late
        j = k - early * is_late
        is_own = jnp.minimum(j // other, 1)
        row = (half * other + j) * (1 - is_own) + (
            2 * other + half * (count - other) + j - other
        ) * is_own
        return pl.multiple_of((2 * early * is_late + row) * piece, piece)

    def own(k):
        is_late = jnp.minimum(k // early, 1)
        other = early_other * (1 - is_late) + late_other * is_late
        return jnp.minimum((k - early * is_late) // other, 1)

    def rows_at(ref, row):
        return ref.at[pl.ds(row, piece), :]

    def sums_at(batch, row):
        return sums_ref.at[batch, pl.ds(row, piece), :]

    def back_copy(half, k, side, target):
        at = rows_at(mine, place(half, k))
        return remote(at, at, back_sends.at[side, half, k], back_recvs.at[half, k], target)

    def row_copy(half, k):
        row = place(half, k)
        return remote(rows_at(mine, row), sums_at(b, row), *sem(row_sems, half, k), across)

    def keep_copy(half, k):
        row = place(half, k)
        return pltpu.make_async_copy(rows_at(mine, row), sums_at(b, row), keep_sems.at[half, k])

    def chip_copy(d, half, k, from_mine):
        row = place(half, k)
        source = rows_at(mine, row) if from_mine else sums_at(b, row)
        return remote(source, sums_at(b, row), *sem(chip_sems, d, half, k), peers[d])

    def core_copy(d, half, k, from_mine, batch):
        row = place(half, k)
        source = rows_at(mine, row) if from_mine else sums_at(batch, row)
        return remote(source, sums_at(batch, row), *sem(core_sems, d, half, k), sibling)

    def spread(half, k, from_mine):
        for d in range(chips - 1):
            chip_copy(d, half, k, from_mine).start()
        core_copy(0, half, k, from_mine, b).start()

    def arrived(half, k):
        for d in range(chips - 1):
            chip_copy(d, half, k, False).wait_recv()
            core_copy(1 + d, half, k, False, sources[d]).start()

    def finish(half, k):
        @pl.when(own(k) == 0)
        def _():
            row_copy(half, k).start()

        @pl.when(own(k) == 1)
        def _():
            keep_copy(half, k).start()
            spread(half, k, True)

    left = (b, (z + last) % context_count, y)
    right = (b, (z + 1) % context_count, y)

    def reduce_copy(half, k, source, stream, target):
        row = place(half, k)
        if stream:
            landing = reduced_right.at[pl.ds(pl.multiple_of(k * piece, piece), piece), :]
        else:
            landing = rows_at(reduced, row)
        return remote(
            rows_at(source, row), landing, *sem(reduce_sems, stream, half, k), target
        )

    def pieces(t, half):
        root = last // 2 if half == 0 else context_count // 2
        depth = max(root, last - root)
        at_root = z == root
        is_left = z < root
        distance = jnp.where(is_left, root - z, z - root)
        leaf = (z == 0) | (z == last)
        k = t - LAG * (depth - distance)

        def send(source):
            @pl.when(z == root + 1)
            def _():
                reduce_copy(half, k, source, 1, left).start()

            @pl.when(z > root + 1)
            def _():
                reduce_copy(half, k, source, 0, left).start()

            @pl.when(is_left)
            def _():
                reduce_copy(half, k, source, 0, right).start()

        @pl.when((k >= 0) & (k < steps))
        def _():
            row = place(half, k)
            here_at = pl.ds(row, piece)

            @pl.when(at_root)
            def _():
                value = part[here_at, :].astype(f32)
                if root > 0:
                    reduce_copy(half, k, part, 0, right).wait_recv()
                    value = value + reduced[here_at, :].astype(f32)
                if root < last:
                    reduce_copy(half, k, part, 1, left).wait_recv()
                    came = reduced_right[pl.ds(pl.multiple_of(k * piece, piece), piece), :]
                    value = value + came.astype(f32)
                mine[here_at, :] = value.astype(half_type)
                if root > 0:
                    back_copy(half, k, 0, left).start()
                if root < last:
                    back_copy(half, k, 1, right).start()
                finish(half, k)

            @pl.when(leaf & jnp.logical_not(at_root))
            def _():
                send(part)

            @pl.when(jnp.logical_not(leaf | at_root))
            def _():
                reduce_copy(half, k, part, 0, right).wait_recv()
                value = part[here_at, :].astype(f32) + reduced[here_at, :].astype(f32)
                reduced[here_at, :] = value.astype(half_type)
                send(reduced)

        k_back = t - LAG * (depth + distance)

        @pl.when(jnp.logical_not(at_root) & (k_back >= 0) & (k_back < steps))
        def _():
            back_copy(half, k_back, 0, left).wait_recv()

            @pl.when(is_left & (z > 0))
            def _():
                back_copy(half, k_back, 0, left).start()

            @pl.when((z > root) & (z < last))
            def _():
                back_copy(half, k_back, 1, right).start()

            finish(half, k_back)

        k_row = k_back - LAG

        @pl.when((k_row >= 0) & (k_row < steps))
        def _():
            @pl.when(own(k_row) == 0)
            def _():
                row_copy(half, k_row).wait_recv()
                spread(half, k_row, False)

            @pl.when(own(k_row) == 1)
            def _():
                arrived(half, k_row)

        k_chip = k_row - 2 * LAG + 1

        @pl.when((k_chip >= 0) & (k_chip < steps))
        def _():
            @pl.when(own(k_chip) == 0)
            def _():
                arrived(half, k_chip)

    def drain(k, carry):
        for half in range(2):
            root = last // 2 if half == 0 else context_count // 2
            for d in range(chips):
                core_copy(d, half, k, False, b).wait_recv()
                core_copy(d, half, k, False, b).wait_send()
                if d:
                    chip_copy(d - 1, half, k, False).wait_send()

            @pl.when(z == root + 1)
            def _():
                reduce_copy(half, k, part, 1, left).wait_send()

            @pl.when((z < root) | (z > root + 1))
            def _():
                reduce_copy(half, k, part, 0, left).wait_send()

            @pl.when((z <= root) & (z > 0))
            def _():
                back_copy(half, k, 0, left).wait_send()

            @pl.when((z >= root) & (z < last))
            def _():
                back_copy(half, k, 1, right).wait_send()

            @pl.when(own(k) == 0)
            def _():
                row_copy(half, k).wait_send()

            @pl.when(own(k) == 1)
            def _():
                keep_copy(half, k).wait()

        return carry


    def attend(n):
        s, h = (n // heads, n % heads)
        columns = [mixed[s, :, i * cols : (i + 1) * cols] for i in range(4)]
        head = lax.broadcasted_iota(jnp.int32, (length, cols), 1) // HEAD_DIM
        picked = head == h
        blank = jnp.zeros((length, cols), half_type)
        _, keys, values, _ = columns
        queries_h, keys_h, values_h, upstream_h = [
            jnp.where(picked, column, blank) for column in columns
        ]
        scale = 1.0 / math.sqrt(HEAD_DIM)
        allowed = positions((1, length), 1) <= positions((length, 1), 0)
        scores = dot(queries_h, keys, ((1,), (1,))) * scale
        scores = jnp.where(allowed, scores, MASKED)
        peak = jnp.max(scores, axis=1, keepdims=True)
        log_total = peak + jnp.log(jnp.sum(jnp.exp(scores - peak), axis=1, keepdims=True))
        probs = jnp.exp(scores - log_total)
        soft = probs.astype(half_type)
        context = dot(soft, values_h)
        delta = jnp.sum(
            upstream_h.astype(f32) * context.astype(half_type).astype(f32), axis=1, keepdims=True
        )
        probs_grad = dot(upstream_h, values, ((1,), (1,)))
        score_grad = (probs * (probs_grad - delta) * scale).astype(half_type)
        results = (
            context,
            dot(score_grad, keys_h),
            dot(score_grad, queries_h, ((0,), (0,))),
            dot(soft, upstream_h, ((0,), (0,))),
        )
        for i, value in enumerate(results):

            @pl.when(h == 0)
            def _():
                heads_sum[i] = value

            @pl.when(h > 0)
            def _():
                heads_sum[i] += value

        @pl.when(h == heads - 1)
        def _():
            back_out[s, :, :cols] = heads_sum[0].astype(half_type)
            for i in range(1, 4):
                value = heads_sum[i]
                if i < 3:
                    value = turn(value, slice(None), -1.0)
                back_out[s, :, i * cols : (i + 1) * cols] = value.astype(half_type)
                total = jnp.sum(value, axis=0, keepdims=True)

                @pl.when(s == 0)
                def _():
                    inward_sum[i - 1 : i, :] = total

                @pl.when(s > 0)
                def _():
                    inward_sum[i - 1 : i, :] += total

            for d in range(context_count):
                turn_copy(s, d).start()

    def turn_copy(s, d):
        target = (z + d) % context_count
        source = back_out.at[s, pl.ds(pl.multiple_of(target * tokens, tokens), tokens), :]
        row = pl.multiple_of((z * own_sequences + s) * tokens, tokens)
        destination = back_in.at[pl.ds(row, tokens), :]
        if d == 0:
            return pltpu.make_async_copy(source, destination, back_own.at[s])
        return remote(source, destination, *sem(turn_sems, s, d - 1), others[d - 1])

    def turned():
        for s in range(own_sequences):
            turn_copy(s, 0).wait()
            for d in range(1, context_count):
                turn_copy(s, d).wait_recv()


    def head_gradients():
        delta = dot(back_in[:, :cols], grads[...], ((0,), (0,))).astype(half_type)
        part[early_rows + 4 * late_other * piece :, :] = delta
        group = cols * half_width // width

        def half_rows(s, carry):
            owner = (1 - y) * (1 - s) + y * s
            column = pl.multiple_of(owner * half_width, half_width)
            delta = dot(
                first_rows[:, pl.ds(column, half_width)], back_in[:, cols:], ((0,), (0,))
            ).astype(half_type)
            top = pl.multiple_of(early_rows + s * 3 * group, group)
            for i in range(3):
                for j in range(width // cols):
                    part[pl.ds(top + i * group, group), j * cols : (j + 1) * cols] = delta[
                        j * group : (j + 1) * group, i * cols : (i + 1) * cols
                    ]
            return carry

        lax.fori_loop(0, 2, half_rows, 0)

    def output_rows():
        def step(i, carry):
            rows = pl.ds(pl.multiple_of(i * group_rows, group_rows), group_rows)
            value = dot(back_in[rows, :cols], outward[...])
            out_rows[rows, :] = (out_rows[rows, :].astype(f32) + value).astype(half_type)
            return carry

        lax.fori_loop(0, batch_count, step, 0)

    vector_start = len(stages)

    def first_back_rows():
        def step(i, carry):
            scale_total, shift_total = carry
            rows = pl.ds(pl.multiple_of(i * group_rows, group_rows), group_rows)
            value = dot(back_in[rows, cols:], inward[...], ((1,), (1,)))
            scaled[rows, :] = (scaled[rows, :].astype(f32) + value * gains[0]).astype(half_type)
            return (
                scale_total + jnp.sum(value * normed_rows(rows), axis=0, keepdims=True),
                shift_total + jnp.sum(value, axis=0, keepdims=True),
            )

        first_sums = lax.fori_loop(0, batch_count, step, (nothing, nothing))
        out = vector_sum.at[vector_start]
        out[...] = jnp.zeros(out.shape, f32)

        def put(line, value):
            for j in range(value.shape[1] // 128):
                out[pl.ds(line + j, 1), :] = value[:, j * 128 : (j + 1) * 128]

        for i in range(3):
            put(i * lines + index * (cols // 128), inward_sum[i : i + 1, :])
        first = 3 * lines
        own_rows = pl.ds(pl.multiple_of((b * fsdp_count + y) * tokens, tokens), tokens)
        put(first, jnp.sum(grads[own_rows, :].astype(f32), axis=0, keepdims=True))
        first += lines
        put(first + index * (unit // 128), forward_sums[0])
        first += unit * plane // 128
        for value in forward_sums[1:] + first_sums:
            put(first, value)
            first += lines

    def vector_copy(i):
        source = vector_sum.at[vector_start if i == 0 else i - 1]
        return remote(source, vector_in.at[i], *sem(vector_sems, i), stages[i])


    arrays = (out_rows, scaled)

    def near_copy(a, c):
        row = pl.multiple_of((c * CORES + 1 - core) * group_rows, group_rows)
        return remote(
            arrays[a].at[pl.ds(row, group_rows), :],
            near.at[a, pl.ds(c * group_rows, group_rows), :],
            *sem(near_sems, a, c),
            sibling,
        )

    def across_copy(a, c):
        row = pl.multiple_of(c * group_rows + (1 - y) * tokens, tokens)
        return remote(
            near.at[a, pl.ds(row, tokens), :],
            across_in.at[a, pl.ds(c * tokens, tokens), :],
            *sem(across_sems, a, c),
            across,
        )

    def far_copy(a, d):
        row = pl.multiple_of((chip + d + 1) % chips * tokens, tokens)
        return remote(
            across_in.at[a, pl.ds(row, tokens), :], far.at[a, d], *sem(far_sems, a, d), peers[d]
        )

    def scatter_first(a):
        for c in range(chips):
            near_copy(a, c).start()

    def scatter_second(a):
        for c in range(chips):
            near_copy(a, c).wait_recv()

            def step(i, carry):
                row = pl.multiple_of((c * CORES + core) * group_rows + i * tokens, tokens)
                value = arrays[a][pl.ds(row, tokens), :].astype(f32)
                at = pl.ds(pl.multiple_of(c * group_rows + i * tokens, tokens), tokens)
                near[a, at, :] = (value + near[a, at, :].astype(f32)).astype(half_type)
                return carry

            lax.fori_loop(0, fsdp_count, step, 0)
            across_copy(a, c).start()

    def scatter_third(a):
        for c in range(chips):
            across_copy(a, c).wait_recv()

        def both(c):
            row = pl.multiple_of(c * group_rows + y * tokens, tokens)
            at = pl.ds(pl.multiple_of(c * tokens, tokens), tokens)
            return (
                near[a, pl.ds(row, tokens), :].astype(f32) + across_in[a, at, :].astype(f32),
                at,
            )

        for d in range(chips - 1):
            value, at = both((chip + d + 1) % chips)
            across_in[a, at, :] = value.astype(half_type)
            far_copy(a, d).start()
        token_sum[a] = both(chip)[0]

    def scatter_last(a):
        value = token_sum[a]
        for d in range(chips - 1):
            far_copy(a, d).wait_recv()
            value = value + far[a, d].astype(f32)
        own_rows = pl.ds(pl.multiple_of((b * fsdp_count + y) * tokens, tokens), tokens)
        x = inputs[own_rows, :].astype(f32)
        if a == 0:
            result_ref[...] = (x + (value + whole(1)) + whole(3)).astype(half_type)
            return
        normed = normed_rows(own_rows)
        middle = jnp.mean(value, axis=-1, keepdims=True)
        coupled = jnp.mean(value * normed, axis=-1, keepdims=True)
        back = stats[own_rows, 1:2] * (value - middle - normed * coupled)
        input_grad_ref[...] = grads[own_rows, :].astype(f32) + back


    problems = own_sequences * heads
    ready = max(early - 4, problems)
    plan = {}

    def at(slot, work):
        plan.setdefault(slot, []).append(work)

    def scatter(a, slot):
        at(slot, lambda: scatter_first(a))
        at(slot + 3, lambda: scatter_second(a))
        at(slot + 6, lambda: scatter_third(a))
        at(slot + 9, lambda: scatter_last(a))

    for s in range(own_sequences):
        at(s * heads, lambda s=s: there(s))
    at(ready, turned)
    at(ready, head_gradients)
    at(ready + 1, output_rows)
    scatter(0, ready + 1)
    at(ready + 2, first_back_rows)
    scatter(1, ready + 2)
    at(ready + 2, lambda: vector_copy(0).start())
    for i in range(len(stages)):

        def vector_step(i=i):
            vector_copy(i).wait_recv()
            before = vector_sum[vector_start if i == 0 else i - 1]
            vector_sum[i] = before + vector_in[i]
            if i + 1 < len(stages):
                vector_copy(i + 1).start()

        at(ready + 4 + 2 * i, vector_step)

    def slot_step(t, carry):
        for half in range(2):
            pieces(t, half)

        for slot, works in sorted(plan.items()):

            @pl.when(t == slot)
            def _():
                for work in works:
                    work()

        @pl.when(t < problems)
        def _():
            attend(t)

        return carry

    depth = context_count // 2
    tail = LAG * (2 * depth + 1)
    slots = max(steps + tail, early + late_other + tail + 2 * LAG - 1, max(plan) + 1)
    lax.fori_loop(0, slots, slot_step, 0)
    first = 0
    out_first = 0
    for count in (3 * lines, lines, unit * plane // 128, lines, lines, lines, lines):
        share_lines = count // fsdp_count
        for j in range(share_lines):
            line = first + y * share_lines + j
            shifts_ref[out_first + j : out_first + j + 1, :] = vector_sum[
                len(stages) - 1, pl.ds(line, 1), :
            ]
        first += count
        out_first += share_lines

    lax.fori_loop(0, steps, drain, 0)
    small_copy.wait_send()
    for send in weight_sends:
        send.wait_send()
    for array in range(2):
        to_across(array).wait_send()
        for d in range(chips - 1):
            to_peer(array, d).wait_send()
            on_to_peer(array, d).wait_send()
        for i in range(2 * chips):
            share(array, i).wait_send()
    for p in range(plane):
        _, _, source, target = there_copy(p)

        @pl.when(p // own_sequences != z)
        def _():
            remote(
                source, target, there_sends.at[p], there_recvs.at[0, 0], others[0]
            ).wait_send()

    for i in range(len(stages)):
        vector_copy(i).wait_send()
    for s in range(own_sequences):
        for d in range(1, context_count):
            turn_copy(s, d).wait_send()
    for a in range(2):
        for c in range(chips):
            near_copy(a, c).wait_send()
            across_copy(a, c).wait_send()
        for d in range(chips - 1):
            far_copy(a, d).wait_send()


def layer(layer_input, out_grad, span_order, small, inward, outward, expand, contract):
    sizes = tuple(lax.axis_size(name) for name in ("batch", "ctx", "fsdp"))
    batch_count, context_count, fsdp_count = sizes
    plane = batch_count * fsdp_count
    chips = batch_count // CORES
    tokens, width = layer_input.shape[1:]
    hidden = expand.shape[1]
    cols = width // plane
    heads = cols // HEAD_DIM
    length = tokens * context_count
    own_sequences = plane // context_count
    half = width // 2
    unit = hidden // plane
    early_other, early = (unit * half // width, 2 * unit * half // width + unit)
    late_other, late = (3 * cols * half // width, 6 * cols * half // width + cols)
    piece = 32
    for rows in (early_other, early - early_other, late_other, late - late_other):
        piece = math.gcd(piece, rows // 2)
    counts = tuple(n // 2 // piece for n in (early_other, early, late_other, late))
    steps = counts[1] + counts[3]
    rows = early + late
    stage_count = (plane * context_count).bit_length() - 1
    all_tokens = plane * tokens
    vector_lines = (8 * width + hidden) // 128
    dma = pltpu.SemaphoreType.DMA
    f32, half_type = (jnp.float32, layer_input.dtype)
    vmem = pl.BlockSpec(memory_space=pltpu.VMEM)
    hbm = pl.BlockSpec(memory_space=pl.ANY)

    def held(*shape, dtype=half_type):
        return pltpu.VMEM(shape, dtype)

    return pl.pallas_call(
        functools.partial(layer_kernel, sizes, tokens, heads, counts, piece),
        out_shape=(
            jax.ShapeDtypeStruct((batch_count, rows, width), half_type),
            jax.ShapeDtypeStruct((tokens, width), half_type),
            jax.ShapeDtypeStruct((tokens, width), f32),
            jax.ShapeDtypeStruct((vector_lines // fsdp_count, 128), f32),
        ),
        in_specs=[hbm, hbm, pl.BlockSpec(memory_space=pltpu.SMEM), vmem] + [hbm] * 4,
        out_specs=(hbm, vmem, vmem, vmem),
        scratch_shapes=[
            held(all_tokens, width),
            held(all_tokens, width),
            held(2, *small.shape, dtype=f32),
            held(width, 3 * cols),
            held(cols, width),
            held(width, unit),
            held(unit, width),
            held(length, cols, dtype=f32),
            held(length, cols, dtype=f32),
            held(all_tokens, 2, dtype=f32),
            held(all_tokens, width),
            held(all_tokens, width),
            held(all_tokens, 2 * unit),
            held(all_tokens, width),
            held(all_tokens, width),
            held(all_tokens, 4 * cols),
            held(own_sequences, length, 4 * cols),
            held(4, length, cols, dtype=f32),
            held(own_sequences, length, 4 * cols),
            held(all_tokens, 4 * cols),
            held(8, cols, dtype=f32),
            held(rows, width),
            held(rows, width),
            held(rows, width),
            held(rows // 2, width),
            held(2, chips * fsdp_count * tokens, width),
            held(2, chips * tokens, width),
            held(2, chips - 1, tokens, width),
            held(2, tokens, width, dtype=f32),
            held(stage_count, vector_lines, 128, dtype=f32),
            held(stage_count + 1, vector_lines, 128, dtype=f32),
            dma((8,)),
            dma((2, 1)),
            dma((2, 4)),
            dma((2, 2, 2 * chips - 1)),
            dma((2, 2, 2 * chips)),
            dma((plane,)),
            dma((own_sequences, context_count)),
            dma((own_sequences,)),
            dma((own_sequences,)),
            dma((2, own_sequences, context_count - 1)),
            dma((2, 2, 2, steps)),
            dma((2, 2, steps)),
            dma((2, steps)),
            dma((2, 2, steps)),
            dma((2, chips - 1, 2, steps)),
            dma((2, chips, 2, steps)),
            dma((2, steps)),
            dma((2, 2, chips)),
            dma((2, 2, chips)),
            dma((2, 2, chips - 1)),
            dma((2, stage_count)),
        ],
        name="layer",
        compiler_params=pltpu.CompilerParams(
            collective_id=0, has_side_effects=True, vmem_limit_bytes=VMEM_LIMIT
        ),
    )(layer_input, out_grad, span_order, small, inward, outward, expand, contract)


def widen_kernel(
    cols,
    unit,
    turn_ref,
    all_ref,
    result_in,
    input_in,
    shifts_in,
    result_ref,
    input_ref,
    inward_ref,
    inward_shift,
    outward_ref,
    outward_shift,
    expand_ref,
    expand_shift,
    contract_ref,
    contract_shift,
    first_scale,
    first_shift,
    second_scale,
    second_shift,
    held,
    inward,
    outward,
    expand,
    contract,
    in_sems,
    out_sems,
):
    batch_count, rows, width = all_ref.shape
    half = inward_ref.shape[0]
    unit_rows, unit_blocks = (unit * half // width, width // unit)
    head_rows, head_blocks = (cols * half // width, width // cols)
    late = 2 * unit_rows + unit
    bounds = ((late, rows - late), (0, unit_rows), (unit_rows, unit_rows), (late - unit, unit))
    y = turn_ref[0]

    def load(b, part):
        first, count = bounds[part]
        at = pl.ds(first, count)
        return pltpu.make_async_copy(
            all_ref.at[b, at, :], held.at[b % 2, at, :], in_sems.at[b % 2, part]
        )

    def stores(b, part):
        at = b % 2
        pairs = []
        if part == 0:
            pairs.append((outward.at[at], outward_ref.at[pl.ds(b * cols, cols), :]))
            for s in range(2):
                owner = y if s else 1 - y
                for i in range(3):
                    column = pl.multiple_of(i * width + (owner * batch_count + b) * cols, cols)
                    pairs.append((inward.at[at, s, i], inward_ref.at[:, pl.ds(column, cols)]))
        elif part < 3:
            owner = y if part == 2 else 1 - y
            column = pl.multiple_of((owner * batch_count + b) * unit, unit)
            pairs.append((expand.at[at, part - 1], expand_ref.at[:, pl.ds(column, unit)]))
        else:
            pairs.append((contract.at[at], contract_ref.at[pl.ds(b * unit, unit), :]))
        return [
            pltpu.make_async_copy(source, target, out_sems.at[at, part, i])
            for i, (source, target) in enumerate(pairs)
        ]

    for part in range(4):
        load(0, part).start()
    result_ref[0] = result_in[...]
    input_ref[0] = input_in[...]
    line = 0
    for target in (
        inward_shift,
        outward_shift,
        expand_shift,
        second_scale,
        second_shift,
        first_scale,
        first_shift,
    ):
        count = target.shape[0]
        target[...] = shifts_in[line : line + count, :]
        line += count
    contract_shift[...] = outward_shift[...]

    def step(b, carry):
        at = b % 2
        for part in range(4):
            load(b, part).wait()

            @pl.when(b + 1 < batch_count)
            def _():
                load(b + 1, part).start()

            @pl.when(b >= 2)
            def _():
                for copy in stores(b - 2, part):
                    copy.wait()

            if part == 0:
                for s in range(2):
                    for i in range(3):
                        top = late + (s * 3 + i) * head_rows
                        for j in range(head_blocks):
                            inward[at, s, i, j * head_rows : (j + 1) * head_rows, :] = held[
                                at, top : top + head_rows, j * cols : (j + 1) * cols
                            ].astype(jnp.float32)
                outward[at] = held[at, late + 6 * head_rows :, :].astype(jnp.float32)
            elif part < 3:
                first = (part - 1) * unit_rows
                for j in range(unit_blocks):
                    expand[at, part - 1, j * unit_rows : (j + 1) * unit_rows, :] = held[
                        at, first : first + unit_rows, j * unit : (j + 1) * unit
                    ].astype(jnp.float32)
            else:
                contract[at] = held[at, late - unit : late, :].astype(jnp.float32)
            for copy in stores(b, part):
                copy.start()
        return carry

    lax.fori_loop(0, batch_count, step, 0)
    for b in range(max(0, batch_count - 2), batch_count):
        for part in range(4):
            for copy in stores(b, part):
                copy.wait()


def widen(gathered, result, input_delta, shifts, cols, unit):
    batch_count, rows, width = gathered.shape
    fsdp_count = lax.axis_size("fsdp")
    hidden = unit * batch_count * fsdp_count
    half = width // 2
    turn = lax.axis_index("fsdp").astype(jnp.int32)[None]
    f32 = jnp.float32
    dma = pltpu.SemaphoreType.DMA
    hbm = pl.BlockSpec(memory_space=pl.ANY)
    vmem = pl.BlockSpec(memory_space=pltpu.VMEM)

    def matrix(rows, columns):
        return jax.ShapeDtypeStruct((rows, columns), f32)

    def vector(size):
        return jax.ShapeDtypeStruct((size // fsdp_count // 128, 128), f32)

    out = pl.pallas_call(
        functools.partial(widen_kernel, cols, unit),
        out_shape=(
            jax.ShapeDtypeStruct((1,) + result.shape, result.dtype),
            jax.ShapeDtypeStruct((1,) + input_delta.shape, f32),
            matrix(half, 3 * width),
            vector(3 * width),
            matrix(half, width),
            vector(width),
            matrix(half, hidden),
            vector(hidden),
            matrix(hidden // 2, width),
            vector(width),
        )
        + (vector(width),) * 4,
        in_specs=[pl.BlockSpec(memory_space=pltpu.SMEM), hbm, vmem, vmem, vmem],
        out_specs=(vmem, vmem) + (hbm, vmem) * 4 + (vmem,) * 4,
        scratch_shapes=[
            pltpu.VMEM((2, rows, width), gathered.dtype),
            pltpu.VMEM((2, 2, 3, half, cols), f32),
            pltpu.VMEM((2, cols, width), f32),
            pltpu.VMEM((2, 2, half, unit), f32),
            pltpu.VMEM((2, unit, width), f32),
            dma((2, 4)),
            dma((2, 4, 7)),
        ],
        name="widen",
        compiler_params=pltpu.CompilerParams(vmem_limit_bytes=VMEM_LIMIT),
    )(turn, gathered, result, input_delta, shifts)
    return tuple(a.reshape(-1) if a.ndim == 2 and a.shape[1] == 128 else a for a in out)


def dot(left, right, contract=((1,), (0,))):
    return lax.dot_general(left, right, (contract, ((), ())), preferred_element_type=jnp.float32)


def normalize(values):
    center = values - jnp.mean(values, axis=-1, keepdims=True)
    inverse = lax.rsqrt(jnp.mean(center * center, axis=-1, keepdims=True) + EPSILON)
    return (center * inverse, inverse)


def norm_backward(upstream, normed, inverse, factor):
    scaled = upstream * factor
    middle = jnp.mean(scaled, axis=-1, keepdims=True)
    coupled = jnp.mean(scaled * normed, axis=-1, keepdims=True)
    result = inverse * (scaled - middle - normed * coupled)
    return (result, jnp.sum(upstream * normed, axis=0), jnp.sum(upstream, axis=0))


def slot_positions(span_order, first_slot, slot_count, span_size):
    slot_index = first_slot + jnp.arange(slot_count, dtype=jnp.int32)
    owners = slot_index // (2 * span_size)
    places = jnp.arange(span_order.shape[0], dtype=jnp.int32)
    leading = jnp.sum(jnp.where(owners[:, None] == places[None, :], span_order[None, :], 0), axis=1)
    spans = 2 * span_order.shape[0]
    picked = jnp.where(slot_index // span_size % 2 == 0, leading, spans - 1 - leading)
    return picked * span_size + slot_index % span_size


def rotary_tables(positions):
    half_rot = ROT // 2
    angular = jnp.exp(
        jnp.arange(half_rot, dtype=jnp.float32) * (-2.0 * math.log(ROTARY_BASE) / ROT)
    )
    angles = positions.astype(jnp.float32)[:, None] * angular[None, :]
    angles = jnp.concatenate([angles, angles], axis=1)
    return (jnp.cos(angles), jnp.sin(angles))


def rotate(tensor, cosine, sine_table):
    half_rot = ROT // 2
    leading_part = tensor[..., :ROT]
    turned = jnp.concatenate([-leading_part[..., half_rot:], leading_part[..., :half_rot]], axis=-1)
    rotated = leading_part * cosine[:, None, :] + turned * sine_table[:, None, :]
    return jnp.concatenate([rotated, tensor[..., ROT:]], axis=-1)


def unrotate(tensor, cosine, sine_table):
    half_rot = ROT // 2
    leading_part = tensor[..., :ROT]
    weighted = leading_part * sine_table[:, None, :]
    turned = jnp.concatenate([weighted[..., half_rot:], -weighted[..., :half_rot]], axis=-1)
    return jnp.concatenate([leading_part * cosine[:, None, :] + turned, tensor[..., ROT:]], axis=-1)


def attention(mixed, place, cosine, sine_table, heads):
    sequences, length, _ = mixed.shape
    parts = mixed.reshape(sequences, length, 4, heads, HEAD_DIM)
    queries, keys, values, grads = (parts[:, :, i] for i in range(4))
    scale = 1.0 / math.sqrt(HEAD_DIM)
    scores = jnp.einsum("sqhd,skhd->shqk", queries, keys, preferred_element_type=jnp.float32)
    allowed = place[None, :] <= place[:, None]
    scores = jnp.where(allowed, scores * scale, MASKED)
    peak = jnp.max(scores, axis=-1, keepdims=True)
    log_total = peak + jnp.log(jnp.sum(jnp.exp(scores - peak), axis=-1, keepdims=True))
    probs = jnp.exp(scores - log_total)
    soft = probs.astype(jnp.bfloat16)
    context = jnp.einsum("shqk,skhd->sqhd", soft, values, preferred_element_type=jnp.float32)
    context = context.astype(jnp.bfloat16)
    delta = jnp.einsum(
        "sqhd,sqhd->shq", grads.astype(jnp.float32), context.astype(jnp.float32)
    )
    value_grad = jnp.einsum("shqk,sqhd->skhd", soft, grads, preferred_element_type=jnp.float32)
    probs_grad = jnp.einsum("sqhd,skhd->shqk", grads, values, preferred_element_type=jnp.float32)
    score_grad = (probs * (probs_grad - delta[..., None]) * scale).astype(jnp.bfloat16)
    query_grad = jnp.einsum("shqk,skhd->sqhd", score_grad, keys, preferred_element_type=jnp.float32)
    key_grad = jnp.einsum("shqk,sqhd->skhd", score_grad, queries, preferred_element_type=jnp.float32)
    query_grad = unrotate(query_grad, cosine, sine_table)
    key_grad = unrotate(key_grad, cosine, sine_table)
    back = jnp.stack([query_grad, key_grad, value_grad], axis=2)
    shift = jnp.sum(back, axis=(0, 1)).reshape(-1)
    full = jnp.concatenate([context[:, :, None], back.astype(jnp.bfloat16)], axis=2)
    return (full.reshape(sequences, length, 4 * heads * HEAD_DIM), shift)


def plain_body(
    layer_input,
    out_grad,
    span_order,
    inward,
    inward_bias,
    outward,
    outward_bias,
    expand,
    expand_bias,
    contract,
    contract_bias,
    first_gain,
    first_bias,
    second_gain,
    second_bias,
):
    batch_count, fsdp_count = (lax.axis_size("batch"), lax.axis_size("fsdp"))
    context_count = lax.axis_size("ctx")
    context_index = lax.axis_index("ctx")
    batch_index, fsdp_index = (lax.axis_index("batch"), lax.axis_index("fsdp"))
    plane = batch_count * fsdp_count
    tokens, width = layer_input.shape[1:]
    hidden_units = expand.shape[1]
    head_cols = width // plane
    unit_cols = hidden_units // plane
    heads = head_cols // HEAD_DIM
    length = tokens * context_count
    span_size = tokens // 2
    own_sequences = plane // context_count

    def full_vectors(*vectors):
        sizes = [v.shape[0] for v in vectors]
        gathered = lax.all_gather(jnp.concatenate(vectors), "fsdp")
        out, start = ([], 0)
        for size in sizes:
            out.append(gathered[:, start : start + size].reshape(-1).astype(jnp.float32))
            start += size
        return out

    (
        inward_offset,
        outward_offset,
        expand_offset,
        contract_offset,
        gain_first,
        offset_first,
        gain_second,
        offset_second,
    ) = full_vectors(
        inward_bias,
        outward_bias,
        expand_bias,
        contract_bias,
        first_gain,
        first_bias,
        second_gain,
        second_bias,
    )

    def chunk(array, cols):
        rows = array.shape[0]
        parts = array.reshape(rows, -1, fsdp_count, batch_count, cols)
        mine = lax.dynamic_index_in_dim(parts, batch_index, 3, keepdims=False)
        return mine.transpose(2, 0, 1, 3).reshape(fsdp_count, rows, -1)

    to_send = jnp.concatenate([chunk(inward, head_cols), chunk(expand, unit_cols)], axis=2)
    weights = lax.all_to_all(to_send, "fsdp", 0, 0).reshape(width, -1)
    inward_cols = weights[:, : 3 * head_cols]
    expand_cols = weights[:, 3 * head_cols :]
    outward_rows = lax.dynamic_slice_in_dim(outward, batch_index * head_cols, head_cols, 0)
    contract_rows = lax.dynamic_slice_in_dim(contract, batch_index * unit_cols, unit_cols, 0)
    plane_index = fsdp_index * batch_count + batch_index
    inward_shift_in = lax.dynamic_index_in_dim(
        inward_offset.reshape(3, plane, head_cols), plane_index, 1, keepdims=False
    ).reshape(-1)
    expand_shift_in = lax.dynamic_slice_in_dim(expand_offset, plane_index * unit_cols, unit_cols, 0)

    pair = jnp.stack([layer_input[0], out_grad[0]])
    pair_all = lax.all_gather(pair, PLANE, axis=1, tiled=True)
    grads_all = pair_all[1]
    rows_all = pair_all[0].astype(jnp.float32)
    normed, inverse = normalize(rows_all)
    first_rows = (normed * gain_first + offset_first).astype(jnp.bfloat16)
    second_rows = (normed * gain_second + offset_second).astype(jnp.bfloat16)

    local_place = slot_positions(span_order, context_index * tokens, tokens, span_size)
    cosine, sine_table = rotary_tables(local_place)
    cosine_plane = jnp.tile(cosine, (plane, 1))
    sine_plane = jnp.tile(sine_table, (plane, 1))
    projected = dot(first_rows, inward_cols) + inward_shift_in
    projected = projected.reshape(plane * tokens, 3 * heads, HEAD_DIM)
    turned = rotate(projected[:, : 2 * heads], cosine_plane, sine_plane)
    context_grad = dot(grads_all, outward_rows, ((1,), (1,)))
    mixed = jnp.concatenate(
        [
            turned.reshape(plane * tokens, -1),
            projected[:, 2 * heads :].reshape(plane * tokens, -1),
            context_grad,
        ],
        axis=1,
    ).astype(jnp.bfloat16)
    mixed = mixed.reshape(context_count, own_sequences, tokens, 4 * head_cols)
    mixed = lax.all_to_all(mixed, "ctx", 0, 0)
    mixed = mixed.transpose(1, 0, 2, 3).reshape(own_sequences, length, 4 * head_cols)
    place = slot_positions(span_order, 0, length, span_size)
    cosine_all, sine_all = rotary_tables(place)

    before = dot(second_rows, expand_cols) + expand_shift_in
    tail = 1.0 + lax.erf(before * HALF_ROOT)
    activated = (0.5 * before * tail).astype(jnp.bfloat16)
    slope = 0.5 * tail + before * jnp.exp(-0.5 * before * before) * NORMAL_PEAK
    before_grad = dot(grads_all, contract_rows, ((1,), (1,))) * slope
    expand_sum = jnp.sum(before_grad, axis=0)
    before_rows = before_grad.astype(jnp.bfloat16)
    expand_delta = dot(second_rows, before_rows, ((0,), (0,)))
    contract_delta = dot(activated, grads_all, ((0,), (0,)))
    out_part = dot(activated, contract_rows)
    second_part = dot(before_rows, expand_cols, ((1,), (1,)))

    hidden = layer_input[0].astype(jnp.float32)
    grad_float = out_grad[0].astype(jnp.float32)
    normed_mine, inverse_mine = normalize(hidden)
    half = width // fsdp_count

    def spread(values, sizes):
        wide = jnp.zeros((sizes[0], plane, sizes[1]), jnp.float32)
        values = values.reshape(sizes[0], sizes[1])
        return lax.dynamic_update_index_in_dim(wide, values, plane_index, 1).reshape(-1)

    bias_total = jnp.sum(grad_float, axis=0)
    expand_wide = spread(expand_sum, (1, unit_cols))

    back, inward_sum = attention(mixed, place, cosine_all, sine_all, heads)
    back = back.reshape(own_sequences, context_count, tokens, 4 * head_cols)
    back = lax.all_to_all(back.transpose(1, 0, 2, 3), "ctx", 0, 0)
    back = back.reshape(plane * tokens, 4 * head_cols)
    context_rows = back[:, :head_cols]
    projected_rows = back[:, head_cols:]
    inward_delta = dot(first_rows, projected_rows, ((0,), (0,)))
    outward_delta = dot(context_rows, grads_all, ((0,), (0,)))
    out_part = out_part + dot(context_rows, outward_rows)
    first_part = dot(projected_rows, inward_cols, ((1,), (1,)))
    stacked = jnp.stack([second_part, out_part, first_part], axis=1).astype(jnp.bfloat16)
    mine = lax.psum_scatter(stacked, PLANE, scatter_dimension=0, tiled=True)
    mine = mine.transpose(1, 0, 2).astype(jnp.float32)
    columns = jnp.concatenate([inward_delta, expand_delta], axis=1).astype(jnp.bfloat16)
    rows = jnp.concatenate([outward_delta, contract_delta], axis=0).astype(jnp.bfloat16)
    columns, rows = lax.psum((columns, rows), "ctx")
    columns = lax.all_to_all(columns.reshape(fsdp_count, half, -1), "fsdp", 0, 0)
    columns = lax.all_gather(columns, "batch")
    rows = lax.all_gather(rows, "batch").astype(jnp.float32)
    columns = columns.transpose(2, 1, 0, 3).astype(jnp.float32)
    inward_total = columns[..., : 3 * head_cols].reshape(
        half, fsdp_count, batch_count, 3, head_cols
    )
    totals = (
        inward_total.transpose(0, 3, 1, 2, 4).reshape(half, 3 * width),
        rows[:, :head_cols].reshape(half, width),
        columns[..., 3 * head_cols :].reshape(half, hidden_units),
        rows[:, head_cols:].reshape(-1, width),
    )
    _, second_scale, second_shift = norm_backward(
        mine[0], normed_mine, inverse_mine, gain_second
    )
    _, first_scale, first_shift = norm_backward(mine[2], normed_mine, inverse_mine, gain_first)
    vectors = [
        spread(inward_sum, (3, head_cols)),
        bias_total,
        expand_wide,
        first_scale,
        first_shift,
        second_scale,
        second_shift,
    ]
    whole = lax.psum(jnp.concatenate(vectors), ("batch", "ctx", "fsdp"))

    result = (hidden + (mine[1] + outward_offset) + contract_offset).astype(jnp.bfloat16)
    second_input, _, _ = norm_backward(mine[0], normed_mine, inverse_mine, gain_second)
    first_input, _, _ = norm_backward(mine[2], normed_mine, inverse_mine, gain_first)
    input_delta = grad_float + first_input + second_input
    halves, start = ([], 0)
    for vector in vectors:
        size = vector.shape[0] // fsdp_count
        halves.append(lax.dynamic_slice_in_dim(whole, start + fsdp_index * size, size, 0))
        start += vector.shape[0]
    return (
        result[None],
        input_delta[None],
        totals[0],
        halves[0],
        totals[1],
        halves[1],
        totals[2],
        halves[2],
        totals[3],
        halves[1],
        halves[3],
        halves[4],
        halves[5],
        halves[6],
    )


def body(
    layer_input,
    out_grad,
    span_order,
    inward,
    inward_bias,
    outward,
    outward_bias,
    expand,
    expand_bias,
    contract,
    contract_bias,
    first_gain,
    first_bias,
    second_gain,
    second_bias,
):
    plane = lax.axis_size("batch") * lax.axis_size("fsdp")
    width = layer_input.shape[2]
    if width // plane % 128:
        return plain_body(
            layer_input,
            out_grad,
            span_order,
            inward,
            inward_bias,
            outward,
            outward_bias,
            expand,
            expand_bias,
            contract,
            contract_bias,
            first_gain,
            first_bias,
            second_gain,
            second_bias,
        )
    vectors = (
        inward_bias,
        outward_bias,
        expand_bias,
        contract_bias,
        first_gain,
        first_bias,
        second_gain,
        second_bias,
    )
    ends = [sum(v.shape[0] for v in vectors[: i + 1]) for i in range(len(vectors))]
    room = ends[-1] + -ends[-1] % 1024
    small = sum(
        jnp.pad(v.astype(jnp.float32), (end - v.shape[0], room - end))
        for v, end in zip(vectors, ends)
    ).reshape(-1, 128)
    sums, result, input_delta, shifts = layer(
        layer_input, out_grad, span_order, small, inward, outward, expand, contract
    )
    return widen(sums, result, input_delta, shifts, width // plane, expand.shape[1] // plane)


def solution(mesh):
    rows = P(PLANE, "ctx", None)
    matrix, vector = (P("fsdp", None), P("fsdp"))
    in_specs = (rows, rows, P()) + (matrix, vector) * 4 + (vector,) * 4
    out_specs = (rows, rows) + (matrix, vector) * 4 + (vector,) * 4
    return jax.shard_map(body, mesh=mesh, in_specs=in_specs, out_specs=out_specs, check_vma=False)
```

```python
import functools
import math

import jax
import jax.numpy as jnp
from jax import lax
from jax.experimental import pallas as pl
from jax.experimental.pallas import tpu as pltpu
from jax.sharding import PartitionSpec as P

HEAD_DIM = 64
ROT = 16

EPSILON = 1e-05
ROTARY_BASE = 10000.0
MASKED = -1e30
HALF_ROOT = 0.7071067811865476
NORMAL_PEAK = 0.3989422804014327
PLANE = ("batch", "fsdp")


MESH = pl.DeviceIdType.MESH
CORES = 2
VMEM_LIMIT = 56 * 2**20


def here():
    return (lax.axis_index("batch"), lax.axis_index("ctx"), lax.axis_index("fsdp"))


def swapped(index, step):
    return index + step * (1 - 2 * (index // step % 2))


def greet(partners):
    barrier = pltpu.get_barrier_semaphore()
    for partner in partners:
        pl.semaphore_signal(barrier, inc=1, device_id=partner, device_id_type=MESH)
    pl.semaphore_wait(barrier, len(partners))


def remote(src, dst, send, recv, target):
    return pltpu.make_async_remote_copy(
        src_ref=src,
        dst_ref=dst,
        send_sem=send,
        recv_sem=recv,
        device_id=target,
        device_id_type=MESH,
    )


LAG = 2
LB = 2
LX = 2
LY = 3
AHEAD = 2
ATT = 4
READY = 11


def layer_kernel(
    sizes,
    tokens,
    heads,
    counts,
    piece,
    input_ref,
    grad_ref,
    order_ref,
    small_ref,
    inward_ref,
    outward_ref,
    expand_ref,
    contract_ref,
    sums_ref,
    result_ref,
    input_grad_ref,
    shifts_ref,
    inputs,
    grads,
    small,
    inward,
    outward,
    expand,
    contract,
    cosine,
    sine,
    stats,
    first_rows,
    second_rows,
    work,
    before,
    hidden_back,
    out_rows,
    scaled,
    mixed_out,
    mixed,
    heads_sum,
    back_out,
    back_in,
    inward_sum,
    row_sums,
    part,
    mine,
    reduced,
    reduced_right,
    near,
    across_in,
    far,
    token_sum,
    vector_in,
    vector_sum,
    load_sems,
    small_sems,
    weight_sems,
    pair_sems,
    gather_sems,
    share_sems,
    there_sends,
    there_recvs,
    there_own,
    back_own,
    turn_sems,
    reduce_sends,
    reduce_recvs,
    right_recvs,
    back_sends,
    back_recvs,
    row_sends,
    row_recvs,
    chip_sends,
    chip_recvs,
    core_sems,
    keep_sem,
    near_sems,
    across_sems,
    far_sems,
    vector_sems,
):
    batch_count, context_count, fsdp_count = sizes
    early_other, early, late_other, late = counts
    b, z, y = here()
    chips = batch_count // CORES
    core = b % CORES
    chip = b // CORES
    width = part.shape[1]
    half_width = width // 2
    cols = heads * HEAD_DIM
    unit = contract.shape[0]
    plane = batch_count * fsdp_count
    index = y * batch_count + b
    own_sequences = plane // context_count
    length = tokens * context_count
    steps = early + late
    early_rows = 2 * early * piece
    last = context_count - 1
    lines = width // 128
    f32, half_type = (jnp.float32, part.dtype)
    group_rows = fsdp_count * tokens

    sibling = (chip * CORES + (1 - core), z, y)
    across = (b, z, 1 - y)
    peers = [((chip + d) % chips * CORES + core, z, y) for d in range(1, chips)]
    sources = [(chip + chips - d) % chips * CORES + core for d in range(1, chips)]
    others = [(b, (z + d) % context_count, y) for d in range(1, context_count)]
    stages = []
    step = 1
    while step < batch_count:
        stages.append((swapped(b, step), z, y))
        step *= 2
    stages.append(across)
    step = 1
    while step < context_count:
        stages.append((b, swapped(z, step), y))
        step *= 2

    def sem(sems, *index):
        return (sems.at[(0, *index)], sems.at[(1, *index)])


    plane_arrays = (inputs, grads)
    plane_sources = (input_ref.at[0], grad_ref.at[0])

    def block(array, batch, fsdp):
        row = pl.multiple_of((batch * fsdp_count + fsdp) * tokens, tokens)
        return plane_arrays[array].at[pl.ds(row, tokens), :]

    def own_load(array):
        return pltpu.make_async_copy(
            plane_sources[array], block(array, b, y), load_sems.at[array]
        )

    def to_across(array):
        return remote(
            plane_sources[array], block(array, b, y), *sem(gather_sems, array, 0), across
        )

    def to_peer(array, d):
        return remote(
            plane_sources[array], block(array, b, y), *sem(gather_sems, array, 1 + d), peers[d]
        )

    def on_to_peer(array, d):
        at = block(array, b, 1 - y)
        return remote(at, at, *sem(gather_sems, array, chips + d), peers[d])

    def share(array, i):
        if i == 0:
            return remote(
                plane_sources[array], block(array, b, y), *sem(share_sems, array, 0), sibling
            )
        if i == 1:
            at = block(array, b, 1 - y)
        else:
            d = (i - 2) % (chips - 1)
            at = block(array, sources[d], y if i - 2 < chips - 1 else 1 - y)
        return remote(at, at, *sem(share_sems, array, i), sibling)

    def columns_of(owner, i):
        place = owner * batch_count + b
        if i < 3:
            return pl.ds(pl.multiple_of(i * width + place * cols, cols), cols)
        return pl.ds(pl.multiple_of(place * unit, unit), unit)

    part_rows = half_width // 2
    parity = z % 2
    pair = (b, swapped(z, 1), y)

    def inward_part(owner, parity):
        first = pl.multiple_of(owner * half_width + parity * part_rows, part_rows)
        return inward.at[pl.ds(first, part_rows), :]

    def weight_copies():
        source_rows = pl.ds(pl.multiple_of(parity * part_rows, part_rows), part_rows)
        rows = pl.ds(pl.multiple_of(y * half_width, half_width), half_width)
        out = [
            remote(
                inward_ref.at[source_rows, columns_of(1 - y, i)],
                inward_part(y, parity).at[:, i * cols : (i + 1) * cols],
                *sem(weight_sems, 0),
                across,
            )
            for i in range(3)
        ]
        out.append(
            remote(
                expand_ref.at[:, columns_of(1 - y, 3)],
                expand.at[rows, :],
                *sem(weight_sems, 1),
                across,
            )
        )
        return out

    def weight_own():
        rows = pl.ds(pl.multiple_of(y * half_width, half_width), half_width)
        pairs = [
            (inward_ref.at[:, columns_of(y, i)], inward.at[rows, i * cols : (i + 1) * cols])
            for i in range(3)
        ]
        pairs.append((expand_ref.at[:, columns_of(y, 3)], expand.at[rows, :]))
        return [
            pltpu.make_async_copy(source, target, load_sems.at[2 + i])
            for i, (source, target) in enumerate(pairs)
        ]

    def inward_brought():
        at = inward_part(1 - y, parity)
        return remote(at, at, *sem(weight_sems, 0), across)

    def to_pair(parity):
        at = inward_part(1 - y, parity)
        return remote(at, at, *sem(pair_sems), pair)

    row_loads = [
        pltpu.make_async_copy(
            outward_ref.at[pl.ds(pl.multiple_of(b * cols, cols), cols), :],
            outward,
            load_sems.at[6],
        ),
        pltpu.make_async_copy(
            contract_ref.at[pl.ds(pl.multiple_of(b * unit, unit), unit), :],
            contract,
            load_sems.at[7],
        ),
    ]
    weight_loads = weight_own()
    weight_sends = weight_copies()
    small_copy = remote(small_ref, small.at[1], *sem(small_sems, 0), across)

    own_load(0).start()
    own_load(1).start()
    for load in weight_loads + row_loads:
        load.start()
    greet([sibling, across] + peers + others)
    small_copy.start()

    def offer(array):
        to_across(array).start()
        share(array, 0).start()

    def offer_peers(array):
        for d in range(chips - 1):
            to_peer(array, d).start()

    for send in weight_sends[:3]:
        send.start()
    offer(0)
    offer_peers(0)
    small[0] = small_ref[...]


    def positions(shape, dimension):
        slot = lax.broadcasted_iota(jnp.int32, shape, dimension)
        owner = slot // tokens
        leading = jnp.zeros(shape, jnp.int32)
        for c in range(context_count):
            leading = jnp.where(owner == c, order_ref[c], leading)
        span = tokens // 2
        second = slot // span % 2
        picked = jnp.where(second == 0, leading, 2 * context_count - 1 - leading)
        return picked * span + slot % span

    half_rot = ROT // 2
    lane = lax.broadcasted_iota(jnp.int32, (1, cols), 1) % HEAD_DIM
    angular = jnp.exp((lane % half_rot).astype(f32) * (-2.0 * math.log(ROTARY_BASE) / ROT))
    angles = positions((length, cols), 0).astype(f32) * angular
    cosine[...] = jnp.where(lane < ROT, jnp.cos(angles), 1.0)
    sine[...] = jnp.where(lane < ROT, jnp.sin(angles), 0.0)
    low = (lane < half_rot).astype(f32)
    high = 1.0 - low

    def turn(value, rows, sign):
        weight = sine[rows, :] * sign
        return (
            value * cosine[rows, :]
            - pltpu.roll(value, cols - half_rot, 1) * (weight * low)
            + pltpu.roll(value, half_rot, 1) * (weight * high)
        )


    small_copy.wait_recv()
    vector_rows = [3 * lines, lines, unit * plane // 128] + [lines] * 5
    starts = [sum(vector_rows[:i]) // fsdp_count for i in range(8)]

    def vector_line(which, line):
        share_lines = vector_rows[which] // fsdp_count
        owner = line // share_lines
        at = (owner - y) * (owner - y)
        return small[at, pl.ds(starts[which] + line % share_lines, 1), :]

    def whole(which):
        return jnp.concatenate([vector_line(which, line) for line in range(lines)], axis=1)

    def chunk(which, first, count):
        return jnp.concatenate([vector_line(which, first + i) for i in range(count)], axis=1)


    def group(u):
        return (chip + u // CORES) % chips * CORES + (core + u % CORES) % CORES

    def rows_of(u):
        return pl.ds(pl.multiple_of(group(u) * group_rows, group_rows), group_rows)

    def bring(array, u):
        distance, other = (u // CORES, u % CORES)
        if other == 0 and distance == 0:
            own_load(array).wait()
            if array == 0:
                to_across(array).wait_recv()
            for d in range(chips - 1):
                on_to_peer(array, d).start()
            share(array, 1).start()
        elif other == 0:
            d = chips - distance - 1
            to_peer(array, d).wait_recv()
            share(array, 2 + d).start()
            on_to_peer(array, d).wait_recv()
            share(array, 1 + chips + d).start()
        elif distance == 0:
            share(array, 0).wait_recv()
            share(array, 1).wait_recv()
        else:
            d = chips - distance - 1
            share(array, 2 + d).wait_recv()
            share(array, 1 + chips + d).wait_recv()

    gains = [whole(4), whole(5), whole(6), whole(7)]
    inward_bias = jnp.concatenate(
        [
            chunk(0, i * lines + index * (cols // 128), cols // 128)
            for i in range(3)
        ],
        axis=1,
    )

    def norm(u):
        rows = rows_of(u)
        x = inputs[rows, :].astype(f32)
        mean = jnp.mean(x, axis=-1, keepdims=True)
        center = x - mean
        inverse = lax.rsqrt(jnp.mean(center * center, axis=-1, keepdims=True) + EPSILON)
        stats[rows, 0:1] = mean
        stats[rows, 1:2] = inverse
        normed = center * inverse
        first_rows[rows, :] = (normed * gains[0] + gains[1]).astype(half_type)
        second_rows[rows, :] = (normed * gains[2] + gains[3]).astype(half_type)

    there_columns = ((0, 3 * cols), (3 * cols, cols))

    def there_copy(u, f, kind):
        p = group(u) * fsdp_count + f
        owner, s = (p // own_sequences, p % own_sequences)
        first, count = there_columns[kind]
        columns = pl.ds(first, count)
        source = mixed_out.at[pl.ds(pl.multiple_of(p * tokens, tokens), tokens), columns]
        at = pl.ds(pl.multiple_of(z * tokens, tokens), tokens)
        target = mixed.at[s, at, columns]

        @pl.when(owner == z)
        def _():
            pltpu.make_async_copy(source, target, there_own.at[s, kind]).start()

        @pl.when(owner != z)
        def _():
            remote(
                source, target, there_sends.at[kind], there_recvs.at[s, z, kind], (b, owner, y)
            ).start()

    def project(u):
        projected = dot(first_rows[rows_of(u), :], inward[...]) + inward_bias
        local = pl.ds(pl.multiple_of(z * tokens, tokens), tokens)
        for f in range(fsdp_count):
            at = pl.ds(pl.multiple_of((group(u) * fsdp_count + f) * tokens, tokens), tokens)
            piece_rows = projected[f * tokens : (f + 1) * tokens, :]
            for i in range(3):
                value = piece_rows[:, i * cols : (i + 1) * cols]
                if i < 2:
                    value = turn(value, local, 1.0)
                mixed_out[at, i * cols : (i + 1) * cols] = value.astype(half_type)
            there_copy(u, f, 0)

    def upstream(u):
        rows = rows_of(u)
        value = dot(grads[rows, :], outward[...], ((1,), (1,)))
        mixed_out[rows, 3 * cols :] = value.astype(half_type)
        for f in range(fsdp_count):
            there_copy(u, f, 1)

    def there(s):
        for kind, (first, count) in enumerate(there_columns):
            columns = pl.ds(first, count)
            block_at = mixed.at[s, pl.ds(0, tokens), columns]
            pltpu.make_async_copy(block_at, block_at, there_own.at[s, kind]).wait()
            for d in range(1, context_count):
                source = (z + d) % context_count
                at = mixed.at[s, pl.ds(pl.multiple_of(source * tokens, tokens), tokens), columns]
                recv = there_recvs.at[s, source, kind]
                remote(at, at, there_sends.at[kind], recv, others[0]).wait_recv()

    order = [u for u in range(0, batch_count, CORES)] + [u for u in range(1, batch_count, CORES)]
    bring(0, 0)
    offer(1)
    inward_brought().wait_recv()
    to_pair(parity).start()
    norm(0)
    for i in range(3):
        weight_loads[i].wait()
    to_pair(1 - parity).wait_recv()
    project(0)
    to_across(1).wait_recv()
    weight_sends[3].start()
    for u in order[1:chips]:
        bring(0, u)
    offer_peers(1)
    bring(1, 0)
    row_loads[0].wait()
    for u in order[1:]:
        if u % CORES:
            bring(0, u)
        norm(u)
        project(u)
    upstream(0)
    for u in order[1:]:
        bring(1, u)
        upstream(u)


    row_loads[1].wait()
    weight_loads[3].wait()
    expand_bias = chunk(2, index * (unit // 128), unit // 128)
    nothing = jnp.zeros((1, width), f32)

    def normed_rows(rows):
        return (inputs[rows, :].astype(f32) - stats[rows, 0:1]) * stats[rows, 1:2]

    own_half = pl.ds(pl.multiple_of(y * half_width, half_width), half_width)
    other_half = pl.ds(pl.multiple_of((1 - y) * half_width, half_width), half_width)

    def early_tile(i, carry):
        rows = pl.ds(pl.multiple_of(i * group_rows, group_rows), group_rows)
        before[rows, :] = dot(second_rows[rows, own_half], expand[own_half, :]) + expand_bias
        hidden_back[rows, :] = dot(grads[rows, :], contract[...], ((1,), (1,)))
        return carry

    lax.fori_loop(0, batch_count, early_tile, 0)
    weight_sends[3].wait_recv()

    def forward_tile(i, expand_total):
        rows = pl.ds(pl.multiple_of(i * group_rows, group_rows), group_rows)
        value = before[rows, :] + dot(second_rows[rows, other_half], expand[other_half, :])
        tail = 1.0 + lax.erf(value * HALF_ROOT)
        slope = 0.5 * tail + value * jnp.exp(-0.5 * value * value) * NORMAL_PEAK
        before_grad = hidden_back[rows, :] * slope
        work[rows, :unit] = (0.5 * value * tail).astype(half_type)
        work[rows, unit:] = before_grad.astype(half_type)
        return expand_total + jnp.sum(before_grad, axis=0, keepdims=True)

    expand_total = lax.fori_loop(0, batch_count, forward_tile, jnp.zeros((1, unit), f32))
    row_sums[...] = jnp.zeros(row_sums.shape, f32)

    def hidden_tile(i):
        rows = pl.ds(pl.multiple_of(i * group_rows, group_rows), group_rows)
        out_rows[rows, :] = dot(work[rows, :unit], contract[...]).astype(half_type)
        value = dot(work[rows, unit:], expand[...], ((1,), (1,)))
        scaled[rows, :] = (value * gains[2]).astype(half_type)
        row_sums[0:1, :] += jnp.sum(value * normed_rows(rows), axis=0, keepdims=True)
        row_sums[1:2, :] += jnp.sum(value, axis=0, keepdims=True)

    def expand_half(s):
        owner = (1 - y) * (1 - s) + y * s
        column = pl.multiple_of(owner * half_width, half_width)
        delta = dot(second_rows[:, pl.ds(column, half_width)], work[:, unit:], ((0,), (0,)))
        group = unit * half_width // width
        at = pl.ds(pl.multiple_of(s * group, group), group)
        for j in range(width // unit):
            part[at, j * unit : (j + 1) * unit] = delta[j * group : (j + 1) * group, :].astype(
                half_type
            )

    def contract_rows():
        part[early_rows - unit : early_rows, :] = dot(
            work[:, :unit], grads[...], ((0,), (0,))
        ).astype(half_type)

    expand_half(0)


    def place(half, k):
        is_late = jnp.minimum(k // early, 1)
        other = early_other * (1 - is_late) + late_other * is_late
        count = early * (1 - is_late) + late * is_late
        j = k - early * is_late
        is_own = jnp.minimum(j // other, 1)
        row = (half * other + j) * (1 - is_own) + (
            2 * other + half * (count - other) + j - other
        ) * is_own
        return pl.multiple_of((2 * early * is_late + row) * piece, piece)

    def other_index(k):
        return k - (early - early_other) * jnp.minimum(k // early, 1)

    def own(k):
        is_late = jnp.minimum(k // early, 1)
        other = early_other * (1 - is_late) + late_other * is_late
        return jnp.minimum((k - early * is_late) // other, 1)

    def rows_at(ref, row):
        return ref.at[pl.ds(row, piece), :]

    def sums_at(batch, row):
        return sums_ref.at[batch, pl.ds(row, piece), :]

    def back_copy(half, k, side, target):
        at = rows_at(mine, place(half, k))
        return remote(at, at, back_sends.at[side, half], back_recvs.at[half, k], target)

    def row_copy(half, k):
        row = place(half, k)
        recv = row_recvs.at[half, other_index(k)]
        return remote(rows_at(mine, row), sums_at(b, row), row_sends, recv, across)

    def keep_copy(half, k):
        row = place(half, k)
        return pltpu.make_async_copy(rows_at(mine, row), sums_at(b, row), keep_sem)

    def chip_copy(d, half, k, from_mine):
        row = place(half, k)
        source = rows_at(mine, row) if from_mine else sums_at(b, row)
        return remote(
            source, sums_at(b, row), chip_sends.at[d], chip_recvs.at[d, half, k], peers[d]
        )

    def core_copy(half, k, from_mine, batch):
        row = place(half, k)
        source = rows_at(mine, row) if from_mine else sums_at(batch, row)
        return remote(
            source, sums_at(batch, row), core_sems.at[0], core_sems.at[1], sibling
        )

    def spread(half, k, from_mine):
        for d in range(chips - 1):
            chip_copy(d, half, k, from_mine).start()
        core_copy(half, k, from_mine, b).start()

    def arrived(half, k):
        for d in range(chips - 1):
            chip_copy(d, half, k, False).wait_recv()
            core_copy(half, k, False, sources[d]).start()

    def finish(half, k):
        @pl.when(own(k) == 0)
        def _():
            row_copy(half, k).start()

        @pl.when(own(k) == 1)
        def _():
            keep_copy(half, k).start()
            spread(half, k, True)

    left = (b, (z + last) % context_count, y)
    right = (b, (z + 1) % context_count, y)

    def reduce_copy(half, k, source, stream, target):
        row = place(half, k)
        if stream:
            landing = reduced_right.at[pl.ds(pl.multiple_of(k * piece, piece), piece), :]
            recv = right_recvs.at[k]
        else:
            landing = rows_at(reduced, row)
            recv = reduce_recvs.at[half, k]
        return remote(rows_at(source, row), landing, reduce_sends.at[half], recv, target)

    def ends(half):
        root = last // 2 if half == 0 else context_count // 2
        depth = max(root, last - root)
        at_root = z == root
        is_left = z < root
        distance = jnp.where(is_left, root - z, z - root)
        leaf = (z == 0) | (z == last)
        return root, depth, at_root, is_left, distance, leaf

    def pass_on(half, k, source):
        root = last // 2 if half == 0 else context_count // 2

        @pl.when(z == root + 1)
        def _():
            reduce_copy(half, k, source, 1, left).start()

        @pl.when(z > root + 1)
        def _():
            reduce_copy(half, k, source, 0, left).start()

        @pl.when(z < root)
        def _():
            reduce_copy(half, k, source, 0, right).start()

    def leaf_send(half, k):
        pass_on(half, k, part)

    def reduce_step(t, half):
        root, depth, at_root, is_left, distance, leaf = ends(half)
        k = t - LAG * (depth - distance)

        def send(source):
            pass_on(half, k, source)

        k_leaf = t + AHEAD

        @pl.when(leaf & jnp.logical_not(at_root) & (k_leaf < steps))
        def _():
            leaf_send(half, k_leaf)

        @pl.when(jnp.logical_not(leaf) & (k >= 0) & (k < steps))
        def _():
            row = place(half, k)
            here_at = pl.ds(row, piece)

            @pl.when(at_root)
            def _():
                value = part[here_at, :].astype(f32)
                if root > 0:
                    reduce_copy(half, k, part, 0, right).wait_recv()
                    value = value + reduced[here_at, :].astype(f32)
                if root < last:
                    reduce_copy(half, k, part, 1, left).wait_recv()
                    came = reduced_right[pl.ds(pl.multiple_of(k * piece, piece), piece), :]
                    value = value + came.astype(f32)
                mine[here_at, :] = value.astype(half_type)
                if root > 0:
                    back_copy(half, k, 0, left).start()
                if root < last:
                    back_copy(half, k, 1, right).start()
                finish(half, k)

            @pl.when(jnp.logical_not(at_root))
            def _():
                reduce_copy(half, k, part, 0, right).wait_recv()
                value = part[here_at, :].astype(f32) + reduced[here_at, :].astype(f32)
                reduced[here_at, :] = value.astype(half_type)
                send(reduced)

    def back_step(t, half):
        root, depth, at_root, is_left, distance, leaf = ends(half)
        k_back = t - LAG * depth - LB * distance

        @pl.when(jnp.logical_not(at_root) & (k_back >= 0) & (k_back < steps))
        def _():
            back_copy(half, k_back, 0, left).wait_recv()

            @pl.when(is_left & (z > 0))
            def _():
                back_copy(half, k_back, 0, left).start()

            @pl.when((z > root) & (z < last))
            def _():
                back_copy(half, k_back, 1, right).start()

            finish(half, k_back)

    def side_step(t, half):
        root, depth, at_root, is_left, distance, leaf = ends(half)
        k_row = t - LAG * depth - LB * distance - LX

        @pl.when((k_row >= 0) & (k_row < steps))
        def _():
            @pl.when(own(k_row) == 0)
            def _():
                row_copy(half, k_row).wait_recv()
                spread(half, k_row, False)

            @pl.when(own(k_row) == 1)
            def _():
                arrived(half, k_row)

        k_chip = k_row - LY

        @pl.when((k_chip >= 0) & (k_chip < steps))
        def _():
            @pl.when(own(k_chip) == 0)
            def _():
                arrived(half, k_chip)

    def drain():
        half_rows = pl.ds(0, steps * piece)
        other_count = 2 * (early_other + late_other) * piece

        def sent(ref, semaphore):
            remote(ref, ref, semaphore, core_sems.at[1], sibling).wait_send()

        everything = sums_ref.at[pl.ds(0, chips)]
        from_sibling = remote(everything, everything, core_sems.at[0], core_sems.at[1], sibling)
        from_sibling.wait_send()
        for d in range(chips - 1):
            sent(mine, chip_sends.at[d])
        sent(mine.at[pl.ds(0, other_count), :], row_sends)
        kept = mine.at[pl.ds(0, mine.shape[0] - other_count), :]
        pltpu.make_async_copy(kept, kept, keep_sem).wait()
        for half in range(2):
            root = last // 2 if half == 0 else context_count // 2

            @pl.when(z != root)
            def _():
                sent(mine.at[half_rows, :], reduce_sends.at[half])

            @pl.when((z <= root) & (z > 0))
            def _():
                sent(mine.at[half_rows, :], back_sends.at[0, half])

            @pl.when((z >= root) & (z < last))
            def _():
                sent(mine.at[half_rows, :], back_sends.at[1, half])

        from_sibling.wait_recv()


    def attend(n):
        s, h = (n // heads, n % heads)
        columns = [mixed[s, :, i * cols : (i + 1) * cols] for i in range(4)]
        head = lax.broadcasted_iota(jnp.int32, (length, cols), 1) // HEAD_DIM
        picked = head == h
        blank = jnp.zeros((length, cols), half_type)
        _, keys, values, _ = columns
        queries_h, keys_h, values_h, upstream_h = [
            jnp.where(picked, column, blank) for column in columns
        ]
        scale = 1.0 / math.sqrt(HEAD_DIM)
        allowed = positions((1, length), 1) <= positions((length, 1), 0)
        scores = dot(queries_h, keys, ((1,), (1,))) * scale
        scores = jnp.where(allowed, scores, MASKED)
        peak = jnp.max(scores, axis=1, keepdims=True)
        log_total = peak + jnp.log(jnp.sum(jnp.exp(scores - peak), axis=1, keepdims=True))
        probs = jnp.exp(scores - log_total)
        soft = probs.astype(half_type)
        context = dot(soft, values_h)
        delta = jnp.sum(
            upstream_h.astype(f32) * context.astype(half_type).astype(f32), axis=1, keepdims=True
        )
        probs_grad = dot(upstream_h, values, ((1,), (1,)))
        score_grad = (probs * (probs_grad - delta) * scale).astype(half_type)
        results = (
            context,
            dot(score_grad, keys_h),
            dot(score_grad, queries_h, ((0,), (0,))),
            dot(soft, upstream_h, ((0,), (0,))),
        )
        for i, value in enumerate(results):

            @pl.when(h == 0)
            def _():
                heads_sum[i] = value

            @pl.when(h > 0)
            def _():
                heads_sum[i] += value

        @pl.when(h == heads - 1)
        def _():
            back_out[s, :, :cols] = heads_sum[0].astype(half_type)
            for i in range(1, 4):
                value = heads_sum[i]
                if i < 3:
                    value = turn(value, slice(None), -1.0)
                back_out[s, :, i * cols : (i + 1) * cols] = value.astype(half_type)
                total = jnp.sum(value, axis=0, keepdims=True)

                @pl.when(s == 0)
                def _():
                    inward_sum[i - 1 : i, :] = total

                @pl.when(s > 0)
                def _():
                    inward_sum[i - 1 : i, :] += total

            for d in range(context_count):
                turn_copy(s, d).start()

    def turn_copy(s, d):
        target = (z + d) % context_count
        source = back_out.at[s, pl.ds(pl.multiple_of(target * tokens, tokens), tokens), :]
        row = pl.multiple_of((z * own_sequences + s) * tokens, tokens)
        destination = back_in.at[pl.ds(row, tokens), :]
        if d == 0:
            return pltpu.make_async_copy(source, destination, back_own.at[s])
        return remote(source, destination, *sem(turn_sems, s, d - 1), others[d - 1])

    def turned():
        for s in range(own_sequences):
            turn_copy(s, 0).wait()
            for d in range(1, context_count):
                turn_copy(s, d).wait_recv()


    def head_gradients():
        delta = dot(back_in[:, :cols], grads[...], ((0,), (0,))).astype(half_type)
        part[early_rows + 4 * late_other * piece :, :] = delta
        group = cols * half_width // width

        def half_rows(s, carry):
            owner = (1 - y) * (1 - s) + y * s
            column = pl.multiple_of(owner * half_width, half_width)
            delta = dot(
                first_rows[:, pl.ds(column, half_width)], back_in[:, cols:], ((0,), (0,))
            ).astype(half_type)
            top = pl.multiple_of(early_rows + s * 3 * group, group)
            for i in range(3):
                for j in range(width // cols):
                    part[pl.ds(top + i * group, group), j * cols : (j + 1) * cols] = delta[
                        j * group : (j + 1) * group, i * cols : (i + 1) * cols
                    ]
            return carry

        lax.fori_loop(0, 2, half_rows, 0)

    def output_rows():
        def step(i, carry):
            rows = pl.ds(pl.multiple_of(i * group_rows, group_rows), group_rows)
            value = dot(back_in[rows, :cols], outward[...])
            out_rows[rows, :] = (out_rows[rows, :].astype(f32) + value).astype(half_type)
            return carry

        lax.fori_loop(0, batch_count, step, 0)

    vector_start = len(stages)

    def first_back_rows():
        def step(i, carry):
            rows = pl.ds(pl.multiple_of(i * group_rows, group_rows), group_rows)
            value = dot(back_in[rows, cols:], inward[...], ((1,), (1,)))
            scaled[rows, :] = (scaled[rows, :].astype(f32) + value * gains[0]).astype(half_type)
            row_sums[2:3, :] += jnp.sum(value * normed_rows(rows), axis=0, keepdims=True)
            row_sums[3:4, :] += jnp.sum(value, axis=0, keepdims=True)
            return carry

        lax.fori_loop(0, batch_count, step, 0)
        out = vector_sum.at[vector_start]
        out[...] = jnp.zeros(out.shape, f32)

        def put(line, value):
            for j in range(value.shape[1] // 128):
                out[pl.ds(line + j, 1), :] = value[:, j * 128 : (j + 1) * 128]

        for i in range(3):
            put(i * lines + index * (cols // 128), inward_sum[i : i + 1, :])
        first = 3 * lines
        own_rows = pl.ds(pl.multiple_of((b * fsdp_count + y) * tokens, tokens), tokens)
        put(first, jnp.sum(grads[own_rows, :].astype(f32), axis=0, keepdims=True))
        first += lines
        put(first + index * (unit // 128), expand_total)
        first += unit * plane // 128
        for i in range(4):
            put(first, row_sums[i : i + 1, :])
            first += lines

    def vector_copy(i):
        source = vector_sum.at[vector_start if i == 0 else i - 1]
        return remote(source, vector_in.at[i], *sem(vector_sems, i), stages[i])


    arrays = (out_rows, scaled)

    def near_copy(a, c):
        row = pl.multiple_of((c * CORES + 1 - core) * group_rows, group_rows)
        return remote(
            arrays[a].at[pl.ds(row, group_rows), :],
            near.at[a, pl.ds(c * group_rows, group_rows), :],
            *sem(near_sems, a, c),
            sibling,
        )

    def across_copy(a, c):
        row = pl.multiple_of(c * group_rows + (1 - y) * tokens, tokens)
        return remote(
            near.at[a, pl.ds(row, tokens), :],
            across_in.at[a, pl.ds(c * tokens, tokens), :],
            *sem(across_sems, a, c),
            across,
        )

    def far_copy(a, d):
        row = pl.multiple_of((chip + d + 1) % chips * tokens, tokens)
        return remote(
            across_in.at[a, pl.ds(row, tokens), :], far.at[a, d], *sem(far_sems, a, d), peers[d]
        )

    def scatter_first(a):
        for c in range(chips):
            near_copy(a, c).start()

    def scatter_second(a):
        for c in range(chips):
            near_copy(a, c).wait_recv()

            def step(i, carry):
                row = pl.multiple_of((c * CORES + core) * group_rows + i * tokens, tokens)
                value = arrays[a][pl.ds(row, tokens), :].astype(f32)
                at = pl.ds(pl.multiple_of(c * group_rows + i * tokens, tokens), tokens)
                near[a, at, :] = (value + near[a, at, :].astype(f32)).astype(half_type)
                return carry

            lax.fori_loop(0, fsdp_count, step, 0)
            across_copy(a, c).start()

    def scatter_third(a):
        for c in range(chips):
            across_copy(a, c).wait_recv()

        def both(c):
            row = pl.multiple_of(c * group_rows + y * tokens, tokens)
            at = pl.ds(pl.multiple_of(c * tokens, tokens), tokens)
            return (
                near[a, pl.ds(row, tokens), :].astype(f32) + across_in[a, at, :].astype(f32),
                at,
            )

        for d in range(chips - 1):
            value, at = both((chip + d + 1) % chips)
            across_in[a, at, :] = value.astype(half_type)
            far_copy(a, d).start()
        token_sum[a] = both(chip)[0]

    def scatter_last(a):
        value = token_sum[a]
        for d in range(chips - 1):
            far_copy(a, d).wait_recv()
            value = value + far[a, d].astype(f32)
        own_rows = pl.ds(pl.multiple_of((b * fsdp_count + y) * tokens, tokens), tokens)
        x = inputs[own_rows, :].astype(f32)
        if a == 0:
            result_ref[...] = (x + (value + whole(1)) + whole(3)).astype(half_type)
            return
        normed = normed_rows(own_rows)
        middle = jnp.mean(value, axis=-1, keepdims=True)
        coupled = jnp.mean(value * normed, axis=-1, keepdims=True)
        back = stats[own_rows, 1:2] * (value - middle - normed * coupled)
        input_grad_ref[...] = grads[own_rows, :].astype(f32) + back


    problems = own_sequences * heads
    ready = READY
    if ready < ATT + problems or early <= ready + AHEAD:
        raise ValueError("schedule")
    plan = {}

    def at(slot, work):
        plan.setdefault(slot, []).append(work)

    def scatter(a, slot):
        at(slot, lambda: scatter_first(a))
        at(slot + 3, lambda: scatter_second(a))
        at(slot + 6, lambda: scatter_third(a))
        at(slot + 9, lambda: scatter_last(a))

    at(0, lambda: expand_half(1))
    at(1, contract_rows)
    for s in range(own_sequences):
        at(ATT + s * heads, lambda s=s: there(s))
    for i in range(batch_count):
        at(min(ATT + problems + i, ready), lambda i=i: hidden_tile(i))
    at(ready, turned)
    at(ready, head_gradients)
    at(ready + 1, output_rows)
    scatter(0, ready + 1)
    at(ready + 2, first_back_rows)
    scatter(1, ready + 2)
    at(ready + 2, lambda: vector_copy(0).start())
    for i in range(len(stages)):

        def vector_step(i=i):
            vector_copy(i).wait_recv()
            before = vector_sum[vector_start if i == 0 else i - 1]
            vector_sum[i] = before + vector_in[i]
            if i + 1 < len(stages):
                vector_copy(i + 1).start()

        at(ready + 4 + 2 * i, vector_step)

    def slot_step(t, carry):
        for work in (reduce_step, back_step, side_step):
            for half in range(2):
                work(t, half)

        for slot, works in sorted(plan.items()):

            @pl.when(t == slot)
            def _():
                for work in works:
                    work()

        @pl.when((t >= ATT) & (t < ATT + problems))
        def _():
            attend(t - ATT)

        return carry

    for half in range(2):

        @pl.when((z == 0) | (z == last))
        def _():
            for k in range(AHEAD):
                leaf_send(half, k)

    depth = context_count // 2
    tail = (LAG + LB) * depth + LX
    slots = max(steps + tail, early + late_other + tail + LY, max(plan) + 1)
    lax.fori_loop(0, slots, slot_step, 0)
    first = 0
    out_first = 0
    for count in (3 * lines, lines, unit * plane // 128, lines, lines, lines, lines):
        share_lines = count // fsdp_count
        for j in range(share_lines):
            line = first + y * share_lines + j
            shifts_ref[out_first + j : out_first + j + 1, :] = vector_sum[
                len(stages) - 1, pl.ds(line, 1), :
            ]
        first += count
        out_first += share_lines

    drain()
    small_copy.wait_send()
    inward_brought().wait_send()
    to_pair(parity).wait_send()
    weight_sends[3].wait_send()
    for array in range(2):
        to_across(array).wait_send()
        for d in range(chips - 1):
            to_peer(array, d).wait_send()
            on_to_peer(array, d).wait_send()
        for i in range(2 * chips):
            share(array, i).wait_send()
    away = (plane - own_sequences) * tokens
    for kind, (first, count) in enumerate(there_columns):
        at = mixed_out.at[pl.ds(0, away), pl.ds(first, count)]
        remote(at, at, there_sends.at[kind], there_recvs.at[0, 0, kind], others[0]).wait_send()
    for i in range(len(stages)):
        vector_copy(i).wait_send()
    for s in range(own_sequences):
        for d in range(1, context_count):
            turn_copy(s, d).wait_send()
    for a in range(2):
        for c in range(chips):
            near_copy(a, c).wait_send()
            across_copy(a, c).wait_send()
        for d in range(chips - 1):
            far_copy(a, d).wait_send()


def layer(layer_input, out_grad, span_order, small, inward, outward, expand, contract):
    sizes = tuple(lax.axis_size(name) for name in ("batch", "ctx", "fsdp"))
    batch_count, context_count, fsdp_count = sizes
    plane = batch_count * fsdp_count
    chips = batch_count // CORES
    tokens, width = layer_input.shape[1:]
    hidden = expand.shape[1]
    cols = width // plane
    heads = cols // HEAD_DIM
    length = tokens * context_count
    own_sequences = plane // context_count
    half = width // 2
    unit = hidden // plane
    early_other, early = (unit * half // width, 2 * unit * half // width + unit)
    late_other, late = (3 * cols * half // width, 6 * cols * half // width + cols)
    piece = 32
    for rows in (early_other, early - early_other, late_other, late - late_other):
        piece = math.gcd(piece, rows // 2)
    counts = tuple(n // 2 // piece for n in (early_other, early, late_other, late))
    steps = counts[1] + counts[3]
    rows = early + late
    stage_count = (plane * context_count).bit_length() - 1
    all_tokens = plane * tokens
    vector_lines = (8 * width + hidden) // 128
    dma = pltpu.SemaphoreType.DMA
    f32, half_type = (jnp.float32, layer_input.dtype)
    vmem = pl.BlockSpec(memory_space=pltpu.VMEM)
    hbm = pl.BlockSpec(memory_space=pl.ANY)

    def held(*shape, dtype=half_type):
        return pltpu.VMEM(shape, dtype)

    return pl.pallas_call(
        functools.partial(layer_kernel, sizes, tokens, heads, counts, piece),
        out_shape=(
            jax.ShapeDtypeStruct((batch_count, rows, width), half_type),
            jax.ShapeDtypeStruct((tokens, width), half_type),
            jax.ShapeDtypeStruct((tokens, width), f32),
            jax.ShapeDtypeStruct((vector_lines // fsdp_count, 128), f32),
        ),
        in_specs=[hbm, hbm, pl.BlockSpec(memory_space=pltpu.SMEM), vmem] + [hbm] * 4,
        out_specs=(hbm, vmem, vmem, vmem),
        scratch_shapes=[
            held(all_tokens, width),
            held(all_tokens, width),
            held(2, *small.shape, dtype=f32),
            held(width, 3 * cols),
            held(cols, width),
            held(width, unit),
            held(unit, width),
            held(length, cols, dtype=f32),
            held(length, cols, dtype=f32),
            held(all_tokens, 2, dtype=f32),
            held(all_tokens, width),
            held(all_tokens, width),
            held(all_tokens, 2 * unit),
            held(all_tokens, unit, dtype=f32),
            held(all_tokens, unit, dtype=f32),
            held(all_tokens, width),
            held(all_tokens, width),
            held(all_tokens, 4 * cols),
            held(own_sequences, length, 4 * cols),
            held(4, length, cols, dtype=f32),
            held(own_sequences, length, 4 * cols),
            held(all_tokens, 4 * cols),
            held(8, cols, dtype=f32),
            held(8, width, dtype=f32),
            held(rows, width),
            held(rows, width),
            held(rows, width),
            held(rows // 2, width),
            held(2, chips * fsdp_count * tokens, width),
            held(2, chips * tokens, width),
            held(2, chips - 1, tokens, width),
            held(2, tokens, width, dtype=f32),
            held(stage_count, vector_lines, 128, dtype=f32),
            held(stage_count + 1, vector_lines, 128, dtype=f32),
            dma((8,)),
            dma((2, 1)),
            dma((2, 2)),
            dma((2,)),
            dma((2, 2, 2 * chips - 1)),
            dma((2, 2, 2 * chips)),
            dma((2,)),
            dma((own_sequences, context_count, 2)),
            dma((own_sequences, 2)),
            dma((own_sequences,)),
            dma((2, own_sequences, context_count - 1)),
            dma((2,)),
            dma((2, steps)),
            dma((steps,)),
            dma((2, 2)),
            dma((2, steps)),
            dma,
            dma((2, counts[0] + counts[2])),
            dma((chips - 1,)),
            dma((chips - 1, 2, steps)),
            dma((2,)),
            dma,
            dma((2, 2, chips)),
            dma((2, 2, chips)),
            dma((2, 2, chips - 1)),
            dma((2, stage_count)),
        ],
        name="layer",
        compiler_params=pltpu.CompilerParams(
            collective_id=0, has_side_effects=True, vmem_limit_bytes=VMEM_LIMIT
        ),
    )(layer_input, out_grad, span_order, small, inward, outward, expand, contract)


def widen_kernel(
    cols,
    unit,
    turn_ref,
    all_ref,
    result_in,
    input_in,
    shifts_in,
    result_ref,
    input_ref,
    inward_ref,
    inward_shift,
    outward_ref,
    outward_shift,
    expand_ref,
    expand_shift,
    contract_ref,
    contract_shift,
    first_scale,
    first_shift,
    second_scale,
    second_shift,
    held,
    inward,
    outward,
    expand,
    contract,
    in_sems,
    out_sems,
):
    batch_count, rows, width = all_ref.shape
    half = inward_ref.shape[0]
    unit_rows, unit_blocks = (unit * half // width, width // unit)
    head_rows, head_blocks = (cols * half // width, width // cols)
    late = 2 * unit_rows + unit
    bounds = ((late, rows - late), (0, unit_rows), (unit_rows, unit_rows), (late - unit, unit))
    y = turn_ref[0]

    def load(b, part):
        first, count = bounds[part]
        at = pl.ds(first, count)
        return pltpu.make_async_copy(
            all_ref.at[b, at, :], held.at[b, at, :], in_sems.at[b, part]
        )

    def stores(b, part):
        at = b % 2
        pairs = []
        if part == 0:
            pairs.append((outward.at[at], outward_ref.at[pl.ds(b * cols, cols), :]))
            for s in range(2):
                owner = y if s else 1 - y
                for i in range(3):
                    column = pl.multiple_of(i * width + (owner * batch_count + b) * cols, cols)
                    pairs.append((inward.at[at, s, i], inward_ref.at[:, pl.ds(column, cols)]))
        elif part < 3:
            owner = y if part == 2 else 1 - y
            column = pl.multiple_of((owner * batch_count + b) * unit, unit)
            pairs.append((expand.at[at, part - 1], expand_ref.at[:, pl.ds(column, unit)]))
        else:
            pairs.append((contract.at[at], contract_ref.at[pl.ds(b * unit, unit), :]))
        return [
            pltpu.make_async_copy(source, target, out_sems.at[at, part, i])
            for i, (source, target) in enumerate(pairs)
        ]

    for b in range(batch_count):
        for part in range(4):
            load(b, part).start()
    result_ref[0] = result_in[...]
    input_ref[0] = input_in[...]
    line = 0
    for target in (
        inward_shift,
        outward_shift,
        expand_shift,
        second_scale,
        second_shift,
        first_scale,
        first_shift,
    ):
        count = target.shape[0]
        target[...] = shifts_in[line : line + count, :]
        line += count
    contract_shift[...] = outward_shift[...]

    def step(b, carry):
        at = b % 2
        for part in range(4):
            load(b, part).wait()

            @pl.when(b >= 2)
            def _():
                for copy in stores(b - 2, part):
                    copy.wait()

            if part == 0:
                for s in range(2):
                    for i in range(3):
                        top = late + (s * 3 + i) * head_rows
                        for j in range(head_blocks):
                            inward[at, s, i, j * head_rows : (j + 1) * head_rows, :] = held[
                                b, top : top + head_rows, j * cols : (j + 1) * cols
                            ].astype(jnp.float32)
                outward[at] = held[b, late + 6 * head_rows :, :].astype(jnp.float32)
            elif part < 3:
                first = (part - 1) * unit_rows
                for j in range(unit_blocks):
                    expand[at, part - 1, j * unit_rows : (j + 1) * unit_rows, :] = held[
                        b, first : first + unit_rows, j * unit : (j + 1) * unit
                    ].astype(jnp.float32)
            else:
                contract[at] = held[b, late - unit : late, :].astype(jnp.float32)
            for copy in stores(b, part):
                copy.start()
        return carry

    lax.fori_loop(0, batch_count, step, 0)
    for b in range(max(0, batch_count - 2), batch_count):
        for part in range(4):
            for copy in stores(b, part):
                copy.wait()


def widen(gathered, result, input_delta, shifts, cols, unit):
    batch_count, rows, width = gathered.shape
    fsdp_count = lax.axis_size("fsdp")
    hidden = unit * batch_count * fsdp_count
    half = width // 2
    turn = lax.axis_index("fsdp").astype(jnp.int32)[None]
    f32 = jnp.float32
    dma = pltpu.SemaphoreType.DMA
    hbm = pl.BlockSpec(memory_space=pl.ANY)
    vmem = pl.BlockSpec(memory_space=pltpu.VMEM)

    def matrix(rows, columns):
        return jax.ShapeDtypeStruct((rows, columns), f32)

    def vector(size):
        return jax.ShapeDtypeStruct((size // fsdp_count // 128, 128), f32)

    out = pl.pallas_call(
        functools.partial(widen_kernel, cols, unit),
        out_shape=(
            jax.ShapeDtypeStruct((1,) + result.shape, result.dtype),
            jax.ShapeDtypeStruct((1,) + input_delta.shape, f32),
            matrix(half, 3 * width),
            vector(3 * width),
            matrix(half, width),
            vector(width),
            matrix(half, hidden),
            vector(hidden),
            matrix(hidden // 2, width),
            vector(width),
        )
        + (vector(width),) * 4,
        in_specs=[pl.BlockSpec(memory_space=pltpu.SMEM), hbm, vmem, vmem, vmem],
        out_specs=(vmem, vmem) + (hbm, vmem) * 4 + (vmem,) * 4,
        scratch_shapes=[
            pltpu.VMEM((batch_count, rows, width), gathered.dtype),
            pltpu.VMEM((2, 2, 3, half, cols), f32),
            pltpu.VMEM((2, cols, width), f32),
            pltpu.VMEM((2, 2, half, unit), f32),
            pltpu.VMEM((2, unit, width), f32),
            dma((batch_count, 4)),
            dma((2, 4, 7)),
        ],
        name="widen",
        compiler_params=pltpu.CompilerParams(vmem_limit_bytes=VMEM_LIMIT),
    )(turn, gathered, result, input_delta, shifts)
    return tuple(a.reshape(-1) if a.ndim == 2 and a.shape[1] == 128 else a for a in out)


def dot(left, right, contract=((1,), (0,))):
    return lax.dot_general(left, right, (contract, ((), ())), preferred_element_type=jnp.float32)


def normalize(values):
    center = values - jnp.mean(values, axis=-1, keepdims=True)
    inverse = lax.rsqrt(jnp.mean(center * center, axis=-1, keepdims=True) + EPSILON)
    return (center * inverse, inverse)


def norm_backward(upstream, normed, inverse, factor):
    scaled = upstream * factor
    middle = jnp.mean(scaled, axis=-1, keepdims=True)
    coupled = jnp.mean(scaled * normed, axis=-1, keepdims=True)
    result = inverse * (scaled - middle - normed * coupled)
    return (result, jnp.sum(upstream * normed, axis=0), jnp.sum(upstream, axis=0))


def slot_positions(span_order, first_slot, slot_count, span_size):
    slot_index = first_slot + jnp.arange(slot_count, dtype=jnp.int32)
    owners = slot_index // (2 * span_size)
    places = jnp.arange(span_order.shape[0], dtype=jnp.int32)
    leading = jnp.sum(jnp.where(owners[:, None] == places[None, :], span_order[None, :], 0), axis=1)
    spans = 2 * span_order.shape[0]
    picked = jnp.where(slot_index // span_size % 2 == 0, leading, spans - 1 - leading)
    return picked * span_size + slot_index % span_size


def rotary_tables(positions):
    half_rot = ROT // 2
    angular = jnp.exp(
        jnp.arange(half_rot, dtype=jnp.float32) * (-2.0 * math.log(ROTARY_BASE) / ROT)
    )
    angles = positions.astype(jnp.float32)[:, None] * angular[None, :]
    angles = jnp.concatenate([angles, angles], axis=1)
    return (jnp.cos(angles), jnp.sin(angles))


def rotate(tensor, cosine, sine_table):
    half_rot = ROT // 2
    leading_part = tensor[..., :ROT]
    turned = jnp.concatenate([-leading_part[..., half_rot:], leading_part[..., :half_rot]], axis=-1)
    rotated = leading_part * cosine[:, None, :] + turned * sine_table[:, None, :]
    return jnp.concatenate([rotated, tensor[..., ROT:]], axis=-1)


def unrotate(tensor, cosine, sine_table):
    half_rot = ROT // 2
    leading_part = tensor[..., :ROT]
    weighted = leading_part * sine_table[:, None, :]
    turned = jnp.concatenate([weighted[..., half_rot:], -weighted[..., :half_rot]], axis=-1)
    return jnp.concatenate([leading_part * cosine[:, None, :] + turned, tensor[..., ROT:]], axis=-1)


def attention(mixed, place, cosine, sine_table, heads):
    sequences, length, _ = mixed.shape
    parts = mixed.reshape(sequences, length, 4, heads, HEAD_DIM)
    queries, keys, values, grads = (parts[:, :, i] for i in range(4))
    scale = 1.0 / math.sqrt(HEAD_DIM)
    scores = jnp.einsum("sqhd,skhd->shqk", queries, keys, preferred_element_type=jnp.float32)
    allowed = place[None, :] <= place[:, None]
    scores = jnp.where(allowed, scores * scale, MASKED)
    peak = jnp.max(scores, axis=-1, keepdims=True)
    log_total = peak + jnp.log(jnp.sum(jnp.exp(scores - peak), axis=-1, keepdims=True))
    probs = jnp.exp(scores - log_total)
    soft = probs.astype(jnp.bfloat16)
    context = jnp.einsum("shqk,skhd->sqhd", soft, values, preferred_element_type=jnp.float32)
    context = context.astype(jnp.bfloat16)
    delta = jnp.einsum(
        "sqhd,sqhd->shq", grads.astype(jnp.float32), context.astype(jnp.float32)
    )
    value_grad = jnp.einsum("shqk,sqhd->skhd", soft, grads, preferred_element_type=jnp.float32)
    probs_grad = jnp.einsum("sqhd,skhd->shqk", grads, values, preferred_element_type=jnp.float32)
    score_grad = (probs * (probs_grad - delta[..., None]) * scale).astype(jnp.bfloat16)
    query_grad = jnp.einsum("shqk,skhd->sqhd", score_grad, keys, preferred_element_type=jnp.float32)
    key_grad = jnp.einsum("shqk,sqhd->skhd", score_grad, queries, preferred_element_type=jnp.float32)
    query_grad = unrotate(query_grad, cosine, sine_table)
    key_grad = unrotate(key_grad, cosine, sine_table)
    back = jnp.stack([query_grad, key_grad, value_grad], axis=2)
    shift = jnp.sum(back, axis=(0, 1)).reshape(-1)
    full = jnp.concatenate([context[:, :, None], back.astype(jnp.bfloat16)], axis=2)
    return (full.reshape(sequences, length, 4 * heads * HEAD_DIM), shift)


def plain_body(
    layer_input,
    out_grad,
    span_order,
    inward,
    inward_bias,
    outward,
    outward_bias,
    expand,
    expand_bias,
    contract,
    contract_bias,
    first_gain,
    first_bias,
    second_gain,
    second_bias,
):
    batch_count, fsdp_count = (lax.axis_size("batch"), lax.axis_size("fsdp"))
    context_count = lax.axis_size("ctx")
    context_index = lax.axis_index("ctx")
    batch_index, fsdp_index = (lax.axis_index("batch"), lax.axis_index("fsdp"))
    plane = batch_count * fsdp_count
    tokens, width = layer_input.shape[1:]
    hidden_units = expand.shape[1]
    head_cols = width // plane
    unit_cols = hidden_units // plane
    heads = head_cols // HEAD_DIM
    length = tokens * context_count
    span_size = tokens // 2
    own_sequences = plane // context_count

    def full_vectors(*vectors):
        sizes = [v.shape[0] for v in vectors]
        gathered = lax.all_gather(jnp.concatenate(vectors), "fsdp")
        out, start = ([], 0)
        for size in sizes:
            out.append(gathered[:, start : start + size].reshape(-1).astype(jnp.float32))
            start += size
        return out

    (
        inward_offset,
        outward_offset,
        expand_offset,
        contract_offset,
        gain_first,
        offset_first,
        gain_second,
        offset_second,
    ) = full_vectors(
        inward_bias,
        outward_bias,
        expand_bias,
        contract_bias,
        first_gain,
        first_bias,
        second_gain,
        second_bias,
    )

    def chunk(array, cols):
        rows = array.shape[0]
        parts = array.reshape(rows, -1, fsdp_count, batch_count, cols)
        mine = lax.dynamic_index_in_dim(parts, batch_index, 3, keepdims=False)
        return mine.transpose(2, 0, 1, 3).reshape(fsdp_count, rows, -1)

    to_send = jnp.concatenate([chunk(inward, head_cols), chunk(expand, unit_cols)], axis=2)
    weights = lax.all_to_all(to_send, "fsdp", 0, 0).reshape(width, -1)
    inward_cols = weights[:, : 3 * head_cols]
    expand_cols = weights[:, 3 * head_cols :]
    outward_rows = lax.dynamic_slice_in_dim(outward, batch_index * head_cols, head_cols, 0)
    contract_rows = lax.dynamic_slice_in_dim(contract, batch_index * unit_cols, unit_cols, 0)
    plane_index = fsdp_index * batch_count + batch_index
    inward_shift_in = lax.dynamic_index_in_dim(
        inward_offset.reshape(3, plane, head_cols), plane_index, 1, keepdims=False
    ).reshape(-1)
    expand_shift_in = lax.dynamic_slice_in_dim(expand_offset, plane_index * unit_cols, unit_cols, 0)

    pair = jnp.stack([layer_input[0], out_grad[0]])
    pair_all = lax.all_gather(pair, PLANE, axis=1, tiled=True)
    grads_all = pair_all[1]
    rows_all = pair_all[0].astype(jnp.float32)
    normed, inverse = normalize(rows_all)
    first_rows = (normed * gain_first + offset_first).astype(jnp.bfloat16)
    second_rows = (normed * gain_second + offset_second).astype(jnp.bfloat16)

    local_place = slot_positions(span_order, context_index * tokens, tokens, span_size)
    cosine, sine_table = rotary_tables(local_place)
    cosine_plane = jnp.tile(cosine, (plane, 1))
    sine_plane = jnp.tile(sine_table, (plane, 1))
    projected = dot(first_rows, inward_cols) + inward_shift_in
    projected = projected.reshape(plane * tokens, 3 * heads, HEAD_DIM)
    turned = rotate(projected[:, : 2 * heads], cosine_plane, sine_plane)
    context_grad = dot(grads_all, outward_rows, ((1,), (1,)))
    mixed = jnp.concatenate(
        [
            turned.reshape(plane * tokens, -1),
            projected[:, 2 * heads :].reshape(plane * tokens, -1),
            context_grad,
        ],
        axis=1,
    ).astype(jnp.bfloat16)
    mixed = mixed.reshape(context_count, own_sequences, tokens, 4 * head_cols)
    mixed = lax.all_to_all(mixed, "ctx", 0, 0)
    mixed = mixed.transpose(1, 0, 2, 3).reshape(own_sequences, length, 4 * head_cols)
    place = slot_positions(span_order, 0, length, span_size)
    cosine_all, sine_all = rotary_tables(place)

    before = dot(second_rows, expand_cols) + expand_shift_in
    tail = 1.0 + lax.erf(before * HALF_ROOT)
    activated = (0.5 * before * tail).astype(jnp.bfloat16)
    slope = 0.5 * tail + before * jnp.exp(-0.5 * before * before) * NORMAL_PEAK
    before_grad = dot(grads_all, contract_rows, ((1,), (1,))) * slope
    expand_sum = jnp.sum(before_grad, axis=0)
    before_rows = before_grad.astype(jnp.bfloat16)
    expand_delta = dot(second_rows, before_rows, ((0,), (0,)))
    contract_delta = dot(activated, grads_all, ((0,), (0,)))
    out_part = dot(activated, contract_rows)
    second_part = dot(before_rows, expand_cols, ((1,), (1,)))

    hidden = layer_input[0].astype(jnp.float32)
    grad_float = out_grad[0].astype(jnp.float32)
    normed_mine, inverse_mine = normalize(hidden)
    half = width // fsdp_count

    def spread(values, sizes):
        wide = jnp.zeros((sizes[0], plane, sizes[1]), jnp.float32)
        values = values.reshape(sizes[0], sizes[1])
        return lax.dynamic_update_index_in_dim(wide, values, plane_index, 1).reshape(-1)

    bias_total = jnp.sum(grad_float, axis=0)
    expand_wide = spread(expand_sum, (1, unit_cols))

    back, inward_sum = attention(mixed, place, cosine_all, sine_all, heads)
    back = back.reshape(own_sequences, context_count, tokens, 4 * head_cols)
    back = lax.all_to_all(back.transpose(1, 0, 2, 3), "ctx", 0, 0)
    back = back.reshape(plane * tokens, 4 * head_cols)
    context_rows = back[:, :head_cols]
    projected_rows = back[:, head_cols:]
    inward_delta = dot(first_rows, projected_rows, ((0,), (0,)))
    outward_delta = dot(context_rows, grads_all, ((0,), (0,)))
    out_part = out_part + dot(context_rows, outward_rows)
    first_part = dot(projected_rows, inward_cols, ((1,), (1,)))
    stacked = jnp.stack([second_part, out_part, first_part], axis=1).astype(jnp.bfloat16)
    mine = lax.psum_scatter(stacked, PLANE, scatter_dimension=0, tiled=True)
    mine = mine.transpose(1, 0, 2).astype(jnp.float32)
    columns = jnp.concatenate([inward_delta, expand_delta], axis=1).astype(jnp.bfloat16)
    rows = jnp.concatenate([outward_delta, contract_delta], axis=0).astype(jnp.bfloat16)
    columns, rows = lax.psum((columns, rows), "ctx")
    columns = lax.all_to_all(columns.reshape(fsdp_count, half, -1), "fsdp", 0, 0)
    columns = lax.all_gather(columns, "batch")
    rows = lax.all_gather(rows, "batch").astype(jnp.float32)
    columns = columns.transpose(2, 1, 0, 3).astype(jnp.float32)
    inward_total = columns[..., : 3 * head_cols].reshape(
        half, fsdp_count, batch_count, 3, head_cols
    )
    totals = (
        inward_total.transpose(0, 3, 1, 2, 4).reshape(half, 3 * width),
        rows[:, :head_cols].reshape(half, width),
        columns[..., 3 * head_cols :].reshape(half, hidden_units),
        rows[:, head_cols:].reshape(-1, width),
    )
    _, second_scale, second_shift = norm_backward(
        mine[0], normed_mine, inverse_mine, gain_second
    )
    _, first_scale, first_shift = norm_backward(mine[2], normed_mine, inverse_mine, gain_first)
    vectors = [
        spread(inward_sum, (3, head_cols)),
        bias_total,
        expand_wide,
        first_scale,
        first_shift,
        second_scale,
        second_shift,
    ]
    whole = lax.psum(jnp.concatenate(vectors), ("batch", "ctx", "fsdp"))

    result = (hidden + (mine[1] + outward_offset) + contract_offset).astype(jnp.bfloat16)
    second_input, _, _ = norm_backward(mine[0], normed_mine, inverse_mine, gain_second)
    first_input, _, _ = norm_backward(mine[2], normed_mine, inverse_mine, gain_first)
    input_delta = grad_float + first_input + second_input
    halves, start = ([], 0)
    for vector in vectors:
        size = vector.shape[0] // fsdp_count
        halves.append(lax.dynamic_slice_in_dim(whole, start + fsdp_index * size, size, 0))
        start += vector.shape[0]
    return (
        result[None],
        input_delta[None],
        totals[0],
        halves[0],
        totals[1],
        halves[1],
        totals[2],
        halves[2],
        totals[3],
        halves[1],
        halves[3],
        halves[4],
        halves[5],
        halves[6],
    )


def body(
    layer_input,
    out_grad,
    span_order,
    inward,
    inward_bias,
    outward,
    outward_bias,
    expand,
    expand_bias,
    contract,
    contract_bias,
    first_gain,
    first_bias,
    second_gain,
    second_bias,
):
    plane = lax.axis_size("batch") * lax.axis_size("fsdp")
    width = layer_input.shape[2]
    if width // plane % 128:
        return plain_body(
            layer_input,
            out_grad,
            span_order,
            inward,
            inward_bias,
            outward,
            outward_bias,
            expand,
            expand_bias,
            contract,
            contract_bias,
            first_gain,
            first_bias,
            second_gain,
            second_bias,
        )
    vectors = (
        inward_bias,
        outward_bias,
        expand_bias,
        contract_bias,
        first_gain,
        first_bias,
        second_gain,
        second_bias,
    )
    ends = [sum(v.shape[0] for v in vectors[: i + 1]) for i in range(len(vectors))]
    room = ends[-1] + -ends[-1] % 1024
    small = sum(
        jnp.pad(v.astype(jnp.float32), (end - v.shape[0], room - end))
        for v, end in zip(vectors, ends)
    ).reshape(-1, 128)
    sums, result, input_delta, shifts = layer(
        layer_input, out_grad, span_order, small, inward, outward, expand, contract
    )
    return widen(sums, result, input_delta, shifts, width // plane, expand.shape[1] // plane)


def solution(mesh):
    rows = P(PLANE, "ctx", None)
    matrix, vector = (P("fsdp", None), P("fsdp"))
    in_specs = (rows, rows, P()) + (matrix, vector) * 4 + (vector,) * 4
    out_specs = (rows, rows) + (matrix, vector) * 4 + (vector,) * 4
    return jax.shard_map(body, mesh=mesh, in_specs=in_specs, out_specs=out_specs, check_vma=False)
```

```python
import functools
import math

import jax
import jax.numpy as jnp
from jax import lax
from jax.experimental import pallas as pl
from jax.experimental.pallas import tpu as pltpu
from jax.sharding import PartitionSpec as P

HEAD_DIM = 64
ROT = 16

EPSILON = 1e-05
ROTARY_BASE = 10000.0
MASKED = -1e30
HALF_ROOT = 0.7071067811865476
NORMAL_PEAK = 0.3989422804014327
PLANE = ("batch", "fsdp")


MESH = pl.DeviceIdType.MESH
CORES = 2
VMEM_LIMIT = 56 * 2**20


def here():
    return (lax.axis_index("batch"), lax.axis_index("ctx"), lax.axis_index("fsdp"))


def swapped(index, step):
    return index + step * (1 - 2 * (index // step % 2))


def greet(partners):
    barrier = pltpu.get_barrier_semaphore()
    for partner in partners:
        pl.semaphore_signal(barrier, inc=1, device_id=partner, device_id_type=MESH)
    pl.semaphore_wait(barrier, len(partners))


def remote(src, dst, send, recv, target):
    return pltpu.make_async_remote_copy(
        src_ref=src,
        dst_ref=dst,
        send_sem=send,
        recv_sem=recv,
        device_id=target,
        device_id_type=MESH,
    )


LAG = 2
LB = 2
LX = 2
LY = 3
AHEAD = 2
ATT = 4
READY = 11


def layer_kernel(
    sizes,
    tokens,
    heads,
    counts,
    piece,
    input_ref,
    grad_ref,
    order_ref,
    small_ref,
    inward_ref,
    outward_ref,
    expand_ref,
    contract_ref,
    sums_ref,
    result_ref,
    input_grad_ref,
    shifts_ref,
    inputs,
    grads,
    small,
    inward,
    outward,
    expand,
    contract,
    cosine,
    sine,
    stats,
    first_rows,
    second_rows,
    work,
    before,
    hidden_back,
    out_rows,
    scaled,
    mixed_out,
    mixed,
    heads_sum,
    back_out,
    back_in,
    inward_sum,
    row_sums,
    part,
    mine,
    reduced,
    reduced_right,
    near,
    across_in,
    far,
    token_sum,
    vector_in,
    vector_sum,
    load_sems,
    small_sems,
    weight_sems,
    pair_sems,
    gather_sems,
    share_sems,
    there_sends,
    there_recvs,
    there_own,
    back_own,
    turn_sems,
    reduce_sends,
    reduce_recvs,
    right_recvs,
    back_sends,
    back_recvs,
    row_sends,
    row_recvs,
    chip_sends,
    chip_recvs,
    core_sems,
    keep_sem,
    near_sems,
    across_sems,
    far_sems,
    vector_sems,
):
    batch_count, context_count, fsdp_count = sizes
    early_other, early, late_other, late = counts
    b, z, y = here()
    chips = batch_count // CORES
    core = b % CORES
    chip = b // CORES
    width = part.shape[1]
    half_width = width // 2
    cols = heads * HEAD_DIM
    unit = contract.shape[0]
    plane = batch_count * fsdp_count
    index = y * batch_count + b
    own_sequences = plane // context_count
    length = tokens * context_count
    steps = early + late
    early_rows = 2 * early * piece
    last = context_count - 1
    lines = width // 128
    f32, half_type = (jnp.float32, part.dtype)
    group_rows = fsdp_count * tokens

    sibling = (chip * CORES + (1 - core), z, y)
    across = (b, z, 1 - y)
    peers = [((chip + d) % chips * CORES + core, z, y) for d in range(1, chips)]
    sources = [(chip + chips - d) % chips * CORES + core for d in range(1, chips)]
    others = [(b, (z + d) % context_count, y) for d in range(1, context_count)]
    stages = []
    step = 1
    while step < batch_count:
        stages.append((swapped(b, step), z, y))
        step *= 2
    stages.append(across)
    step = 1
    while step < context_count:
        stages.append((b, swapped(z, step), y))
        step *= 2

    def sem(sems, *index):
        return (sems.at[(0, *index)], sems.at[(1, *index)])


    plane_arrays = (inputs, grads)
    plane_sources = (input_ref.at[0], grad_ref.at[0])

    def block(array, batch, fsdp):
        row = pl.multiple_of((batch * fsdp_count + fsdp) * tokens, tokens)
        return plane_arrays[array].at[pl.ds(row, tokens), :]

    def own_load(array):
        return pltpu.make_async_copy(
            plane_sources[array], block(array, b, y), load_sems.at[array]
        )

    def to_across(array):
        return remote(
            plane_sources[array], block(array, b, y), *sem(gather_sems, array, 0), across
        )

    def to_peer(array, d):
        return remote(
            plane_sources[array], block(array, b, y), *sem(gather_sems, array, 1 + d), peers[d]
        )

    def on_to_peer(array, d):
        at = block(array, b, 1 - y)
        return remote(at, at, *sem(gather_sems, array, chips + d), peers[d])

    def share(array, i):
        if i == 0:
            return remote(
                plane_sources[array], block(array, b, y), *sem(share_sems, array, 0), sibling
            )
        if i == 1:
            at = block(array, b, 1 - y)
        else:
            d = (i - 2) % (chips - 1)
            at = block(array, sources[d], y if i - 2 < chips - 1 else 1 - y)
        return remote(at, at, *sem(share_sems, array, i), sibling)

    def columns_of(owner, i):
        place = owner * batch_count + b
        if i < 3:
            return pl.ds(pl.multiple_of(i * width + place * cols, cols), cols)
        return pl.ds(pl.multiple_of(place * unit, unit), unit)

    part_rows = half_width // 2
    parity = z % 2
    pair = (b, swapped(z, 1), y)

    def inward_part(owner, parity):
        first = pl.multiple_of(owner * half_width + parity * part_rows, part_rows)
        return inward.at[pl.ds(first, part_rows), :]

    def weight_copies():
        source_rows = pl.ds(pl.multiple_of(parity * part_rows, part_rows), part_rows)
        rows = pl.ds(pl.multiple_of(y * half_width, half_width), half_width)
        out = [
            remote(
                inward_ref.at[source_rows, columns_of(1 - y, i)],
                inward_part(y, parity).at[:, i * cols : (i + 1) * cols],
                *sem(weight_sems, 0),
                across,
            )
            for i in range(3)
        ]
        out.append(
            remote(
                expand_ref.at[:, columns_of(1 - y, 3)],
                expand.at[rows, :],
                *sem(weight_sems, 1),
                across,
            )
        )
        return out

    def weight_own():
        rows = pl.ds(pl.multiple_of(y * half_width, half_width), half_width)
        pairs = [
            (inward_ref.at[:, columns_of(y, i)], inward.at[rows, i * cols : (i + 1) * cols])
            for i in range(3)
        ]
        pairs.append((expand_ref.at[:, columns_of(y, 3)], expand.at[rows, :]))
        return [
            pltpu.make_async_copy(source, target, load_sems.at[2 + i])
            for i, (source, target) in enumerate(pairs)
        ]

    def inward_brought():
        at = inward_part(1 - y, parity)
        return remote(at, at, *sem(weight_sems, 0), across)

    def to_pair(parity):
        at = inward_part(1 - y, parity)
        return remote(at, at, *sem(pair_sems), pair)

    row_loads = [
        pltpu.make_async_copy(
            outward_ref.at[pl.ds(pl.multiple_of(b * cols, cols), cols), :],
            outward,
            load_sems.at[6],
        ),
        pltpu.make_async_copy(
            contract_ref.at[pl.ds(pl.multiple_of(b * unit, unit), unit), :],
            contract,
            load_sems.at[7],
        ),
    ]
    weight_loads = weight_own()
    weight_sends = weight_copies()
    small_copy = remote(small_ref, small.at[1], *sem(small_sems, 0), across)

    own_load(0).start()
    own_load(1).start()
    for load in weight_loads + row_loads:
        load.start()
    greet([sibling, across] + peers + others)
    small_copy.start()

    def offer(array):
        to_across(array).start()
        share(array, 0).start()

    def offer_peers(array):
        for d in range(chips - 1):
            to_peer(array, d).start()

    for send in weight_sends[:3]:
        send.start()
    offer(0)
    offer_peers(0)
    offer(1)
    offer_peers(1)
    weight_sends[3].start()
    small[0] = small_ref[...]


    def positions(shape, dimension):
        slot = lax.broadcasted_iota(jnp.int32, shape, dimension)
        owner = slot // tokens
        leading = jnp.zeros(shape, jnp.int32)
        for c in range(context_count):
            leading = jnp.where(owner == c, order_ref[c], leading)
        span = tokens // 2
        second = slot // span % 2
        picked = jnp.where(second == 0, leading, 2 * context_count - 1 - leading)
        return picked * span + slot % span

    half_rot = ROT // 2
    lane = lax.broadcasted_iota(jnp.int32, (1, cols), 1) % HEAD_DIM
    angular = jnp.exp((lane % half_rot).astype(f32) * (-2.0 * math.log(ROTARY_BASE) / ROT))
    angles = positions((length, cols), 0).astype(f32) * angular
    cosine[...] = jnp.where(lane < ROT, jnp.cos(angles), 1.0)
    sine[...] = jnp.where(lane < ROT, jnp.sin(angles), 0.0)
    low = (lane < half_rot).astype(f32)
    high = 1.0 - low

    def turn(value, rows, sign):
        weight = sine[rows, :] * sign
        return (
            value * cosine[rows, :]
            - pltpu.roll(value, cols - half_rot, 1) * (weight * low)
            + pltpu.roll(value, half_rot, 1) * (weight * high)
        )


    small_copy.wait_recv()
    vector_rows = [3 * lines, lines, unit * plane // 128] + [lines] * 5
    starts = [sum(vector_rows[:i]) // fsdp_count for i in range(8)]

    def vector_line(which, line):
        share_lines = vector_rows[which] // fsdp_count
        owner = line // share_lines
        at = (owner - y) * (owner - y)
        return small[at, pl.ds(starts[which] + line % share_lines, 1), :]

    def whole(which):
        return jnp.concatenate([vector_line(which, line) for line in range(lines)], axis=1)

    def chunk(which, first, count):
        return jnp.concatenate([vector_line(which, first + i) for i in range(count)], axis=1)


    def group(u):
        return (chip + u // CORES) % chips * CORES + (core + u % CORES) % CORES

    def rows_of(u):
        return pl.ds(pl.multiple_of(group(u) * group_rows, group_rows), group_rows)

    def bring(array, u):
        distance, other = (u // CORES, u % CORES)
        if other == 0 and distance == 0:
            own_load(array).wait()
            if array == 0:
                to_across(array).wait_recv()
            for d in range(chips - 1):
                on_to_peer(array, d).start()
            share(array, 1).start()
        elif other == 0:
            d = chips - distance - 1
            to_peer(array, d).wait_recv()
            share(array, 2 + d).start()
            on_to_peer(array, d).wait_recv()
            share(array, 1 + chips + d).start()
        elif distance == 0:
            share(array, 0).wait_recv()
            share(array, 1).wait_recv()
        else:
            d = chips - distance - 1
            share(array, 2 + d).wait_recv()
            share(array, 1 + chips + d).wait_recv()

    gains = [whole(4), whole(5), whole(6), whole(7)]
    inward_bias = jnp.concatenate(
        [
            chunk(0, i * lines + index * (cols // 128), cols // 128)
            for i in range(3)
        ],
        axis=1,
    )

    def norm(u):
        rows = rows_of(u)
        x = inputs[rows, :].astype(f32)
        mean = jnp.mean(x, axis=-1, keepdims=True)
        center = x - mean
        inverse = lax.rsqrt(jnp.mean(center * center, axis=-1, keepdims=True) + EPSILON)
        stats[rows, 0:1] = mean
        stats[rows, 1:2] = inverse
        normed = center * inverse
        first_rows[rows, :] = (normed * gains[0] + gains[1]).astype(half_type)
        second_rows[rows, :] = (normed * gains[2] + gains[3]).astype(half_type)

    there_columns = ((0, 3 * cols), (3 * cols, cols))

    def there_copy(u, f, kind):
        p = group(u) * fsdp_count + f
        owner, s = (p // own_sequences, p % own_sequences)
        first, count = there_columns[kind]
        columns = pl.ds(first, count)
        source = mixed_out.at[pl.ds(pl.multiple_of(p * tokens, tokens), tokens), columns]
        at = pl.ds(pl.multiple_of(z * tokens, tokens), tokens)
        target = mixed.at[s, at, columns]

        @pl.when(owner == z)
        def _():
            pltpu.make_async_copy(source, target, there_own.at[s, kind]).start()

        @pl.when(owner != z)
        def _():
            remote(
                source, target, there_sends.at[kind], there_recvs.at[s, z, kind], (b, owner, y)
            ).start()

    def project(u):
        projected = dot(first_rows[rows_of(u), :], inward[...]) + inward_bias
        local = pl.ds(pl.multiple_of(z * tokens, tokens), tokens)
        for f in range(fsdp_count):
            at = pl.ds(pl.multiple_of((group(u) * fsdp_count + f) * tokens, tokens), tokens)
            piece_rows = projected[f * tokens : (f + 1) * tokens, :]
            for i in range(3):
                value = piece_rows[:, i * cols : (i + 1) * cols]
                if i < 2:
                    value = turn(value, local, 1.0)
                mixed_out[at, i * cols : (i + 1) * cols] = value.astype(half_type)
            there_copy(u, f, 0)

    def upstream(u):
        rows = rows_of(u)
        value = dot(grads[rows, :], outward[...], ((1,), (1,)))
        mixed_out[rows, 3 * cols :] = value.astype(half_type)
        for f in range(fsdp_count):
            there_copy(u, f, 1)

    def there(s):
        for kind, (first, count) in enumerate(there_columns):
            columns = pl.ds(first, count)
            block_at = mixed.at[s, pl.ds(0, tokens), columns]
            pltpu.make_async_copy(block_at, block_at, there_own.at[s, kind]).wait()
            for d in range(1, context_count):
                source = (z + d) % context_count
                at = mixed.at[s, pl.ds(pl.multiple_of(source * tokens, tokens), tokens), columns]
                recv = there_recvs.at[s, source, kind]
                remote(at, at, there_sends.at[kind], recv, others[0]).wait_recv()

    order = [u for u in range(0, batch_count, CORES)] + [u for u in range(1, batch_count, CORES)]
    bring(0, 0)
    inward_brought().wait_recv()
    to_pair(parity).start()
    norm(0)
    for i in range(3):
        weight_loads[i].wait()
    to_pair(1 - parity).wait_recv()
    project(0)
    to_across(1).wait_recv()
    for u in order[1:chips]:
        bring(0, u)
    bring(1, 0)
    row_loads[0].wait()
    for u in order[1:]:
        if u % CORES:
            bring(0, u)
        norm(u)
        project(u)
    upstream(0)
    for u in order[1:]:
        bring(1, u)
        upstream(u)


    row_loads[1].wait()
    weight_loads[3].wait()
    expand_bias = chunk(2, index * (unit // 128), unit // 128)
    nothing = jnp.zeros((1, width), f32)

    def normed_rows(rows):
        return (inputs[rows, :].astype(f32) - stats[rows, 0:1]) * stats[rows, 1:2]

    own_half = pl.ds(pl.multiple_of(y * half_width, half_width), half_width)
    other_half = pl.ds(pl.multiple_of((1 - y) * half_width, half_width), half_width)

    def early_tile(i, carry):
        rows = pl.ds(pl.multiple_of(i * group_rows, group_rows), group_rows)
        before[rows, :] = dot(second_rows[rows, own_half], expand[own_half, :]) + expand_bias
        hidden_back[rows, :] = dot(grads[rows, :], contract[...], ((1,), (1,)))
        return carry

    lax.fori_loop(0, batch_count, early_tile, 0)
    weight_sends[3].wait_recv()

    def forward_tile(i, expand_total):
        rows = pl.ds(pl.multiple_of(i * group_rows, group_rows), group_rows)
        value = before[rows, :] + dot(second_rows[rows, other_half], expand[other_half, :])
        tail = 1.0 + lax.erf(value * HALF_ROOT)
        slope = 0.5 * tail + value * jnp.exp(-0.5 * value * value) * NORMAL_PEAK
        before_grad = hidden_back[rows, :] * slope
        work[rows, :unit] = (0.5 * value * tail).astype(half_type)
        work[rows, unit:] = before_grad.astype(half_type)
        return expand_total + jnp.sum(before_grad, axis=0, keepdims=True)

    expand_total = lax.fori_loop(0, batch_count, forward_tile, jnp.zeros((1, unit), f32))
    row_sums[...] = jnp.zeros(row_sums.shape, f32)

    def hidden_tile(i):
        rows = pl.ds(pl.multiple_of(i * group_rows, group_rows), group_rows)
        out_rows[rows, :] = dot(work[rows, :unit], contract[...]).astype(half_type)
        value = dot(work[rows, unit:], expand[...], ((1,), (1,)))
        scaled[rows, :] = (value * gains[2]).astype(half_type)
        row_sums[0:1, :] += jnp.sum(value * normed_rows(rows), axis=0, keepdims=True)
        row_sums[1:2, :] += jnp.sum(value, axis=0, keepdims=True)

    def expand_half(s):
        owner = (1 - y) * (1 - s) + y * s
        column = pl.multiple_of(owner * half_width, half_width)
        delta = dot(second_rows[:, pl.ds(column, half_width)], work[:, unit:], ((0,), (0,)))
        group = unit * half_width // width
        at = pl.ds(pl.multiple_of(s * group, group), group)
        for j in range(width // unit):
            part[at, j * unit : (j + 1) * unit] = delta[j * group : (j + 1) * group, :].astype(
                half_type
            )

    def contract_rows():
        part[early_rows - unit : early_rows, :] = dot(
            work[:, :unit], grads[...], ((0,), (0,))
        ).astype(half_type)

    expand_half(0)


    def place(half, k):
        is_late = jnp.minimum(k // early, 1)
        other = early_other * (1 - is_late) + late_other * is_late
        count = early * (1 - is_late) + late * is_late
        j = k - early * is_late
        is_own = jnp.minimum(j // other, 1)
        row = (half * other + j) * (1 - is_own) + (
            2 * other + half * (count - other) + j - other
        ) * is_own
        return pl.multiple_of((2 * early * is_late + row) * piece, piece)

    def other_index(k):
        return k - (early - early_other) * jnp.minimum(k // early, 1)

    def own(k):
        is_late = jnp.minimum(k // early, 1)
        other = early_other * (1 - is_late) + late_other * is_late
        return jnp.minimum((k - early * is_late) // other, 1)

    def rows_at(ref, row):
        return ref.at[pl.ds(row, piece), :]

    def sums_at(batch, row):
        return sums_ref.at[batch, pl.ds(row, piece), :]

    def back_copy(half, k, side, target):
        at = rows_at(mine, place(half, k))
        return remote(at, at, back_sends.at[side, half], back_recvs.at[half, k], target)

    def row_copy(half, k):
        row = place(half, k)
        recv = row_recvs.at[half, other_index(k)]
        return remote(rows_at(mine, row), sums_at(b, row), row_sends, recv, across)

    def keep_copy(half, k):
        row = place(half, k)
        return pltpu.make_async_copy(rows_at(mine, row), sums_at(b, row), keep_sem)

    def chip_copy(d, half, k, from_mine):
        row = place(half, k)
        source = rows_at(mine, row) if from_mine else sums_at(b, row)
        return remote(
            source, sums_at(b, row), chip_sends.at[d], chip_recvs.at[d, half, k], peers[d]
        )

    def core_copy(half, k, from_mine, batch):
        row = place(half, k)
        source = rows_at(mine, row) if from_mine else sums_at(batch, row)
        return remote(
            source, sums_at(batch, row), core_sems.at[0], core_sems.at[1], sibling
        )

    def spread(half, k, from_mine):
        for d in range(chips - 1):
            chip_copy(d, half, k, from_mine).start()
        core_copy(half, k, from_mine, b).start()

    def arrived(half, k):
        for d in range(chips - 1):
            chip_copy(d, half, k, False).wait_recv()
            core_copy(half, k, False, sources[d]).start()

    def finish(half, k):
        @pl.when(own(k) == 0)
        def _():
            row_copy(half, k).start()

        @pl.when(own(k) == 1)
        def _():
            keep_copy(half, k).start()
            spread(half, k, True)

    left = (b, (z + last) % context_count, y)
    right = (b, (z + 1) % context_count, y)

    def reduce_copy(half, k, source, stream, target):
        row = place(half, k)
        if stream:
            landing = reduced_right.at[pl.ds(pl.multiple_of(k * piece, piece), piece), :]
            recv = right_recvs.at[k]
        else:
            landing = rows_at(reduced, row)
            recv = reduce_recvs.at[half, k]
        return remote(rows_at(source, row), landing, reduce_sends.at[half], recv, target)

    def ends(half):
        root = last // 2 if half == 0 else context_count // 2
        depth = max(root, last - root)
        at_root = z == root
        is_left = z < root
        distance = jnp.where(is_left, root - z, z - root)
        leaf = (z == 0) | (z == last)
        return root, depth, at_root, is_left, distance, leaf

    def pass_on(half, k, source):
        root = last // 2 if half == 0 else context_count // 2

        @pl.when(z == root + 1)
        def _():
            reduce_copy(half, k, source, 1, left).start()

        @pl.when(z > root + 1)
        def _():
            reduce_copy(half, k, source, 0, left).start()

        @pl.when(z < root)
        def _():
            reduce_copy(half, k, source, 0, right).start()

    def leaf_send(half, k):
        pass_on(half, k, part)

    def reduce_step(t, half):
        root, depth, at_root, is_left, distance, leaf = ends(half)
        k = t - LAG * (depth - distance)

        def send(source):
            pass_on(half, k, source)

        k_leaf = t + AHEAD

        @pl.when(leaf & jnp.logical_not(at_root) & (k_leaf < steps))
        def _():
            leaf_send(half, k_leaf)

        @pl.when(jnp.logical_not(leaf) & (k >= 0) & (k < steps))
        def _():
            row = place(half, k)
            here_at = pl.ds(row, piece)

            @pl.when(at_root)
            def _():
                value = part[here_at, :].astype(f32)
                if root > 0:
                    reduce_copy(half, k, part, 0, right).wait_recv()
                    value = value + reduced[here_at, :].astype(f32)
                if root < last:
                    reduce_copy(half, k, part, 1, left).wait_recv()
                    came = reduced_right[pl.ds(pl.multiple_of(k * piece, piece), piece), :]
                    value = value + came.astype(f32)
                mine[here_at, :] = value.astype(half_type)
                if root > 0:
                    back_copy(half, k, 0, left).start()
                if root < last:
                    back_copy(half, k, 1, right).start()
                finish(half, k)

            @pl.when(jnp.logical_not(at_root))
            def _():
                reduce_copy(half, k, part, 0, right).wait_recv()
                value = part[here_at, :].astype(f32) + reduced[here_at, :].astype(f32)
                reduced[here_at, :] = value.astype(half_type)
                send(reduced)

    def back_step(t, half):
        root, depth, at_root, is_left, distance, leaf = ends(half)
        k_back = t - LAG * depth - LB * distance

        @pl.when(jnp.logical_not(at_root) & (k_back >= 0) & (k_back < steps))
        def _():
            back_copy(half, k_back, 0, left).wait_recv()

            @pl.when(is_left & (z > 0))
            def _():
                back_copy(half, k_back, 0, left).start()

            @pl.when((z > root) & (z < last))
            def _():
                back_copy(half, k_back, 1, right).start()

            finish(half, k_back)

    def side_step(t, half):
        root, depth, at_root, is_left, distance, leaf = ends(half)
        k_row = t - LAG * depth - LB * distance - LX

        @pl.when((k_row >= 0) & (k_row < steps))
        def _():
            @pl.when(own(k_row) == 0)
            def _():
                row_copy(half, k_row).wait_recv()
                spread(half, k_row, False)

            @pl.when(own(k_row) == 1)
            def _():
                arrived(half, k_row)

        k_chip = k_row - LY

        @pl.when((k_chip >= 0) & (k_chip < steps))
        def _():
            @pl.when(own(k_chip) == 0)
            def _():
                arrived(half, k_chip)

    def drain():
        half_rows = pl.ds(0, steps * piece)
        other_count = 2 * (early_other + late_other) * piece

        def sent(ref, semaphore):
            remote(ref, ref, semaphore, core_sems.at[1], sibling).wait_send()

        everything = sums_ref.at[pl.ds(0, chips)]
        from_sibling = remote(everything, everything, core_sems.at[0], core_sems.at[1], sibling)
        from_sibling.wait_send()
        for d in range(chips - 1):
            sent(mine, chip_sends.at[d])
        sent(mine.at[pl.ds(0, other_count), :], row_sends)
        kept = mine.at[pl.ds(0, mine.shape[0] - other_count), :]
        pltpu.make_async_copy(kept, kept, keep_sem).wait()
        for half in range(2):
            root = last // 2 if half == 0 else context_count // 2

            @pl.when(z != root)
            def _():
                sent(mine.at[half_rows, :], reduce_sends.at[half])

            @pl.when((z <= root) & (z > 0))
            def _():
                sent(mine.at[half_rows, :], back_sends.at[0, half])

            @pl.when((z >= root) & (z < last))
            def _():
                sent(mine.at[half_rows, :], back_sends.at[1, half])

        from_sibling.wait_recv()


    def attend(n):
        s, h = (n // heads, n % heads)
        columns = [mixed[s, :, i * cols : (i + 1) * cols] for i in range(4)]
        head = lax.broadcasted_iota(jnp.int32, (length, cols), 1) // HEAD_DIM
        picked = head == h
        blank = jnp.zeros((length, cols), half_type)
        _, keys, values, _ = columns
        queries_h, keys_h, values_h, upstream_h = [
            jnp.where(picked, column, blank) for column in columns
        ]
        scale = 1.0 / math.sqrt(HEAD_DIM)
        allowed = positions((1, length), 1) <= positions((length, 1), 0)
        scores = dot(queries_h, keys, ((1,), (1,))) * scale
        scores = jnp.where(allowed, scores, MASKED)
        peak = jnp.max(scores, axis=1, keepdims=True)
        log_total = peak + jnp.log(jnp.sum(jnp.exp(scores - peak), axis=1, keepdims=True))
        probs = jnp.exp(scores - log_total)
        soft = probs.astype(half_type)
        context = dot(soft, values_h)
        delta = jnp.sum(
            upstream_h.astype(f32) * context.astype(half_type).astype(f32), axis=1, keepdims=True
        )
        probs_grad = dot(upstream_h, values, ((1,), (1,)))
        score_grad = (probs * (probs_grad - delta) * scale).astype(half_type)
        results = (
            context,
            dot(score_grad, keys_h),
            dot(score_grad, queries_h, ((0,), (0,))),
            dot(soft, upstream_h, ((0,), (0,))),
        )
        for i, value in enumerate(results):

            @pl.when(h == 0)
            def _():
                heads_sum[i] = value

            @pl.when(h > 0)
            def _():
                heads_sum[i] += value

        @pl.when(h == heads - 1)
        def _():
            back_out[s, :, :cols] = heads_sum[0].astype(half_type)
            for i in range(1, 4):
                value = heads_sum[i]
                if i < 3:
                    value = turn(value, slice(None), -1.0)
                back_out[s, :, i * cols : (i + 1) * cols] = value.astype(half_type)
                total = jnp.sum(value, axis=0, keepdims=True)

                @pl.when(s == 0)
                def _():
                    inward_sum[i - 1 : i, :] = total

                @pl.when(s > 0)
                def _():
                    inward_sum[i - 1 : i, :] += total

            for d in range(context_count):
                turn_copy(s, d).start()

    def turn_copy(s, d):
        target = (z + d) % context_count
        source = back_out.at[s, pl.ds(pl.multiple_of(target * tokens, tokens), tokens), :]
        row = pl.multiple_of((z * own_sequences + s) * tokens, tokens)
        destination = back_in.at[pl.ds(row, tokens), :]
        if d == 0:
            return pltpu.make_async_copy(source, destination, back_own.at[s])
        return remote(source, destination, *sem(turn_sems, s, d - 1), others[d - 1])

    def turned():
        for s in range(own_sequences):
            turn_copy(s, 0).wait()
            for d in range(1, context_count):
                turn_copy(s, d).wait_recv()


    def head_gradients():
        delta = dot(back_in[:, :cols], grads[...], ((0,), (0,))).astype(half_type)
        part[early_rows + 4 * late_other * piece :, :] = delta
        group = cols * half_width // width

        def half_rows(s, carry):
            owner = (1 - y) * (1 - s) + y * s
            column = pl.multiple_of(owner * half_width, half_width)
            delta = dot(
                first_rows[:, pl.ds(column, half_width)], back_in[:, cols:], ((0,), (0,))
            ).astype(half_type)
            top = pl.multiple_of(early_rows + s * 3 * group, group)
            for i in range(3):
                for j in range(width // cols):
                    part[pl.ds(top + i * group, group), j * cols : (j + 1) * cols] = delta[
                        j * group : (j + 1) * group, i * cols : (i + 1) * cols
                    ]
            return carry

        lax.fori_loop(0, 2, half_rows, 0)

    def output_rows():
        def step(i, carry):
            rows = pl.ds(pl.multiple_of(i * group_rows, group_rows), group_rows)
            value = dot(back_in[rows, :cols], outward[...])
            out_rows[rows, :] = (out_rows[rows, :].astype(f32) + value).astype(half_type)
            return carry

        lax.fori_loop(0, batch_count, step, 0)

    vector_start = len(stages)

    def first_back_rows():
        def step(i, carry):
            rows = pl.ds(pl.multiple_of(i * group_rows, group_rows), group_rows)
            value = dot(back_in[rows, cols:], inward[...], ((1,), (1,)))
            scaled[rows, :] = (scaled[rows, :].astype(f32) + value * gains[0]).astype(half_type)
            row_sums[2:3, :] += jnp.sum(value * normed_rows(rows), axis=0, keepdims=True)
            row_sums[3:4, :] += jnp.sum(value, axis=0, keepdims=True)
            return carry

        lax.fori_loop(0, batch_count, step, 0)
        out = vector_sum.at[vector_start]
        out[...] = jnp.zeros(out.shape, f32)

        def put(line, value):
            for j in range(value.shape[1] // 128):
                out[pl.ds(line + j, 1), :] = value[:, j * 128 : (j + 1) * 128]

        for i in range(3):
            put(i * lines + index * (cols // 128), inward_sum[i : i + 1, :])
        first = 3 * lines
        own_rows = pl.ds(pl.multiple_of((b * fsdp_count + y) * tokens, tokens), tokens)
        put(first, jnp.sum(grads[own_rows, :].astype(f32), axis=0, keepdims=True))
        first += lines
        put(first + index * (unit // 128), expand_total)
        first += unit * plane // 128
        for i in range(4):
            put(first, row_sums[i : i + 1, :])
            first += lines

    def vector_copy(i):
        source = vector_sum.at[vector_start if i == 0 else i - 1]
        return remote(source, vector_in.at[i], *sem(vector_sems, i), stages[i])


    arrays = (out_rows, scaled)

    def near_copy(a, c):
        row = pl.multiple_of((c * CORES + 1 - core) * group_rows, group_rows)
        return remote(
            arrays[a].at[pl.ds(row, group_rows), :],
            near.at[a, pl.ds(c * group_rows, group_rows), :],
            *sem(near_sems, a, c),
            sibling,
        )

    def across_copy(a, c):
        row = pl.multiple_of(c * group_rows + (1 - y) * tokens, tokens)
        return remote(
            near.at[a, pl.ds(row, tokens), :],
            across_in.at[a, pl.ds(c * tokens, tokens), :],
            *sem(across_sems, a, c),
            across,
        )

    def far_copy(a, d):
        row = pl.multiple_of((chip + d + 1) % chips * tokens, tokens)
        return remote(
            across_in.at[a, pl.ds(row, tokens), :], far.at[a, d], *sem(far_sems, a, d), peers[d]
        )

    def scatter_first(a):
        for c in range(chips):
            near_copy(a, c).start()

    def scatter_second(a):
        for c in range(chips):
            near_copy(a, c).wait_recv()

            def step(i, carry):
                row = pl.multiple_of((c * CORES + core) * group_rows + i * tokens, tokens)
                value = arrays[a][pl.ds(row, tokens), :].astype(f32)
                at = pl.ds(pl.multiple_of(c * group_rows + i * tokens, tokens), tokens)
                near[a, at, :] = (value + near[a, at, :].astype(f32)).astype(half_type)
                return carry

            lax.fori_loop(0, fsdp_count, step, 0)
            across_copy(a, c).start()

    def scatter_third(a):
        for c in range(chips):
            across_copy(a, c).wait_recv()

        def both(c):
            row = pl.multiple_of(c * group_rows + y * tokens, tokens)
            at = pl.ds(pl.multiple_of(c * tokens, tokens), tokens)
            return (
                near[a, pl.ds(row, tokens), :].astype(f32) + across_in[a, at, :].astype(f32),
                at,
            )

        for d in range(chips - 1):
            value, at = both((chip + d + 1) % chips)
            across_in[a, at, :] = value.astype(half_type)
            far_copy(a, d).start()
        token_sum[a] = both(chip)[0]

    def scatter_last(a):
        value = token_sum[a]
        for d in range(chips - 1):
            far_copy(a, d).wait_recv()
            value = value + far[a, d].astype(f32)
        own_rows = pl.ds(pl.multiple_of((b * fsdp_count + y) * tokens, tokens), tokens)
        x = inputs[own_rows, :].astype(f32)
        if a == 0:
            result_ref[...] = (x + (value + whole(1)) + whole(3)).astype(half_type)
            return
        normed = normed_rows(own_rows)
        middle = jnp.mean(value, axis=-1, keepdims=True)
        coupled = jnp.mean(value * normed, axis=-1, keepdims=True)
        back = stats[own_rows, 1:2] * (value - middle - normed * coupled)
        input_grad_ref[...] = grads[own_rows, :].astype(f32) + back


    problems = own_sequences * heads
    ready = READY
    if ready < ATT + problems or early <= ready + AHEAD:
        raise ValueError("schedule")
    plan = {}

    def at(slot, work):
        plan.setdefault(slot, []).append(work)

    def scatter(a, slot):
        at(slot, lambda: scatter_first(a))
        at(slot + 3, lambda: scatter_second(a))
        at(slot + 6, lambda: scatter_third(a))
        at(slot + 9, lambda: scatter_last(a))

    at(0, lambda: expand_half(1))
    at(1, contract_rows)
    for s in range(own_sequences):
        at(ATT + s * heads, lambda s=s: there(s))
    for i in range(batch_count):
        at(min(ATT + problems + i, ready), lambda i=i: hidden_tile(i))
    at(ready, turned)
    at(ready, head_gradients)
    at(ready + 1, output_rows)
    scatter(0, ready + 1)
    at(ready + 2, first_back_rows)
    scatter(1, ready + 2)
    at(ready + 2, lambda: vector_copy(0).start())
    for i in range(len(stages)):

        def vector_step(i=i):
            vector_copy(i).wait_recv()
            before = vector_sum[vector_start if i == 0 else i - 1]
            vector_sum[i] = before + vector_in[i]
            if i + 1 < len(stages):
                vector_copy(i + 1).start()

        at(ready + 4 + 2 * i, vector_step)

    def slot_step(t, carry):
        for work in (reduce_step, back_step, side_step):
            for half in range(2):
                work(t, half)

        for slot, works in sorted(plan.items()):

            @pl.when(t == slot)
            def _():
                for work in works:
                    work()

        @pl.when((t >= ATT) & (t < ATT + problems))
        def _():
            attend(t - ATT)

        return carry

    for half in range(2):

        @pl.when((z == 0) | (z == last))
        def _():
            for k in range(AHEAD):
                leaf_send(half, k)

    depth = context_count // 2
    tail = (LAG + LB) * depth + LX
    slots = max(steps + tail, early + late_other + tail + LY, max(plan) + 1)
    lax.fori_loop(0, slots, slot_step, 0)
    first = 0
    out_first = 0
    for count in (3 * lines, lines, unit * plane // 128, lines, lines, lines, lines):
        share_lines = count // fsdp_count
        for j in range(share_lines):
            line = first + y * share_lines + j
            shifts_ref[out_first + j : out_first + j + 1, :] = vector_sum[
                len(stages) - 1, pl.ds(line, 1), :
            ]
        first += count
        out_first += share_lines

    drain()
    small_copy.wait_send()
    inward_brought().wait_send()
    to_pair(parity).wait_send()
    weight_sends[3].wait_send()
    for array in range(2):
        to_across(array).wait_send()
        for d in range(chips - 1):
            to_peer(array, d).wait_send()
            on_to_peer(array, d).wait_send()
        for i in range(2 * chips):
            share(array, i).wait_send()
    away = (plane - own_sequences) * tokens
    for kind, (first, count) in enumerate(there_columns):
        at = mixed_out.at[pl.ds(0, away), pl.ds(first, count)]
        remote(at, at, there_sends.at[kind], there_recvs.at[0, 0, kind], others[0]).wait_send()
    for i in range(len(stages)):
        vector_copy(i).wait_send()
    for s in range(own_sequences):
        for d in range(1, context_count):
            turn_copy(s, d).wait_send()
    for a in range(2):
        for c in range(chips):
            near_copy(a, c).wait_send()
            across_copy(a, c).wait_send()
        for d in range(chips - 1):
            far_copy(a, d).wait_send()


def layer(layer_input, out_grad, span_order, small, inward, outward, expand, contract):
    sizes = tuple(lax.axis_size(name) for name in ("batch", "ctx", "fsdp"))
    batch_count, context_count, fsdp_count = sizes
    plane = batch_count * fsdp_count
    chips = batch_count // CORES
    tokens, width = layer_input.shape[1:]
    hidden = expand.shape[1]
    cols = width // plane
    heads = cols // HEAD_DIM
    length = tokens * context_count
    own_sequences = plane // context_count
    half = width // 2
    unit = hidden // plane
    early_other, early = (unit * half // width, 2 * unit * half // width + unit)
    late_other, late = (3 * cols * half // width, 6 * cols * half // width + cols)
    piece = 32
    for rows in (early_other, early - early_other, late_other, late - late_other):
        piece = math.gcd(piece, rows // 2)
    counts = tuple(n // 2 // piece for n in (early_other, early, late_other, late))
    steps = counts[1] + counts[3]
    rows = early + late
    stage_count = (plane * context_count).bit_length() - 1
    all_tokens = plane * tokens
    vector_lines = (8 * width + hidden) // 128
    dma = pltpu.SemaphoreType.DMA
    f32, half_type = (jnp.float32, layer_input.dtype)
    vmem = pl.BlockSpec(memory_space=pltpu.VMEM)
    hbm = pl.BlockSpec(memory_space=pl.ANY)

    def held(*shape, dtype=half_type):
        return pltpu.VMEM(shape, dtype)

    return pl.pallas_call(
        functools.partial(layer_kernel, sizes, tokens, heads, counts, piece),
        out_shape=(
            jax.ShapeDtypeStruct((batch_count, rows, width), half_type),
            jax.ShapeDtypeStruct((tokens, width), half_type),
            jax.ShapeDtypeStruct((tokens, width), f32),
            jax.ShapeDtypeStruct((vector_lines // fsdp_count, 128), f32),
        ),
        in_specs=[hbm, hbm, pl.BlockSpec(memory_space=pltpu.SMEM), vmem] + [hbm] * 4,
        out_specs=(hbm, vmem, vmem, vmem),
        scratch_shapes=[
            held(all_tokens, width),
            held(all_tokens, width),
            held(2, *small.shape, dtype=f32),
            held(width, 3 * cols),
            held(cols, width),
            held(width, unit),
            held(unit, width),
            held(length, cols, dtype=f32),
            held(length, cols, dtype=f32),
            held(all_tokens, 2, dtype=f32),
            held(all_tokens, width),
            held(all_tokens, width),
            held(all_tokens, 2 * unit),
            held(all_tokens, unit, dtype=f32),
            held(all_tokens, unit, dtype=f32),
            held(all_tokens, width),
            held(all_tokens, width),
            held(all_tokens, 4 * cols),
            held(own_sequences, length, 4 * cols),
            held(4, length, cols, dtype=f32),
            held(own_sequences, length, 4 * cols),
            held(all_tokens, 4 * cols),
            held(8, cols, dtype=f32),
            held(8, width, dtype=f32),
            held(rows, width),
            held(rows, width),
            held(rows, width),
            held(rows // 2, width),
            held(2, chips * fsdp_count * tokens, width),
            held(2, chips * tokens, width),
            held(2, chips - 1, tokens, width),
            held(2, tokens, width, dtype=f32),
            held(stage_count, vector_lines, 128, dtype=f32),
            held(stage_count + 1, vector_lines, 128, dtype=f32),
            dma((8,)),
            dma((2, 1)),
            dma((2, 2)),
            dma((2,)),
            dma((2, 2, 2 * chips - 1)),
            dma((2, 2, 2 * chips)),
            dma((2,)),
            dma((own_sequences, context_count, 2)),
            dma((own_sequences, 2)),
            dma((own_sequences,)),
            dma((2, own_sequences, context_count - 1)),
            dma((2,)),
            dma((2, steps)),
            dma((steps,)),
            dma((2, 2)),
            dma((2, steps)),
            dma,
            dma((2, counts[0] + counts[2])),
            dma((chips - 1,)),
            dma((chips - 1, 2, steps)),
            dma((2,)),
            dma,
            dma((2, 2, chips)),
            dma((2, 2, chips)),
            dma((2, 2, chips - 1)),
            dma((2, stage_count)),
        ],
        name="layer",
        compiler_params=pltpu.CompilerParams(
            collective_id=0, has_side_effects=True, vmem_limit_bytes=VMEM_LIMIT
        ),
    )(layer_input, out_grad, span_order, small, inward, outward, expand, contract)


def widen_kernel(
    cols,
    unit,
    turn_ref,
    all_ref,
    result_in,
    input_in,
    shifts_in,
    result_ref,
    input_ref,
    inward_ref,
    inward_shift,
    outward_ref,
    outward_shift,
    expand_ref,
    expand_shift,
    contract_ref,
    contract_shift,
    first_scale,
    first_shift,
    second_scale,
    second_shift,
    held,
    inward,
    outward,
    expand,
    contract,
    in_sems,
    out_sems,
    outward_sems,
    wide_sems,
):
    batch_count, rows, width = all_ref.shape
    half = inward_ref.shape[0]
    unit_rows, unit_blocks = (unit * half // width, width // unit)
    head_rows, head_blocks = (cols * half // width, width // cols)
    late = 2 * unit_rows + unit
    bounds = ((late, rows - late), (0, unit_rows), (unit_rows, unit_rows), (late - unit, unit))
    y = turn_ref[0]

    def load(b, part):
        first, count = bounds[part]
        at = pl.ds(first, count)
        return pltpu.make_async_copy(
            all_ref.at[b, at, :], held.at[b, at, :], in_sems.at[b, part]
        )

    def stores(b, part):
        at = b % 2
        pairs = []
        if part == 0:
            pairs.append((outward.at[b], outward_ref.at[pl.ds(b * cols, cols), :]))
        elif part < 3:
            owner = y if part == 2 else 1 - y
            column = pl.multiple_of((owner * batch_count + b) * unit, unit)
            pairs.append((expand.at[at, part - 1], expand_ref.at[:, pl.ds(column, unit)]))
        else:
            pairs.append((contract.at[at], contract_ref.at[pl.ds(b * unit, unit), :]))
        return [
            pltpu.make_async_copy(
                source, target, outward_sems.at[b] if part == 0 else out_sems.at[at, part - 1]
            )
            for source, target in pairs
        ]

    def wide_stores():
        group = batch_count * cols
        out = []
        for s in range(2):
            owner = y if s else 1 - y
            for i in range(3):
                column = pl.multiple_of(i * width + owner * group, group)
                out.append(
                    pltpu.make_async_copy(
                        inward.at[s, i],
                        inward_ref.at[:, pl.ds(column, group)],
                        wide_sems.at[s, i],
                    )
                )
        return out

    for b in range(batch_count):
        load(b, 0).start()
    for b in range(batch_count):
        for part in range(1, 4):
            load(b, part).start()
    result_ref[0] = result_in[...]
    input_ref[0] = input_in[...]
    line = 0
    for target in (
        inward_shift,
        outward_shift,
        expand_shift,
        second_scale,
        second_shift,
        first_scale,
        first_shift,
    ):
        count = target.shape[0]
        target[...] = shifts_in[line : line + count, :]
        line += count
    contract_shift[...] = outward_shift[...]

    for b in range(batch_count):
        load(b, 0).wait()
        for s in range(2):
            for i in range(3):
                top = late + (s * 3 + i) * head_rows
                for j in range(head_blocks):
                    inward[
                        s, i, j * head_rows : (j + 1) * head_rows, b * cols : (b + 1) * cols
                    ] = held[b, top : top + head_rows, j * cols : (j + 1) * cols].astype(jnp.float32)
        outward[b] = held[b, late + 6 * head_rows :, :].astype(jnp.float32)
        for copy in stores(b, 0):
            copy.start()
    for copy in wide_stores():
        copy.start()

    def step(b, carry):
        at = b % 2
        for part in range(1, 4):
            load(b, part).wait()

            @pl.when(b >= 2)
            def _():
                for copy in stores(b - 2, part):
                    copy.wait()

            if part < 3:
                first = (part - 1) * unit_rows
                for j in range(unit_blocks):
                    expand[at, part - 1, j * unit_rows : (j + 1) * unit_rows, :] = held[
                        b, first : first + unit_rows, j * unit : (j + 1) * unit
                    ].astype(jnp.float32)
            else:
                contract[at] = held[b, late - unit : late, :].astype(jnp.float32)
            for copy in stores(b, part):
                copy.start()
        return carry

    lax.fori_loop(0, batch_count, step, 0)
    for b in range(batch_count):
        for part in range(4):
            if part == 0 or b >= batch_count - 2:
                for copy in stores(b, part):
                    copy.wait()
    for copy in wide_stores():
        copy.wait()


def widen(gathered, result, input_delta, shifts, cols, unit):
    batch_count, rows, width = gathered.shape
    fsdp_count = lax.axis_size("fsdp")
    hidden = unit * batch_count * fsdp_count
    half = width // 2
    turn = lax.axis_index("fsdp").astype(jnp.int32)[None]
    f32 = jnp.float32
    dma = pltpu.SemaphoreType.DMA
    hbm = pl.BlockSpec(memory_space=pl.ANY)
    vmem = pl.BlockSpec(memory_space=pltpu.VMEM)

    def matrix(rows, columns):
        return jax.ShapeDtypeStruct((rows, columns), f32)

    def vector(size):
        return jax.ShapeDtypeStruct((size // fsdp_count // 128, 128), f32)

    out = pl.pallas_call(
        functools.partial(widen_kernel, cols, unit),
        out_shape=(
            jax.ShapeDtypeStruct((1,) + result.shape, result.dtype),
            jax.ShapeDtypeStruct((1,) + input_delta.shape, f32),
            matrix(half, 3 * width),
            vector(3 * width),
            matrix(half, width),
            vector(width),
            matrix(half, hidden),
            vector(hidden),
            matrix(hidden // 2, width),
            vector(width),
        )
        + (vector(width),) * 4,
        in_specs=[pl.BlockSpec(memory_space=pltpu.SMEM), hbm, vmem, vmem, vmem],
        out_specs=(vmem, vmem) + (hbm, vmem) * 4 + (vmem,) * 4,
        scratch_shapes=[
            pltpu.VMEM((batch_count, rows, width), gathered.dtype),
            pltpu.VMEM((2, 3, half, batch_count * cols), f32),
            pltpu.VMEM((batch_count, cols, width), f32),
            pltpu.VMEM((2, 2, half, unit), f32),
            pltpu.VMEM((2, unit, width), f32),
            dma((batch_count, 4)),
            dma((2, 3)),
            dma((batch_count,)),
            dma((2, 3)),
        ],
        name="widen",
        compiler_params=pltpu.CompilerParams(vmem_limit_bytes=VMEM_LIMIT),
    )(turn, gathered, result, input_delta, shifts)
    return tuple(a.reshape(-1) if a.ndim == 2 and a.shape[1] == 128 else a for a in out)


def dot(left, right, contract=((1,), (0,))):
    return lax.dot_general(left, right, (contract, ((), ())), preferred_element_type=jnp.float32)


def normalize(values):
    center = values - jnp.mean(values, axis=-1, keepdims=True)
    inverse = lax.rsqrt(jnp.mean(center * center, axis=-1, keepdims=True) + EPSILON)
    return (center * inverse, inverse)


def norm_backward(upstream, normed, inverse, factor):
    scaled = upstream * factor
    middle = jnp.mean(scaled, axis=-1, keepdims=True)
    coupled = jnp.mean(scaled * normed, axis=-1, keepdims=True)
    result = inverse * (scaled - middle - normed * coupled)
    return (result, jnp.sum(upstream * normed, axis=0), jnp.sum(upstream, axis=0))


def slot_positions(span_order, first_slot, slot_count, span_size):
    slot_index = first_slot + jnp.arange(slot_count, dtype=jnp.int32)
    owners = slot_index // (2 * span_size)
    places = jnp.arange(span_order.shape[0], dtype=jnp.int32)
    leading = jnp.sum(jnp.where(owners[:, None] == places[None, :], span_order[None, :], 0), axis=1)
    spans = 2 * span_order.shape[0]
    picked = jnp.where(slot_index // span_size % 2 == 0, leading, spans - 1 - leading)
    return picked * span_size + slot_index % span_size


def rotary_tables(positions):
    half_rot = ROT // 2
    angular = jnp.exp(
        jnp.arange(half_rot, dtype=jnp.float32) * (-2.0 * math.log(ROTARY_BASE) / ROT)
    )
    angles = positions.astype(jnp.float32)[:, None] * angular[None, :]
    angles = jnp.concatenate([angles, angles], axis=1)
    return (jnp.cos(angles), jnp.sin(angles))


def rotate(tensor, cosine, sine_table):
    half_rot = ROT // 2
    leading_part = tensor[..., :ROT]
    turned = jnp.concatenate([-leading_part[..., half_rot:], leading_part[..., :half_rot]], axis=-1)
    rotated = leading_part * cosine[:, None, :] + turned * sine_table[:, None, :]
    return jnp.concatenate([rotated, tensor[..., ROT:]], axis=-1)


def unrotate(tensor, cosine, sine_table):
    half_rot = ROT // 2
    leading_part = tensor[..., :ROT]
    weighted = leading_part * sine_table[:, None, :]
    turned = jnp.concatenate([weighted[..., half_rot:], -weighted[..., :half_rot]], axis=-1)
    return jnp.concatenate([leading_part * cosine[:, None, :] + turned, tensor[..., ROT:]], axis=-1)


def attention(mixed, place, cosine, sine_table, heads):
    sequences, length, _ = mixed.shape
    parts = mixed.reshape(sequences, length, 4, heads, HEAD_DIM)
    queries, keys, values, grads = (parts[:, :, i] for i in range(4))
    scale = 1.0 / math.sqrt(HEAD_DIM)
    scores = jnp.einsum("sqhd,skhd->shqk", queries, keys, preferred_element_type=jnp.float32)
    allowed = place[None, :] <= place[:, None]
    scores = jnp.where(allowed, scores * scale, MASKED)
    peak = jnp.max(scores, axis=-1, keepdims=True)
    log_total = peak + jnp.log(jnp.sum(jnp.exp(scores - peak), axis=-1, keepdims=True))
    probs = jnp.exp(scores - log_total)
    soft = probs.astype(jnp.bfloat16)
    context = jnp.einsum("shqk,skhd->sqhd", soft, values, preferred_element_type=jnp.float32)
    context = context.astype(jnp.bfloat16)
    delta = jnp.einsum(
        "sqhd,sqhd->shq", grads.astype(jnp.float32), context.astype(jnp.float32)
    )
    value_grad = jnp.einsum("shqk,sqhd->skhd", soft, grads, preferred_element_type=jnp.float32)
    probs_grad = jnp.einsum("sqhd,skhd->shqk", grads, values, preferred_element_type=jnp.float32)
    score_grad = (probs * (probs_grad - delta[..., None]) * scale).astype(jnp.bfloat16)
    query_grad = jnp.einsum("shqk,skhd->sqhd", score_grad, keys, preferred_element_type=jnp.float32)
    key_grad = jnp.einsum("shqk,sqhd->skhd", score_grad, queries, preferred_element_type=jnp.float32)
    query_grad = unrotate(query_grad, cosine, sine_table)
    key_grad = unrotate(key_grad, cosine, sine_table)
    back = jnp.stack([query_grad, key_grad, value_grad], axis=2)
    shift = jnp.sum(back, axis=(0, 1)).reshape(-1)
    full = jnp.concatenate([context[:, :, None], back.astype(jnp.bfloat16)], axis=2)
    return (full.reshape(sequences, length, 4 * heads * HEAD_DIM), shift)


def plain_body(
    layer_input,
    out_grad,
    span_order,
    inward,
    inward_bias,
    outward,
    outward_bias,
    expand,
    expand_bias,
    contract,
    contract_bias,
    first_gain,
    first_bias,
    second_gain,
    second_bias,
):
    batch_count, fsdp_count = (lax.axis_size("batch"), lax.axis_size("fsdp"))
    context_count = lax.axis_size("ctx")
    context_index = lax.axis_index("ctx")
    batch_index, fsdp_index = (lax.axis_index("batch"), lax.axis_index("fsdp"))
    plane = batch_count * fsdp_count
    tokens, width = layer_input.shape[1:]
    hidden_units = expand.shape[1]
    head_cols = width // plane
    unit_cols = hidden_units // plane
    heads = head_cols // HEAD_DIM
    length = tokens * context_count
    span_size = tokens // 2
    own_sequences = plane // context_count

    def full_vectors(*vectors):
        sizes = [v.shape[0] for v in vectors]
        gathered = lax.all_gather(jnp.concatenate(vectors), "fsdp")
        out, start = ([], 0)
        for size in sizes:
            out.append(gathered[:, start : start + size].reshape(-1).astype(jnp.float32))
            start += size
        return out

    (
        inward_offset,
        outward_offset,
        expand_offset,
        contract_offset,
        gain_first,
        offset_first,
        gain_second,
        offset_second,
    ) = full_vectors(
        inward_bias,
        outward_bias,
        expand_bias,
        contract_bias,
        first_gain,
        first_bias,
        second_gain,
        second_bias,
    )

    def chunk(array, cols):
        rows = array.shape[0]
        parts = array.reshape(rows, -1, fsdp_count, batch_count, cols)
        mine = lax.dynamic_index_in_dim(parts, batch_index, 3, keepdims=False)
        return mine.transpose(2, 0, 1, 3).reshape(fsdp_count, rows, -1)

    to_send = jnp.concatenate([chunk(inward, head_cols), chunk(expand, unit_cols)], axis=2)
    weights = lax.all_to_all(to_send, "fsdp", 0, 0).reshape(width, -1)
    inward_cols = weights[:, : 3 * head_cols]
    expand_cols = weights[:, 3 * head_cols :]
    outward_rows = lax.dynamic_slice_in_dim(outward, batch_index * head_cols, head_cols, 0)
    contract_rows = lax.dynamic_slice_in_dim(contract, batch_index * unit_cols, unit_cols, 0)
    plane_index = fsdp_index * batch_count + batch_index
    inward_shift_in = lax.dynamic_index_in_dim(
        inward_offset.reshape(3, plane, head_cols), plane_index, 1, keepdims=False
    ).reshape(-1)
    expand_shift_in = lax.dynamic_slice_in_dim(expand_offset, plane_index * unit_cols, unit_cols, 0)

    pair = jnp.stack([layer_input[0], out_grad[0]])
    pair_all = lax.all_gather(pair, PLANE, axis=1, tiled=True)
    grads_all = pair_all[1]
    rows_all = pair_all[0].astype(jnp.float32)
    normed, inverse = normalize(rows_all)
    first_rows = (normed * gain_first + offset_first).astype(jnp.bfloat16)
    second_rows = (normed * gain_second + offset_second).astype(jnp.bfloat16)

    local_place = slot_positions(span_order, context_index * tokens, tokens, span_size)
    cosine, sine_table = rotary_tables(local_place)
    cosine_plane = jnp.tile(cosine, (plane, 1))
    sine_plane = jnp.tile(sine_table, (plane, 1))
    projected = dot(first_rows, inward_cols) + inward_shift_in
    projected = projected.reshape(plane * tokens, 3 * heads, HEAD_DIM)
    turned = rotate(projected[:, : 2 * heads], cosine_plane, sine_plane)
    context_grad = dot(grads_all, outward_rows, ((1,), (1,)))
    mixed = jnp.concatenate(
        [
            turned.reshape(plane * tokens, -1),
            projected[:, 2 * heads :].reshape(plane * tokens, -1),
            context_grad,
        ],
        axis=1,
    ).astype(jnp.bfloat16)
    mixed = mixed.reshape(context_count, own_sequences, tokens, 4 * head_cols)
    mixed = lax.all_to_all(mixed, "ctx", 0, 0)
    mixed = mixed.transpose(1, 0, 2, 3).reshape(own_sequences, length, 4 * head_cols)
    place = slot_positions(span_order, 0, length, span_size)
    cosine_all, sine_all = rotary_tables(place)

    before = dot(second_rows, expand_cols) + expand_shift_in
    tail = 1.0 + lax.erf(before * HALF_ROOT)
    activated = (0.5 * before * tail).astype(jnp.bfloat16)
    slope = 0.5 * tail + before * jnp.exp(-0.5 * before * before) * NORMAL_PEAK
    before_grad = dot(grads_all, contract_rows, ((1,), (1,))) * slope
    expand_sum = jnp.sum(before_grad, axis=0)
    before_rows = before_grad.astype(jnp.bfloat16)
    expand_delta = dot(second_rows, before_rows, ((0,), (0,)))
    contract_delta = dot(activated, grads_all, ((0,), (0,)))
    out_part = dot(activated, contract_rows)
    second_part = dot(before_rows, expand_cols, ((1,), (1,)))

    hidden = layer_input[0].astype(jnp.float32)
    grad_float = out_grad[0].astype(jnp.float32)
    normed_mine, inverse_mine = normalize(hidden)
    half = width // fsdp_count

    def spread(values, sizes):
        wide = jnp.zeros((sizes[0], plane, sizes[1]), jnp.float32)
        values = values.reshape(sizes[0], sizes[1])
        return lax.dynamic_update_index_in_dim(wide, values, plane_index, 1).reshape(-1)

    bias_total = jnp.sum(grad_float, axis=0)
    expand_wide = spread(expand_sum, (1, unit_cols))

    back, inward_sum = attention(mixed, place, cosine_all, sine_all, heads)
    back = back.reshape(own_sequences, context_count, tokens, 4 * head_cols)
    back = lax.all_to_all(back.transpose(1, 0, 2, 3), "ctx", 0, 0)
    back = back.reshape(plane * tokens, 4 * head_cols)
    context_rows = back[:, :head_cols]
    projected_rows = back[:, head_cols:]
    inward_delta = dot(first_rows, projected_rows, ((0,), (0,)))
    outward_delta = dot(context_rows, grads_all, ((0,), (0,)))
    out_part = out_part + dot(context_rows, outward_rows)
    first_part = dot(projected_rows, inward_cols, ((1,), (1,)))
    stacked = jnp.stack([second_part, out_part, first_part], axis=1).astype(jnp.bfloat16)
    mine = lax.psum_scatter(stacked, PLANE, scatter_dimension=0, tiled=True)
    mine = mine.transpose(1, 0, 2).astype(jnp.float32)
    columns = jnp.concatenate([inward_delta, expand_delta], axis=1).astype(jnp.bfloat16)
    rows = jnp.concatenate([outward_delta, contract_delta], axis=0).astype(jnp.bfloat16)
    columns, rows = lax.psum((columns, rows), "ctx")
    columns = lax.all_to_all(columns.reshape(fsdp_count, half, -1), "fsdp", 0, 0)
    columns = lax.all_gather(columns, "batch")
    rows = lax.all_gather(rows, "batch").astype(jnp.float32)
    columns = columns.transpose(2, 1, 0, 3).astype(jnp.float32)
    inward_total = columns[..., : 3 * head_cols].reshape(
        half, fsdp_count, batch_count, 3, head_cols
    )
    totals = (
        inward_total.transpose(0, 3, 1, 2, 4).reshape(half, 3 * width),
        rows[:, :head_cols].reshape(half, width),
        columns[..., 3 * head_cols :].reshape(half, hidden_units),
        rows[:, head_cols:].reshape(-1, width),
    )
    _, second_scale, second_shift = norm_backward(
        mine[0], normed_mine, inverse_mine, gain_second
    )
    _, first_scale, first_shift = norm_backward(mine[2], normed_mine, inverse_mine, gain_first)
    vectors = [
        spread(inward_sum, (3, head_cols)),
        bias_total,
        expand_wide,
        first_scale,
        first_shift,
        second_scale,
        second_shift,
    ]
    whole = lax.psum(jnp.concatenate(vectors), ("batch", "ctx", "fsdp"))

    result = (hidden + (mine[1] + outward_offset) + contract_offset).astype(jnp.bfloat16)
    second_input, _, _ = norm_backward(mine[0], normed_mine, inverse_mine, gain_second)
    first_input, _, _ = norm_backward(mine[2], normed_mine, inverse_mine, gain_first)
    input_delta = grad_float + first_input + second_input
    halves, start = ([], 0)
    for vector in vectors:
        size = vector.shape[0] // fsdp_count
        halves.append(lax.dynamic_slice_in_dim(whole, start + fsdp_index * size, size, 0))
        start += vector.shape[0]
    return (
        result[None],
        input_delta[None],
        totals[0],
        halves[0],
        totals[1],
        halves[1],
        totals[2],
        halves[2],
        totals[3],
        halves[1],
        halves[3],
        halves[4],
        halves[5],
        halves[6],
    )


def body(
    layer_input,
    out_grad,
    span_order,
    inward,
    inward_bias,
    outward,
    outward_bias,
    expand,
    expand_bias,
    contract,
    contract_bias,
    first_gain,
    first_bias,
    second_gain,
    second_bias,
):
    plane = lax.axis_size("batch") * lax.axis_size("fsdp")
    width = layer_input.shape[2]
    if width // plane % 128:
        return plain_body(
            layer_input,
            out_grad,
            span_order,
            inward,
            inward_bias,
            outward,
            outward_bias,
            expand,
            expand_bias,
            contract,
            contract_bias,
            first_gain,
            first_bias,
            second_gain,
            second_bias,
        )
    vectors = (
        inward_bias,
        outward_bias,
        expand_bias,
        contract_bias,
        first_gain,
        first_bias,
        second_gain,
        second_bias,
    )
    ends = [sum(v.shape[0] for v in vectors[: i + 1]) for i in range(len(vectors))]
    room = ends[-1] + -ends[-1] % 1024
    small = sum(
        jnp.pad(v.astype(jnp.float32), (end - v.shape[0], room - end))
        for v, end in zip(vectors, ends)
    ).reshape(-1, 128)
    sums, result, input_delta, shifts = layer(
        layer_input, out_grad, span_order, small, inward, outward, expand, contract
    )
    return widen(sums, result, input_delta, shifts, width // plane, expand.shape[1] // plane)


def solution(mesh):
    rows = P(PLANE, "ctx", None)
    matrix, vector = (P("fsdp", None), P("fsdp"))
    in_specs = (rows, rows, P()) + (matrix, vector) * 4 + (vector,) * 4
    out_specs = (rows, rows) + (matrix, vector) * 4 + (vector,) * 4
    return jax.shard_map(body, mesh=mesh, in_specs=in_specs, out_specs=out_specs, check_vma=False)
```

```python
import functools
import math

import jax
import jax.numpy as jnp
from jax import lax
from jax.experimental import pallas as pl
from jax.experimental.pallas import tpu as pltpu
from jax.sharding import PartitionSpec as P

HEAD_DIM = 64
ROT = 16

EPSILON = 1e-05
ROTARY_BASE = 10000.0
MASKED = -1e30
HALF_ROOT = 0.7071067811865476
NORMAL_PEAK = 0.3989422804014327
PLANE = ("batch", "fsdp")


MESH = pl.DeviceIdType.MESH
CORES = 2
VMEM_LIMIT = 56 * 2**20


def here():
    return (lax.axis_index("batch"), lax.axis_index("ctx"), lax.axis_index("fsdp"))


def swapped(index, step):
    return index + step * (1 - 2 * (index // step % 2))


def greet(partners):
    barrier = pltpu.get_barrier_semaphore()
    for partner in partners:
        pl.semaphore_signal(barrier, inc=1, device_id=partner, device_id_type=MESH)
    pl.semaphore_wait(barrier, len(partners))


def remote(src, dst, send, recv, target):
    return pltpu.make_async_remote_copy(
        src_ref=src,
        dst_ref=dst,
        send_sem=send,
        recv_sem=recv,
        device_id=target,
        device_id_type=MESH,
    )


LAG = 2
LB = 2
LX = 2
LY = 3
AHEAD = 2
ATT = 4
READY = 11


def layer_kernel(
    sizes,
    tokens,
    heads,
    counts,
    piece,
    input_ref,
    grad_ref,
    order_ref,
    small_ref,
    inward_ref,
    outward_ref,
    expand_ref,
    contract_ref,
    sums_ref,
    result_ref,
    input_grad_ref,
    shifts_ref,
    inputs,
    grads,
    small,
    inward,
    outward,
    expand,
    contract,
    cosine,
    sine,
    stats,
    first_rows,
    second_rows,
    work,
    before,
    hidden_back,
    out_rows,
    scaled,
    mixed_out,
    mixed,
    heads_sum,
    back_out,
    back_in,
    inward_sum,
    row_sums,
    part,
    mine,
    reduced,
    reduced_right,
    near,
    across_in,
    far,
    token_sum,
    vector_in,
    vector_sum,
    load_sems,
    small_sems,
    weight_sems,
    pair_sems,
    gather_sems,
    share_sems,
    there_sends,
    there_recvs,
    there_own,
    back_own,
    turn_sems,
    reduce_sends,
    reduce_recvs,
    right_recvs,
    back_sends,
    back_recvs,
    row_sends,
    row_recvs,
    chip_sends,
    chip_recvs,
    core_sems,
    keep_sem,
    near_sems,
    across_sems,
    far_sems,
    vector_sems,
):
    batch_count, context_count, fsdp_count = sizes
    early_other, early, late_other, late = counts
    b, z, y = here()
    chips = batch_count // CORES
    core = b % CORES
    chip = b // CORES
    width = part.shape[1]
    half_width = width // 2
    cols = heads * HEAD_DIM
    unit = contract.shape[0]
    plane = batch_count * fsdp_count
    index = y * batch_count + b
    own_sequences = plane // context_count
    length = tokens * context_count
    steps = early + late
    early_rows = 2 * early * piece
    last = context_count - 1
    lines = width // 128
    f32, half_type = (jnp.float32, part.dtype)
    group_rows = fsdp_count * tokens

    sibling = (chip * CORES + (1 - core), z, y)
    across = (b, z, 1 - y)
    peers = [((chip + d) % chips * CORES + core, z, y) for d in range(1, chips)]
    sources = [(chip + chips - d) % chips * CORES + core for d in range(1, chips)]
    others = [(b, (z + d) % context_count, y) for d in range(1, context_count)]
    stages = []
    step = 1
    while step < batch_count:
        stages.append((swapped(b, step), z, y))
        step *= 2
    stages.append(across)
    step = 1
    while step < context_count:
        stages.append((b, swapped(z, step), y))
        step *= 2

    def sem(sems, *index):
        return (sems.at[(0, *index)], sems.at[(1, *index)])


    plane_arrays = (inputs, grads)
    plane_sources = (input_ref.at[0], grad_ref.at[0])

    def block(array, batch, fsdp):
        row = pl.multiple_of((batch * fsdp_count + fsdp) * tokens, tokens)
        return plane_arrays[array].at[pl.ds(row, tokens), :]

    def own_load(array):
        return pltpu.make_async_copy(
            plane_sources[array], block(array, b, y), load_sems.at[array]
        )

    def to_across(array):
        return remote(
            plane_sources[array], block(array, b, y), *sem(gather_sems, array, 0), across
        )

    def to_peer(array, d):
        return remote(
            plane_sources[array], block(array, b, y), *sem(gather_sems, array, 1 + d), peers[d]
        )

    def on_to_peer(array, d):
        at = block(array, b, 1 - y)
        return remote(at, at, *sem(gather_sems, array, chips + d), peers[d])

    def share(array, i):
        if i == 0:
            return remote(
                plane_sources[array], block(array, b, y), *sem(share_sems, array, 0), sibling
            )
        if i == 1:
            at = block(array, b, 1 - y)
        else:
            d = (i - 2) % (chips - 1)
            at = block(array, sources[d], y if i - 2 < chips - 1 else 1 - y)
        return remote(at, at, *sem(share_sems, array, i), sibling)

    def columns_of(owner, i):
        place = owner * batch_count + b
        if i < 3:
            return pl.ds(pl.multiple_of(i * width + place * cols, cols), cols)
        return pl.ds(pl.multiple_of(place * unit, unit), unit)

    part_rows = half_width // 2
    parity = z % 2
    pair = (b, swapped(z, 1), y)

    def inward_part(owner, parity):
        first = pl.multiple_of(owner * half_width + parity * part_rows, part_rows)
        return inward.at[pl.ds(first, part_rows), :]

    def weight_copies():
        source_rows = pl.ds(pl.multiple_of(parity * part_rows, part_rows), part_rows)
        rows = pl.ds(pl.multiple_of(y * half_width, half_width), half_width)
        out = [
            remote(
                inward_ref.at[source_rows, columns_of(1 - y, i)],
                inward_part(y, parity).at[:, i * cols : (i + 1) * cols],
                *sem(weight_sems, 0),
                across,
            )
            for i in range(3)
        ]
        out.append(
            remote(
                expand_ref.at[:, columns_of(1 - y, 3)],
                expand.at[rows, :],
                *sem(weight_sems, 1),
                across,
            )
        )
        return out

    def weight_own():
        rows = pl.ds(pl.multiple_of(y * half_width, half_width), half_width)
        pairs = [
            (inward_ref.at[:, columns_of(y, i)], inward.at[rows, i * cols : (i + 1) * cols])
            for i in range(3)
        ]
        pairs.append((expand_ref.at[:, columns_of(y, 3)], expand.at[rows, :]))
        return [
            pltpu.make_async_copy(source, target, load_sems.at[2 + i])
            for i, (source, target) in enumerate(pairs)
        ]

    def inward_brought():
        at = inward_part(1 - y, parity)
        return remote(at, at, *sem(weight_sems, 0), across)

    def to_pair(parity):
        at = inward_part(1 - y, parity)
        return remote(at, at, *sem(pair_sems), pair)

    row_loads = [
        pltpu.make_async_copy(
            outward_ref.at[pl.ds(pl.multiple_of(b * cols, cols), cols), :],
            outward,
            load_sems.at[6],
        ),
        pltpu.make_async_copy(
            contract_ref.at[pl.ds(pl.multiple_of(b * unit, unit), unit), :],
            contract,
            load_sems.at[7],
        ),
    ]
    weight_loads = weight_own()
    weight_sends = weight_copies()
    small_copy = remote(small_ref, small.at[1], *sem(small_sems, 0), across)

    own_load(0).start()
    own_load(1).start()
    for load in weight_loads + row_loads:
        load.start()
    greet([sibling, across] + peers + others)
    small_copy.start()

    def offer(array):
        to_across(array).start()
        share(array, 0).start()

    def offer_peers(array):
        for d in range(chips - 1):
            to_peer(array, d).start()

    for send in weight_sends[:3]:
        send.start()
    offer(0)
    offer_peers(0)
    offer(1)
    offer_peers(1)
    weight_sends[3].start()
    small[0] = small_ref[...]


    def positions(shape, dimension):
        slot = lax.broadcasted_iota(jnp.int32, shape, dimension)
        owner = slot // tokens
        leading = jnp.zeros(shape, jnp.int32)
        for c in range(context_count):
            leading = jnp.where(owner == c, order_ref[c], leading)
        span = tokens // 2
        second = slot // span % 2
        picked = jnp.where(second == 0, leading, 2 * context_count - 1 - leading)
        return picked * span + slot % span

    half_rot = ROT // 2
    lane = lax.broadcasted_iota(jnp.int32, (1, cols), 1) % HEAD_DIM
    angular = jnp.exp((lane % half_rot).astype(f32) * (-2.0 * math.log(ROTARY_BASE) / ROT))
    angles = positions((length, cols), 0).astype(f32) * angular
    cosine[...] = jnp.where(lane < ROT, jnp.cos(angles), 1.0)
    sine[...] = jnp.where(lane < ROT, jnp.sin(angles), 0.0)
    low = (lane < half_rot).astype(f32)
    high = 1.0 - low

    def turn(value, rows, sign):
        weight = sine[rows, :] * sign
        return (
            value * cosine[rows, :]
            - pltpu.roll(value, cols - half_rot, 1) * (weight * low)
            + pltpu.roll(value, half_rot, 1) * (weight * high)
        )


    small_copy.wait_recv()
    vector_rows = [3 * lines, lines, unit * plane // 128] + [lines] * 5
    starts = [sum(vector_rows[:i]) // fsdp_count for i in range(8)]

    def vector_line(which, line):
        share_lines = vector_rows[which] // fsdp_count
        owner = line // share_lines
        at = (owner - y) * (owner - y)
        return small[at, pl.ds(starts[which] + line % share_lines, 1), :]

    def whole(which):
        return jnp.concatenate([vector_line(which, line) for line in range(lines)], axis=1)

    def chunk(which, first, count):
        return jnp.concatenate([vector_line(which, first + i) for i in range(count)], axis=1)


    def group(u):
        return (chip + u // CORES) % chips * CORES + (core + u % CORES) % CORES

    def rows_of(u):
        return pl.ds(pl.multiple_of(group(u) * group_rows, group_rows), group_rows)

    def bring(array, u):
        distance, other = (u // CORES, u % CORES)
        if other == 0 and distance == 0:
            own_load(array).wait()
            if array == 0:
                to_across(array).wait_recv()
            for d in range(chips - 1):
                on_to_peer(array, d).start()
            share(array, 1).start()
        elif other == 0:
            d = chips - distance - 1
            to_peer(array, d).wait_recv()
            share(array, 2 + d).start()
            on_to_peer(array, d).wait_recv()
            share(array, 1 + chips + d).start()
        elif distance == 0:
            share(array, 0).wait_recv()
            share(array, 1).wait_recv()
        else:
            d = chips - distance - 1
            share(array, 2 + d).wait_recv()
            share(array, 1 + chips + d).wait_recv()

    gains = [whole(4), whole(5), whole(6), whole(7)]
    inward_bias = jnp.concatenate(
        [
            chunk(0, i * lines + index * (cols // 128), cols // 128)
            for i in range(3)
        ],
        axis=1,
    )

    def norm(u):
        rows = rows_of(u)
        x = inputs[rows, :].astype(f32)
        mean = jnp.mean(x, axis=-1, keepdims=True)
        center = x - mean
        inverse = lax.rsqrt(jnp.mean(center * center, axis=-1, keepdims=True) + EPSILON)
        stats[rows, 0:1] = mean
        stats[rows, 1:2] = inverse
        normed = center * inverse
        first_rows[rows, :] = (normed * gains[0] + gains[1]).astype(half_type)
        second_rows[rows, :] = (normed * gains[2] + gains[3]).astype(half_type)

    there_columns = ((0, 3 * cols), (3 * cols, cols))

    def there_copy(u, f, kind):
        p = group(u) * fsdp_count + f
        owner, s = (p // own_sequences, p % own_sequences)
        first, count = there_columns[kind]
        columns = pl.ds(first, count)
        source = mixed_out.at[pl.ds(pl.multiple_of(p * tokens, tokens), tokens), columns]
        at = pl.ds(pl.multiple_of(z * tokens, tokens), tokens)
        target = mixed.at[s, at, columns]

        @pl.when(owner == z)
        def _():
            pltpu.make_async_copy(source, target, there_own.at[s, kind]).start()

        @pl.when(owner != z)
        def _():
            remote(
                source, target, there_sends.at[kind], there_recvs.at[s, z, kind], (b, owner, y)
            ).start()

    def project(u):
        projected = dot(first_rows[rows_of(u), :], inward[...]) + inward_bias
        local = pl.ds(pl.multiple_of(z * tokens, tokens), tokens)
        for f in range(fsdp_count):
            at = pl.ds(pl.multiple_of((group(u) * fsdp_count + f) * tokens, tokens), tokens)
            piece_rows = projected[f * tokens : (f + 1) * tokens, :]
            for i in range(3):
                value = piece_rows[:, i * cols : (i + 1) * cols]
                if i < 2:
                    value = turn(value, local, 1.0)
                mixed_out[at, i * cols : (i + 1) * cols] = value.astype(half_type)
            there_copy(u, f, 0)

    def upstream(u):
        rows = rows_of(u)
        value = dot(grads[rows, :], outward[...], ((1,), (1,)))
        mixed_out[rows, 3 * cols :] = value.astype(half_type)
        for f in range(fsdp_count):
            there_copy(u, f, 1)

    def there(s):
        for kind, (first, count) in enumerate(there_columns):
            columns = pl.ds(first, count)
            block_at = mixed.at[s, pl.ds(0, tokens), columns]
            pltpu.make_async_copy(block_at, block_at, there_own.at[s, kind]).wait()
            for d in range(1, context_count):
                source = (z + d) % context_count
                at = mixed.at[s, pl.ds(pl.multiple_of(source * tokens, tokens), tokens), columns]
                recv = there_recvs.at[s, source, kind]
                remote(at, at, there_sends.at[kind], recv, others[0]).wait_recv()

    order = [u for u in range(0, batch_count, CORES)] + [u for u in range(1, batch_count, CORES)]
    bring(0, 0)
    inward_brought().wait_recv()
    to_pair(parity).start()
    norm(0)
    for i in range(3):
        weight_loads[i].wait()
    to_pair(1 - parity).wait_recv()
    project(0)
    to_across(1).wait_recv()
    for u in order[1:chips]:
        bring(0, u)
    bring(1, 0)
    row_loads[0].wait()
    for u in order[1:]:
        if u % CORES:
            bring(0, u)
        norm(u)
        project(u)
    upstream(0)
    for u in order[1:]:
        bring(1, u)
        upstream(u)


    row_loads[1].wait()
    weight_loads[3].wait()
    expand_bias = chunk(2, index * (unit // 128), unit // 128)
    nothing = jnp.zeros((1, width), f32)

    def normed_rows(rows):
        return (inputs[rows, :].astype(f32) - stats[rows, 0:1]) * stats[rows, 1:2]

    own_half = pl.ds(pl.multiple_of(y * half_width, half_width), half_width)
    other_half = pl.ds(pl.multiple_of((1 - y) * half_width, half_width), half_width)

    def early_tile(i, carry):
        rows = pl.ds(pl.multiple_of(i * group_rows, group_rows), group_rows)
        before[rows, :] = dot(second_rows[rows, own_half], expand[own_half, :]) + expand_bias
        hidden_back[rows, :] = dot(grads[rows, :], contract[...], ((1,), (1,)))
        return carry

    lax.fori_loop(0, batch_count, early_tile, 0)
    weight_sends[3].wait_recv()

    def forward_tile(i, expand_total):
        rows = pl.ds(pl.multiple_of(i * group_rows, group_rows), group_rows)
        value = before[rows, :] + dot(second_rows[rows, other_half], expand[other_half, :])
        tail = 1.0 + lax.erf(value * HALF_ROOT)
        slope = 0.5 * tail + value * jnp.exp(-0.5 * value * value) * NORMAL_PEAK
        before_grad = hidden_back[rows, :] * slope
        work[rows, :unit] = (0.5 * value * tail).astype(half_type)
        work[rows, unit:] = before_grad.astype(half_type)
        return expand_total + jnp.sum(before_grad, axis=0, keepdims=True)

    expand_total = lax.fori_loop(0, batch_count, forward_tile, jnp.zeros((1, unit), f32))
    row_sums[...] = jnp.zeros(row_sums.shape, f32)

    def hidden_tile(i):
        rows = pl.ds(pl.multiple_of(i * group_rows, group_rows), group_rows)
        out_rows[rows, :] = dot(work[rows, :unit], contract[...]).astype(half_type)
        value = dot(work[rows, unit:], expand[...], ((1,), (1,)))
        scaled[rows, :] = (value * gains[2]).astype(half_type)
        row_sums[0:1, :] += jnp.sum(value * normed_rows(rows), axis=0, keepdims=True)
        row_sums[1:2, :] += jnp.sum(value, axis=0, keepdims=True)

    def expand_half(s):
        owner = (1 - y) * (1 - s) + y * s
        column = pl.multiple_of(owner * half_width, half_width)
        delta = dot(second_rows[:, pl.ds(column, half_width)], work[:, unit:], ((0,), (0,)))
        group = unit * half_width // width
        at = pl.ds(pl.multiple_of(s * group, group), group)
        for j in range(width // unit):
            part[at, j * unit : (j + 1) * unit] = delta[j * group : (j + 1) * group, :].astype(
                half_type
            )

    def contract_rows():
        part[early_rows - unit : early_rows, :] = dot(
            work[:, :unit], grads[...], ((0,), (0,))
        ).astype(half_type)

    expand_half(0)


    def place(half, k):
        is_late = jnp.minimum(k // early, 1)
        other = early_other * (1 - is_late) + late_other * is_late
        count = early * (1 - is_late) + late * is_late
        j = k - early * is_late
        is_own = jnp.minimum(j // other, 1)
        row = (half * other + j) * (1 - is_own) + (
            2 * other + half * (count - other) + j - other
        ) * is_own
        return pl.multiple_of((2 * early * is_late + row) * piece, piece)

    def other_index(k):
        return k - (early - early_other) * jnp.minimum(k // early, 1)

    def own(k):
        is_late = jnp.minimum(k // early, 1)
        other = early_other * (1 - is_late) + late_other * is_late
        return jnp.minimum((k - early * is_late) // other, 1)

    def rows_at(ref, row):
        return ref.at[pl.ds(row, piece), :]

    def sums_at(batch, row):
        return sums_ref.at[batch, pl.ds(row, piece), :]

    def back_copy(half, k, side, target):
        at = rows_at(mine, place(half, k))
        return remote(at, at, back_sends.at[side, half], back_recvs.at[half, k], target)

    def row_copy(half, k):
        row = place(half, k)
        recv = row_recvs.at[half, other_index(k)]
        return remote(rows_at(mine, row), sums_at(b, row), row_sends, recv, across)

    def keep_copy(half, k):
        row = place(half, k)
        return pltpu.make_async_copy(rows_at(mine, row), sums_at(b, row), keep_sem)

    def chip_copy(d, half, k, from_mine):
        row = place(half, k)
        source = rows_at(mine, row) if from_mine else sums_at(b, row)
        return remote(
            source, sums_at(b, row), chip_sends.at[d], chip_recvs.at[d, half, k], peers[d]
        )

    def core_copy(half, k, from_mine, batch):
        row = place(half, k)
        source = rows_at(mine, row) if from_mine else sums_at(batch, row)
        return remote(
            source, sums_at(batch, row), core_sems.at[0], core_sems.at[1], sibling
        )

    def spread(half, k, from_mine):
        for d in range(chips - 1):
            chip_copy(d, half, k, from_mine).start()
        core_copy(half, k, from_mine, b).start()

    def arrived(half, k):
        for d in range(chips - 1):
            chip_copy(d, half, k, False).wait_recv()
            core_copy(half, k, False, sources[d]).start()

    def finish(half, k):
        @pl.when(own(k) == 0)
        def _():
            row_copy(half, k).start()

        @pl.when(own(k) == 1)
        def _():
            keep_copy(half, k).start()
            spread(half, k, True)

    left = (b, (z + last) % context_count, y)
    right = (b, (z + 1) % context_count, y)

    def reduce_copy(half, k, source, stream, target):
        row = place(half, k)
        if stream:
            landing = reduced_right.at[pl.ds(pl.multiple_of(k * piece, piece), piece), :]
            recv = right_recvs.at[k]
        else:
            landing = rows_at(reduced, row)
            recv = reduce_recvs.at[half, k]
        return remote(rows_at(source, row), landing, reduce_sends.at[half], recv, target)

    def ends(half):
        root = last // 2 if half == 0 else context_count // 2
        depth = max(root, last - root)
        at_root = z == root
        is_left = z < root
        distance = jnp.where(is_left, root - z, z - root)
        leaf = (z == 0) | (z == last)
        return root, depth, at_root, is_left, distance, leaf

    def pass_on(half, k, source):
        root = last // 2 if half == 0 else context_count // 2

        @pl.when(z == root + 1)
        def _():
            reduce_copy(half, k, source, 1, left).start()

        @pl.when(z > root + 1)
        def _():
            reduce_copy(half, k, source, 0, left).start()

        @pl.when(z < root)
        def _():
            reduce_copy(half, k, source, 0, right).start()

    def leaf_send(half, k):
        pass_on(half, k, part)

    def reduce_step(t, half):
        root, depth, at_root, is_left, distance, leaf = ends(half)
        k = t - LAG * (depth - distance)

        def send(source):
            pass_on(half, k, source)

        k_leaf = t + AHEAD

        @pl.when(leaf & jnp.logical_not(at_root) & (k_leaf < steps))
        def _():
            leaf_send(half, k_leaf)

        @pl.when(jnp.logical_not(leaf) & (k >= 0) & (k < steps))
        def _():
            row = place(half, k)
            here_at = pl.ds(row, piece)

            @pl.when(at_root)
            def _():
                value = part[here_at, :].astype(f32)
                if root > 0:
                    reduce_copy(half, k, part, 0, right).wait_recv()
                    value = value + reduced[here_at, :].astype(f32)
                if root < last:
                    reduce_copy(half, k, part, 1, left).wait_recv()
                    came = reduced_right[pl.ds(pl.multiple_of(k * piece, piece), piece), :]
                    value = value + came.astype(f32)
                mine[here_at, :] = value.astype(half_type)
                if root > 0:
                    back_copy(half, k, 0, left).start()
                if root < last:
                    back_copy(half, k, 1, right).start()
                finish(half, k)

            @pl.when(jnp.logical_not(at_root))
            def _():
                reduce_copy(half, k, part, 0, right).wait_recv()
                value = part[here_at, :].astype(f32) + reduced[here_at, :].astype(f32)
                reduced[here_at, :] = value.astype(half_type)
                send(reduced)

    def back_step(t, half):
        root, depth, at_root, is_left, distance, leaf = ends(half)
        k_back = t - LAG * depth - LB * distance

        @pl.when(jnp.logical_not(at_root) & (k_back >= 0) & (k_back < steps))
        def _():
            back_copy(half, k_back, 0, left).wait_recv()

            @pl.when(is_left & (z > 0))
            def _():
                back_copy(half, k_back, 0, left).start()

            @pl.when((z > root) & (z < last))
            def _():
                back_copy(half, k_back, 1, right).start()

            finish(half, k_back)

    def side_step(t, half):
        root, depth, at_root, is_left, distance, leaf = ends(half)
        k_row = t - LAG * depth - LB * distance - LX

        @pl.when((k_row >= 0) & (k_row < steps))
        def _():
            @pl.when(own(k_row) == 0)
            def _():
                row_copy(half, k_row).wait_recv()
                spread(half, k_row, False)

            @pl.when(own(k_row) == 1)
            def _():
                arrived(half, k_row)

        k_chip = k_row - LY

        @pl.when((k_chip >= 0) & (k_chip < steps))
        def _():
            @pl.when(own(k_chip) == 0)
            def _():
                arrived(half, k_chip)

    def drain():
        half_rows = pl.ds(0, steps * piece)
        other_count = 2 * (early_other + late_other) * piece

        def sent(ref, semaphore):
            remote(ref, ref, semaphore, core_sems.at[1], sibling).wait_send()

        everything = sums_ref.at[pl.ds(0, chips)]
        from_sibling = remote(everything, everything, core_sems.at[0], core_sems.at[1], sibling)
        from_sibling.wait_send()
        for d in range(chips - 1):
            sent(mine, chip_sends.at[d])
        sent(mine.at[pl.ds(0, other_count), :], row_sends)
        kept = mine.at[pl.ds(0, mine.shape[0] - other_count), :]
        pltpu.make_async_copy(kept, kept, keep_sem).wait()
        for half in range(2):
            root = last // 2 if half == 0 else context_count // 2

            @pl.when(z != root)
            def _():
                sent(mine.at[half_rows, :], reduce_sends.at[half])

            @pl.when((z <= root) & (z > 0))
            def _():
                sent(mine.at[half_rows, :], back_sends.at[0, half])

            @pl.when((z >= root) & (z < last))
            def _():
                sent(mine.at[half_rows, :], back_sends.at[1, half])

        from_sibling.wait_recv()


    def attend(n):
        s, h = (n // heads, n % heads)
        columns = [mixed[s, :, i * cols : (i + 1) * cols] for i in range(4)]
        head = lax.broadcasted_iota(jnp.int32, (length, cols), 1) // HEAD_DIM
        picked = head == h
        blank = jnp.zeros((length, cols), half_type)
        _, keys, values, _ = columns
        queries_h, keys_h, values_h, upstream_h = [
            jnp.where(picked, column, blank) for column in columns
        ]
        scale = 1.0 / math.sqrt(HEAD_DIM)
        allowed = positions((1, length), 1) <= positions((length, 1), 0)
        scores = dot(queries_h, keys, ((1,), (1,))) * scale
        scores = jnp.where(allowed, scores, MASKED)
        peak = jnp.max(scores, axis=1, keepdims=True)
        log_total = peak + jnp.log(jnp.sum(jnp.exp(scores - peak), axis=1, keepdims=True))
        probs = jnp.exp(scores - log_total)
        soft = probs.astype(half_type)
        context = dot(soft, values_h)
        delta = jnp.sum(
            upstream_h.astype(f32) * context.astype(half_type).astype(f32), axis=1, keepdims=True
        )
        probs_grad = dot(upstream_h, values, ((1,), (1,)))
        score_grad = (probs * (probs_grad - delta) * scale).astype(half_type)
        results = (
            context,
            dot(score_grad, keys_h),
            dot(score_grad, queries_h, ((0,), (0,))),
            dot(soft, upstream_h, ((0,), (0,))),
        )
        for i, value in enumerate(results):

            @pl.when(h == 0)
            def _():
                heads_sum[i] = value

            @pl.when(h > 0)
            def _():
                heads_sum[i] += value

        @pl.when(h == heads - 1)
        def _():
            back_out[s, :, :cols] = heads_sum[0].astype(half_type)
            for i in range(1, 4):
                value = heads_sum[i]
                if i < 3:
                    value = turn(value, slice(None), -1.0)
                back_out[s, :, i * cols : (i + 1) * cols] = value.astype(half_type)
                total = jnp.sum(value, axis=0, keepdims=True)

                @pl.when(s == 0)
                def _():
                    inward_sum[i - 1 : i, :] = total

                @pl.when(s > 0)
                def _():
                    inward_sum[i - 1 : i, :] += total

            for d in range(context_count):
                turn_copy(s, d).start()

    def turn_copy(s, d):
        target = (z + d) % context_count
        source = back_out.at[s, pl.ds(pl.multiple_of(target * tokens, tokens), tokens), :]
        row = pl.multiple_of((z * own_sequences + s) * tokens, tokens)
        destination = back_in.at[pl.ds(row, tokens), :]
        if d == 0:
            return pltpu.make_async_copy(source, destination, back_own.at[s])
        return remote(source, destination, *sem(turn_sems, s, d - 1), others[d - 1])

    def turned():
        for s in range(own_sequences):
            turn_copy(s, 0).wait()
            for d in range(1, context_count):
                turn_copy(s, d).wait_recv()


    def head_gradients():
        delta = dot(back_in[:, :cols], grads[...], ((0,), (0,))).astype(half_type)
        part[early_rows + 4 * late_other * piece :, :] = delta
        group = cols * half_width // width

        def half_rows(s, carry):
            owner = (1 - y) * (1 - s) + y * s
            column = pl.multiple_of(owner * half_width, half_width)
            delta = dot(
                first_rows[:, pl.ds(column, half_width)], back_in[:, cols:], ((0,), (0,))
            ).astype(half_type)
            top = pl.multiple_of(early_rows + s * 3 * group, group)
            for i in range(3):
                for j in range(width // cols):
                    part[pl.ds(top + i * group, group), j * cols : (j + 1) * cols] = delta[
                        j * group : (j + 1) * group, i * cols : (i + 1) * cols
                    ]
            return carry

        lax.fori_loop(0, 2, half_rows, 0)

    def output_rows():
        def step(i, carry):
            rows = pl.ds(pl.multiple_of(i * group_rows, group_rows), group_rows)
            value = dot(back_in[rows, :cols], outward[...])
            out_rows[rows, :] = (out_rows[rows, :].astype(f32) + value).astype(half_type)
            return carry

        lax.fori_loop(0, batch_count, step, 0)

    vector_start = len(stages)

    def first_back_rows():
        def step(i, carry):
            rows = pl.ds(pl.multiple_of(i * group_rows, group_rows), group_rows)
            value = dot(back_in[rows, cols:], inward[...], ((1,), (1,)))
            scaled[rows, :] = (scaled[rows, :].astype(f32) + value * gains[0]).astype(half_type)
            row_sums[2:3, :] += jnp.sum(value * normed_rows(rows), axis=0, keepdims=True)
            row_sums[3:4, :] += jnp.sum(value, axis=0, keepdims=True)
            return carry

        lax.fori_loop(0, batch_count, step, 0)
        out = vector_sum.at[vector_start]
        out[...] = jnp.zeros(out.shape, f32)

        def put(line, value):
            for j in range(value.shape[1] // 128):
                out[pl.ds(line + j, 1), :] = value[:, j * 128 : (j + 1) * 128]

        for i in range(3):
            put(i * lines + index * (cols // 128), inward_sum[i : i + 1, :])
        first = 3 * lines
        own_rows = pl.ds(pl.multiple_of((b * fsdp_count + y) * tokens, tokens), tokens)
        put(first, jnp.sum(grads[own_rows, :].astype(f32), axis=0, keepdims=True))
        first += lines
        put(first + index * (unit // 128), expand_total)
        first += unit * plane // 128
        for i in range(4):
            put(first, row_sums[i : i + 1, :])
            first += lines

    def vector_copy(i):
        source = vector_sum.at[vector_start if i == 0 else i - 1]
        return remote(source, vector_in.at[i], *sem(vector_sems, i), stages[i])


    arrays = (out_rows, scaled)

    def near_copy(a, c):
        row = pl.multiple_of((c * CORES + 1 - core) * group_rows, group_rows)
        return remote(
            arrays[a].at[pl.ds(row, group_rows), :],
            near.at[a, pl.ds(c * group_rows, group_rows), :],
            *sem(near_sems, a, c),
            sibling,
        )

    def across_copy(a, c):
        row = pl.multiple_of(c * group_rows + (1 - y) * tokens, tokens)
        return remote(
            near.at[a, pl.ds(row, tokens), :],
            across_in.at[a, pl.ds(c * tokens, tokens), :],
            *sem(across_sems, a, c),
            across,
        )

    def far_copy(a, d):
        row = pl.multiple_of((chip + d + 1) % chips * tokens, tokens)
        return remote(
            across_in.at[a, pl.ds(row, tokens), :], far.at[a, d], *sem(far_sems, a, d), peers[d]
        )

    def scatter_first(a):
        for c in range(chips):
            near_copy(a, c).start()

    def scatter_second(a):
        for c in range(chips):
            near_copy(a, c).wait_recv()

            def step(i, carry):
                row = pl.multiple_of((c * CORES + core) * group_rows + i * tokens, tokens)
                value = arrays[a][pl.ds(row, tokens), :].astype(f32)
                at = pl.ds(pl.multiple_of(c * group_rows + i * tokens, tokens), tokens)
                near[a, at, :] = (value + near[a, at, :].astype(f32)).astype(half_type)
                return carry

            lax.fori_loop(0, fsdp_count, step, 0)
            across_copy(a, c).start()

    def scatter_third(a):
        for c in range(chips):
            across_copy(a, c).wait_recv()

        def both(c):
            row = pl.multiple_of(c * group_rows + y * tokens, tokens)
            at = pl.ds(pl.multiple_of(c * tokens, tokens), tokens)
            return (
                near[a, pl.ds(row, tokens), :].astype(f32) + across_in[a, at, :].astype(f32),
                at,
            )

        for d in range(chips - 1):
            value, at = both((chip + d + 1) % chips)
            across_in[a, at, :] = value.astype(half_type)
            far_copy(a, d).start()
        token_sum[a] = both(chip)[0]

    def scatter_last(a):
        value = token_sum[a]
        for d in range(chips - 1):
            far_copy(a, d).wait_recv()
            value = value + far[a, d].astype(f32)
        own_rows = pl.ds(pl.multiple_of((b * fsdp_count + y) * tokens, tokens), tokens)
        x = inputs[own_rows, :].astype(f32)
        if a == 0:
            result_ref[...] = (x + (value + whole(1)) + whole(3)).astype(half_type)
            return
        normed = normed_rows(own_rows)
        middle = jnp.mean(value, axis=-1, keepdims=True)
        coupled = jnp.mean(value * normed, axis=-1, keepdims=True)
        back = stats[own_rows, 1:2] * (value - middle - normed * coupled)
        input_grad_ref[...] = grads[own_rows, :].astype(f32) + back


    problems = own_sequences * heads
    ready = READY
    if ready < ATT + problems or early <= ready + AHEAD:
        raise ValueError("schedule")
    plan = {}

    def at(slot, work):
        plan.setdefault(slot, []).append(work)

    def scatter(a, slot):
        at(slot, lambda: scatter_first(a))
        at(slot + 3, lambda: scatter_second(a))
        at(slot + 6, lambda: scatter_third(a))
        at(slot + 9, lambda: scatter_last(a))

    at(0, lambda: expand_half(1))
    at(1, contract_rows)
    for s in range(own_sequences):
        at(ATT + s * heads, lambda s=s: there(s))
    for i in range(batch_count):
        at(min(ATT + problems + i, ready), lambda i=i: hidden_tile(i))
    at(ready, turned)
    at(ready, head_gradients)
    at(ready + 1, output_rows)
    scatter(0, ready + 1)
    at(ready + 2, first_back_rows)
    scatter(1, ready + 2)
    at(ready + 2, lambda: vector_copy(0).start())
    for i in range(len(stages)):

        def vector_step(i=i):
            vector_copy(i).wait_recv()
            before = vector_sum[vector_start if i == 0 else i - 1]
            vector_sum[i] = before + vector_in[i]
            if i + 1 < len(stages):
                vector_copy(i + 1).start()

        at(ready + 4 + 3 * i, vector_step)

    def slot_step(t, carry):
        for work in (reduce_step, back_step, side_step):
            for half in range(2):
                work(t, half)

        for slot, works in sorted(plan.items()):

            @pl.when(t == slot)
            def _():
                for work in works:
                    work()

        @pl.when((t >= ATT) & (t < ATT + problems))
        def _():
            attend(t - ATT)

        return carry

    for half in range(2):

        @pl.when((z == 0) | (z == last))
        def _():
            for k in range(AHEAD):
                leaf_send(half, k)

    depth = context_count // 2
    tail = (LAG + LB) * depth + LX
    slots = max(steps + tail, early + late_other + tail + LY, max(plan) + 1)
    lax.fori_loop(0, slots, slot_step, 0)
    first = 0
    out_first = 0
    for count in (3 * lines, lines, unit * plane // 128, lines, lines, lines, lines):
        share_lines = count // fsdp_count
        for j in range(share_lines):
            line = first + y * share_lines + j
            shifts_ref[out_first + j : out_first + j + 1, :] = vector_sum[
                len(stages) - 1, pl.ds(line, 1), :
            ]
        first += count
        out_first += share_lines

    drain()
    small_copy.wait_send()
    inward_brought().wait_send()
    to_pair(parity).wait_send()
    weight_sends[3].wait_send()
    for array in range(2):
        to_across(array).wait_send()
        for d in range(chips - 1):
            to_peer(array, d).wait_send()
            on_to_peer(array, d).wait_send()
        for i in range(2 * chips):
            share(array, i).wait_send()
    away = (plane - own_sequences) * tokens
    for kind, (first, count) in enumerate(there_columns):
        at = mixed_out.at[pl.ds(0, away), pl.ds(first, count)]
        remote(at, at, there_sends.at[kind], there_recvs.at[0, 0, kind], others[0]).wait_send()
    for i in range(len(stages)):
        vector_copy(i).wait_send()
    for s in range(own_sequences):
        for d in range(1, context_count):
            turn_copy(s, d).wait_send()
    for a in range(2):
        for c in range(chips):
            near_copy(a, c).wait_send()
            across_copy(a, c).wait_send()
        for d in range(chips - 1):
            far_copy(a, d).wait_send()


def layer(layer_input, out_grad, span_order, small, inward, outward, expand, contract):
    sizes = tuple(lax.axis_size(name) for name in ("batch", "ctx", "fsdp"))
    batch_count, context_count, fsdp_count = sizes
    plane = batch_count * fsdp_count
    chips = batch_count // CORES
    tokens, width = layer_input.shape[1:]
    hidden = expand.shape[1]
    cols = width // plane
    heads = cols // HEAD_DIM
    length = tokens * context_count
    own_sequences = plane // context_count
    half = width // 2
    unit = hidden // plane
    early_other, early = (unit * half // width, 2 * unit * half // width + unit)
    late_other, late = (3 * cols * half // width, 6 * cols * half // width + cols)
    piece = 32
    for rows in (early_other, early - early_other, late_other, late - late_other):
        piece = math.gcd(piece, rows // 2)
    counts = tuple(n // 2 // piece for n in (early_other, early, late_other, late))
    steps = counts[1] + counts[3]
    rows = early + late
    stage_count = (plane * context_count).bit_length() - 1
    all_tokens = plane * tokens
    vector_lines = (8 * width + hidden) // 128
    dma = pltpu.SemaphoreType.DMA
    f32, half_type = (jnp.float32, layer_input.dtype)
    vmem = pl.BlockSpec(memory_space=pltpu.VMEM)
    hbm = pl.BlockSpec(memory_space=pl.ANY)

    def held(*shape, dtype=half_type):
        return pltpu.VMEM(shape, dtype)

    return pl.pallas_call(
        functools.partial(layer_kernel, sizes, tokens, heads, counts, piece),
        out_shape=(
            jax.ShapeDtypeStruct((batch_count, rows, width), half_type),
            jax.ShapeDtypeStruct((tokens, width), half_type),
            jax.ShapeDtypeStruct((tokens, width), f32),
            jax.ShapeDtypeStruct((vector_lines // fsdp_count, 128), f32),
        ),
        in_specs=[hbm, hbm, pl.BlockSpec(memory_space=pltpu.SMEM), vmem] + [hbm] * 4,
        out_specs=(hbm, vmem, vmem, vmem),
        scratch_shapes=[
            held(all_tokens, width),
            held(all_tokens, width),
            held(2, *small.shape, dtype=f32),
            held(width, 3 * cols),
            held(cols, width),
            held(width, unit),
            held(unit, width),
            held(length, cols, dtype=f32),
            held(length, cols, dtype=f32),
            held(all_tokens, 2, dtype=f32),
            held(all_tokens, width),
            held(all_tokens, width),
            held(all_tokens, 2 * unit),
            held(all_tokens, unit, dtype=f32),
            held(all_tokens, unit, dtype=f32),
            held(all_tokens, width),
            held(all_tokens, width),
            held(all_tokens, 4 * cols),
            held(own_sequences, length, 4 * cols),
            held(4, length, cols, dtype=f32),
            held(own_sequences, length, 4 * cols),
            held(all_tokens, 4 * cols),
            held(8, cols, dtype=f32),
            held(8, width, dtype=f32),
            held(rows, width),
            held(rows, width),
            held(rows, width),
            held(rows // 2, width),
            held(2, chips * fsdp_count * tokens, width),
            held(2, chips * tokens, width),
            held(2, chips - 1, tokens, width),
            held(2, tokens, width, dtype=f32),
            held(stage_count, vector_lines, 128, dtype=f32),
            held(stage_count + 1, vector_lines, 128, dtype=f32),
            dma((8,)),
            dma((2, 1)),
            dma((2, 2)),
            dma((2,)),
            dma((2, 2, 2 * chips - 1)),
            dma((2, 2, 2 * chips)),
            dma((2,)),
            dma((own_sequences, context_count, 2)),
            dma((own_sequences, 2)),
            dma((own_sequences,)),
            dma((2, own_sequences, context_count - 1)),
            dma((2,)),
            dma((2, steps)),
            dma((steps,)),
            dma((2, 2)),
            dma((2, steps)),
            dma,
            dma((2, counts[0] + counts[2])),
            dma((chips - 1,)),
            dma((chips - 1, 2, steps)),
            dma((2,)),
            dma,
            dma((2, 2, chips)),
            dma((2, 2, chips)),
            dma((2, 2, chips - 1)),
            dma((2, stage_count)),
        ],
        name="layer",
        compiler_params=pltpu.CompilerParams(
            collective_id=0, has_side_effects=True, vmem_limit_bytes=VMEM_LIMIT
        ),
    )(layer_input, out_grad, span_order, small, inward, outward, expand, contract)


def widen_kernel(
    cols,
    unit,
    turn_ref,
    all_ref,
    result_in,
    input_in,
    shifts_in,
    result_ref,
    input_ref,
    inward_ref,
    inward_shift,
    outward_ref,
    outward_shift,
    expand_ref,
    expand_shift,
    contract_ref,
    contract_shift,
    first_scale,
    first_shift,
    second_scale,
    second_shift,
    held,
    inward,
    outward,
    expand,
    contract,
    in_sems,
    out_sems,
    outward_sems,
    wide_sems,
):
    batch_count, rows, width = all_ref.shape
    half = inward_ref.shape[0]
    unit_rows, unit_blocks = (unit * half // width, width // unit)
    head_rows, head_blocks = (cols * half // width, width // cols)
    late = 2 * unit_rows + unit
    bounds = ((late, rows - late), (0, unit_rows), (unit_rows, unit_rows), (late - unit, unit))
    y = turn_ref[0]

    def load(b, part):
        first, count = bounds[part]
        at = pl.ds(first, count)
        return pltpu.make_async_copy(
            all_ref.at[b, at, :], held.at[b, at, :], in_sems.at[b, part]
        )

    def stores(b, part):
        at = b % 2
        pairs = []
        if part == 0:
            pairs.append((outward.at[b], outward_ref.at[pl.ds(b * cols, cols), :]))
        elif part < 3:
            owner = y if part == 2 else 1 - y
            column = pl.multiple_of((owner * batch_count + b) * unit, unit)
            pairs.append((expand.at[at, part - 1], expand_ref.at[:, pl.ds(column, unit)]))
        else:
            pairs.append((contract.at[at], contract_ref.at[pl.ds(b * unit, unit), :]))
        return [
            pltpu.make_async_copy(
                source, target, outward_sems.at[b] if part == 0 else out_sems.at[at, part - 1]
            )
            for source, target in pairs
        ]

    def wide_stores():
        group = batch_count * cols
        out = []
        for s in range(2):
            owner = y if s else 1 - y
            for i in range(3):
                column = pl.multiple_of(i * width + owner * group, group)
                out.append(
                    pltpu.make_async_copy(
                        inward.at[s, i],
                        inward_ref.at[:, pl.ds(column, group)],
                        wide_sems.at[s, i],
                    )
                )
        return out

    for b in range(batch_count):
        load(b, 0).start()
    for b in range(batch_count):
        for part in range(1, 4):
            load(b, part).start()
    result_ref[0] = result_in[...]
    input_ref[0] = input_in[...]
    line = 0
    for target in (
        inward_shift,
        outward_shift,
        expand_shift,
        second_scale,
        second_shift,
        first_scale,
        first_shift,
    ):
        count = target.shape[0]
        target[...] = shifts_in[line : line + count, :]
        line += count
    contract_shift[...] = outward_shift[...]

    for b in range(batch_count):
        load(b, 0).wait()
        for s in range(2):
            for i in range(3):
                top = late + (s * 3 + i) * head_rows
                for j in range(head_blocks):
                    inward[
                        s, i, j * head_rows : (j + 1) * head_rows, b * cols : (b + 1) * cols
                    ] = held[b, top : top + head_rows, j * cols : (j + 1) * cols].astype(jnp.float32)
        outward[b] = held[b, late + 6 * head_rows :, :].astype(jnp.float32)
        for copy in stores(b, 0):
            copy.start()
    for copy in wide_stores():
        copy.start()

    def step(b, carry):
        at = b % 2
        for part in range(1, 4):
            load(b, part).wait()

            @pl.when(b >= 2)
            def _():
                for copy in stores(b - 2, part):
                    copy.wait()

            if part < 3:
                first = (part - 1) * unit_rows
                for j in range(unit_blocks):
                    expand[at, part - 1, j * unit_rows : (j + 1) * unit_rows, :] = held[
                        b, first : first + unit_rows, j * unit : (j + 1) * unit
                    ].astype(jnp.float32)
            else:
                contract[at] = held[b, late - unit : late, :].astype(jnp.float32)
            for copy in stores(b, part):
                copy.start()
        return carry

    lax.fori_loop(0, batch_count, step, 0)
    for b in range(batch_count):
        for part in range(4):
            if part == 0 or b >= batch_count - 2:
                for copy in stores(b, part):
                    copy.wait()
    for copy in wide_stores():
        copy.wait()


def widen(gathered, result, input_delta, shifts, cols, unit):
    batch_count, rows, width = gathered.shape
    fsdp_count = lax.axis_size("fsdp")
    hidden = unit * batch_count * fsdp_count
    half = width // 2
    turn = lax.axis_index("fsdp").astype(jnp.int32)[None]
    f32 = jnp.float32
    dma = pltpu.SemaphoreType.DMA
    hbm = pl.BlockSpec(memory_space=pl.ANY)
    vmem = pl.BlockSpec(memory_space=pltpu.VMEM)

    def matrix(rows, columns):
        return jax.ShapeDtypeStruct((rows, columns), f32)

    def vector(size):
        return jax.ShapeDtypeStruct((size // fsdp_count // 128, 128), f32)

    out = pl.pallas_call(
        functools.partial(widen_kernel, cols, unit),
        out_shape=(
            jax.ShapeDtypeStruct((1,) + result.shape, result.dtype),
            jax.ShapeDtypeStruct((1,) + input_delta.shape, f32),
            matrix(half, 3 * width),
            vector(3 * width),
            matrix(half, width),
            vector(width),
            matrix(half, hidden),
            vector(hidden),
            matrix(hidden // 2, width),
            vector(width),
        )
        + (vector(width),) * 4,
        in_specs=[pl.BlockSpec(memory_space=pltpu.SMEM), hbm, vmem, vmem, vmem],
        out_specs=(vmem, vmem) + (hbm, vmem) * 4 + (vmem,) * 4,
        scratch_shapes=[
            pltpu.VMEM((batch_count, rows, width), gathered.dtype),
            pltpu.VMEM((2, 3, half, batch_count * cols), f32),
            pltpu.VMEM((batch_count, cols, width), f32),
            pltpu.VMEM((2, 2, half, unit), f32),
            pltpu.VMEM((2, unit, width), f32),
            dma((batch_count, 4)),
            dma((2, 3)),
            dma((batch_count,)),
            dma((2, 3)),
        ],
        name="widen",
        compiler_params=pltpu.CompilerParams(vmem_limit_bytes=VMEM_LIMIT),
    )(turn, gathered, result, input_delta, shifts)
    return tuple(a.reshape(-1) if a.ndim == 2 and a.shape[1] == 128 else a for a in out)


def dot(left, right, contract=((1,), (0,))):
    return lax.dot_general(left, right, (contract, ((), ())), preferred_element_type=jnp.float32)


def normalize(values):
    center = values - jnp.mean(values, axis=-1, keepdims=True)
    inverse = lax.rsqrt(jnp.mean(center * center, axis=-1, keepdims=True) + EPSILON)
    return (center * inverse, inverse)


def norm_backward(upstream, normed, inverse, factor):
    scaled = upstream * factor
    middle = jnp.mean(scaled, axis=-1, keepdims=True)
    coupled = jnp.mean(scaled * normed, axis=-1, keepdims=True)
    result = inverse * (scaled - middle - normed * coupled)
    return (result, jnp.sum(upstream * normed, axis=0), jnp.sum(upstream, axis=0))


def slot_positions(span_order, first_slot, slot_count, span_size):
    slot_index = first_slot + jnp.arange(slot_count, dtype=jnp.int32)
    owners = slot_index // (2 * span_size)
    places = jnp.arange(span_order.shape[0], dtype=jnp.int32)
    leading = jnp.sum(jnp.where(owners[:, None] == places[None, :], span_order[None, :], 0), axis=1)
    spans = 2 * span_order.shape[0]
    picked = jnp.where(slot_index // span_size % 2 == 0, leading, spans - 1 - leading)
    return picked * span_size + slot_index % span_size


def rotary_tables(positions):
    half_rot = ROT // 2
    angular = jnp.exp(
        jnp.arange(half_rot, dtype=jnp.float32) * (-2.0 * math.log(ROTARY_BASE) / ROT)
    )
    angles = positions.astype(jnp.float32)[:, None] * angular[None, :]
    angles = jnp.concatenate([angles, angles], axis=1)
    return (jnp.cos(angles), jnp.sin(angles))


def rotate(tensor, cosine, sine_table):
    half_rot = ROT // 2
    leading_part = tensor[..., :ROT]
    turned = jnp.concatenate([-leading_part[..., half_rot:], leading_part[..., :half_rot]], axis=-1)
    rotated = leading_part * cosine[:, None, :] + turned * sine_table[:, None, :]
    return jnp.concatenate([rotated, tensor[..., ROT:]], axis=-1)


def unrotate(tensor, cosine, sine_table):
    half_rot = ROT // 2
    leading_part = tensor[..., :ROT]
    weighted = leading_part * sine_table[:, None, :]
    turned = jnp.concatenate([weighted[..., half_rot:], -weighted[..., :half_rot]], axis=-1)
    return jnp.concatenate([leading_part * cosine[:, None, :] + turned, tensor[..., ROT:]], axis=-1)


def attention(mixed, place, cosine, sine_table, heads):
    sequences, length, _ = mixed.shape
    parts = mixed.reshape(sequences, length, 4, heads, HEAD_DIM)
    queries, keys, values, grads = (parts[:, :, i] for i in range(4))
    scale = 1.0 / math.sqrt(HEAD_DIM)
    scores = jnp.einsum("sqhd,skhd->shqk", queries, keys, preferred_element_type=jnp.float32)
    allowed = place[None, :] <= place[:, None]
    scores = jnp.where(allowed, scores * scale, MASKED)
    peak = jnp.max(scores, axis=-1, keepdims=True)
    log_total = peak + jnp.log(jnp.sum(jnp.exp(scores - peak), axis=-1, keepdims=True))
    probs = jnp.exp(scores - log_total)
    soft = probs.astype(jnp.bfloat16)
    context = jnp.einsum("shqk,skhd->sqhd", soft, values, preferred_element_type=jnp.float32)
    context = context.astype(jnp.bfloat16)
    delta = jnp.einsum(
        "sqhd,sqhd->shq", grads.astype(jnp.float32), context.astype(jnp.float32)
    )
    value_grad = jnp.einsum("shqk,sqhd->skhd", soft, grads, preferred_element_type=jnp.float32)
    probs_grad = jnp.einsum("sqhd,skhd->shqk", grads, values, preferred_element_type=jnp.float32)
    score_grad = (probs * (probs_grad - delta[..., None]) * scale).astype(jnp.bfloat16)
    query_grad = jnp.einsum("shqk,skhd->sqhd", score_grad, keys, preferred_element_type=jnp.float32)
    key_grad = jnp.einsum("shqk,sqhd->skhd", score_grad, queries, preferred_element_type=jnp.float32)
    query_grad = unrotate(query_grad, cosine, sine_table)
    key_grad = unrotate(key_grad, cosine, sine_table)
    back = jnp.stack([query_grad, key_grad, value_grad], axis=2)
    shift = jnp.sum(back, axis=(0, 1)).reshape(-1)
    full = jnp.concatenate([context[:, :, None], back.astype(jnp.bfloat16)], axis=2)
    return (full.reshape(sequences, length, 4 * heads * HEAD_DIM), shift)


def plain_body(
    layer_input,
    out_grad,
    span_order,
    inward,
    inward_bias,
    outward,
    outward_bias,
    expand,
    expand_bias,
    contract,
    contract_bias,
    first_gain,
    first_bias,
    second_gain,
    second_bias,
):
    batch_count, fsdp_count = (lax.axis_size("batch"), lax.axis_size("fsdp"))
    context_count = lax.axis_size("ctx")
    context_index = lax.axis_index("ctx")
    batch_index, fsdp_index = (lax.axis_index("batch"), lax.axis_index("fsdp"))
    plane = batch_count * fsdp_count
    tokens, width = layer_input.shape[1:]
    hidden_units = expand.shape[1]
    head_cols = width // plane
    unit_cols = hidden_units // plane
    heads = head_cols // HEAD_DIM
    length = tokens * context_count
    span_size = tokens // 2
    own_sequences = plane // context_count

    def full_vectors(*vectors):
        sizes = [v.shape[0] for v in vectors]
        gathered = lax.all_gather(jnp.concatenate(vectors), "fsdp")
        out, start = ([], 0)
        for size in sizes:
            out.append(gathered[:, start : start + size].reshape(-1).astype(jnp.float32))
            start += size
        return out

    (
        inward_offset,
        outward_offset,
        expand_offset,
        contract_offset,
        gain_first,
        offset_first,
        gain_second,
        offset_second,
    ) = full_vectors(
        inward_bias,
        outward_bias,
        expand_bias,
        contract_bias,
        first_gain,
        first_bias,
        second_gain,
        second_bias,
    )

    def chunk(array, cols):
        rows = array.shape[0]
        parts = array.reshape(rows, -1, fsdp_count, batch_count, cols)
        mine = lax.dynamic_index_in_dim(parts, batch_index, 3, keepdims=False)
        return mine.transpose(2, 0, 1, 3).reshape(fsdp_count, rows, -1)

    to_send = jnp.concatenate([chunk(inward, head_cols), chunk(expand, unit_cols)], axis=2)
    weights = lax.all_to_all(to_send, "fsdp", 0, 0).reshape(width, -1)
    inward_cols = weights[:, : 3 * head_cols]
    expand_cols = weights[:, 3 * head_cols :]
    outward_rows = lax.dynamic_slice_in_dim(outward, batch_index * head_cols, head_cols, 0)
    contract_rows = lax.dynamic_slice_in_dim(contract, batch_index * unit_cols, unit_cols, 0)
    plane_index = fsdp_index * batch_count + batch_index
    inward_shift_in = lax.dynamic_index_in_dim(
        inward_offset.reshape(3, plane, head_cols), plane_index, 1, keepdims=False
    ).reshape(-1)
    expand_shift_in = lax.dynamic_slice_in_dim(expand_offset, plane_index * unit_cols, unit_cols, 0)

    pair = jnp.stack([layer_input[0], out_grad[0]])
    pair_all = lax.all_gather(pair, PLANE, axis=1, tiled=True)
    grads_all = pair_all[1]
    rows_all = pair_all[0].astype(jnp.float32)
    normed, inverse = normalize(rows_all)
    first_rows = (normed * gain_first + offset_first).astype(jnp.bfloat16)
    second_rows = (normed * gain_second + offset_second).astype(jnp.bfloat16)

    local_place = slot_positions(span_order, context_index * tokens, tokens, span_size)
    cosine, sine_table = rotary_tables(local_place)
    cosine_plane = jnp.tile(cosine, (plane, 1))
    sine_plane = jnp.tile(sine_table, (plane, 1))
    projected = dot(first_rows, inward_cols) + inward_shift_in
    projected = projected.reshape(plane * tokens, 3 * heads, HEAD_DIM)
    turned = rotate(projected[:, : 2 * heads], cosine_plane, sine_plane)
    context_grad = dot(grads_all, outward_rows, ((1,), (1,)))
    mixed = jnp.concatenate(
        [
            turned.reshape(plane * tokens, -1),
            projected[:, 2 * heads :].reshape(plane * tokens, -1),
            context_grad,
        ],
        axis=1,
    ).astype(jnp.bfloat16)
    mixed = mixed.reshape(context_count, own_sequences, tokens, 4 * head_cols)
    mixed = lax.all_to_all(mixed, "ctx", 0, 0)
    mixed = mixed.transpose(1, 0, 2, 3).reshape(own_sequences, length, 4 * head_cols)
    place = slot_positions(span_order, 0, length, span_size)
    cosine_all, sine_all = rotary_tables(place)

    before = dot(second_rows, expand_cols) + expand_shift_in
    tail = 1.0 + lax.erf(before * HALF_ROOT)
    activated = (0.5 * before * tail).astype(jnp.bfloat16)
    slope = 0.5 * tail + before * jnp.exp(-0.5 * before * before) * NORMAL_PEAK
    before_grad = dot(grads_all, contract_rows, ((1,), (1,))) * slope
    expand_sum = jnp.sum(before_grad, axis=0)
    before_rows = before_grad.astype(jnp.bfloat16)
    expand_delta = dot(second_rows, before_rows, ((0,), (0,)))
    contract_delta = dot(activated, grads_all, ((0,), (0,)))
    out_part = dot(activated, contract_rows)
    second_part = dot(before_rows, expand_cols, ((1,), (1,)))

    hidden = layer_input[0].astype(jnp.float32)
    grad_float = out_grad[0].astype(jnp.float32)
    normed_mine, inverse_mine = normalize(hidden)
    half = width // fsdp_count

    def spread(values, sizes):
        wide = jnp.zeros((sizes[0], plane, sizes[1]), jnp.float32)
        values = values.reshape(sizes[0], sizes[1])
        return lax.dynamic_update_index_in_dim(wide, values, plane_index, 1).reshape(-1)

    bias_total = jnp.sum(grad_float, axis=0)
    expand_wide = spread(expand_sum, (1, unit_cols))

    back, inward_sum = attention(mixed, place, cosine_all, sine_all, heads)
    back = back.reshape(own_sequences, context_count, tokens, 4 * head_cols)
    back = lax.all_to_all(back.transpose(1, 0, 2, 3), "ctx", 0, 0)
    back = back.reshape(plane * tokens, 4 * head_cols)
    context_rows = back[:, :head_cols]
    projected_rows = back[:, head_cols:]
    inward_delta = dot(first_rows, projected_rows, ((0,), (0,)))
    outward_delta = dot(context_rows, grads_all, ((0,), (0,)))
    out_part = out_part + dot(context_rows, outward_rows)
    first_part = dot(projected_rows, inward_cols, ((1,), (1,)))
    stacked = jnp.stack([second_part, out_part, first_part], axis=1).astype(jnp.bfloat16)
    mine = lax.psum_scatter(stacked, PLANE, scatter_dimension=0, tiled=True)
    mine = mine.transpose(1, 0, 2).astype(jnp.float32)
    columns = jnp.concatenate([inward_delta, expand_delta], axis=1).astype(jnp.bfloat16)
    rows = jnp.concatenate([outward_delta, contract_delta], axis=0).astype(jnp.bfloat16)
    columns, rows = lax.psum((columns, rows), "ctx")
    columns = lax.all_to_all(columns.reshape(fsdp_count, half, -1), "fsdp", 0, 0)
    columns = lax.all_gather(columns, "batch")
    rows = lax.all_gather(rows, "batch").astype(jnp.float32)
    columns = columns.transpose(2, 1, 0, 3).astype(jnp.float32)
    inward_total = columns[..., : 3 * head_cols].reshape(
        half, fsdp_count, batch_count, 3, head_cols
    )
    totals = (
        inward_total.transpose(0, 3, 1, 2, 4).reshape(half, 3 * width),
        rows[:, :head_cols].reshape(half, width),
        columns[..., 3 * head_cols :].reshape(half, hidden_units),
        rows[:, head_cols:].reshape(-1, width),
    )
    _, second_scale, second_shift = norm_backward(
        mine[0], normed_mine, inverse_mine, gain_second
    )
    _, first_scale, first_shift = norm_backward(mine[2], normed_mine, inverse_mine, gain_first)
    vectors = [
        spread(inward_sum, (3, head_cols)),
        bias_total,
        expand_wide,
        first_scale,
        first_shift,
        second_scale,
        second_shift,
    ]
    whole = lax.psum(jnp.concatenate(vectors), ("batch", "ctx", "fsdp"))

    result = (hidden + (mine[1] + outward_offset) + contract_offset).astype(jnp.bfloat16)
    second_input, _, _ = norm_backward(mine[0], normed_mine, inverse_mine, gain_second)
    first_input, _, _ = norm_backward(mine[2], normed_mine, inverse_mine, gain_first)
    input_delta = grad_float + first_input + second_input
    halves, start = ([], 0)
    for vector in vectors:
        size = vector.shape[0] // fsdp_count
        halves.append(lax.dynamic_slice_in_dim(whole, start + fsdp_index * size, size, 0))
        start += vector.shape[0]
    return (
        result[None],
        input_delta[None],
        totals[0],
        halves[0],
        totals[1],
        halves[1],
        totals[2],
        halves[2],
        totals[3],
        halves[1],
        halves[3],
        halves[4],
        halves[5],
        halves[6],
    )


def body(
    layer_input,
    out_grad,
    span_order,
    inward,
    inward_bias,
    outward,
    outward_bias,
    expand,
    expand_bias,
    contract,
    contract_bias,
    first_gain,
    first_bias,
    second_gain,
    second_bias,
):
    plane = lax.axis_size("batch") * lax.axis_size("fsdp")
    width = layer_input.shape[2]
    if width // plane % 128:
        return plain_body(
            layer_input,
            out_grad,
            span_order,
            inward,
            inward_bias,
            outward,
            outward_bias,
            expand,
            expand_bias,
            contract,
            contract_bias,
            first_gain,
            first_bias,
            second_gain,
            second_bias,
        )
    vectors = (
        inward_bias,
        outward_bias,
        expand_bias,
        contract_bias,
        first_gain,
        first_bias,
        second_gain,
        second_bias,
    )
    ends = [sum(v.shape[0] for v in vectors[: i + 1]) for i in range(len(vectors))]
    room = ends[-1] + -ends[-1] % 1024
    small = sum(
        jnp.pad(v.astype(jnp.float32), (end - v.shape[0], room - end))
        for v, end in zip(vectors, ends)
    ).reshape(-1, 128)
    sums, result, input_delta, shifts = layer(
        layer_input, out_grad, span_order, small, inward, outward, expand, contract
    )
    return widen(sums, result, input_delta, shifts, width // plane, expand.shape[1] // plane)


def solution(mesh):
    rows = P(PLANE, "ctx", None)
    matrix, vector = (P("fsdp", None), P("fsdp"))
    in_specs = (rows, rows, P()) + (matrix, vector) * 4 + (vector,) * 4
    out_specs = (rows, rows) + (matrix, vector) * 4 + (vector,) * 4
    return jax.shard_map(body, mesh=mesh, in_specs=in_specs, out_specs=out_specs, check_vma=False)
```

```python
import functools
import math

import jax
import jax.numpy as jnp
from jax import lax
from jax.experimental import pallas as pl
from jax.experimental.pallas import tpu as pltpu
from jax.sharding import PartitionSpec as P

HEAD_DIM = 64
ROT = 16

EPSILON = 1e-05
ROTARY_BASE = 10000.0
MASKED = -1e30
HALF_ROOT = 0.7071067811865476
NORMAL_PEAK = 0.3989422804014327
PLANE = ("batch", "fsdp")


MESH = pl.DeviceIdType.MESH
CORES = 2
VMEM_LIMIT = 56 * 2**20


def here():
    return (lax.axis_index("batch"), lax.axis_index("ctx"), lax.axis_index("fsdp"))


def swapped(index, step):
    return index + step * (1 - 2 * (index // step % 2))


def greet(partners):
    barrier = pltpu.get_barrier_semaphore()
    for partner in partners:
        pl.semaphore_signal(barrier, inc=1, device_id=partner, device_id_type=MESH)
    pl.semaphore_wait(barrier, len(partners))


def remote(src, dst, send, recv, target):
    return pltpu.make_async_remote_copy(
        src_ref=src,
        dst_ref=dst,
        send_sem=send,
        recv_sem=recv,
        device_id=target,
        device_id_type=MESH,
    )


LAG = 2
LB = 2
LX = 2
LY = 3
AHEAD = 2
ATT = 4
READY = 11


def layer_kernel(
    sizes,
    tokens,
    heads,
    counts,
    piece,
    input_ref,
    grad_ref,
    order_ref,
    small_ref,
    inward_ref,
    outward_ref,
    expand_ref,
    contract_ref,
    sums_ref,
    result_ref,
    input_grad_ref,
    shifts_ref,
    inputs,
    grads,
    small,
    inward,
    outward,
    expand,
    contract,
    cosine,
    sine,
    stats,
    first_rows,
    second_rows,
    work,
    before,
    hidden_back,
    out_rows,
    scaled,
    mixed_out,
    mixed,
    heads_sum,
    back_out,
    back_in,
    inward_sum,
    row_sums,
    part,
    mine,
    reduced,
    reduced_right,
    near,
    across_in,
    far,
    token_sum,
    vector_in,
    vector_sum,
    load_sems,
    small_sems,
    weight_sems,
    pair_sems,
    gather_sems,
    share_sems,
    there_sends,
    there_recvs,
    there_own,
    back_own,
    turn_sems,
    reduce_sends,
    reduce_recvs,
    right_recvs,
    back_sends,
    back_recvs,
    row_sends,
    row_recvs,
    chip_sends,
    chip_recvs,
    core_sems,
    keep_sem,
    near_sems,
    across_sems,
    far_sems,
    vector_sems,
):
    batch_count, context_count, fsdp_count = sizes
    early_other, early, late_other, late = counts
    b, z, y = here()
    chips = batch_count // CORES
    core = b % CORES
    chip = b // CORES
    width = part.shape[1]
    half_width = width // 2
    cols = heads * HEAD_DIM
    unit = contract.shape[0]
    plane = batch_count * fsdp_count
    index = y * batch_count + b
    own_sequences = plane // context_count
    length = tokens * context_count
    steps = early + late
    early_rows = 2 * early * piece
    last = context_count - 1
    lines = width // 128
    f32, half_type = (jnp.float32, part.dtype)
    group_rows = fsdp_count * tokens

    sibling = (chip * CORES + (1 - core), z, y)
    across = (b, z, 1 - y)
    peers = [((chip + d) % chips * CORES + core, z, y) for d in range(1, chips)]
    sources = [(chip + chips - d) % chips * CORES + core for d in range(1, chips)]
    others = [(b, (z + d) % context_count, y) for d in range(1, context_count)]
    stages = []
    step = 1
    while step < batch_count:
        stages.append((swapped(b, step), z, y))
        step *= 2
    stages.append(across)
    step = 1
    while step < context_count:
        stages.append((b, swapped(z, step), y))
        step *= 2

    def sem(sems, *index):
        return (sems.at[(0, *index)], sems.at[(1, *index)])


    plane_arrays = (inputs, grads)
    plane_sources = (input_ref.at[0], grad_ref.at[0])

    def block(array, batch, fsdp):
        row = pl.multiple_of((batch * fsdp_count + fsdp) * tokens, tokens)
        return plane_arrays[array].at[pl.ds(row, tokens), :]

    def own_load(array):
        return pltpu.make_async_copy(
            plane_sources[array], block(array, b, y), load_sems.at[array]
        )

    def to_across(array):
        return remote(
            plane_sources[array], block(array, b, y), *sem(gather_sems, array, 0), across
        )

    def to_peer(array, d):
        return remote(
            plane_sources[array], block(array, b, y), *sem(gather_sems, array, 1 + d), peers[d]
        )

    def on_to_peer(array, d):
        at = block(array, b, 1 - y)
        return remote(at, at, *sem(gather_sems, array, chips + d), peers[d])

    def share(array, i):
        if i == 0:
            return remote(
                plane_sources[array], block(array, b, y), *sem(share_sems, array, 0), sibling
            )
        if i == 1:
            at = block(array, b, 1 - y)
        else:
            d = (i - 2) % (chips - 1)
            at = block(array, sources[d], y if i - 2 < chips - 1 else 1 - y)
        return remote(at, at, *sem(share_sems, array, i), sibling)

    def columns_of(owner, i):
        place = owner * batch_count + b
        if i < 3:
            return pl.ds(pl.multiple_of(i * width + place * cols, cols), cols)
        return pl.ds(pl.multiple_of(place * unit, unit), unit)

    part_rows = half_width // 2
    parity = z % 2
    pair = (b, swapped(z, 1), y)

    def inward_part(owner, parity):
        first = pl.multiple_of(owner * half_width + parity * part_rows, part_rows)
        return inward.at[pl.ds(first, part_rows), :]

    def weight_copies():
        source_rows = pl.ds(pl.multiple_of(parity * part_rows, part_rows), part_rows)
        rows = pl.ds(pl.multiple_of(y * half_width, half_width), half_width)
        out = [
            remote(
                inward_ref.at[source_rows, columns_of(1 - y, i)],
                inward_part(y, parity).at[:, i * cols : (i + 1) * cols],
                *sem(weight_sems, 0),
                across,
            )
            for i in range(3)
        ]
        out.append(
            remote(
                expand_ref.at[:, columns_of(1 - y, 3)],
                expand.at[rows, :],
                *sem(weight_sems, 1),
                across,
            )
        )
        return out

    def weight_own():
        rows = pl.ds(pl.multiple_of(y * half_width, half_width), half_width)
        pairs = [
            (inward_ref.at[:, columns_of(y, i)], inward.at[rows, i * cols : (i + 1) * cols])
            for i in range(3)
        ]
        pairs.append((expand_ref.at[:, columns_of(y, 3)], expand.at[rows, :]))
        return [
            pltpu.make_async_copy(source, target, load_sems.at[2 + i])
            for i, (source, target) in enumerate(pairs)
        ]

    def inward_brought():
        at = inward_part(1 - y, parity)
        return remote(at, at, *sem(weight_sems, 0), across)

    def to_pair(parity):
        at = inward_part(1 - y, parity)
        return remote(at, at, *sem(pair_sems), pair)

    row_loads = [
        pltpu.make_async_copy(
            outward_ref.at[pl.ds(pl.multiple_of(b * cols, cols), cols), :],
            outward,
            load_sems.at[6],
        ),
        pltpu.make_async_copy(
            contract_ref.at[pl.ds(pl.multiple_of(b * unit, unit), unit), :],
            contract,
            load_sems.at[7],
        ),
    ]
    weight_loads = weight_own()
    weight_sends = weight_copies()
    small_copy = remote(small_ref, small.at[1], *sem(small_sems, 0), across)

    own_load(0).start()
    own_load(1).start()
    for load in weight_loads + row_loads:
        load.start()
    greet([sibling, across] + peers + others)
    small_copy.start()

    def offer(array):
        to_across(array).start()
        share(array, 0).start()

    def offer_peers(array):
        for d in range(chips - 1):
            to_peer(array, d).start()

    for send in weight_sends[:3]:
        send.start()
    offer(0)
    offer_peers(0)
    offer(1)
    offer_peers(1)
    weight_sends[3].start()
    small[0] = small_ref[...]


    def positions(shape, dimension):
        slot = lax.broadcasted_iota(jnp.int32, shape, dimension)
        owner = slot // tokens
        leading = jnp.zeros(shape, jnp.int32)
        for c in range(context_count):
            leading = jnp.where(owner == c, order_ref[c], leading)
        span = tokens // 2
        second = slot // span % 2
        picked = jnp.where(second == 0, leading, 2 * context_count - 1 - leading)
        return picked * span + slot % span

    half_rot = ROT // 2
    lane = lax.broadcasted_iota(jnp.int32, (1, cols), 1) % HEAD_DIM
    angular = jnp.exp((lane % half_rot).astype(f32) * (-2.0 * math.log(ROTARY_BASE) / ROT))
    angles = positions((length, cols), 0).astype(f32) * angular
    cosine[...] = jnp.where(lane < ROT, jnp.cos(angles), 1.0)
    sine[...] = jnp.where(lane < ROT, jnp.sin(angles), 0.0)
    low = (lane < half_rot).astype(f32)
    high = 1.0 - low

    def turn(value, rows, sign):
        weight = sine[rows, :] * sign
        return (
            value * cosine[rows, :]
            - pltpu.roll(value, cols - half_rot, 1) * (weight * low)
            + pltpu.roll(value, half_rot, 1) * (weight * high)
        )


    small_copy.wait_recv()
    vector_rows = [3 * lines, lines, unit * plane // 128] + [lines] * 5
    starts = [sum(vector_rows[:i]) // fsdp_count for i in range(8)]

    def vector_line(which, line):
        share_lines = vector_rows[which] // fsdp_count
        owner = line // share_lines
        at = (owner - y) * (owner - y)
        return small[at, pl.ds(starts[which] + line % share_lines, 1), :]

    def whole(which):
        return jnp.concatenate([vector_line(which, line) for line in range(lines)], axis=1)

    def chunk(which, first, count):
        return jnp.concatenate([vector_line(which, first + i) for i in range(count)], axis=1)


    def group(u):
        return (chip + u // CORES) % chips * CORES + (core + u % CORES) % CORES

    def rows_of(u):
        return pl.ds(pl.multiple_of(group(u) * group_rows, group_rows), group_rows)

    def bring(array, u):
        distance, other = (u // CORES, u % CORES)
        if other == 0 and distance == 0:
            own_load(array).wait()
            if array == 0:
                to_across(array).wait_recv()
            for d in range(chips - 1):
                on_to_peer(array, d).start()
            share(array, 1).start()
        elif other == 0:
            d = chips - distance - 1
            to_peer(array, d).wait_recv()
            share(array, 2 + d).start()
            on_to_peer(array, d).wait_recv()
            share(array, 1 + chips + d).start()
        elif distance == 0:
            share(array, 0).wait_recv()
            share(array, 1).wait_recv()
        else:
            d = chips - distance - 1
            share(array, 2 + d).wait_recv()
            share(array, 1 + chips + d).wait_recv()

    gains = [whole(4), whole(5), whole(6), whole(7)]
    inward_bias = jnp.concatenate(
        [
            chunk(0, i * lines + index * (cols // 128), cols // 128)
            for i in range(3)
        ],
        axis=1,
    )

    def norm(u):
        rows = rows_of(u)
        x = inputs[rows, :].astype(f32)
        mean = jnp.mean(x, axis=-1, keepdims=True)
        center = x - mean
        inverse = lax.rsqrt(jnp.mean(center * center, axis=-1, keepdims=True) + EPSILON)
        stats[rows, 0:1] = mean
        stats[rows, 1:2] = inverse
        normed = center * inverse
        first_rows[rows, :] = (normed * gains[0] + gains[1]).astype(half_type)
        second_rows[rows, :] = (normed * gains[2] + gains[3]).astype(half_type)

    there_columns = ((0, 3 * cols), (3 * cols, cols))

    def there_copy(u, f, kind):
        p = group(u) * fsdp_count + f
        owner, s = (p // own_sequences, p % own_sequences)
        first, count = there_columns[kind]
        columns = pl.ds(first, count)
        source = mixed_out.at[pl.ds(pl.multiple_of(p * tokens, tokens), tokens), columns]
        at = pl.ds(pl.multiple_of(z * tokens, tokens), tokens)
        target = mixed.at[s, at, columns]

        @pl.when(owner == z)
        def _():
            pltpu.make_async_copy(source, target, there_own.at[s, kind]).start()

        @pl.when(owner != z)
        def _():
            remote(
                source, target, there_sends.at[kind], there_recvs.at[s, z, kind], (b, owner, y)
            ).start()

    def project(u):
        projected = dot(first_rows[rows_of(u), :], inward[...]) + inward_bias
        local = pl.ds(pl.multiple_of(z * tokens, tokens), tokens)
        for f in range(fsdp_count):
            at = pl.ds(pl.multiple_of((group(u) * fsdp_count + f) * tokens, tokens), tokens)
            piece_rows = projected[f * tokens : (f + 1) * tokens, :]
            for i in range(3):
                value = piece_rows[:, i * cols : (i + 1) * cols]
                if i < 2:
                    value = turn(value, local, 1.0)
                mixed_out[at, i * cols : (i + 1) * cols] = value.astype(half_type)
            there_copy(u, f, 0)

    def upstream(u):
        rows = rows_of(u)
        value = dot(grads[rows, :], outward[...], ((1,), (1,)))
        mixed_out[rows, 3 * cols :] = value.astype(half_type)
        for f in range(fsdp_count):
            there_copy(u, f, 1)

    def there(s):
        for kind, (first, count) in enumerate(there_columns):
            columns = pl.ds(first, count)
            block_at = mixed.at[s, pl.ds(0, tokens), columns]
            pltpu.make_async_copy(block_at, block_at, there_own.at[s, kind]).wait()
            for d in range(1, context_count):
                source = (z + d) % context_count
                at = mixed.at[s, pl.ds(pl.multiple_of(source * tokens, tokens), tokens), columns]
                recv = there_recvs.at[s, source, kind]
                remote(at, at, there_sends.at[kind], recv, others[0]).wait_recv()

    order = [u for u in range(0, batch_count, CORES)] + [u for u in range(1, batch_count, CORES)]
    bring(0, 0)
    inward_brought().wait_recv()
    to_pair(parity).start()
    norm(0)
    for i in range(3):
        weight_loads[i].wait()
    to_pair(1 - parity).wait_recv()
    project(0)
    to_across(1).wait_recv()
    for u in order[1:chips]:
        bring(0, u)
    bring(1, 0)
    row_loads[0].wait()
    for u in order[1:]:
        if u % CORES:
            bring(0, u)
        norm(u)
        project(u)
    upstream(0)
    for u in order[1:]:
        bring(1, u)
        upstream(u)


    row_loads[1].wait()
    weight_loads[3].wait()
    expand_bias = chunk(2, index * (unit // 128), unit // 128)
    nothing = jnp.zeros((1, width), f32)

    def normed_rows(rows):
        return (inputs[rows, :].astype(f32) - stats[rows, 0:1]) * stats[rows, 1:2]

    own_half = pl.ds(pl.multiple_of(y * half_width, half_width), half_width)
    other_half = pl.ds(pl.multiple_of((1 - y) * half_width, half_width), half_width)

    def early_tile(i, carry):
        rows = pl.ds(pl.multiple_of(i * group_rows, group_rows), group_rows)
        before[rows, :] = dot(second_rows[rows, own_half], expand[own_half, :]) + expand_bias
        hidden_back[rows, :] = dot(grads[rows, :], contract[...], ((1,), (1,)))
        return carry

    lax.fori_loop(0, batch_count, early_tile, 0)
    weight_sends[3].wait_recv()

    def forward_tile(i, expand_total):
        rows = pl.ds(pl.multiple_of(i * group_rows, group_rows), group_rows)
        value = before[rows, :] + dot(second_rows[rows, other_half], expand[other_half, :])
        tail = 1.0 + lax.erf(value * HALF_ROOT)
        slope = 0.5 * tail + value * jnp.exp(-0.5 * value * value) * NORMAL_PEAK
        before_grad = hidden_back[rows, :] * slope
        work[rows, :unit] = (0.5 * value * tail).astype(half_type)
        work[rows, unit:] = before_grad.astype(half_type)
        return expand_total + jnp.sum(before_grad, axis=0, keepdims=True)

    expand_total = lax.fori_loop(0, batch_count, forward_tile, jnp.zeros((1, unit), f32))
    row_sums[...] = jnp.zeros(row_sums.shape, f32)

    def hidden_tile(i):
        rows = pl.ds(pl.multiple_of(i * group_rows, group_rows), group_rows)
        out_rows[rows, :] = dot(work[rows, :unit], contract[...]).astype(half_type)
        value = dot(work[rows, unit:], expand[...], ((1,), (1,)))
        scaled[rows, :] = (value * gains[2]).astype(half_type)
        row_sums[0:1, :] += jnp.sum(value * normed_rows(rows), axis=0, keepdims=True)
        row_sums[1:2, :] += jnp.sum(value, axis=0, keepdims=True)

    def expand_half(s):
        owner = (1 - y) * (1 - s) + y * s
        column = pl.multiple_of(owner * half_width, half_width)
        delta = dot(second_rows[:, pl.ds(column, half_width)], work[:, unit:], ((0,), (0,)))
        group = unit * half_width // width
        at = pl.ds(pl.multiple_of(s * group, group), group)
        for j in range(width // unit):
            part[at, j * unit : (j + 1) * unit] = delta[j * group : (j + 1) * group, :].astype(
                half_type
            )

    def contract_rows():
        part[early_rows - unit : early_rows, :] = dot(
            work[:, :unit], grads[...], ((0,), (0,))
        ).astype(half_type)

    expand_half(0)


    def place(half, k):
        is_late = jnp.minimum(k // early, 1)
        other = early_other * (1 - is_late) + late_other * is_late
        count = early * (1 - is_late) + late * is_late
        j = k - early * is_late
        is_own = jnp.minimum(j // other, 1)
        row = (half * other + j) * (1 - is_own) + (
            2 * other + half * (count - other) + j - other
        ) * is_own
        return pl.multiple_of((2 * early * is_late + row) * piece, piece)

    def other_index(k):
        return k - (early - early_other) * jnp.minimum(k // early, 1)

    def own(k):
        is_late = jnp.minimum(k // early, 1)
        other = early_other * (1 - is_late) + late_other * is_late
        return jnp.minimum((k - early * is_late) // other, 1)

    def rows_at(ref, row):
        return ref.at[pl.ds(row, piece), :]

    def sums_at(batch, row):
        return sums_ref.at[batch, pl.ds(row, piece), :]

    def back_copy(half, k, side, target):
        at = rows_at(mine, place(half, k))
        return remote(at, at, back_sends.at[side, half], back_recvs.at[half, k], target)

    def row_copy(half, k):
        row = place(half, k)
        recv = row_recvs.at[half, other_index(k)]
        return remote(rows_at(mine, row), sums_at(b, row), row_sends, recv, across)

    def keep_copy(half, k):
        row = place(half, k)
        return pltpu.make_async_copy(rows_at(mine, row), sums_at(b, row), keep_sem)

    def chip_copy(d, half, k, from_mine):
        row = place(half, k)
        source = rows_at(mine, row) if from_mine else sums_at(b, row)
        return remote(
            source, sums_at(b, row), chip_sends.at[d], chip_recvs.at[d, half, k], peers[d]
        )

    def core_copy(half, k, from_mine, batch):
        row = place(half, k)
        source = rows_at(mine, row) if from_mine else sums_at(batch, row)
        return remote(
            source, sums_at(batch, row), core_sems.at[0], core_sems.at[1], sibling
        )

    def spread(half, k, from_mine):
        for d in range(chips - 1):
            chip_copy(d, half, k, from_mine).start()
        core_copy(half, k, from_mine, b).start()

    def arrived(half, k):
        for d in range(chips - 1):
            chip_copy(d, half, k, False).wait_recv()
            core_copy(half, k, False, sources[d]).start()

    def finish(half, k):
        @pl.when(own(k) == 0)
        def _():
            row_copy(half, k).start()

        @pl.when(own(k) == 1)
        def _():
            keep_copy(half, k).start()
            spread(half, k, True)

    left = (b, (z + last) % context_count, y)
    right = (b, (z + 1) % context_count, y)

    def reduce_copy(half, k, source, stream, target):
        row = place(half, k)
        if stream:
            landing = reduced_right.at[pl.ds(pl.multiple_of(k * piece, piece), piece), :]
            recv = right_recvs.at[k]
        else:
            landing = rows_at(reduced, row)
            recv = reduce_recvs.at[half, k]
        return remote(rows_at(source, row), landing, reduce_sends.at[half], recv, target)

    def ends(half):
        root = last // 2 if half == 0 else context_count // 2
        depth = max(root, last - root)
        at_root = z == root
        is_left = z < root
        distance = jnp.where(is_left, root - z, z - root)
        leaf = (z == 0) | (z == last)
        return root, depth, at_root, is_left, distance, leaf

    def pass_on(half, k, source):
        root = last // 2 if half == 0 else context_count // 2

        @pl.when(z == root + 1)
        def _():
            reduce_copy(half, k, source, 1, left).start()

        @pl.when(z > root + 1)
        def _():
            reduce_copy(half, k, source, 0, left).start()

        @pl.when(z < root)
        def _():
            reduce_copy(half, k, source, 0, right).start()

    def leaf_send(half, k):
        pass_on(half, k, part)

    def reduce_step(t, half):
        root, depth, at_root, is_left, distance, leaf = ends(half)
        k = t - LAG * (depth - distance)

        def send(source):
            pass_on(half, k, source)

        k_leaf = t + AHEAD

        @pl.when(leaf & jnp.logical_not(at_root) & (k_leaf < steps))
        def _():
            leaf_send(half, k_leaf)

        @pl.when(jnp.logical_not(leaf) & (k >= 0) & (k < steps))
        def _():
            row = place(half, k)
            here_at = pl.ds(row, piece)

            @pl.when(at_root)
            def _():
                value = part[here_at, :].astype(f32)
                if root > 0:
                    reduce_copy(half, k, part, 0, right).wait_recv()
                    value = value + reduced[here_at, :].astype(f32)
                if root < last:
                    reduce_copy(half, k, part, 1, left).wait_recv()
                    came = reduced_right[pl.ds(pl.multiple_of(k * piece, piece), piece), :]
                    value = value + came.astype(f32)
                mine[here_at, :] = value.astype(half_type)
                if root > 0:
                    back_copy(half, k, 0, left).start()
                if root < last:
                    back_copy(half, k, 1, right).start()
                finish(half, k)

            @pl.when(jnp.logical_not(at_root))
            def _():
                reduce_copy(half, k, part, 0, right).wait_recv()
                value = part[here_at, :].astype(f32) + reduced[here_at, :].astype(f32)
                reduced[here_at, :] = value.astype(half_type)
                send(reduced)

    def back_step(t, half):
        root, depth, at_root, is_left, distance, leaf = ends(half)
        k_back = t - LAG * depth - LB * distance

        @pl.when(jnp.logical_not(at_root) & (k_back >= 0) & (k_back < steps))
        def _():
            back_copy(half, k_back, 0, left).wait_recv()

            @pl.when(is_left & (z > 0))
            def _():
                back_copy(half, k_back, 0, left).start()

            @pl.when((z > root) & (z < last))
            def _():
                back_copy(half, k_back, 1, right).start()

            finish(half, k_back)

    def side_step(t, half):
        root, depth, at_root, is_left, distance, leaf = ends(half)
        k_row = t - LAG * depth - LB * distance - LX

        @pl.when((k_row >= 0) & (k_row < steps))
        def _():
            @pl.when(own(k_row) == 0)
            def _():
                row_copy(half, k_row).wait_recv()
                spread(half, k_row, False)

            @pl.when(own(k_row) == 1)
            def _():
                arrived(half, k_row)

        k_chip = k_row - LY

        @pl.when((k_chip >= 0) & (k_chip < steps))
        def _():
            @pl.when(own(k_chip) == 0)
            def _():
                arrived(half, k_chip)

    def drain():
        half_rows = pl.ds(0, steps * piece)
        other_count = 2 * (early_other + late_other) * piece

        def sent(ref, semaphore):
            remote(ref, ref, semaphore, core_sems.at[1], sibling).wait_send()

        everything = sums_ref.at[pl.ds(0, chips)]
        from_sibling = remote(everything, everything, core_sems.at[0], core_sems.at[1], sibling)
        from_sibling.wait_send()
        for d in range(chips - 1):
            sent(mine, chip_sends.at[d])
        sent(mine.at[pl.ds(0, other_count), :], row_sends)
        kept = mine.at[pl.ds(0, mine.shape[0] - other_count), :]
        pltpu.make_async_copy(kept, kept, keep_sem).wait()
        for half in range(2):
            root = last // 2 if half == 0 else context_count // 2

            @pl.when(z != root)
            def _():
                sent(mine.at[half_rows, :], reduce_sends.at[half])

            @pl.when((z <= root) & (z > 0))
            def _():
                sent(mine.at[half_rows, :], back_sends.at[0, half])

            @pl.when((z >= root) & (z < last))
            def _():
                sent(mine.at[half_rows, :], back_sends.at[1, half])

        from_sibling.wait_recv()


    def attend(n):
        s, h = (n // heads, n % heads)
        columns = [mixed[s, :, i * cols : (i + 1) * cols] for i in range(4)]
        head = lax.broadcasted_iota(jnp.int32, (length, cols), 1) // HEAD_DIM
        picked = head == h
        blank = jnp.zeros((length, cols), half_type)
        _, keys, values, _ = columns
        queries_h, keys_h, values_h, upstream_h = [
            jnp.where(picked, column, blank) for column in columns
        ]
        scale = 1.0 / math.sqrt(HEAD_DIM)
        allowed = positions((1, length), 1) <= positions((length, 1), 0)
        scores = dot(queries_h, keys, ((1,), (1,))) * scale
        scores = jnp.where(allowed, scores, MASKED)
        peak = jnp.max(scores, axis=1, keepdims=True)
        log_total = peak + jnp.log(jnp.sum(jnp.exp(scores - peak), axis=1, keepdims=True))
        probs = jnp.exp(scores - log_total)
        soft = probs.astype(half_type)
        context = dot(soft, values_h)
        delta = jnp.sum(
            upstream_h.astype(f32) * context.astype(half_type).astype(f32), axis=1, keepdims=True
        )
        probs_grad = dot(upstream_h, values, ((1,), (1,)))
        score_grad = (probs * (probs_grad - delta) * scale).astype(half_type)
        results = (
            context,
            dot(score_grad, keys_h),
            dot(score_grad, queries_h, ((0,), (0,))),
            dot(soft, upstream_h, ((0,), (0,))),
        )
        for i, value in enumerate(results):

            @pl.when(h == 0)
            def _():
                heads_sum[i] = value

            @pl.when(h > 0)
            def _():
                heads_sum[i] += value

        @pl.when(h == heads - 1)
        def _():
            back_out[s, :, :cols] = heads_sum[0].astype(half_type)
            for i in range(1, 4):
                value = heads_sum[i]
                if i < 3:
                    value = turn(value, slice(None), -1.0)
                back_out[s, :, i * cols : (i + 1) * cols] = value.astype(half_type)
                total = jnp.sum(value, axis=0, keepdims=True)

                @pl.when(s == 0)
                def _():
                    inward_sum[i - 1 : i, :] = total

                @pl.when(s > 0)
                def _():
                    inward_sum[i - 1 : i, :] += total

            for d in range(context_count):
                turn_copy(s, d).start()

    def turn_copy(s, d):
        target = (z + d) % context_count
        source = back_out.at[s, pl.ds(pl.multiple_of(target * tokens, tokens), tokens), :]
        row = pl.multiple_of((z * own_sequences + s) * tokens, tokens)
        destination = back_in.at[pl.ds(row, tokens), :]
        if d == 0:
            return pltpu.make_async_copy(source, destination, back_own.at[s])
        return remote(source, destination, *sem(turn_sems, s, d - 1), others[d - 1])

    def turned():
        for s in range(own_sequences):
            turn_copy(s, 0).wait()
            for d in range(1, context_count):
                turn_copy(s, d).wait_recv()


    def head_gradients():
        delta = dot(back_in[:, :cols], grads[...], ((0,), (0,))).astype(half_type)
        part[early_rows + 4 * late_other * piece :, :] = delta
        group = cols * half_width // width

        def half_rows(s, carry):
            owner = (1 - y) * (1 - s) + y * s
            column = pl.multiple_of(owner * half_width, half_width)
            delta = dot(
                first_rows[:, pl.ds(column, half_width)], back_in[:, cols:], ((0,), (0,))
            ).astype(half_type)
            top = pl.multiple_of(early_rows + s * 3 * group, group)
            for i in range(3):
                for j in range(width // cols):
                    part[pl.ds(top + i * group, group), j * cols : (j + 1) * cols] = delta[
                        j * group : (j + 1) * group, i * cols : (i + 1) * cols
                    ]
            return carry

        lax.fori_loop(0, 2, half_rows, 0)

    def output_rows():
        def step(i, carry):
            rows = pl.ds(pl.multiple_of(i * group_rows, group_rows), group_rows)
            value = dot(back_in[rows, :cols], outward[...])
            out_rows[rows, :] = (out_rows[rows, :].astype(f32) + value).astype(half_type)
            return carry

        lax.fori_loop(0, batch_count, step, 0)

    vector_start = len(stages)

    def first_back_rows():
        def step(i, carry):
            rows = pl.ds(pl.multiple_of(i * group_rows, group_rows), group_rows)
            value = dot(back_in[rows, cols:], inward[...], ((1,), (1,)))
            scaled[rows, :] = (scaled[rows, :].astype(f32) + value * gains[0]).astype(half_type)
            row_sums[2:3, :] += jnp.sum(value * normed_rows(rows), axis=0, keepdims=True)
            row_sums[3:4, :] += jnp.sum(value, axis=0, keepdims=True)
            return carry

        lax.fori_loop(0, batch_count, step, 0)
        out = vector_sum.at[vector_start]
        out[...] = jnp.zeros(out.shape, f32)

        def put(line, value):
            for j in range(value.shape[1] // 128):
                out[pl.ds(line + j, 1), :] = value[:, j * 128 : (j + 1) * 128]

        for i in range(3):
            put(i * lines + index * (cols // 128), inward_sum[i : i + 1, :])
        first = 3 * lines
        own_rows = pl.ds(pl.multiple_of((b * fsdp_count + y) * tokens, tokens), tokens)
        put(first, jnp.sum(grads[own_rows, :].astype(f32), axis=0, keepdims=True))
        first += lines
        put(first + index * (unit // 128), expand_total)
        first += unit * plane // 128
        for i in range(4):
            put(first, row_sums[i : i + 1, :])
            first += lines

    def vector_copy(i):
        source = vector_sum.at[vector_start if i == 0 else i - 1]
        return remote(source, vector_in.at[i], *sem(vector_sems, i), stages[i])


    arrays = (out_rows, scaled)

    def near_copy(a, c):
        row = pl.multiple_of((c * CORES + 1 - core) * group_rows, group_rows)
        return remote(
            arrays[a].at[pl.ds(row, group_rows), :],
            near.at[a, pl.ds(c * group_rows, group_rows), :],
            *sem(near_sems, a, c),
            sibling,
        )

    def across_copy(a, c):
        row = pl.multiple_of(c * group_rows + (1 - y) * tokens, tokens)
        return remote(
            near.at[a, pl.ds(row, tokens), :],
            across_in.at[a, pl.ds(c * tokens, tokens), :],
            *sem(across_sems, a, c),
            across,
        )

    def far_copy(a, d):
        row = pl.multiple_of((chip + d + 1) % chips * tokens, tokens)
        return remote(
            across_in.at[a, pl.ds(row, tokens), :], far.at[a, d], *sem(far_sems, a, d), peers[d]
        )

    def scatter_first(a):
        for c in range(chips):
            near_copy(a, c).start()

    def scatter_second(a):
        for c in range(chips):
            near_copy(a, c).wait_recv()

            def step(i, carry):
                row = pl.multiple_of((c * CORES + core) * group_rows + i * tokens, tokens)
                value = arrays[a][pl.ds(row, tokens), :].astype(f32)
                at = pl.ds(pl.multiple_of(c * group_rows + i * tokens, tokens), tokens)
                near[a, at, :] = (value + near[a, at, :].astype(f32)).astype(half_type)
                return carry

            lax.fori_loop(0, fsdp_count, step, 0)
            across_copy(a, c).start()

    def scatter_third(a):
        for c in range(chips):
            across_copy(a, c).wait_recv()

        def both(c):
            row = pl.multiple_of(c * group_rows + y * tokens, tokens)
            at = pl.ds(pl.multiple_of(c * tokens, tokens), tokens)
            return (
                near[a, pl.ds(row, tokens), :].astype(f32) + across_in[a, at, :].astype(f32),
                at,
            )

        for d in range(chips - 1):
            value, at = both((chip + d + 1) % chips)
            across_in[a, at, :] = value.astype(half_type)
            far_copy(a, d).start()
        token_sum[a] = both(chip)[0]

    def scatter_last(a):
        value = token_sum[a]
        for d in range(chips - 1):
            far_copy(a, d).wait_recv()
            value = value + far[a, d].astype(f32)
        own_rows = pl.ds(pl.multiple_of((b * fsdp_count + y) * tokens, tokens), tokens)
        x = inputs[own_rows, :].astype(f32)
        if a == 0:
            result_ref[...] = (x + (value + whole(1)) + whole(3)).astype(half_type)
            return
        normed = normed_rows(own_rows)
        middle = jnp.mean(value, axis=-1, keepdims=True)
        coupled = jnp.mean(value * normed, axis=-1, keepdims=True)
        back = stats[own_rows, 1:2] * (value - middle - normed * coupled)
        input_grad_ref[...] = grads[own_rows, :].astype(f32) + back


    problems = own_sequences * heads
    ready = READY
    if ready < ATT + problems or early <= ready + AHEAD:
        raise ValueError("schedule")
    plan = {}

    def at(slot, work):
        plan.setdefault(slot, []).append(work)

    def scatter(a, slot):
        at(slot, lambda: scatter_first(a))
        at(slot + 3, lambda: scatter_second(a))
        at(slot + 6, lambda: scatter_third(a))
        at(slot + 9, lambda: scatter_last(a))

    at(0, lambda: expand_half(1))
    at(1, contract_rows)
    for s in range(own_sequences):
        at(ATT + s * heads, lambda s=s: there(s))
    for i in range(batch_count):
        at(2 + i // 2, lambda i=i: hidden_tile(i))
    at(ready, turned)
    at(ready, head_gradients)
    at(ready + 1, output_rows)
    scatter(0, ready + 1)
    at(ready + 2, first_back_rows)
    scatter(1, ready + 2)
    at(ready + 2, lambda: vector_copy(0).start())
    for i in range(len(stages)):

        def vector_step(i=i):
            vector_copy(i).wait_recv()
            before = vector_sum[vector_start if i == 0 else i - 1]
            vector_sum[i] = before + vector_in[i]
            if i + 1 < len(stages):
                vector_copy(i + 1).start()

        at(ready + 5 + 4 * i, vector_step)

    def slot_step(t, carry):
        for work in (reduce_step, back_step, side_step):
            for half in range(2):
                work(t, half)

        for slot, works in sorted(plan.items()):

            @pl.when(t == slot)
            def _():
                for work in works:
                    work()

        @pl.when((t >= ATT) & (t < ATT + problems))
        def _():
            attend(t - ATT)

        return carry

    for half in range(2):

        @pl.when((z == 0) | (z == last))
        def _():
            for k in range(AHEAD):
                leaf_send(half, k)

    depth = context_count // 2
    tail = (LAG + LB) * depth + LX
    slots = max(steps + tail, early + late_other + tail + LY, max(plan) + 1)
    lax.fori_loop(0, slots, slot_step, 0)
    first = 0
    out_first = 0
    for count in (3 * lines, lines, unit * plane // 128, lines, lines, lines, lines):
        share_lines = count // fsdp_count
        for j in range(share_lines):
            line = first + y * share_lines + j
            shifts_ref[out_first + j : out_first + j + 1, :] = vector_sum[
                len(stages) - 1, pl.ds(line, 1), :
            ]
        first += count
        out_first += share_lines

    drain()
    small_copy.wait_send()
    inward_brought().wait_send()
    to_pair(parity).wait_send()
    weight_sends[3].wait_send()
    for array in range(2):
        to_across(array).wait_send()
        for d in range(chips - 1):
            to_peer(array, d).wait_send()
            on_to_peer(array, d).wait_send()
        for i in range(2 * chips):
            share(array, i).wait_send()
    away = (plane - own_sequences) * tokens
    for kind, (first, count) in enumerate(there_columns):
        at = mixed_out.at[pl.ds(0, away), pl.ds(first, count)]
        remote(at, at, there_sends.at[kind], there_recvs.at[0, 0, kind], others[0]).wait_send()
    for i in range(len(stages)):
        vector_copy(i).wait_send()
    for s in range(own_sequences):
        for d in range(1, context_count):
            turn_copy(s, d).wait_send()
    for a in range(2):
        for c in range(chips):
            near_copy(a, c).wait_send()
            across_copy(a, c).wait_send()
        for d in range(chips - 1):
            far_copy(a, d).wait_send()


def layer(layer_input, out_grad, span_order, small, inward, outward, expand, contract):
    sizes = tuple(lax.axis_size(name) for name in ("batch", "ctx", "fsdp"))
    batch_count, context_count, fsdp_count = sizes
    plane = batch_count * fsdp_count
    chips = batch_count // CORES
    tokens, width = layer_input.shape[1:]
    hidden = expand.shape[1]
    cols = width // plane
    heads = cols // HEAD_DIM
    length = tokens * context_count
    own_sequences = plane // context_count
    half = width // 2
    unit = hidden // plane
    early_other, early = (unit * half // width, 2 * unit * half // width + unit)
    late_other, late = (3 * cols * half // width, 6 * cols * half // width + cols)
    piece = 32
    for rows in (early_other, early - early_other, late_other, late - late_other):
        piece = math.gcd(piece, rows // 2)
    counts = tuple(n // 2 // piece for n in (early_other, early, late_other, late))
    steps = counts[1] + counts[3]
    rows = early + late
    stage_count = (plane * context_count).bit_length() - 1
    all_tokens = plane * tokens
    vector_lines = (8 * width + hidden) // 128
    dma = pltpu.SemaphoreType.DMA
    f32, half_type = (jnp.float32, layer_input.dtype)
    vmem = pl.BlockSpec(memory_space=pltpu.VMEM)
    hbm = pl.BlockSpec(memory_space=pl.ANY)

    def held(*shape, dtype=half_type):
        return pltpu.VMEM(shape, dtype)

    return pl.pallas_call(
        functools.partial(layer_kernel, sizes, tokens, heads, counts, piece),
        out_shape=(
            jax.ShapeDtypeStruct((batch_count, rows, width), half_type),
            jax.ShapeDtypeStruct((tokens, width), half_type),
            jax.ShapeDtypeStruct((tokens, width), f32),
            jax.ShapeDtypeStruct((vector_lines // fsdp_count, 128), f32),
        ),
        in_specs=[hbm, hbm, pl.BlockSpec(memory_space=pltpu.SMEM), vmem] + [hbm] * 4,
        out_specs=(hbm, vmem, vmem, vmem),
        scratch_shapes=[
            held(all_tokens, width),
            held(all_tokens, width),
            held(2, *small.shape, dtype=f32),
            held(width, 3 * cols),
            held(cols, width),
            held(width, unit),
            held(unit, width),
            held(length, cols, dtype=f32),
            held(length, cols, dtype=f32),
            held(all_tokens, 2, dtype=f32),
            held(all_tokens, width),
            held(all_tokens, width),
            held(all_tokens, 2 * unit),
            held(all_tokens, unit, dtype=f32),
            held(all_tokens, unit, dtype=f32),
            held(all_tokens, width),
            held(all_tokens, width),
            held(all_tokens, 4 * cols),
            held(own_sequences, length, 4 * cols),
            held(4, length, cols, dtype=f32),
            held(own_sequences, length, 4 * cols),
            held(all_tokens, 4 * cols),
            held(8, cols, dtype=f32),
            held(8, width, dtype=f32),
            held(rows, width),
            held(rows, width),
            held(rows, width),
            held(rows // 2, width),
            held(2, chips * fsdp_count * tokens, width),
            held(2, chips * tokens, width),
            held(2, chips - 1, tokens, width),
            held(2, tokens, width, dtype=f32),
            held(stage_count, vector_lines, 128, dtype=f32),
            held(stage_count + 1, vector_lines, 128, dtype=f32),
            dma((8,)),
            dma((2, 1)),
            dma((2, 2)),
            dma((2,)),
            dma((2, 2, 2 * chips - 1)),
            dma((2, 2, 2 * chips)),
            dma((2,)),
            dma((own_sequences, context_count, 2)),
            dma((own_sequences, 2)),
            dma((own_sequences,)),
            dma((2, own_sequences, context_count - 1)),
            dma((2,)),
            dma((2, steps)),
            dma((steps,)),
            dma((2, 2)),
            dma((2, steps)),
            dma,
            dma((2, counts[0] + counts[2])),
            dma((chips - 1,)),
            dma((chips - 1, 2, steps)),
            dma((2,)),
            dma,
            dma((2, 2, chips)),
            dma((2, 2, chips)),
            dma((2, 2, chips - 1)),
            dma((2, stage_count)),
        ],
        name="layer",
        compiler_params=pltpu.CompilerParams(
            collective_id=0, has_side_effects=True, vmem_limit_bytes=VMEM_LIMIT
        ),
    )(layer_input, out_grad, span_order, small, inward, outward, expand, contract)


def widen_kernel(
    cols,
    unit,
    turn_ref,
    all_ref,
    result_in,
    input_in,
    shifts_in,
    result_ref,
    input_ref,
    inward_ref,
    inward_shift,
    outward_ref,
    outward_shift,
    expand_ref,
    expand_shift,
    contract_ref,
    contract_shift,
    first_scale,
    first_shift,
    second_scale,
    second_shift,
    held,
    inward,
    outward,
    expand,
    contract,
    in_sems,
    out_sems,
    outward_sems,
    wide_sems,
):
    batch_count, rows, width = all_ref.shape
    half = inward_ref.shape[0]
    unit_rows, unit_blocks = (unit * half // width, width // unit)
    head_rows, head_blocks = (cols * half // width, width // cols)
    late = 2 * unit_rows + unit
    bounds = ((late, rows - late), (0, unit_rows), (unit_rows, unit_rows), (late - unit, unit))
    y = turn_ref[0]

    def load(b, part):
        first, count = bounds[part]
        at = pl.ds(first, count)
        return pltpu.make_async_copy(
            all_ref.at[b, at, :], held.at[b, at, :], in_sems.at[b, part]
        )

    def stores(b, part):
        at = b % 2
        pairs = []
        if part == 0:
            pairs.append((outward.at[b], outward_ref.at[pl.ds(b * cols, cols), :]))
        elif part < 3:
            owner = y if part == 2 else 1 - y
            column = pl.multiple_of((owner * batch_count + b) * unit, unit)
            pairs.append((expand.at[at, part - 1], expand_ref.at[:, pl.ds(column, unit)]))
        else:
            pairs.append((contract.at[at], contract_ref.at[pl.ds(b * unit, unit), :]))
        return [
            pltpu.make_async_copy(
                source, target, outward_sems.at[b] if part == 0 else out_sems.at[at, part - 1]
            )
            for source, target in pairs
        ]

    def wide_stores():
        group = batch_count * cols
        out = []
        for s in range(2):
            owner = y if s else 1 - y
            for i in range(3):
                column = pl.multiple_of(i * width + owner * group, group)
                out.append(
                    pltpu.make_async_copy(
                        inward.at[s, i],
                        inward_ref.at[:, pl.ds(column, group)],
                        wide_sems.at[s, i],
                    )
                )
        return out

    for b in range(batch_count):
        load(b, 0).start()
    for b in range(batch_count):
        for part in range(1, 4):
            load(b, part).start()
    result_ref[0] = result_in[...]
    input_ref[0] = input_in[...]
    line = 0
    for target in (
        inward_shift,
        outward_shift,
        expand_shift,
        second_scale,
        second_shift,
        first_scale,
        first_shift,
    ):
        count = target.shape[0]
        target[...] = shifts_in[line : line + count, :]
        line += count
    contract_shift[...] = outward_shift[...]

    for b in range(batch_count):
        load(b, 0).wait()
        for s in range(2):
            for i in range(3):
                top = late + (s * 3 + i) * head_rows
                for j in range(head_blocks):
                    inward[
                        s, i, j * head_rows : (j + 1) * head_rows, b * cols : (b + 1) * cols
                    ] = held[b, top : top + head_rows, j * cols : (j + 1) * cols].astype(jnp.float32)
        outward[b] = held[b, late + 6 * head_rows :, :].astype(jnp.float32)
        for copy in stores(b, 0):
            copy.start()
    for copy in wide_stores():
        copy.start()

    def step(b, carry):
        at = b % 2
        for part in range(1, 4):
            load(b, part).wait()

            @pl.when(b >= 2)
            def _():
                for copy in stores(b - 2, part):
                    copy.wait()

            if part < 3:
                first = (part - 1) * unit_rows
                for j in range(unit_blocks):
                    expand[at, part - 1, j * unit_rows : (j + 1) * unit_rows, :] = held[
                        b, first : first + unit_rows, j * unit : (j + 1) * unit
                    ].astype(jnp.float32)
            else:
                contract[at] = held[b, late - unit : late, :].astype(jnp.float32)
            for copy in stores(b, part):
                copy.start()
        return carry

    lax.fori_loop(0, batch_count, step, 0)
    for b in range(batch_count):
        for part in range(4):
            if part == 0 or b >= batch_count - 2:
                for copy in stores(b, part):
                    copy.wait()
    for copy in wide_stores():
        copy.wait()


def widen(gathered, result, input_delta, shifts, cols, unit):
    batch_count, rows, width = gathered.shape
    fsdp_count = lax.axis_size("fsdp")
    hidden = unit * batch_count * fsdp_count
    half = width // 2
    turn = lax.axis_index("fsdp").astype(jnp.int32)[None]
    f32 = jnp.float32
    dma = pltpu.SemaphoreType.DMA
    hbm = pl.BlockSpec(memory_space=pl.ANY)
    vmem = pl.BlockSpec(memory_space=pltpu.VMEM)

    def matrix(rows, columns):
        return jax.ShapeDtypeStruct((rows, columns), f32)

    def vector(size):
        return jax.ShapeDtypeStruct((size // fsdp_count // 128, 128), f32)

    out = pl.pallas_call(
        functools.partial(widen_kernel, cols, unit),
        out_shape=(
            jax.ShapeDtypeStruct((1,) + result.shape, result.dtype),
            jax.ShapeDtypeStruct((1,) + input_delta.shape, f32),
            matrix(half, 3 * width),
            vector(3 * width),
            matrix(half, width),
            vector(width),
            matrix(half, hidden),
            vector(hidden),
            matrix(hidden // 2, width),
            vector(width),
        )
        + (vector(width),) * 4,
        in_specs=[pl.BlockSpec(memory_space=pltpu.SMEM), hbm, vmem, vmem, vmem],
        out_specs=(vmem, vmem) + (hbm, vmem) * 4 + (vmem,) * 4,
        scratch_shapes=[
            pltpu.VMEM((batch_count, rows, width), gathered.dtype),
            pltpu.VMEM((2, 3, half, batch_count * cols), f32),
            pltpu.VMEM((batch_count, cols, width), f32),
            pltpu.VMEM((2, 2, half, unit), f32),
            pltpu.VMEM((2, unit, width), f32),
            dma((batch_count, 4)),
            dma((2, 3)),
            dma((batch_count,)),
            dma((2, 3)),
        ],
        name="widen",
        compiler_params=pltpu.CompilerParams(vmem_limit_bytes=VMEM_LIMIT),
    )(turn, gathered, result, input_delta, shifts)
    return tuple(a.reshape(-1) if a.ndim == 2 and a.shape[1] == 128 else a for a in out)


def dot(left, right, contract=((1,), (0,))):
    return lax.dot_general(left, right, (contract, ((), ())), preferred_element_type=jnp.float32)


def normalize(values):
    center = values - jnp.mean(values, axis=-1, keepdims=True)
    inverse = lax.rsqrt(jnp.mean(center * center, axis=-1, keepdims=True) + EPSILON)
    return (center * inverse, inverse)


def norm_backward(upstream, normed, inverse, factor):
    scaled = upstream * factor
    middle = jnp.mean(scaled, axis=-1, keepdims=True)
    coupled = jnp.mean(scaled * normed, axis=-1, keepdims=True)
    result = inverse * (scaled - middle - normed * coupled)
    return (result, jnp.sum(upstream * normed, axis=0), jnp.sum(upstream, axis=0))


def slot_positions(span_order, first_slot, slot_count, span_size):
    slot_index = first_slot + jnp.arange(slot_count, dtype=jnp.int32)
    owners = slot_index // (2 * span_size)
    places = jnp.arange(span_order.shape[0], dtype=jnp.int32)
    leading = jnp.sum(jnp.where(owners[:, None] == places[None, :], span_order[None, :], 0), axis=1)
    spans = 2 * span_order.shape[0]
    picked = jnp.where(slot_index // span_size % 2 == 0, leading, spans - 1 - leading)
    return picked * span_size + slot_index % span_size


def rotary_tables(positions):
    half_rot = ROT // 2
    angular = jnp.exp(
        jnp.arange(half_rot, dtype=jnp.float32) * (-2.0 * math.log(ROTARY_BASE) / ROT)
    )
    angles = positions.astype(jnp.float32)[:, None] * angular[None, :]
    angles = jnp.concatenate([angles, angles], axis=1)
    return (jnp.cos(angles), jnp.sin(angles))


def rotate(tensor, cosine, sine_table):
    half_rot = ROT // 2
    leading_part = tensor[..., :ROT]
    turned = jnp.concatenate([-leading_part[..., half_rot:], leading_part[..., :half_rot]], axis=-1)
    rotated = leading_part * cosine[:, None, :] + turned * sine_table[:, None, :]
    return jnp.concatenate([rotated, tensor[..., ROT:]], axis=-1)


def unrotate(tensor, cosine, sine_table):
    half_rot = ROT // 2
    leading_part = tensor[..., :ROT]
    weighted = leading_part * sine_table[:, None, :]
    turned = jnp.concatenate([weighted[..., half_rot:], -weighted[..., :half_rot]], axis=-1)
    return jnp.concatenate([leading_part * cosine[:, None, :] + turned, tensor[..., ROT:]], axis=-1)


def attention(mixed, place, cosine, sine_table, heads):
    sequences, length, _ = mixed.shape
    parts = mixed.reshape(sequences, length, 4, heads, HEAD_DIM)
    queries, keys, values, grads = (parts[:, :, i] for i in range(4))
    scale = 1.0 / math.sqrt(HEAD_DIM)
    scores = jnp.einsum("sqhd,skhd->shqk", queries, keys, preferred_element_type=jnp.float32)
    allowed = place[None, :] <= place[:, None]
    scores = jnp.where(allowed, scores * scale, MASKED)
    peak = jnp.max(scores, axis=-1, keepdims=True)
    log_total = peak + jnp.log(jnp.sum(jnp.exp(scores - peak), axis=-1, keepdims=True))
    probs = jnp.exp(scores - log_total)
    soft = probs.astype(jnp.bfloat16)
    context = jnp.einsum("shqk,skhd->sqhd", soft, values, preferred_element_type=jnp.float32)
    context = context.astype(jnp.bfloat16)
    delta = jnp.einsum(
        "sqhd,sqhd->shq", grads.astype(jnp.float32), context.astype(jnp.float32)
    )
    value_grad = jnp.einsum("shqk,sqhd->skhd", soft, grads, preferred_element_type=jnp.float32)
    probs_grad = jnp.einsum("sqhd,skhd->shqk", grads, values, preferred_element_type=jnp.float32)
    score_grad = (probs * (probs_grad - delta[..., None]) * scale).astype(jnp.bfloat16)
    query_grad = jnp.einsum("shqk,skhd->sqhd", score_grad, keys, preferred_element_type=jnp.float32)
    key_grad = jnp.einsum("shqk,sqhd->skhd", score_grad, queries, preferred_element_type=jnp.float32)
    query_grad = unrotate(query_grad, cosine, sine_table)
    key_grad = unrotate(key_grad, cosine, sine_table)
    back = jnp.stack([query_grad, key_grad, value_grad], axis=2)
    shift = jnp.sum(back, axis=(0, 1)).reshape(-1)
    full = jnp.concatenate([context[:, :, None], back.astype(jnp.bfloat16)], axis=2)
    return (full.reshape(sequences, length, 4 * heads * HEAD_DIM), shift)


def plain_body(
    layer_input,
    out_grad,
    span_order,
    inward,
    inward_bias,
    outward,
    outward_bias,
    expand,
    expand_bias,
    contract,
    contract_bias,
    first_gain,
    first_bias,
    second_gain,
    second_bias,
):
    batch_count, fsdp_count = (lax.axis_size("batch"), lax.axis_size("fsdp"))
    context_count = lax.axis_size("ctx")
    context_index = lax.axis_index("ctx")
    batch_index, fsdp_index = (lax.axis_index("batch"), lax.axis_index("fsdp"))
    plane = batch_count * fsdp_count
    tokens, width = layer_input.shape[1:]
    hidden_units = expand.shape[1]
    head_cols = width // plane
    unit_cols = hidden_units // plane
    heads = head_cols // HEAD_DIM
    length = tokens * context_count
    span_size = tokens // 2
    own_sequences = plane // context_count

    def full_vectors(*vectors):
        sizes = [v.shape[0] for v in vectors]
        gathered = lax.all_gather(jnp.concatenate(vectors), "fsdp")
        out, start = ([], 0)
        for size in sizes:
            out.append(gathered[:, start : start + size].reshape(-1).astype(jnp.float32))
            start += size
        return out

    (
        inward_offset,
        outward_offset,
        expand_offset,
        contract_offset,
        gain_first,
        offset_first,
        gain_second,
        offset_second,
    ) = full_vectors(
        inward_bias,
        outward_bias,
        expand_bias,
        contract_bias,
        first_gain,
        first_bias,
        second_gain,
        second_bias,
    )

    def chunk(array, cols):
        rows = array.shape[0]
        parts = array.reshape(rows, -1, fsdp_count, batch_count, cols)
        mine = lax.dynamic_index_in_dim(parts, batch_index, 3, keepdims=False)
        return mine.transpose(2, 0, 1, 3).reshape(fsdp_count, rows, -1)

    to_send = jnp.concatenate([chunk(inward, head_cols), chunk(expand, unit_cols)], axis=2)
    weights = lax.all_to_all(to_send, "fsdp", 0, 0).reshape(width, -1)
    inward_cols = weights[:, : 3 * head_cols]
    expand_cols = weights[:, 3 * head_cols :]
    outward_rows = lax.dynamic_slice_in_dim(outward, batch_index * head_cols, head_cols, 0)
    contract_rows = lax.dynamic_slice_in_dim(contract, batch_index * unit_cols, unit_cols, 0)
    plane_index = fsdp_index * batch_count + batch_index
    inward_shift_in = lax.dynamic_index_in_dim(
        inward_offset.reshape(3, plane, head_cols), plane_index, 1, keepdims=False
    ).reshape(-1)
    expand_shift_in = lax.dynamic_slice_in_dim(expand_offset, plane_index * unit_cols, unit_cols, 0)

    pair = jnp.stack([layer_input[0], out_grad[0]])
    pair_all = lax.all_gather(pair, PLANE, axis=1, tiled=True)
    grads_all = pair_all[1]
    rows_all = pair_all[0].astype(jnp.float32)
    normed, inverse = normalize(rows_all)
    first_rows = (normed * gain_first + offset_first).astype(jnp.bfloat16)
    second_rows = (normed * gain_second + offset_second).astype(jnp.bfloat16)

    local_place = slot_positions(span_order, context_index * tokens, tokens, span_size)
    cosine, sine_table = rotary_tables(local_place)
    cosine_plane = jnp.tile(cosine, (plane, 1))
    sine_plane = jnp.tile(sine_table, (plane, 1))
    projected = dot(first_rows, inward_cols) + inward_shift_in
    projected = projected.reshape(plane * tokens, 3 * heads, HEAD_DIM)
    turned = rotate(projected[:, : 2 * heads], cosine_plane, sine_plane)
    context_grad = dot(grads_all, outward_rows, ((1,), (1,)))
    mixed = jnp.concatenate(
        [
            turned.reshape(plane * tokens, -1),
            projected[:, 2 * heads :].reshape(plane * tokens, -1),
            context_grad,
        ],
        axis=1,
    ).astype(jnp.bfloat16)
    mixed = mixed.reshape(context_count, own_sequences, tokens, 4 * head_cols)
    mixed = lax.all_to_all(mixed, "ctx", 0, 0)
    mixed = mixed.transpose(1, 0, 2, 3).reshape(own_sequences, length, 4 * head_cols)
    place = slot_positions(span_order, 0, length, span_size)
    cosine_all, sine_all = rotary_tables(place)

    before = dot(second_rows, expand_cols) + expand_shift_in
    tail = 1.0 + lax.erf(before * HALF_ROOT)
    activated = (0.5 * before * tail).astype(jnp.bfloat16)
    slope = 0.5 * tail + before * jnp.exp(-0.5 * before * before) * NORMAL_PEAK
    before_grad = dot(grads_all, contract_rows, ((1,), (1,))) * slope
    expand_sum = jnp.sum(before_grad, axis=0)
    before_rows = before_grad.astype(jnp.bfloat16)
    expand_delta = dot(second_rows, before_rows, ((0,), (0,)))
    contract_delta = dot(activated, grads_all, ((0,), (0,)))
    out_part = dot(activated, contract_rows)
    second_part = dot(before_rows, expand_cols, ((1,), (1,)))

    hidden = layer_input[0].astype(jnp.float32)
    grad_float = out_grad[0].astype(jnp.float32)
    normed_mine, inverse_mine = normalize(hidden)
    half = width // fsdp_count

    def spread(values, sizes):
        wide = jnp.zeros((sizes[0], plane, sizes[1]), jnp.float32)
        values = values.reshape(sizes[0], sizes[1])
        return lax.dynamic_update_index_in_dim(wide, values, plane_index, 1).reshape(-1)

    bias_total = jnp.sum(grad_float, axis=0)
    expand_wide = spread(expand_sum, (1, unit_cols))

    back, inward_sum = attention(mixed, place, cosine_all, sine_all, heads)
    back = back.reshape(own_sequences, context_count, tokens, 4 * head_cols)
    back = lax.all_to_all(back.transpose(1, 0, 2, 3), "ctx", 0, 0)
    back = back.reshape(plane * tokens, 4 * head_cols)
    context_rows = back[:, :head_cols]
    projected_rows = back[:, head_cols:]
    inward_delta = dot(first_rows, projected_rows, ((0,), (0,)))
    outward_delta = dot(context_rows, grads_all, ((0,), (0,)))
    out_part = out_part + dot(context_rows, outward_rows)
    first_part = dot(projected_rows, inward_cols, ((1,), (1,)))
    stacked = jnp.stack([second_part, out_part, first_part], axis=1).astype(jnp.bfloat16)
    mine = lax.psum_scatter(stacked, PLANE, scatter_dimension=0, tiled=True)
    mine = mine.transpose(1, 0, 2).astype(jnp.float32)
    columns = jnp.concatenate([inward_delta, expand_delta], axis=1).astype(jnp.bfloat16)
    rows = jnp.concatenate([outward_delta, contract_delta], axis=0).astype(jnp.bfloat16)
    columns, rows = lax.psum((columns, rows), "ctx")
    columns = lax.all_to_all(columns.reshape(fsdp_count, half, -1), "fsdp", 0, 0)
    columns = lax.all_gather(columns, "batch")
    rows = lax.all_gather(rows, "batch").astype(jnp.float32)
    columns = columns.transpose(2, 1, 0, 3).astype(jnp.float32)
    inward_total = columns[..., : 3 * head_cols].reshape(
        half, fsdp_count, batch_count, 3, head_cols
    )
    totals = (
        inward_total.transpose(0, 3, 1, 2, 4).reshape(half, 3 * width),
        rows[:, :head_cols].reshape(half, width),
        columns[..., 3 * head_cols :].reshape(half, hidden_units),
        rows[:, head_cols:].reshape(-1, width),
    )
    _, second_scale, second_shift = norm_backward(
        mine[0], normed_mine, inverse_mine, gain_second
    )
    _, first_scale, first_shift = norm_backward(mine[2], normed_mine, inverse_mine, gain_first)
    vectors = [
        spread(inward_sum, (3, head_cols)),
        bias_total,
        expand_wide,
        first_scale,
        first_shift,
        second_scale,
        second_shift,
    ]
    whole = lax.psum(jnp.concatenate(vectors), ("batch", "ctx", "fsdp"))

    result = (hidden + (mine[1] + outward_offset) + contract_offset).astype(jnp.bfloat16)
    second_input, _, _ = norm_backward(mine[0], normed_mine, inverse_mine, gain_second)
    first_input, _, _ = norm_backward(mine[2], normed_mine, inverse_mine, gain_first)
    input_delta = grad_float + first_input + second_input
    halves, start = ([], 0)
    for vector in vectors:
        size = vector.shape[0] // fsdp_count
        halves.append(lax.dynamic_slice_in_dim(whole, start + fsdp_index * size, size, 0))
        start += vector.shape[0]
    return (
        result[None],
        input_delta[None],
        totals[0],
        halves[0],
        totals[1],
        halves[1],
        totals[2],
        halves[2],
        totals[3],
        halves[1],
        halves[3],
        halves[4],
        halves[5],
        halves[6],
    )


def body(
    layer_input,
    out_grad,
    span_order,
    inward,
    inward_bias,
    outward,
    outward_bias,
    expand,
    expand_bias,
    contract,
    contract_bias,
    first_gain,
    first_bias,
    second_gain,
    second_bias,
):
    plane = lax.axis_size("batch") * lax.axis_size("fsdp")
    width = layer_input.shape[2]
    if width // plane % 128:
        return plain_body(
            layer_input,
            out_grad,
            span_order,
            inward,
            inward_bias,
            outward,
            outward_bias,
            expand,
            expand_bias,
            contract,
            contract_bias,
            first_gain,
            first_bias,
            second_gain,
            second_bias,
        )
    vectors = (
        inward_bias,
        outward_bias,
        expand_bias,
        contract_bias,
        first_gain,
        first_bias,
        second_gain,
        second_bias,
    )
    ends = [sum(v.shape[0] for v in vectors[: i + 1]) for i in range(len(vectors))]
    room = ends[-1] + -ends[-1] % 1024
    small = sum(
        jnp.pad(v.astype(jnp.float32), (end - v.shape[0], room - end))
        for v, end in zip(vectors, ends)
    ).reshape(-1, 128)
    sums, result, input_delta, shifts = layer(
        layer_input, out_grad, span_order, small, inward, outward, expand, contract
    )
    return widen(sums, result, input_delta, shifts, width // plane, expand.shape[1] // plane)


def solution(mesh):
    rows = P(PLANE, "ctx", None)
    matrix, vector = (P("fsdp", None), P("fsdp"))
    in_specs = (rows, rows, P()) + (matrix, vector) * 4 + (vector,) * 4
    out_specs = (rows, rows) + (matrix, vector) * 4 + (vector,) * 4
    return jax.shard_map(body, mesh=mesh, in_specs=in_specs, out_specs=out_specs, check_vma=False)
```
